32 devices in a mesh: section: 2 (over core), seq: 4 (over y, x), dp: 4 (over z).
Axes of the slice: x: 2, y: 2, z: 4, core: 2. Of those that a mesh axis runs over, the one named last changes fastest.
Arguments:
- inputs: bfloat16 [2, 4, 1024, 1024], P(None, 'dp', 'seq'), may hold values from -6 to 6
- cotangent: bfloat16 [2, 4, 1024, 1024], P(None, 'dp', 'seq'), may hold values from -6 to 6
- segments: int32 [2, 4, 1024], P(None, 'dp'), may hold values from 0 to 5, never falling along the last dimension, each value on 1 to 800 neighbouring positions
- buckets: int32 [2048], replicated, may hold values from 0 to 31
- query_weight: bfloat16 [2, 1024, 1024], P('section', 'dp'), may hold values from -0.0234375 to 0.0234375
- key_weight: bfloat16 [2, 1024, 1024], P('section', 'dp'), may hold values from -0.1875 to 0.1875
- value_weight: bfloat16 [2, 1024, 1024], P('section', 'dp'), may hold values from -0.1875 to 0.1875
- out_weight: bfloat16 [2, 1024, 1024], P('section', 'dp'), may hold values from -0.75 to 0.75
- up_weight: bfloat16 [2, 1024, 4096], P('section', 'dp'), may hold values from -0.1875 to 0.1875
- down_weight: bfloat16 [2, 4096, 1024], P('section', 'dp'), may hold values from -0.09375 to 0.09375
- attn_gain: bfloat16 [2, 1024], P('section', 'dp'), may hold values from 0.099609375 to 1.8984375
- ffn_gain: bfloat16 [2, 1024], P('section', 'dp'), may hold values from 0.099609375 to 1.8984375
- bias_table: bfloat16 [2, 32, 16], P('section', None, 'seq'), may hold values from -4 to 4
Outputs:
- section_outputs: bfloat16 [2, 2, 4, 1024, 1024], P('section', None, 'dp', 'seq')
- input_grads: float32 [2, 2, 4, 1024, 1024], P('section', None, 'dp', 'seq')
- grad_query: float32 [2, 1024, 1024], P('section', 'dp')
- grad_key: float32 [2, 1024, 1024], P('section', 'dp')
- grad_value: float32 [2, 1024, 1024], P('section', 'dp')
- grad_out: float32 [2, 1024, 1024], P('section', 'dp')
- grad_up: float32 [2, 1024, 4096], P('section', 'dp')
- grad_down: float32 [2, 4096, 1024], P('section', 'dp')
- grad_attn_gain: float32 [2, 1024], P('section', 'dp')
- grad_ffn_gain: float32 [2, 1024], P('section', 'dp')
- grad_table: float32 [2, 32, 16], P('section', 'dp', 'seq')
The draws below stay inside these ranges and needn't reach their ends.
Inputs may be any that keep to these rules, and one draw needn't show every extreme that they name: `segments`: document numbers never fall along a sequence, each document holds 1 to 800 tokens, and one holds exactly 800.
All inputs are finite; a program needn't handle non-finite values.
Results may differ from the reference program's by a relative error of at most 0.025.
Values may be sent and summed in bfloat16 or wider, within the bound.
A program may use at most 576 MiB of HBM per device.

```python
import math
import jax
import jax.numpy as jnp
import numpy as np
from jax import lax

D = 1024
H = 16
DK = 64
FF = 4096
NB = 32
L = 1024
MB = 2
SEQS = 4
DOCS = 6
DOC_MOST = 800


def touch_ends(entries, rng, smallest, largest):
    longest = entries.shape.index(max(entries.shape))
    spots = []
    for shift in (0, 1):
        where = [jax.random.randint(jax.random.fold_in(rng, axis), (), 0, length) for axis, length in enumerate(entries.shape)]
        where[longest] = (where[longest] + shift) % entries.shape[longest]
        spots.append(tuple(where))
    return entries.at[spots[0]].set(smallest).at[spots[1]].set(largest)


def block_scale(own_key, dims, pieces, least, top_value):
    level, own = 1.0, jax.random.fold_in(own_key, 6)
    for dim, shards_of in pieces:
        steps = jnp.exp(jax.random.uniform(jax.random.fold_in(own, dim), (shards_of,), jnp.float32, least / len(pieces), top_value / len(pieces)))
        level = level * jnp.repeat(steps, dims[dim] // shards_of).reshape([-1 if axis == dim else 1 for axis in range(len(dims))])
    return level


def profile(amount, total, limit, lean):
    loads = [(1 << 20) // math.isqrt(standing ** lean) + 1 for standing in range(2, amount + 1)]
    spare, given = total - limit - (amount - 1), [1] * (amount - 1)
    while spare > 0:
        candidates = [i for i in range(amount - 1) if given[i] < limit]
        mass, remaining = sum([loads[i] for i in candidates]), spare
        for i in candidates:
            more = min(limit - given[i], max(1, remaining * loads[i] // mass), spare)
            given[i] = given[i] + more
            spare = spare - more
    return np.array([limit] + given)


def uneven_parts(own_key, count, total, reach, slope):
    if count == 2:
        one = jax.random.randint(own_key, (), max(1, total - reach), min(reach, total - 1) + 1)
        return jnp.stack([one, total - one])
    tallies = jnp.asarray(profile(count, total, reach, slope), jnp.int32)
    pairs = (count - 1) // 2
    donor, receiver = tallies[1:1 + 2 * pairs:2], tallies[2:2 + 2 * pairs:2]
    slack = jnp.minimum(donor - 1, reach - receiver)
    shifted = jax.random.randint(jax.random.fold_in(own_key, 1), (pairs,), 0, 1 << 20) % (slack + 1)
    tallies = tallies.at[1:1 + 2 * pairs:2].set(donor - shifted).at[2:2 + 2 * pairs:2].set(receiver + shifted)
    return tallies[jax.random.permutation(jax.random.fold_in(own_key, 2), count)]


def scatter_about(stream_key, dims, deviation, reach, shards=(), kind=jnp.bfloat16):
    drawn = deviation * jax.random.normal(stream_key, dims, jnp.float32)
    if shards:
        drawn = drawn * block_scale(stream_key, dims, shards, -0.22, 0.18)
    return jnp.clip(drawn, -reach, reach).astype(kind)


def setup_inputs(seed: int = 0) -> dict:
    keys = jax.random.split(jax.random.key(seed), 14)
    return {
        "inputs": scatter_about(keys[0], (MB, SEQS, L, D), 1.0, 6.0, ((1, 4), (2, 4))),
        "cotangent": scatter_about(keys[1], (MB, SEQS, L, D), 1.0, 6.0, ((1, 4), (2, 4))),
        "segments": jax.vmap(lambda own: jnp.searchsorted(jnp.cumsum(uneven_parts(own, DOCS, L, DOC_MOST, 0)), jnp.arange(L), side="right"))(jax.random.split(keys[2], MB * SEQS)).reshape((MB, SEQS, L)).astype(jnp.int32),
        "buckets": touch_ends(jax.random.randint(keys[3], (2 * L,), 0, NB), jax.random.fold_in(keys[3], 1), 0, NB - 1).astype(jnp.int32),
        "query_weight": scatter_about(keys[4], (2, D, H * DK), (D * DK) ** -0.5, 0.0234375, ((0, 2), (1, 4))),
        "key_weight": scatter_about(keys[5], (2, D, H * DK), D ** -0.5, 0.1875, ((0, 2), (1, 4))),
        "value_weight": scatter_about(keys[6], (2, D, H * DK), D ** -0.5, 0.1875, ((0, 2), (1, 4))),
        "out_weight": scatter_about(keys[7], (2, H * DK, D), (H * DK // 16) ** -0.5, 0.75, ((0, 2), (1, 4))),
        "up_weight": scatter_about(keys[8], (2, D, FF), D ** -0.5, 0.1875, ((0, 2), (1, 4))),
        "down_weight": scatter_about(keys[9], (2, FF, D), FF ** -0.5, 0.09375, ((0, 2), (1, 4))),
        "attn_gain": jnp.clip(1.0 + 0.18 * jax.random.normal(keys[10], (2, D), jnp.float32), 0.099609375, 1.8984375).astype(jnp.bfloat16),
        "ffn_gain": jnp.clip(1.0 + 0.18 * jax.random.normal(keys[11], (2, D), jnp.float32), 0.099609375, 1.8984375).astype(jnp.bfloat16),
        "bias_table": scatter_about(keys[12], (2, NB, H), 1.0, 4.0, ((0, 2), (2, 4))),
    }


HIGH = lax.Precision.HIGHEST
EPSILON = 1e-06
NEG = -1e+30

@jax.custom_vjp
def low(v):
    return lax.optimization_barrier(v.astype(jnp.bfloat16)).astype(jnp.float32)

@jax.custom_vjp
def low_back(v):
    return v

def low_keep(v):
    return (low(v), None)

def low_pass(kept, grad):
    return (grad,)

def back_keep(v):
    return (v, None)

def back_low(kept, grad):
    return (low(grad),)
low.defvjp(low_keep, low_pass)
low_back.defvjp(back_keep, back_low)

def norm_rows(rows, gain):
    return rows * lax.rsqrt(lax.optimization_barrier(jnp.mean(rows * rows, axis=-1, keepdims=True)) + EPSILON) * gain

def project(rows, weight):
    return jnp.einsum('btd,df->btf', rows, weight, precision=HIGH)

def attend_one(item, bias):
    query, key, value, seg = item
    scores = low_back(jnp.einsum('qhd,khd->hqk', query, key, precision=HIGH)) + bias
    same = seg[:, None] == seg[None, :]
    scores = jnp.where(same[None], scores, NEG)
    peak = lax.optimization_barrier(jnp.max(scores, axis=-1, keepdims=True))
    expo = jnp.exp(scores - peak)
    prob = low(expo / lax.optimization_barrier(jnp.sum(expo, axis=-1, keepdims=True)))
    return jnp.einsum('hqk,khd->qhd', prob, value, precision=HIGH)

def layer(rows, seg, params, buckets):
    w_query, w_key, w_value, w_out, w_up, w_down, g_attn, g_ffn, table = params
    batch = rows.shape[0]
    normed = low(norm_rows(rows, g_attn))
    query = low(low_back(project(normed, w_query))).reshape(batch, L, H, DK)
    key = low(low_back(project(normed, w_key))).reshape(batch, L, H, DK)
    value = low(low_back(project(normed, w_value))).reshape(batch, L, H, DK)
    offsets = (jnp.arange(L)[None, :] - jnp.arange(L)[:, None] + L).astype(jnp.int32)
    bias = jnp.transpose(table[buckets[offsets]], (2, 0, 1))
    single = jax.checkpoint(attend_one)

    def apply_one(item):
        return single(item, bias)
    mixed = lax.map(apply_one, (query, key, value, seg))
    mixed = low(low_back(mixed.reshape(batch, L, H * DK)))
    after = rows + low_back(project(mixed, w_out))
    normed2 = low(norm_rows(after, g_ffn))
    pre = low_back(project(normed2, w_up))
    hidden = low(jax.nn.gelu(pre, approximate=False))
    return after + low_back(project(hidden, w_down))

def reference(inputs, cotangent, segments, buckets, query_weight, key_weight, value_weight, out_weight, up_weight, down_weight, attn_gain, ffn_gain, bias_table):
    total = MB * SEQS
    seg = segments.reshape(total, L)
    start = inputs.astype(jnp.float32).reshape(total, L, D)
    params = tuple((w.astype(jnp.float32) for w in (query_weight, key_weight, value_weight, out_weight, up_weight, down_weight, attn_gain, ffn_gain, bias_table)))

    def forward(first_in, extra, weights):
        first_params = tuple((w[0] for w in weights))
        second_params = tuple((w[1] for w in weights))
        first_out = layer(first_in, seg, first_params, buckets)
        second_in = low(low_back(first_out)) + extra
        second_out = layer(second_in, seg, second_params, buckets)
        return (first_out, second_out)
    outs, pullback = jax.vjp(forward, start, jnp.zeros_like(start), params)
    first_out, second_out = outs
    grad_start, grad_extra, grad_params = pullback((jnp.zeros_like(first_out), cotangent.astype(jnp.float32).reshape(total, L, D)))
    section_outputs = jnp.stack([first_out, second_out]).reshape(2, MB, SEQS, L, D).astype(jnp.bfloat16)
    input_grads = jnp.stack([grad_start, grad_extra]).reshape(2, MB, SEQS, L, D)
    return (section_outputs, input_grads, grad_params[0], grad_params[1], grad_params[2], grad_params[3], grad_params[4], grad_params[5], grad_params[6], grad_params[7], grad_params[8])
```

```python
import functools
import math

import jax
import jax.numpy as jnp
from jax import lax
from jax.experimental import pallas as pl
from jax.experimental.pallas import tpu as pltpu
from jax.sharding import PartitionSpec as P

EPSILON = 1e-06
NEG = -1e30
HIGH = lax.Precision.HIGHEST
MESH = pl.DeviceIdType.MESH
F32 = jnp.float32
BF16 = jnp.bfloat16
LANES = 128
QB = 256
VMEM_BYTES = 56 << 20

WHOLE = pl.BlockSpec(memory_space=pltpu.VMEM)
AWAY = pl.BlockSpec(memory_space=pl.ANY)


def mm(left, right):
    return jnp.dot(left, right, preferred_element_type=F32)


def mm_nt(left, right):
    return lax.dot_general(left, right, (((1,), (1,)), ((), ())), preferred_element_type=F32)


def mm_tn(left, right):
    return lax.dot_general(left, right, (((0,), (0,)), ((), ())), preferred_element_type=F32)


def inverse_rms(rows):
    return lax.rsqrt(jnp.mean(rows * rows, axis=-1, keepdims=True) + EPSILON)


def aligned(start, size):
    return pl.ds(pl.multiple_of(start, size), size)


def greet(n):
    me = lax.axis_index("seq")
    barrier = pltpu.get_barrier_semaphore()
    for k in range(1, n):
        pl.semaphore_signal(
            barrier, inc=1, device_id={"seq": lax.rem(me + k, n)}, device_id_type=MESH
        )
    pl.semaphore_wait(barrier, n - 1)


def push(src, dst, send_sem, recv_sem, peer):
    return pltpu.make_async_remote_copy(
        src_ref=src,
        dst_ref=dst,
        send_sem=send_sem,
        recv_sem=recv_sem,
        device_id={"seq": peer},
        device_id_type=MESH,
    )


def params(collective_id=None):
    return pltpu.CompilerParams(
        collective_id=collective_id,
        has_side_effects=collective_id is not None,
        vmem_limit_bytes=VMEM_BYTES,
    )


def shape(dims, dtype):
    return jax.ShapeDtypeStruct(dims, dtype)


def gather_kernel(n, x_ref, gain_ref, out_ref, send, recv):
    tl = x_ref.shape[0]
    me = lax.axis_index("seq")
    mine = aligned(me * tl, tl)
    rows = x_ref[...].astype(F32)
    out_ref[mine] = (rows * inverse_rms(rows) * gain_ref[...]).astype(BF16)
    greet(n)
    copies = []
    for k in range(1, n):
        copy = push(
            out_ref.at[mine], out_ref.at[mine], send.at[k], recv.at[k], lax.rem(me + k, n)
        )
        copy.start()
        copies.append(copy)
    for copy in copies:
        copy.wait()


def norm_gather(n, x, gain):
    tl, width = x.shape
    return pl.pallas_call(
        functools.partial(gather_kernel, n),
        out_shape=shape((n * tl, width), BF16),
        in_specs=[WHOLE] * 2,
        out_specs=WHOLE,
        scratch_shapes=[pltpu.SemaphoreType.DMA((n,)), pltpu.SemaphoreType.DMA((n,))],
        compiler_params=params(0),
        name="norm_gather",
    )(x, gain)


def toeplitz_rows(offset_row):
    spread = jnp.broadcast_to(offset_row, (LANES, offset_row.shape[1]))
    return pltpu.roll(spread, 0, 1, stride=1, stride_axis=0)


def attend_kernel(heads, dk, q_ref, k_ref, v_ref, eq_ref, ek_ref, rows_ref, o_ref, lse_ref,
                  bias_ref, kt_ref, qa_ref):
    length = q_ref.shape[0]
    lane = lax.broadcasted_iota(jnp.int32, (length, LANES), 1)
    lane_q = lax.broadcasted_iota(jnp.int32, (LANES, LANES), 1)
    for head in range(heads):
        pair = pl.ds((head // 2) * LANES, LANES)
        inside = (lane >= dk) if head % 2 else (lane < dk)
        qa_ref[...] = jnp.where(inside, q_ref[:, pair], eq_ref[...])
        kt_ref[...] = jnp.where(inside, k_ref[:, pair], ek_ref[...]).T
        bias_ref[...] = toeplitz_rows(rows_ref[head : head + 1, :])
        inside_q = (lane_q >= dk) if head % 2 else (lane_q < dk)

        def block(b, carry, head=head, pair=pair, inside_q=inside_q):
            scores = mm(qa_ref[aligned(b * QB, QB), :], kt_ref[...])
            for a in range(QB // LANES):
                tile = b * (QB // LANES) + a
                where = aligned(tile * LANES, LANES)
                off = aligned(length - tile * LANES, LANES)
                off = pl.ds(off.start, length)
                part = scores[a * LANES : (a + 1) * LANES] + bias_ref[:, off]
                peak = jnp.max(part, axis=-1, keepdims=True)
                expo = jnp.exp(part - peak)
                total = jnp.sum(expo, axis=-1, keepdims=True)
                mixed = mm(expo.astype(BF16), v_ref[:, pair]) * (1.0 / total)
                lse = peak + jnp.log(total)
                if head % 2:
                    o_ref[where, pair] = jnp.where(inside_q, mixed.astype(BF16), o_ref[where, pair])
                else:
                    o_ref[where, pair] = mixed.astype(BF16)
                if head:
                    lse_ref[where, :] = jnp.where(lane_q == head, lse, lse_ref[where, :])
                else:
                    lse_ref[where, :] = jnp.broadcast_to(lse, (LANES, LANES))
            return carry

        lax.fori_loop(0, length // QB, block, 0)


def attend(heads, dk, q, k, v, ext_q, ext_k, offset_rows):
    length, width = q.shape
    span = offset_rows.shape[1]
    return pl.pallas_call(
        functools.partial(attend_kernel, heads, dk),
        out_shape=(shape((length, width), BF16), shape((length, LANES), F32)),
        in_specs=[WHOLE] * 6,
        out_specs=(WHOLE, WHOLE),
        scratch_shapes=[
            pltpu.VMEM((LANES, span), F32),
            pltpu.VMEM((LANES, length), BF16),
            pltpu.VMEM((length, LANES), BF16),
        ],
        compiler_params=params(),
        name="attend",
    )(q, k, v, ext_q, ext_k, offset_rows)


def three_parts(lane, value):
    first = value.astype(BF16).astype(F32)
    rest = value - first
    second = rest.astype(BF16).astype(F32)
    third = rest - second
    at = lax.rem(lane, 64)
    return jnp.where(at == 8, first, jnp.where(at == 9, second, jnp.where(at == 10, third, 0.0)))


def attend_back_kernel(heads, dk, q_ref, k_ref, v_ref, do_ref, o_ref, lse_ref, eq_ref, ek_ref,
                       rows_ref, dq_ref, dk_ref, dv_ref, dr_ref,
                       bias_ref, kt_ref, vt_ref, qa_ref, da_ref, qt_ref, dot_ref,
                       dkt_ref, dvt_ref, dbias_ref):
    length = q_ref.shape[0]
    span = rows_ref.shape[1]
    lane = lax.broadcasted_iota(jnp.int32, (length, LANES), 1)
    lane_q = lax.broadcasted_iota(jnp.int32, (QB, LANES), 1)
    at = lax.rem(lane, 64)
    parts = (at >= 8) & (at <= 10)
    ones = jnp.where(parts, 1.0, 0.0)
    for head in range(heads):
        pair = pl.ds((head // 2) * LANES, LANES)
        upper = head % 2 == 1
        inside = (lane >= dk) if upper else (lane < dk)
        inside_q = (lane_q >= dk) if upper else (lane_q < dk)
        q_pair, k_pair, v_pair, do_pair = q_ref[:, pair], k_ref[:, pair], v_ref[:, pair], do_ref[:, pair]
        if not upper:
            qt_ref[...] = q_pair.T
            dot_ref[...] = do_pair.T
        lse = lse_ref[:, head : head + 1]
        eq = (eq_ref[...].astype(F32) - three_parts(lane, lse)).astype(BF16)
        ek = (ek_ref[...].astype(F32) + ones).astype(BF16)
        qa_ref[...] = jnp.where(inside, q_pair, eq)
        kt_ref[...] = jnp.where(inside, k_pair, ek).T
        weighed = do_pair.astype(F32) * o_ref[:, pair].astype(F32)
        delta = jnp.sum(jnp.where(inside, weighed, 0.0), axis=-1, keepdims=True)
        da_ref[...] = jnp.where(inside, do_pair, (-three_parts(lane, delta)).astype(BF16))
        vt_ref[...] = jnp.where(inside, v_pair, ones.astype(BF16)).T
        bias_ref[...] = toeplitz_rows(rows_ref[head : head + 1, :])
        dkt_ref[...] = jnp.zeros_like(dkt_ref)
        dvt_ref[...] = jnp.zeros_like(dvt_ref)
        dbias_ref[...] = jnp.zeros_like(dbias_ref)
        half = pl.ds(dk if upper else 0, dk)

        def block(b, carry, pair=pair, inside_q=inside_q, upper=upper, half=half):
            where = aligned(b * QB, QB)
            scores = mm(qa_ref[where, :], kt_ref[...])
            lifted = mm(da_ref[where, :], vt_ref[...])
            probs, grads = [], []
            for a in range(QB // LANES):
                cut = slice(a * LANES, (a + 1) * LANES)
                tile = b * (QB // LANES) + a
                off = pl.ds(pl.multiple_of(length - tile * LANES, LANES), length)
                prob = jnp.exp(scores[cut] + bias_ref[:, off])
                grad = prob * lifted[cut]
                dbias_ref[:, off] += grad
                probs.append(prob.astype(BF16))
                grads.append(grad.astype(BF16))
            prob = jnp.concatenate(probs, axis=0)
            grad = jnp.concatenate(grads, axis=0)
            dq = mm(grad, k_ref[:, pair]).astype(BF16)
            if upper:
                dq_ref[where, pair] = jnp.where(inside_q, dq, dq_ref[where, pair])
            else:
                dq_ref[where, pair] = dq
            dkt_ref[half, :] += mm(qt_ref[half, where], grad)
            dvt_ref[half, :] += mm(dot_ref[half, where], prob)
            return carry

        lax.fori_loop(0, length // QB, block, 0)
        if upper:
            dk_ref[:, pair] = jnp.where(inside, dkt_ref[...].T.astype(BF16), dk_ref[:, pair])
            dv_ref[:, pair] = jnp.where(inside, dvt_ref[...].T.astype(BF16), dv_ref[:, pair])
        else:
            dk_ref[:, pair] = dkt_ref[...].T.astype(BF16)
            dv_ref[:, pair] = dvt_ref[...].T.astype(BF16)
        folded = dbias_ref[...]
        rows = LANES
        while rows > 8:
            rows //= 2
            folded = folded[:rows] + pltpu.roll(folded[rows:], span - rows, 1)
        place = lax.broadcasted_iota(jnp.int32, (8, span), 0)
        for bit in (4, 2, 1):
            folded = jnp.where(
                lax.rem(lax.div(place, bit), 2) == 1, pltpu.roll(folded, span - bit, 1), folded
            )
        dr_ref[head : head + 1, :] = jnp.sum(folded, axis=0, keepdims=True)


def attend_back(heads, dk, q, k, v, do, o, lse, ext_q, ext_k, offset_rows):
    length, width = q.shape
    span = offset_rows.shape[1]
    out = shape((length, width), BF16)
    return pl.pallas_call(
        functools.partial(attend_back_kernel, heads, dk),
        out_shape=(out, out, out, shape((heads, span), F32)),
        in_specs=[WHOLE] * 9,
        out_specs=(WHOLE,) * 4,
        scratch_shapes=[
            pltpu.VMEM((LANES, span), F32),
            pltpu.VMEM((LANES, length), BF16),
            pltpu.VMEM((LANES, length), BF16),
            pltpu.VMEM((length, LANES), BF16),
            pltpu.VMEM((length, LANES), BF16),
            pltpu.VMEM((LANES, length), BF16),
            pltpu.VMEM((LANES, length), BF16),
            pltpu.VMEM((LANES, length), F32),
            pltpu.VMEM((LANES, length), F32),
            pltpu.VMEM((LANES, span), F32),
        ],
        compiler_params=params(),
        name="attend_back",
    )(q, k, v, do, o, lse, ext_q, ext_k, offset_rows)


def mix_kernel(n, o_ref, x_ref, gain_ref, wo_any, up_any, down_any,
               y_ref, x1_ref, n2_ref, slope_ref, hid_ref, back_ref,
               wo_ref, up_ref, down_ref, out_ref, got_ref, total_ref,
               load, send_o, recv_o, send_n, recv_n, send_y, recv_y):
    tl = x_ref.shape[0]
    hw = o_ref.shape[1]
    me = lax.axis_index("seq")
    mine = aligned(me * tl, tl)
    loads = [
        pltpu.make_async_copy(wo_any, wo_ref, load.at[0]),
        pltpu.make_async_copy(up_any, up_ref, load.at[1]),
        pltpu.make_async_copy(down_any, down_ref, load.at[2]),
    ]
    for copy in loads:
        copy.start()
    greet(n)
    sent = []
    for k in range(1, n):
        peer = lax.rem(me + k, n)
        copy = push(o_ref.at[aligned(peer * tl, tl)], back_ref.at[me], send_o.at[k], recv_o.at[k], peer)
        copy.start()
        sent.append(copy)
    back_ref[me] = o_ref[mine]
    loads[0].wait()
    total_ref[...] = x_ref[...].astype(F32) + mm(back_ref[me], wo_ref[aligned(me * hw, hw), :])
    for k in range(1, n):
        source = lax.rem(me + n - k, n)
        sent[k - 1].wait_recv()
        total_ref[...] += mm(back_ref[source], wo_ref[aligned(source * hw, hw), :])
    x1 = total_ref[...]
    x1_ref[...] = x1
    n2_ref[mine] = (x1 * inverse_rms(x1) * gain_ref[...]).astype(BF16)
    spread = []
    for k in range(1, n):
        copy = push(n2_ref.at[mine], n2_ref.at[mine], send_n.at[k], recv_n.at[k], lax.rem(me + k, n))
        copy.start()
        spread.append(copy)
    loads[1].wait()
    loads[2].wait()

    def chunk(k, carry):
        source = lax.rem(me + n - k, n)
        where = aligned(source * tl, tl)

        @pl.when(k > 0)
        def _():
            push(n2_ref.at[mine], n2_ref.at[where], send_n.at[k], recv_n.at[k], source).wait_recv()

        u = mm(n2_ref[where], up_ref[...])
        half = 0.5 + 0.5 * lax.erf(u * math.sqrt(0.5))
        hid = (u * half).astype(BF16)
        hid_ref[where] = hid
        slope_ref[where] = (
            half + u * (jnp.exp(-0.5 * u * u) * (1.0 / math.sqrt(2.0 * math.pi)))
        ).astype(BF16)
        part = mm(hid, down_ref[...])

        @pl.when(k == 0)
        def _():
            total_ref[...] += part

        @pl.when(k > 0)
        def _():
            out_ref[k] = part.astype(BF16)
            push(out_ref.at[k], got_ref.at[k], send_y.at[k], recv_y.at[k], source).start()

        return carry

    lax.fori_loop(0, n, chunk, 0)
    for k in range(1, n):
        push(out_ref.at[k], got_ref.at[k], send_y.at[k], recv_y.at[k], me).wait_recv()
        total_ref[...] += got_ref[k].astype(F32)
    y_ref[...] = total_ref[...].astype(BF16)
    for copy in sent + spread:
        copy.wait_send()
    for k in range(1, n):
        push(out_ref.at[k], got_ref.at[k], send_y.at[k], recv_y.at[k], me).wait_send()


def mix(n, o, x, gain, wo, up, down):
    tl, width = x.shape
    hw = o.shape[1]
    ff = up.shape[1]
    sems = pltpu.SemaphoreType.DMA((n,))
    return pl.pallas_call(
        functools.partial(mix_kernel, n),
        out_shape=(
            shape((tl, width), BF16),
            shape((tl, width), F32),
            shape((n * tl, width), BF16),
            shape((n * tl, ff), BF16),
            shape((n * tl, ff), BF16),
            shape((n, tl, hw), BF16),
        ),
        in_specs=[WHOLE] * 3 + [AWAY] * 3,
        out_specs=(WHOLE,) * 6,
        scratch_shapes=[
            pltpu.VMEM(wo.shape, BF16),
            pltpu.VMEM(up.shape, BF16),
            pltpu.VMEM(down.shape, BF16),
            pltpu.VMEM((n, tl, width), BF16),
            pltpu.VMEM((n, tl, width), BF16),
            pltpu.VMEM((tl, width), F32),
            pltpu.SemaphoreType.DMA((3,)),
            sems, sems, sems, sems, sems, sems,
        ],
        compiler_params=params(1),
        name="mix",
    )(o, x, gain, wo, up, down)


def mix_back_kernel(n, dy_ref, x1_ref, gain_ref, slope_ref, hid_ref, n2_ref, back_ref,
                    wo_any, up_any, down_any,
                    dx1_ref, do_ref, g_down_ref, g_up_ref, g_out_ref, g_gain_ref,
                    wo_ref, up_ref, down_ref, dy_all, out_ref, got_ref, total_ref,
                    sum_down, sum_up, do_out,
                    load, send_d, recv_d, send_n, recv_n, send_o, recv_o):
    tl = dy_ref.shape[0]
    hw = do_ref.shape[1]
    me = lax.axis_index("seq")
    mine = aligned(me * tl, tl)
    loads = [
        pltpu.make_async_copy(down_any, down_ref, load.at[0]),
        pltpu.make_async_copy(up_any, up_ref, load.at[1]),
        pltpu.make_async_copy(wo_any, wo_ref, load.at[2]),
    ]
    for copy in loads:
        copy.start()
    greet(n)
    spread = []
    for k in range(1, n):
        copy = push(dy_ref, dy_all.at[mine], send_d.at[k], recv_d.at[k], lax.rem(me + k, n))
        copy.start()
        spread.append(copy)
    dy_all[mine] = dy_ref[...]
    sum_down[...] = jnp.zeros_like(sum_down)
    sum_up[...] = jnp.zeros_like(sum_up)
    loads[0].wait()
    loads[1].wait()

    def chunk(k, carry):
        source = lax.rem(me + n - k, n)
        where = aligned(source * tl, tl)

        @pl.when(k > 0)
        def _():
            push(dy_ref, dy_all.at[where], send_d.at[k], recv_d.at[k], source).wait_recv()

        dy = dy_all[where]
        du = (mm_nt(dy, down_ref[...]) * slope_ref[where].astype(F32)).astype(BF16)
        part = mm_nt(du, up_ref[...])

        @pl.when(k == 0)
        def _():
            total_ref[...] = part

        @pl.when(k > 0)
        def _():
            out_ref[k] = part.astype(BF16)
            push(out_ref.at[k], got_ref.at[k], send_n.at[k], recv_n.at[k], source).start()

        sum_down[...] += mm_tn(hid_ref[where], dy)
        sum_up[...] += mm_tn(n2_ref[where], du)
        return carry

    lax.fori_loop(0, n, chunk, 0)
    g_down_ref[...] = sum_down[...].astype(BF16)
    g_up_ref[...] = sum_up[...].astype(BF16)
    for k in range(1, n):
        push(out_ref.at[k], got_ref.at[k], send_n.at[k], recv_n.at[k], me).wait_recv()
        total_ref[...] += got_ref[k].astype(F32)
    dn2 = total_ref[...]
    x1 = x1_ref[...]
    inv = inverse_rms(x1)
    scaled = x1 * inv
    g_gain_ref[...] = jnp.sum(dn2 * scaled, axis=0, keepdims=True)
    lifted = dn2 * gain_ref[...]
    dx1 = dy_ref[...].astype(F32) + inv * (
        lifted - scaled * jnp.mean(lifted * scaled, axis=-1, keepdims=True)
    )
    dx1_ref[...] = dx1
    d_attn = dx1.astype(BF16)
    loads[2].wait()
    returned = []
    for k in range(1, n):
        peer = lax.rem(me + k, n)
        do_out[k] = mm_nt(d_attn, wo_ref[aligned(peer * hw, hw), :]).astype(BF16)
        copy = push(do_out.at[k], do_ref.at[mine], send_o.at[k], recv_o.at[k], peer)
        copy.start()
        returned.append(copy)
    do_ref[mine] = mm_nt(d_attn, wo_ref[aligned(me * hw, hw), :]).astype(BF16)
    for s in range(n):
        g_out_ref[s] = mm_tn(back_ref[s], d_attn).astype(BF16)
    for copy in spread:
        copy.wait_send()
    for k in range(1, n):
        push(out_ref.at[k], got_ref.at[k], send_n.at[k], recv_n.at[k], me).wait_send()
    for copy in returned:
        copy.wait()


def mix_back(n, dy, x1, gain, slope, hid, n2, back, wo, up, down):
    tl, width = dy.shape
    hw = back.shape[2]
    ff = up.shape[1]
    sems = pltpu.SemaphoreType.DMA((n,))
    return pl.pallas_call(
        functools.partial(mix_back_kernel, n),
        out_shape=(
            shape((tl, width), F32),
            shape((n * tl, hw), BF16),
            shape((ff, width), BF16),
            shape((width, ff), BF16),
            shape((n, hw, width), BF16),
            shape((1, width), F32),
        ),
        in_specs=[WHOLE] * 7 + [AWAY] * 3,
        out_specs=(WHOLE,) * 6,
        scratch_shapes=[
            pltpu.VMEM(wo.shape, BF16),
            pltpu.VMEM(up.shape, BF16),
            pltpu.VMEM(down.shape, BF16),
            pltpu.VMEM((n * tl, width), BF16),
            pltpu.VMEM((n, tl, width), BF16),
            pltpu.VMEM((n, tl, width), BF16),
            pltpu.VMEM((tl, width), F32),
            pltpu.VMEM((ff, width), F32),
            pltpu.VMEM((width, ff), F32),
            pltpu.VMEM((n, tl, hw), BF16),
            pltpu.SemaphoreType.DMA((3,)),
            sems, sems, sems, sems, sems, sems,
        ],
        compiler_params=params(2),
        name="mix_back",
    )(dy, x1, gain, slope, hid, n2, back, wo, up, down)


def project_back_kernel(n, dqkv_ref, x_ref, dx1_ref, gain_ref, n1_ref, w_any,
                        dx_ref, low_ref, g_w_ref, g_gain_ref,
                        w_ref, out_ref, got_ref, total_ref, load, send, recv):
    tl = x_ref.shape[0]
    me = lax.axis_index("seq")
    mine = aligned(me * tl, tl)
    weight = pltpu.make_async_copy(w_any, w_ref, load.at[0])
    weight.start()
    greet(n)
    weight.wait()
    copies = []
    for k in range(1, n):
        peer = lax.rem(me + k, n)
        out_ref[k] = mm_nt(dqkv_ref[aligned(peer * tl, tl), :], w_ref[...]).astype(BF16)
        copy = push(out_ref.at[k], got_ref.at[k], send.at[k], recv.at[k], peer)
        copy.start()
        copies.append(copy)
    total_ref[...] = mm_nt(dqkv_ref[mine, :], w_ref[...])
    g_w_ref[...] = mm_tn(n1_ref[...], dqkv_ref[...]).astype(BF16)
    for k in range(1, n):
        copies[k - 1].wait_recv()
        total_ref[...] += got_ref[k].astype(F32)
    dn1 = total_ref[...]
    rows = x_ref[...].astype(F32)
    inv = inverse_rms(rows)
    scaled = rows * inv
    g_gain_ref[...] = jnp.sum(dn1 * scaled, axis=0, keepdims=True)
    lifted = dn1 * gain_ref[...]
    dx = dx1_ref[...] + inv * (lifted - scaled * jnp.mean(lifted * scaled, axis=-1, keepdims=True))
    dx_ref[...] = dx
    low_ref[...] = dx.astype(BF16)
    for copy in copies:
        copy.wait_send()


def project_back(n, dqkv, x, dx1, gain, n1, w):
    tl, width = x.shape
    sems = pltpu.SemaphoreType.DMA((n,))
    return pl.pallas_call(
        functools.partial(project_back_kernel, n),
        out_shape=(
            shape((tl, width), F32),
            shape((tl, width), BF16),
            shape(w.shape, BF16),
            shape((1, width), F32),
        ),
        in_specs=[WHOLE] * 5 + [AWAY],
        out_specs=(WHOLE,) * 4,
        scratch_shapes=[
            pltpu.VMEM(w.shape, BF16),
            pltpu.VMEM((n, tl, width), BF16),
            pltpu.VMEM((n, tl, width), BF16),
            pltpu.VMEM((tl, width), F32),
            pltpu.SemaphoreType.DMA((1,)),
            sems, sems,
        ],
        compiler_params=params(3),
        name="project_back",
    )(dqkv, x, dx1, gain, n1, w)


def swapped(value):
    return lax.ppermute(value, "section", [(0, 1), (1, 0)])


def body(inputs, cotangent, segments, buckets, query_weight, key_weight, value_weight, out_weight,
         up_weight, down_weight, attn_gain, ffn_gain, bias_table):
    first = lax.axis_index("section") == 0
    turn = lax.axis_index("seq")
    n = lax.axis_size("seq")
    shards = lax.axis_size("dp")
    depth, width = query_weight.shape[1:]
    ff = up_weight.shape[2]
    heads = bias_table.shape[2]
    hw = width // n
    dk = hw // heads
    kept = down_weight.shape[1] // n
    length = segments.shape[-1]
    model = inputs.shape[-1]

    x_in = jnp.where(first, inputs[0, 0], inputs[1, 0])
    d_out = jnp.where(first, cotangent[0, 0], cotangent[1, 0])
    seg = jnp.where(first, segments[0, 0], segments[1, 0])

    def columns(weight):
        return lax.dynamic_slice_in_dim(weight[0], turn * hw, hw, axis=1)

    own_qkv = jnp.concatenate([columns(query_weight), columns(key_weight), columns(value_weight)], axis=1)
    own_up = lax.dynamic_index_in_dim(
        up_weight[0].reshape(depth, shards, n, kept), turn, axis=2, keepdims=False
    ).reshape(depth, shards * kept)
    own_down = lax.dynamic_slice_in_dim(down_weight[0], turn * kept, kept, axis=0)
    gains = jnp.stack([attn_gain[0], ffn_gain[0]])
    table = bias_table[0]

    def halves(own):
        rows = own.shape[0] // 2
        low, high = own[:rows], own[rows:]
        other = swapped(jnp.where(first, high, low))
        return jnp.where(first, low, other), jnp.where(first, other, high)

    def gathered(piece):
        return lax.all_gather(piece, ("dp", "section"), axis=0, tiled=True)

    qkv_halves = halves(own_qkv)
    out_halves = halves(out_weight[0])
    up_halves = halves(own_up)
    down_halves = halves(own_down)
    other_gains, other_table = swapped(gains), swapped(table)
    both_gains = jnp.stack([jnp.where(first, gains, other_gains), jnp.where(first, other_gains, gains)])
    both_gains = lax.all_gather(both_gains, "dp", axis=2, tiled=True).astype(F32)
    tables = (jnp.where(first, table, other_table), jnp.where(first, other_table, table))
    weights = [
        (
            gathered(qkv_halves[layer]),
            gathered(out_halves[layer]),
            gathered(up_halves[layer]),
            gathered(down_halves[layer]),
            both_gains[layer, 0:1],
            both_gains[layer, 1:2],
        )
        for layer in range(2)
    ]

    bucket_count = table.shape[0]
    onehot = (buckets[None, :] == jnp.arange(bucket_count, dtype=jnp.int32)[:, None]).astype(F32)
    offset_rows = [
        lax.dot_general(
            t.astype(F32), onehot, (((0,), (0,)), ((), ())), precision=HIGH, preferred_element_type=F32
        )
        for t in tables
    ]

    lanes = jnp.arange(LANES, dtype=jnp.int32) % 64
    same = seg[:, None] == lanes[None, :]
    ext_q = jnp.where((lanes < 8)[None, :] & ~same, NEG, 0.0).astype(BF16)
    ext_k = jnp.where((lanes < 8)[None, :] & same, 1.0, 0.0).astype(BF16)

    padded = max(hw, LANES)

    def pad(value):
        return value if hw == padded else jnp.pad(value, ((0, 0), (0, padded - hw)))

    saved = []
    x = x_in
    outs = []
    for layer in range(2):
        w_qkv, w_out, w_up, w_down, g_attn, g_ffn = weights[layer]
        n1 = norm_gather(n, x, g_attn)
        qkv = jnp.dot(n1, w_qkv, preferred_element_type=F32).astype(BF16)
        q, k, v = (pad(qkv[:, i * hw : (i + 1) * hw]) for i in range(3))
        o, lse = attend(heads, dk, q, k, v, ext_q, ext_k, offset_rows[layer])
        y, x1, n2, slope, hid, back = mix(n, o[:, :hw], x, g_ffn, w_out, w_up, w_down)
        saved.append((x, n1, q, k, v, o, lse, x1, n2, slope, hid, back))
        outs.append(y)
        x = y

    other = swapped(jnp.where(first, outs[1], outs[0]))
    section_outputs = jnp.stack(
        [jnp.where(first, outs[0], other), jnp.where(first, other, outs[1])]
    )[None, :, None]

    grads = [None, None]
    dxs = [None, None]
    smalls = [None, None]
    dy = d_out
    for layer in (1, 0):
        w_qkv, w_out, w_up, w_down, g_attn, g_ffn = weights[layer]
        x, n1, q, k, v, o, lse, x1, n2, slope, hid, back = saved[layer]
        dx1, do, gr_down, gr_up, gr_out, gr_ffn = mix_back(
            n, dy, x1, g_ffn, slope, hid, n2, back, w_out, w_up, w_down
        )
        dq, d_key, dv, d_rows = attend_back(
            heads, dk, q, k, v, pad(do), o, lse, ext_q, ext_k, offset_rows[layer]
        )
        dqkv = jnp.concatenate([dq[:, :hw], d_key[:, :hw], dv[:, :hw]], axis=1)
        dx, dy, gr_qkv, gr_attn = project_back(n, dqkv, x, dx1, g_attn, n1, w_qkv)
        dxs[layer] = dx
        gr_table = lax.dot_general(
            onehot, d_rows, (((1,), (1,)), ((), ())), precision=HIGH, preferred_element_type=F32
        )
        smalls[layer] = (gr_attn[0], gr_ffn[0], gr_table)

        def scattered(value):
            return lax.psum_scatter(value, ("dp", "section"), scatter_dimension=0, tiled=True)

        half_down = scattered(gr_down)
        half_up = scattered(gr_up)
        half_out = lax.psum(scattered(gr_out.reshape(width, model)), "seq")
        half_qkv = scattered(gr_qkv)
        grads[layer] = (
            lax.all_gather(half_qkv, "seq", axis=0),
            lax.all_gather(half_up, "seq", axis=0),
            lax.all_gather(half_down, "seq", axis=0),
            half_out,
        )

    other = swapped(jnp.where(first, dxs[1], dxs[0]))
    input_grads = jnp.stack(
        [jnp.where(first, dxs[0], other), jnp.where(first, other, dxs[1])]
    )[None, :, None]

    def joined(index):
        other = swapped(jnp.where(first, grads[1][index], grads[0][index]))
        low = jnp.where(first, grads[0][index], other)
        high = jnp.where(first, other, grads[1][index])
        return low.astype(F32), high.astype(F32)

    low, high = joined(0)
    whole = jnp.concatenate([low, high], axis=1).reshape(n, depth, 3, hw)
    g_query, g_key, g_value = (
        whole[:, :, i].transpose(1, 0, 2).reshape(1, depth, width) for i in range(3)
    )
    low, high = joined(1)
    whole = jnp.concatenate([low, high], axis=1).reshape(n, depth, shards, kept)
    g_up = whole.transpose(1, 2, 0, 3).reshape(1, depth, ff)
    low, high = joined(2)
    g_down = jnp.concatenate([low, high], axis=1).reshape(1, n * kept, model)
    low, high = joined(3)
    g_out = jnp.concatenate([low, high], axis=0)[None]

    place = jnp.arange(n, dtype=jnp.int32) == turn
    flat = []
    for layer in range(2):
        gr_attn, gr_ffn, gr_table = smalls[layer]
        spread = jnp.where(place[:, None, None], gr_table[None], 0.0)
        flat.append(jnp.concatenate([gr_attn, gr_ffn, spread.reshape(-1)]))
    flat = lax.psum(jnp.stack(flat), ("section", "dp", "seq"))
    flat = jnp.where(first, flat[0], flat[1])
    row = lax.axis_index("dp")
    cut = model // shards
    g_attn = lax.dynamic_slice_in_dim(flat[:model], row * cut, cut)[None]
    g_ffn = lax.dynamic_slice_in_dim(flat[model : 2 * model], row * cut, cut)[None]
    whole = flat[2 * model :].reshape(n, bucket_count, heads)
    mine = lax.dynamic_index_in_dim(whole, turn, axis=0, keepdims=False)
    cut = bucket_count // shards
    g_table = lax.dynamic_slice_in_dim(mine, row * cut, cut, axis=0)[None]

    return (
        section_outputs,
        input_grads,
        g_query,
        g_key,
        g_value,
        g_out,
        g_up,
        g_down,
        g_attn,
        g_ffn,
        g_table,
    )


def solution(mesh):
    return jax.shard_map(
        body,
        mesh=mesh,
        in_specs=(
            P(None, "dp", "seq", None),
            P(None, "dp", "seq", None),
            P(None, "dp", None),
            P(),
            P("section", "dp", None),
            P("section", "dp", None),
            P("section", "dp", None),
            P("section", "dp", None),
            P("section", "dp", None),
            P("section", "dp", None),
            P("section", "dp"),
            P("section", "dp"),
            P("section", None, "seq"),
        ),
        out_specs=(
            P("section", None, "dp", "seq", None),
            P("section", None, "dp", "seq", None),
            P("section", "dp", None),
            P("section", "dp", None),
            P("section", "dp", None),
            P("section", "dp", None),
            P("section", "dp", None),
            P("section", "dp", None),
            P("section", "dp"),
            P("section", "dp"),
            P("section", "dp", "seq"),
        ),
        check_vma=False,
    )
```

```python
import functools
import math

import jax
import jax.numpy as jnp
from jax import lax
from jax.experimental import pallas as pl
from jax.experimental.pallas import tpu as pltpu
from jax.sharding import PartitionSpec as P

EPSILON = 1e-06
NEG = -1e30
HIGH = lax.Precision.HIGHEST
MESH = pl.DeviceIdType.MESH
F32 = jnp.float32
BF16 = jnp.bfloat16
LANES = 128
QB = 256
VMEM_BYTES = 56 << 20

WHOLE = pl.BlockSpec(memory_space=pltpu.VMEM)
AWAY = pl.BlockSpec(memory_space=pl.ANY)


def mm(left, right):
    return jnp.dot(left, right, preferred_element_type=F32)


def mm_nt(left, right):
    return lax.dot_general(left, right, (((1,), (1,)), ((), ())), preferred_element_type=F32)


def mm_tn(left, right):
    return lax.dot_general(left, right, (((0,), (0,)), ((), ())), preferred_element_type=F32)


def inverse_rms(rows):
    return lax.rsqrt(jnp.mean(rows * rows, axis=-1, keepdims=True) + EPSILON)


def aligned(start, size):
    return pl.ds(pl.multiple_of(start, size), size)


def signal_and_wait(peers):
    barrier = pltpu.get_barrier_semaphore()
    for peer in peers:
        pl.semaphore_signal(barrier, inc=1, device_id=peer, device_id_type=MESH)
    pl.semaphore_wait(barrier, len(peers))


def others(axis, n):
    me = lax.axis_index(axis)
    return [{axis: lax.rem(me + k, n)} for k in range(1, n)]


def near(n):
    me = lax.axis_index("seq")
    return [{"seq": peer} for peer in (square(me) if n == 4 else ring(n, me))]


def square(me):
    return me + 1 - 2 * lax.rem(me, 2), lax.rem(me + 2, 4)


def ring(n, me):
    return [lax.rem(me + k, n) for k in range(1, n)]


def push(src, dst, send_sem, recv_sem, peer):
    return pltpu.make_async_remote_copy(
        src_ref=src,
        dst_ref=dst,
        send_sem=send_sem,
        recv_sem=recv_sem,
        device_id=peer if isinstance(peer, dict) else {"seq": peer},
        device_id_type=MESH,
    )


def sources(n):
    me = lax.axis_index("seq")
    if n == 4:
        along_x, along_y = square(me)
        return [me, along_x, along_y, square(along_y)[0]]
    return [lax.rem(me + n - k, n) for k in range(n)]


class Spread:
    def __init__(self, n, source, slot, rows, sems):
        self.n = n
        me = lax.axis_index("seq")
        self.order = sources(n)
        send, recv = sems
        if n != 4:
            self.copies = [
                push(source, slot(me, 0, rows), send.at[k], recv.at[k], peer)
                for k, peer in enumerate(ring(n, me), 1)
            ]
            return
        along_x, along_y = square(me)
        half = rows // 2

        def copy(number, owner, part, peer):
            here = source.at[pl.ds(part * half, half)] if owner is me else slot(owner, part * half, half)
            return push(here, slot(owner, part * half, half), send.at[number], recv.at[number], peer)

        self.copies = [
            copy(0, me, 0, along_x),
            copy(1, me, 1, along_y),
            copy(2, me, 1, along_x),
            copy(3, me, 0, along_y),
            copy(4, along_x, 0, along_y),
            copy(5, along_y, 1, along_x),
        ]

    def start(self):
        for copy in self.copies[:4] if self.n == 4 else self.copies:
            copy.start()

    def forward(self):
        if self.n == 4:
            for first, second in ((0, 4), (1, 5)):
                self.copies[first].wait_recv()
                self.copies[second].start()

    def arrive(self, k):
        if self.n == 4:
            for number in ((), (2,), (3,), (4, 5))[k]:
                self.copies[number].wait_recv()
        else:
            self.copies[k - 1].wait_recv()

    def sent(self):
        for copy in self.copies:
            copy.wait_send()

    def all(self):
        self.start()
        self.forward()
        for k in range(1, self.n):
            self.arrive(k)
        self.sent()


class Collect:
    def __init__(self, n, out, got, sems):
        self.n = n
        self.out, self.got = out, got
        self.half = out.shape[1] // 2
        me = lax.axis_index("seq")
        self.order = sources(n)
        send, recv = sems
        if n != 4:
            self.copies = [
                push(out.at[k], got.at[k], send.at[k], recv.at[k], self.order[k]) for k in range(1, n)
            ]
            return
        along_x, along_y = square(me)

        def copy(number, chunk, part, peer):
            return push(self.piece(out, chunk, part), self.landing(number), send.at[number], recv.at[number], peer)

        self.copies = [
            copy(0, 1, 0, along_x),
            copy(1, 2, 1, along_y),
            copy(2, 3, 0, along_x),
            copy(3, 3, 1, along_y),
            copy(4, 2, 0, along_y),
            copy(5, 1, 1, along_x),
        ]

    def piece(self, ref, chunk, part):
        return ref.at[chunk, pl.ds(part * self.half, self.half)]

    def landing(self, number):
        return self.piece(self.got, number // 2, number % 2)

    def give(self, k, value):
        self.out[k] = value.astype(BF16)
        if self.n == 4:
            for number in ((), (0,), (1,), (2, 3))[k]:
                self.copies[number].start()
        else:
            self.copies[k - 1].start()

    def relay(self):
        if self.n == 4:
            for number, chunk, part in ((2, 2, 0), (3, 1, 1)):
                self.copies[number].wait_recv()
                mine = self.piece(self.out, chunk, part)
                mine[...] = (mine[...].astype(F32) + self.landing(number)[...].astype(F32)).astype(BF16)
                self.copies[number + 2].start()

    def add_to(self, total):
        if self.n == 4:
            for number, part in ((0, 0), (1, 1), (4, 0), (5, 1)):
                self.copies[number].wait_recv()
                total[pl.ds(part * self.half, self.half)] += self.landing(number)[...].astype(F32)
        else:
            for k in range(1, self.n):
                self.copies[k - 1].wait_recv()
                total[...] += self.got[k].astype(F32)

    def sent(self):
        for copy in self.copies:
            copy.wait_send()


def way_sems(n):
    count = max(n, 6)
    return [pltpu.SemaphoreType.DMA((count,)), pltpu.SemaphoreType.DMA((count,))]


def row_slots(ref, tl):
    return lambda owner, first, rows: ref.at[pl.ds(pl.multiple_of(owner * tl + first, rows), rows)]


def chunk_slots(ref):
    return lambda owner, first, rows: ref.at[owner, pl.ds(first, rows)]


def cost(microseconds):
    return pl.CostEstimate(flops=int(microseconds * 1e9), bytes_accessed=0, transcendentals=0)


def params(collective_id=None):
    return pltpu.CompilerParams(
        collective_id=collective_id,
        has_side_effects=collective_id is not None,
        vmem_limit_bytes=VMEM_BYTES,
    )


def shape(dims, dtype):
    return jax.ShapeDtypeStruct(dims, dtype)


def start_kernel(n, shards, x_ref, own_ref, out_ref, a0_ref, f0_ref, a1_ref, f1_ref,
                 all_ref, send, recv, send_g, recv_g):
    tl = x_ref.shape[0]
    cut = own_ref.shape[1]
    me = lax.axis_index("seq")
    layer = lax.axis_index("section")
    row = lax.axis_index("dp")
    mine = aligned(me * tl, tl)
    peers = [
        {"section": lax.rem(layer + i, 2), "dp": lax.rem(row + j, shards)}
        for i in range(2)
        for j in range(shards)
        if i + j
    ]
    signal_and_wait(peers + near(n))
    copies = [
        push(own_ref, all_ref.at[layer, row], send_g.at[i], recv_g.at[i], peer)
        for i, peer in enumerate(peers)
    ]
    for copy in copies:
        copy.start()
    all_ref[layer, row] = own_ref[...]
    rows = x_ref[...].astype(F32)
    inv = inverse_rms(rows)
    for copy in copies:
        copy.wait()
    for z in range(shards):
        part = slice(z * cut, (z + 1) * cut)
        a0_ref[:, part] = all_ref[0, z, 0:1, :].astype(F32)
        f0_ref[:, part] = all_ref[0, z, 1:2, :].astype(F32)
        a1_ref[:, part] = all_ref[1, z, 0:1, :].astype(F32)
        f1_ref[:, part] = all_ref[1, z, 1:2, :].astype(F32)
    out_ref[mine] = (rows * inv * a0_ref[...]).astype(BF16)
    Spread(n, out_ref.at[mine], row_slots(out_ref, tl), tl, (send, recv)).all()


def start(n, shards, x, gains):
    tl, width = x.shape
    gain = shape((1, width), F32)
    return pl.pallas_call(
        functools.partial(start_kernel, n, shards),
        out_shape=(shape((n * tl, width), BF16), gain, gain, gain, gain),
        in_specs=[WHOLE] * 2,
        out_specs=(WHOLE,) * 5,
        scratch_shapes=[
            pltpu.VMEM((2, shards) + gains.shape, BF16),
            *way_sems(n),
            pltpu.SemaphoreType.DMA((2 * shards - 1,)),
            pltpu.SemaphoreType.DMA((2 * shards - 1,)),
        ],
        compiler_params=params(6),
        cost_estimate=cost(28),
        name="start",
    )(x, gains)


def gather_kernel(n, x_ref, gain_ref, out_ref, send, recv):
    tl = x_ref.shape[0]
    mine = aligned(lax.axis_index("seq") * tl, tl)
    rows = x_ref[...].astype(F32)
    out_ref[mine] = (rows * inverse_rms(rows) * gain_ref[...]).astype(BF16)
    signal_and_wait(near(n))
    Spread(n, out_ref.at[mine], row_slots(out_ref, tl), tl, (send, recv)).all()


def norm_gather(n, x, gain):
    tl, width = x.shape
    return pl.pallas_call(
        functools.partial(gather_kernel, n),
        out_shape=shape((n * tl, width), BF16),
        in_specs=[WHOLE] * 2,
        out_specs=WHOLE,
        scratch_shapes=way_sems(n),
        compiler_params=params(0),
        cost_estimate=cost(25),
        name="norm_gather",
    )(x, gain)


def toeplitz_rows(offset_row):
    spread = jnp.broadcast_to(offset_row, (LANES, offset_row.shape[1]))
    return pltpu.roll(spread, 0, 1, stride=1, stride_axis=0)


def attend_kernel(n, heads, dk, extra, *refs):
    if extra:
        (qkv_ref, eq_ref, ek_ref, rows_ref, dy_ref, o_ref, lse_ref, back_ref, dy_all,
         bias_ref, kt_ref, qa_ref, send, recv, send_d, recv_d) = refs
    else:
        (qkv_ref, eq_ref, ek_ref, rows_ref, o_ref, lse_ref, back_ref,
         bias_ref, kt_ref, qa_ref, send, recv) = refs
    length, wide = o_ref.shape
    tl = length // n
    me = lax.axis_index("seq")
    mine = aligned(me * tl, tl)
    signal_and_wait(others("seq", n))
    copies = []
    if extra:
        spread = Spread(n, dy_ref, row_slots(dy_all, tl), tl, (send_d, recv_d))
        spread.start()
        dy_all[mine] = dy_ref[...]
    lane = lax.broadcasted_iota(jnp.int32, (length, LANES), 1)
    lane_q = lax.broadcasted_iota(jnp.int32, (LANES, LANES), 1)
    for head in range(heads):
        pair = pl.ds((head // 2) * LANES, LANES)
        k_pair = pl.ds(wide + (head // 2) * LANES, LANES)
        v_pair = pl.ds(2 * wide + (head // 2) * LANES, LANES)
        inside = (lane >= dk) if head % 2 else (lane < dk)
        qa_ref[...] = jnp.where(inside, qkv_ref[:, pair], eq_ref[...])
        kt_ref[...] = jnp.where(inside, qkv_ref[:, k_pair], ek_ref[...]).T
        bias_ref[...] = toeplitz_rows(rows_ref[head : head + 1, :])
        inside_q = (lane_q >= dk) if head % 2 else (lane_q < dk)

        def block(b, carry, head=head, pair=pair, v_pair=v_pair, inside_q=inside_q):
            scores = mm(qa_ref[aligned(b * QB, QB), :], kt_ref[...])
            for a in range(QB // LANES):
                tile = b * (QB // LANES) + a
                where = aligned(tile * LANES, LANES)
                off = aligned(length - tile * LANES, LANES)
                off = pl.ds(off.start, length)
                part = scores[a * LANES : (a + 1) * LANES] + bias_ref[:, off]
                peak = jnp.max(part, axis=-1, keepdims=True)
                expo = jnp.exp(part - peak)
                total = jnp.sum(expo, axis=-1, keepdims=True)
                mixed = mm(expo.astype(BF16), qkv_ref[:, v_pair]) * (1.0 / total)
                lse = peak + jnp.log(total)
                if head % 2:
                    o_ref[where, pair] = jnp.where(inside_q, mixed.astype(BF16), o_ref[where, pair])
                else:
                    o_ref[where, pair] = mixed.astype(BF16)
                if head:
                    lse_ref[where, :] = jnp.where(lane_q == head, lse, lse_ref[where, :])
                else:
                    lse_ref[where, :] = jnp.broadcast_to(lse, (LANES, LANES))
            return carry

        lax.fori_loop(0, length // QB, block, 0)
        if head % 2 or head == heads - 1:
            for k in range(1, n):
                peer = lax.rem(me + k, n)
                copy = push(
                    o_ref.at[aligned(peer * tl, tl), pair],
                    back_ref.at[me, :, pair],
                    send.at[head // 2, k],
                    recv.at[head // 2, k],
                    peer,
                )
                copy.start()
                copies.append(copy)
            back_ref[me, :, pair] = o_ref[mine, pair]
        if extra and head == 0:
            spread.forward()
    if extra:
        for k in range(1, n):
            spread.arrive(k)
        spread.sent()
    for copy in copies:
        copy.wait()


def attend(n, heads, dk, qkv, ext_q, ext_k, offset_rows, dy=None):
    length, width = qkv.shape[0], qkv.shape[1] // 3
    span = offset_rows.shape[1]
    extra = dy is not None
    pair_sems = pltpu.SemaphoreType.DMA(((heads + 1) // 2, n))
    out_shape = [
        shape((length, width), BF16),
        shape((length, LANES), F32),
        shape((n, length // n, width), BF16),
    ]
    operands = [qkv, ext_q, ext_k, offset_rows]
    if extra:
        out_shape.append(shape((length, dy.shape[1]), BF16))
        operands.append(dy)
    return pl.pallas_call(
        functools.partial(attend_kernel, n, heads, dk, extra),
        out_shape=out_shape,
        in_specs=[WHOLE] * len(operands),
        out_specs=[WHOLE] * len(out_shape),
        scratch_shapes=[
            pltpu.VMEM((LANES, span), F32),
            pltpu.VMEM((LANES, length), BF16),
            pltpu.VMEM((length, LANES), BF16),
            pair_sems,
            pair_sems,
        ]
        + (way_sems(n) if extra else []),
        compiler_params=params(4 if extra else 5),
        cost_estimate=cost(20),
        name="attend_gather" if extra else "attend",
    )(*operands)


def three_parts(lane, value):
    first = value.astype(BF16).astype(F32)
    rest = value - first
    second = rest.astype(BF16).astype(F32)
    third = rest - second
    at = lax.rem(lane, 64)
    return jnp.where(at == 8, first, jnp.where(at == 9, second, jnp.where(at == 10, third, 0.0)))


def attend_back_kernel(n, heads, dk, extra, *refs):
    qkv_ref, do_ref, o_ref, lse_ref, eq_ref, ek_ref, rows_ref = refs[:7]
    refs = refs[7:]
    if extra:
        g_ref = refs[0]
        refs = refs[1:]
    dqkv_ref, dr_ref = refs[:2]
    refs = refs[2:]
    if extra:
        all_g = refs[0]
        refs = refs[1:]
    (bias_ref, kt_ref, vt_ref, qa_ref, da_ref, qt_ref, dot_ref, dkt_ref, dvt_ref, dbias_ref) = refs[:10]
    length, wide = o_ref.shape
    span = rows_ref.shape[1]
    if extra:
        signal_and_wait(near(n))
        spread = Spread(n, g_ref, chunk_slots(all_g), g_ref.shape[0], refs[10:])
        spread.start()
        all_g[lax.axis_index("seq")] = g_ref[...]
    lane = lax.broadcasted_iota(jnp.int32, (length, LANES), 1)
    lane_q = lax.broadcasted_iota(jnp.int32, (QB, LANES), 1)
    at = lax.rem(lane, 64)
    parts = (at >= 8) & (at <= 10)
    ones = jnp.where(parts, 1.0, 0.0)
    for head in range(heads):
        pair = pl.ds((head // 2) * LANES, LANES)
        upper = head % 2 == 1
        inside = (lane >= dk) if upper else (lane < dk)
        inside_q = (lane_q >= dk) if upper else (lane_q < dk)
        k_lanes = pl.ds(wide + (head // 2) * LANES, LANES)
        v_lanes = pl.ds(2 * wide + (head // 2) * LANES, LANES)
        q_pair, k_pair, v_pair, do_pair = (
            qkv_ref[:, pair], qkv_ref[:, k_lanes], qkv_ref[:, v_lanes], do_ref[:, pair]
        )
        if not upper:
            qt_ref[...] = q_pair.T
            dot_ref[...] = do_pair.T
        lse = lse_ref[:, head : head + 1]
        eq = (eq_ref[...].astype(F32) - three_parts(lane, lse)).astype(BF16)
        ek = (ek_ref[...].astype(F32) + ones).astype(BF16)
        qa_ref[...] = jnp.where(inside, q_pair, eq)
        kt_ref[...] = jnp.where(inside, k_pair, ek).T
        weighed = do_pair.astype(F32) * o_ref[:, pair].astype(F32)
        delta = jnp.sum(jnp.where(inside, weighed, 0.0), axis=-1, keepdims=True)
        da_ref[...] = jnp.where(inside, do_pair, (-three_parts(lane, delta)).astype(BF16))
        vt_ref[...] = jnp.where(inside, v_pair, ones.astype(BF16)).T
        bias_ref[...] = toeplitz_rows(rows_ref[head : head + 1, :])
        dkt_ref[...] = jnp.zeros_like(dkt_ref)
        dvt_ref[...] = jnp.zeros_like(dvt_ref)
        dbias_ref[...] = jnp.zeros_like(dbias_ref)
        half = pl.ds(dk if upper else 0, dk)

        def block(b, carry, pair=pair, k_lanes=k_lanes, inside_q=inside_q, upper=upper, half=half):
            where = aligned(b * QB, QB)
            scores = mm(qa_ref[where, :], kt_ref[...])
            lifted = mm(da_ref[where, :], vt_ref[...])
            probs, grads = [], []
            for a in range(QB // LANES):
                cut = slice(a * LANES, (a + 1) * LANES)
                tile = b * (QB // LANES) + a
                off = pl.ds(pl.multiple_of(length - tile * LANES, LANES), length)
                prob = jnp.exp(scores[cut] + bias_ref[:, off])
                grad = prob * lifted[cut]
                dbias_ref[:, off] += grad
                probs.append(prob.astype(BF16))
                grads.append(grad.astype(BF16))
            prob = jnp.concatenate(probs, axis=0)
            grad = jnp.concatenate(grads, axis=0)
            dq = mm(grad, qkv_ref[:, k_lanes]).astype(BF16)
            if upper:
                dqkv_ref[where, pair] = jnp.where(inside_q, dq, dqkv_ref[where, pair])
            else:
                dqkv_ref[where, pair] = dq
            dkt_ref[half, :] += mm(qt_ref[half, where], grad)
            dvt_ref[half, :] += mm(dot_ref[half, where], prob)
            return carry

        lax.fori_loop(0, length // QB, block, 0)
        for lanes, grad_ref in ((k_lanes, dkt_ref), (v_lanes, dvt_ref)):
            turned = grad_ref[...].T.astype(BF16)
            dqkv_ref[:, lanes] = jnp.where(inside, turned, dqkv_ref[:, lanes]) if upper else turned
        folded = dbias_ref[...]
        rows = LANES
        while rows > 8:
            rows //= 2
            folded = folded[:rows] + pltpu.roll(folded[rows:], span - rows, 1)
        place = lax.broadcasted_iota(jnp.int32, (8, span), 0)
        for bit in (4, 2, 1):
            folded = jnp.where(
                lax.rem(lax.div(place, bit), 2) == 1, pltpu.roll(folded, span - bit, 1), folded
            )
        dr_ref[head : head + 1, :] = jnp.sum(folded, axis=0, keepdims=True)
        if extra and head == 0:
            spread.forward()
    if extra:
        for k in range(1, n):
            spread.arrive(k)
        spread.sent()


def attend_back(n, heads, dk, qkv, do, o, lse, ext_q, ext_k, offset_rows, g=None):
    length, width = o.shape
    span = offset_rows.shape[1]
    extra = g is not None
    operands = [qkv, do, o, lse, ext_q, ext_k, offset_rows]
    out_shape = [shape((length, 3 * width), BF16), shape((heads, span), F32)]
    if extra:
        operands.append(g)
        out_shape.append(shape((n,) + g.shape, BF16))
    return pl.pallas_call(
        functools.partial(attend_back_kernel, n, heads, dk, extra),
        out_shape=out_shape,
        in_specs=[WHOLE] * len(operands),
        out_specs=[WHOLE] * len(out_shape),
        scratch_shapes=[
            pltpu.VMEM((LANES, span), F32),
            pltpu.VMEM((LANES, length), BF16),
            pltpu.VMEM((LANES, length), BF16),
            pltpu.VMEM((length, LANES), BF16),
            pltpu.VMEM((length, LANES), BF16),
            pltpu.VMEM((LANES, length), BF16),
            pltpu.VMEM((LANES, length), BF16),
            pltpu.VMEM((LANES, length), F32),
            pltpu.VMEM((LANES, length), F32),
            pltpu.VMEM((LANES, span), F32),
        ]
        + (way_sems(n) if extra else []),
        compiler_params=params(9 if extra else None),
        cost_estimate=cost(25),
        name="gather_attend_back" if extra else "attend_back",
    )(*operands)


def weight_loads(sources, targets, sems):
    if len(sources) == len(targets):
        return [
            [pltpu.make_async_copy(src, dst, sems.at[j])]
            for j, (src, dst) in enumerate(zip(sources, targets))
        ]
    (packed,) = sources
    pieces, count, rows = packed.shape[:3]
    return [
        [
            pltpu.make_async_copy(
                packed.at[i, j], targets[j].at[pl.ds(i * rows, rows)], sems.at[j * pieces + i]
            )
            for i in range(pieces)
        ]
        for j in range(count)
    ]


def arrive(copies):
    for copy in copies:
        copy.wait()


def mix_kernel(n, hw, many, *refs):
    x_ref, gain_ref, back_ref = refs[:3]
    sources = refs[3 : 3 + many]
    (y_ref, x1_ref, n2_ref, slope_ref, hid_ref,
     wo_ref, up_ref, down_ref, out_ref, got_ref, total_ref,
     load, send_n, recv_n, send_y, recv_y) = refs[3 + many :]
    tl = x_ref.shape[0]
    me = lax.axis_index("seq")
    mine = aligned(me * tl, tl)
    loads = weight_loads(sources, (wo_ref, up_ref, down_ref), load)
    for group in loads:
        for copy in group:
            copy.start()
    signal_and_wait(near(n))
    arrive(loads[0])
    total = x_ref[...].astype(F32)
    for s in range(n):
        total += mm(back_ref[s][:, :hw], wo_ref[s * hw : (s + 1) * hw, :])
    total_ref[...] = total
    x1 = total_ref[...]
    x1_ref[...] = x1
    n2_ref[mine] = (x1 * inverse_rms(x1) * gain_ref[...]).astype(BF16)
    spread = Spread(n, n2_ref.at[mine], row_slots(n2_ref, tl), tl, (send_n, recv_n))
    collect = Collect(n, out_ref, got_ref, (send_y, recv_y))
    spread.start()
    arrive(loads[1])
    arrive(loads[2])
    for k in range(n):
        where = aligned(spread.order[k] * tl, tl)
        if k:
            spread.arrive(k)
        u = mm(n2_ref[where], up_ref[...])
        half = 0.5 + 0.5 * lax.erf(u * math.sqrt(0.5))
        hid = (u * half).astype(BF16)
        hid_ref[where] = hid
        slope_ref[where] = (
            half + u * (jnp.exp(-0.5 * u * u) * (1.0 / math.sqrt(2.0 * math.pi)))
        ).astype(BF16)
        part = mm(hid, down_ref[...])
        if k:
            collect.give(k, part)
        else:
            total_ref[...] += part
            spread.forward()
    collect.relay()
    collect.add_to(total_ref)
    y_ref[...] = total_ref[...].astype(BF16)
    spread.sent()
    collect.sent()


def mix(n, hw, ff, x, gain, back, weights):
    tl, width = x.shape
    return pl.pallas_call(
        functools.partial(mix_kernel, n, hw, len(weights)),
        out_shape=(
            shape((tl, width), BF16),
            shape((tl, width), F32),
            shape((n * tl, width), BF16),
            shape((n * tl, ff), BF16),
            shape((n * tl, ff), BF16),
        ),
        in_specs=[WHOLE] * 3 + [AWAY] * len(weights),
        out_specs=(WHOLE,) * 5,
        scratch_shapes=[
            pltpu.VMEM((n * hw, width), BF16),
            pltpu.VMEM((width, ff), BF16),
            pltpu.VMEM((ff, width), BF16),
            pltpu.VMEM((n, tl, width), BF16),
            pltpu.VMEM((n, tl, width), BF16),
            pltpu.VMEM((tl, width), F32),
            pltpu.SemaphoreType.DMA((3 * weights[0].shape[0] if len(weights) == 1 else 3,)),
            *way_sems(n),
            *way_sems(n),
        ],
        compiler_params=params(1),
        cost_estimate=cost(55),
        name="mix",
    )(x, gain, back, *weights)


def mix_back_kernel(n, shards, hw, many, spread_out, *refs):
    dy_ref, x1_ref, gain_ref, slope_ref, hid_ref, n2_ref, back_ref = refs[:7]
    sources_w = refs[7 : 7 + many]
    given_ref = refs[7 + many]
    refs = refs[8 + many :]
    dx1_ref, do_ref, g_gain_ref = refs[:3]
    g_refs = refs[3:4] if many == 1 else refs[3:6]
    refs = refs[3 + len(g_refs) :]
    if not spread_out:
        share_ref = refs[0]
        refs = refs[1:]
    (wo_ref, up_ref, down_ref, du_ref, out_ref, got_ref, total_ref, do_out,
     load, send_n, recv_n, send_o, recv_o) = refs[:13]
    tl = dy_ref.shape[0]
    me = lax.axis_index("seq")
    mine = aligned(me * tl, tl)
    loads = weight_loads(sources_w, (wo_ref, up_ref, down_ref), load)
    for group in reversed(loads):
        for copy in group:
            copy.start()
    collect = Collect(n, out_ref, got_ref, (send_n, recv_n))
    if spread_out:
        dy_all = given_ref
        signal_and_wait(others("seq", n))
        steps = [3, 1, 2, 0] if n == 4 else [*range(1, n), 0]
    else:
        dy_all, got_z, send_d, recv_d, send_z, recv_z = refs[13:]
        row = lax.axis_index("dp")
        rows_g = share_ref.shape[0]
        signal_and_wait(others("seq", n) + others("dp", shards))
        spread = Spread(n, dy_ref, row_slots(dy_all, tl), tl, (send_d, recv_d))
        spread.start()
        along = []
        for k in range(1, shards):
            peer = lax.rem(row + k, shards)
            copy = push(
                given_ref.at[aligned(peer * rows_g, rows_g)],
                got_z.at[k], send_z.at[k], recv_z.at[k], {"dp": peer},
            )
            copy.start()
            along.append(copy)
        dy_all[mine] = dy_ref[...]
        steps = range(n)
    arrive(loads[2])
    arrive(loads[1])
    for k in steps:
        where = aligned(collect.order[k] * tl, tl)
        if k and not spread_out:
            spread.arrive(k)
        du = (mm_nt(dy_all[where], down_ref[...]) * slope_ref[where].astype(F32)).astype(BF16)
        du_ref[where] = du
        part = mm_nt(du, up_ref[...])
        if k:
            collect.give(k, part)
        else:
            if spread_out:
                collect.relay()
            else:
                spread.forward()
            total_ref[...] = part
    store_grad(g_refs, 0, hid_ref, dy_all)
    if not spread_out:
        collect.relay()
    store_grad(g_refs, 1, n2_ref, du_ref)
    collect.add_to(total_ref)
    dn2 = total_ref[...]
    x1 = x1_ref[...]
    inv = inverse_rms(x1)
    scaled = x1 * inv
    g_gain_ref[...] = jnp.sum(dn2 * scaled, axis=0, keepdims=True)
    lifted = dn2 * gain_ref[...]
    dx1 = dy_ref[...].astype(F32) + inv * (
        lifted - scaled * jnp.mean(lifted * scaled, axis=-1, keepdims=True)
    )
    dx1_ref[...] = dx1
    d_attn = dx1.astype(BF16)
    arrive(loads[0])
    returned = []
    for k in range(1, n):
        peer = lax.rem(me + k, n)
        do_out[k] = mm_nt(d_attn, wo_ref[aligned(peer * hw, hw), :]).astype(BF16)
        copy = push(do_out.at[k], do_ref.at[mine], send_o.at[k], recv_o.at[k], peer)
        copy.start()
        returned.append(copy)
    do_ref[mine] = mm_nt(d_attn, wo_ref[aligned(me * hw, hw), :]).astype(BF16)
    for s in range(n):
        store_rows(g_refs, 2, s * hw, mm_tn(back_ref[s][:, :hw], d_attn).astype(BF16))
    if not spread_out:
        share = given_ref[aligned(row * rows_g, rows_g), :].astype(F32)
        for k in range(1, shards):
            along[k - 1].wait()
            share += got_z[k].astype(F32)
        share_ref[...] = share.astype(BF16)
        spread.sent()
    collect.sent()
    for copy in returned:
        copy.wait()


def store_rows(refs, index, first, value):
    if len(refs) == 1 and len(refs[0].shape) == 4:
        rows = refs[0].shape[2]
        for i in range(value.shape[0] // rows):
            refs[0][first // rows + i, index] = value[i * rows : (i + 1) * rows]
    else:
        refs[index][pl.ds(first, value.shape[0]), :] = value


def store_grad(refs, index, left_ref, right_ref):
    rows = min(256, left_ref.shape[1])

    def block(b, carry):
        first = pl.multiple_of(b * rows, rows)
        store_rows(refs, index, first, mm_tn(left_ref[:, pl.ds(first, rows)], right_ref[...]).astype(BF16))
        return carry

    lax.fori_loop(0, left_ref.shape[1] // rows, block, 0)


def mix_back(n, shards, hw, ff, dy, x1, gain, slope, hid, n2, back, weights, dy_all=None, g_w=None):
    tl, width = dy.shape
    if len(weights) == 1:
        grads = [shape(weights[0].shape, BF16)]
    else:
        grads = [shape((ff, width), BF16), shape((width, ff), BF16), shape((n * hw, width), BF16)]
    sems = pltpu.SemaphoreType.DMA((n,))
    spread_out = dy_all is not None
    operands = [dy, x1, gain, slope, hid, n2, back, *weights, dy_all if spread_out else g_w]
    extra, scratch = [], []
    if not spread_out:
        share = (g_w.shape[0] // shards, g_w.shape[1])
        row_sems = pltpu.SemaphoreType.DMA((shards,))
        extra = [shape(share, BF16)]
        scratch = [
            pltpu.VMEM((n * tl, width), BF16),
            pltpu.VMEM((shards,) + share, BF16),
            *way_sems(n),
            row_sems,
            row_sems,
        ]
    out_shape = [
        shape((tl, width), F32),
        shape((n * tl, hw), BF16),
        shape((1, width), F32),
        *grads,
        *extra,
    ]
    return pl.pallas_call(
        functools.partial(mix_back_kernel, n, shards, hw, len(weights), spread_out),
        out_shape=out_shape,
        in_specs=[WHOLE] * 7 + [AWAY] * len(weights) + [WHOLE],
        out_specs=[WHOLE] * len(out_shape),
        scratch_shapes=[
            pltpu.VMEM((n * hw, width), BF16),
            pltpu.VMEM((width, ff), BF16),
            pltpu.VMEM((ff, width), BF16),
            pltpu.VMEM((n * tl, ff), BF16),
            pltpu.VMEM((n, tl, width), BF16),
            pltpu.VMEM((n, tl, width), BF16),
            pltpu.VMEM((tl, width), F32),
            pltpu.VMEM((n, tl, hw), BF16),
            pltpu.SemaphoreType.DMA((3 * weights[0].shape[0] if len(weights) == 1 else 3,)),
            *way_sems(n),
            sems,
            sems,
        ]
        + scratch,
        compiler_params=params(2 if spread_out else 7),
        cost_estimate=cost(40 if spread_out else 60),
        name="mix_back" if spread_out else "gather_mix_back",
    )(*operands)


def project_back_kernel(n, dqkv_ref, x_ref, dx1_ref, gain_ref, n1_ref, w_any,
                        dx_ref, low_ref, g_w_ref, g_gain_ref,
                        w_ref, out_ref, got_ref, total_ref, load, send, recv):
    tl = x_ref.shape[0]
    weight = pltpu.make_async_copy(w_any, w_ref, load.at[0])
    weight.start()
    signal_and_wait(near(n))
    weight.wait()
    collect = Collect(n, out_ref, got_ref, (send, recv))

    def part(k):
        return mm_nt(dqkv_ref[aligned(collect.order[k] * tl, tl), :], w_ref[...])

    for k in (3, 1, 2) if n == 4 else range(1, n):
        collect.give(k, part(k))
    total_ref[...] = part(0)
    collect.relay()
    store_grad([g_w_ref], 0, n1_ref, dqkv_ref)
    collect.add_to(total_ref)
    dn1 = total_ref[...]
    rows = x_ref[...].astype(F32)
    inv = inverse_rms(rows)
    scaled = rows * inv
    g_gain_ref[...] = jnp.sum(dn1 * scaled, axis=0, keepdims=True)
    lifted = dn1 * gain_ref[...]
    dx = dx1_ref[...] + inv * (lifted - scaled * jnp.mean(lifted * scaled, axis=-1, keepdims=True))
    dx_ref[...] = dx
    low_ref[...] = dx.astype(BF16)
    collect.sent()


def project_back(n, dqkv, x, dx1, gain, n1, w):
    tl, width = x.shape
    return pl.pallas_call(
        functools.partial(project_back_kernel, n),
        out_shape=(
            shape((tl, width), F32),
            shape((tl, width), BF16),
            shape(w.shape, BF16),
            shape((1, width), F32),
        ),
        in_specs=[WHOLE] * 5 + [AWAY],
        out_specs=(WHOLE,) * 4,
        scratch_shapes=[
            pltpu.VMEM(w.shape, BF16),
            pltpu.VMEM((n, tl, width), BF16),
            pltpu.VMEM((n, tl, width), BF16),
            pltpu.VMEM((tl, width), F32),
            pltpu.SemaphoreType.DMA((1,)),
            *way_sems(n),
        ],
        compiler_params=params(3),
        cost_estimate=cost(30),
        name="project_back",
    )(dqkv, x, dx1, gain, n1, w)


def finish_kernel(n, shards, small_ref, g0_ref, w0_ref, g1_ref, share1_ref,
                  all_g, all_w0, all_w1, other_g, other_w, sums_ref,
                  got_c, got_c1, sent_z, got_z, small_got, tile_got,
                  send_g, recv_g, send_w0, recv_w0, send_w1, recv_w1,
                  send_c, recv_c, send_z, recv_z, send_x, recv_x, send_s, recv_s, send_t, recv_t):
    me = lax.axis_index("seq")
    core = lax.axis_index("section")
    row = lax.axis_index("dp")
    rows = sent_z.shape[1]
    other = {"section": 1 - core}
    peers = [
        (lax.rem(core + i, 2), lax.rem(row + j, shards))
        for i in range(2)
        for j in range(shards)
        if i + j
    ]
    signal_and_wait([{"section": c, "dp": z} for c, z in peers] + others("seq", n))

    spread_g = Spread(n, g0_ref, chunk_slots(all_g), g0_ref.shape[0], (send_g, recv_g))
    spread_g.start()
    crossed = [
        push(w0_ref.at[aligned((2 * z + 1 - core) * rows, rows)], got_c.at[z], send_c.at[z], recv_c.at[z], other)
        for z in range(shards)
    ] + [
        push(share1_ref.at[aligned((1 - core) * rows, rows)], got_c1, send_c.at[shards], recv_c.at[shards], other)
    ]
    for copy in crossed:
        copy.start()
    smalls = [
        push(small_ref.at[c, z], small_got.at[i], send_s.at[i], recv_s.at[i], {"section": c, "dp": z})
        for i, (c, z) in enumerate(peers)
    ]
    for copy in smalls:
        copy.start()

    def cross(source, target, t, number):
        sem = number * n + t
        return push(source, target.at[t], send_x.at[sem], recv_x.at[sem], other)

    @pl.when(core == 0)
    def _():
        for t in range(n):
            cross(g1_ref.at[t], other_g, t, 0).start()

    @pl.when(core == 1)
    def _():
        cross(g0_ref, other_g, me, 0).start()

    all_g[me] = g0_ref[...]
    for copy in crossed:
        copy.wait_recv()
    along = []
    for k in range(1, shards):
        peer = lax.rem(row + k, shards)
        both = w0_ref[aligned((2 * peer + core) * rows, rows), :].astype(F32) + got_c[peer].astype(F32)
        sent_z[k] = both.astype(BF16)
        copy = push(sent_z.at[k], got_z.at[k], send_z.at[k], recv_z.at[k], {"dp": peer})
        copy.start()
        along.append(copy)
    half = share1_ref[aligned(core * rows, rows), :].astype(F32) + got_c1[...].astype(F32)
    all_w1[me] = half.astype(BF16)
    spread_w1 = Spread(n, all_w1.at[me], chunk_slots(all_w1), rows, (send_w1, recv_w1))
    spread_w1.start()

    tile = small_ref[core, row]
    for i, copy in enumerate(smalls):
        copy.wait()
        tile += small_got[i]
    tile_got[0] = tile
    tiles = []
    for k in range(1, n):
        copy = push(tile_got.at[0], tile_got.at[k], send_t.at[k], recv_t.at[k], lax.rem(me + k, n))
        copy.start()
        tiles.append(copy)

    spread_g.forward()
    half = w0_ref[aligned((2 * row + core) * rows, rows), :].astype(F32) + got_c[row].astype(F32)
    for k in range(1, shards):
        along[k - 1].wait()
        half += got_z[k].astype(F32)
    all_w0[me] = half.astype(BF16)
    spread_w0 = Spread(n, all_w0.at[me], chunk_slots(all_w0), rows, (send_w0, recv_w0))
    spread_w0.start()
    spread_w1.forward()
    spread_w0.forward()

    @pl.when(core == 0)
    def _():
        cross(all_w1.at[me], other_w, me, 1).start()

    @pl.when(core == 1)
    def _():
        cross(all_w0.at[me], other_w, me, 1).start()

    for k in range(1, n):
        source = spread_g.order[k]
        spread_g.arrive(k)

        @pl.when(core == 1)
        def _():
            cross(all_g.at[source], other_g, source, 0).start()

    total = tile
    for k in range(1, n):
        tiles[k - 1].wait()
        total += tile_got[k]
    line = lax.broadcasted_iota(jnp.int32, tile.shape, 0)
    sums_ref[...] = jnp.where(line < 2, total, tile)
    for k in range(1, n):
        source = spread_g.order[k]
        spread_w1.arrive(k)
        spread_w0.arrive(k)

        @pl.when(core == 0)
        def _():
            cross(all_w1.at[source], other_w, source, 1).start()

        @pl.when(core == 1)
        def _():
            cross(all_w0.at[source], other_w, source, 1).start()

    for t in range(n):
        cross(g0_ref, other_g, t, 0).wait()
        cross(got_c1, other_w, t, 1).wait()
    for copy in crossed:
        copy.wait_send()
    for spread in (spread_g, spread_w0, spread_w1):
        spread.sent()


def finish(n, shards, small, g0, w0, g1, share1):
    sems = pltpu.SemaphoreType.DMA((n,))
    cross_sems = pltpu.SemaphoreType.DMA((2 * n,))
    core_sems = pltpu.SemaphoreType.DMA((shards + 1,))
    row_sems = pltpu.SemaphoreType.DMA((shards,))
    small_sems = pltpu.SemaphoreType.DMA((2 * shards - 1,))
    tile = small.shape[2:]
    half = (share1.shape[0] // 2, share1.shape[1])
    gathered_w = shape((n,) + half, BF16)
    return pl.pallas_call(
        functools.partial(finish_kernel, n, shards),
        out_shape=(
            shape(g1.shape, BF16),
            gathered_w,
            gathered_w,
            shape(g1.shape, BF16),
            gathered_w,
            shape(tile, F32),
        ),
        in_specs=[WHOLE] * 5,
        out_specs=(WHOLE,) * 6,
        scratch_shapes=[
            pltpu.VMEM((shards,) + half, BF16),
            pltpu.VMEM(half, BF16),
            pltpu.VMEM((shards,) + half, BF16),
            pltpu.VMEM((shards,) + half, BF16),
            pltpu.VMEM((2 * shards - 1,) + tile, F32),
            pltpu.VMEM((n,) + tile, F32),
            *way_sems(n),
            *way_sems(n),
            *way_sems(n),
            core_sems, core_sems, row_sems, row_sems, cross_sems, cross_sems,
            small_sems, small_sems, sems, sems,
        ],
        compiler_params=params(8),
        cost_estimate=cost(45),
        name="finish",
    )(small, g0, w0, g1, share1)


def assemble_kernel(n, shards, g0_ref, g1_ref, other_g, w0_ref, w1_ref, other_w,
                    down_ref, up_ref, out_ref, q_ref, k_ref, v_ref):
    first = lax.axis_index("section") == 0
    quarter = other_w.shape[1]
    hw = other_w.shape[2] // 3
    kept = 2 * quarter
    total = [None, None]
    for t in range(n):
        for half in range(2):
            if half == 0:
                g = jnp.where(first, g0_ref[t], other_g[t]).astype(F32)
                w = jnp.where(first, w0_ref[t], other_w[t]).astype(F32)
            else:
                g = jnp.where(first, other_g[t], g1_ref[t]).astype(F32)
                w = jnp.where(first, other_w[t], w1_ref[t]).astype(F32)
            rows = slice(half * quarter, (half + 1) * quarter)
            down_ref[t * kept + half * quarter : t * kept + (half + 1) * quarter, :] = g[:quarter]
            for z in range(shards):
                at = (z * n + t) * kept
                up_ref[rows, at : at + kept] = g[quarter : 2 * quarter, z * kept : (z + 1) * kept]
            share = g[2 * quarter :]
            total[half] = share if t == 0 else total[half] + share
            if t == n - 1:
                out_ref[rows, :] = total[half]
            for i, ref in enumerate((q_ref, k_ref, v_ref)):
                ref[rows, t * hw : (t + 1) * hw] = w[:, i * hw : (i + 1) * hw]


def assemble(n, shards, g0, g1, other_g, w0, w1, other_w):
    quarter = other_w.shape[1]
    model = other_g.shape[2]
    hw = other_w.shape[2] // 3
    kept = 2 * quarter
    square = shape((2 * quarter, n * hw), F32)
    return pl.pallas_call(
        functools.partial(assemble_kernel, n, shards),
        out_shape=(
            shape((n * kept, model), F32),
            shape((2 * quarter, n * shards * kept), F32),
            shape((2 * quarter, model), F32),
            square, square, square,
        ),
        in_specs=[WHOLE] * 6,
        out_specs=(WHOLE,) * 6,
        compiler_params=params(),
        cost_estimate=cost(12),
        name="assemble",
    )(g0, g1, other_g, w0, w1, other_w)


def swapped(value):
    return lax.ppermute(value, "section", [(0, 1), (1, 0)])


def body(inputs, cotangent, segments, buckets, query_weight, key_weight, value_weight, out_weight,
         up_weight, down_weight, attn_gain, ffn_gain, bias_table):
    first = lax.axis_index("section") == 0
    turn = lax.axis_index("seq")
    n = lax.axis_size("seq")
    shards = lax.axis_size("dp")
    depth, width = query_weight.shape[1:]
    ff = up_weight.shape[2]
    heads = bias_table.shape[2]
    hw = width // n
    dk = hw // heads
    kept = down_weight.shape[1] // n
    hidden = ff // n
    model = inputs.shape[-1]
    quarter = model // (2 * shards)
    packed = hidden == model == width

    x_in = jnp.where(first, inputs[0, 0], inputs[1, 0])
    d_out = jnp.where(first, cotangent[0, 0], cotangent[1, 0])
    seg = jnp.where(first, segments[0, 0], segments[1, 0])

    def columns(weight):
        return lax.dynamic_slice_in_dim(weight[0], turn * hw, hw, axis=1)

    own_qkv = jnp.concatenate([columns(query_weight), columns(key_weight), columns(value_weight)], axis=1)
    own_up = lax.dynamic_index_in_dim(
        up_weight[0].reshape(depth, shards, n, kept), turn, axis=2, keepdims=False
    ).reshape(depth, hidden)
    own_down = lax.dynamic_slice_in_dim(down_weight[0], turn * kept, kept, axis=0)
    table = bias_table[0]

    def halves(own):
        rows = own.shape[0] // 2
        low, high = own[:rows], own[rows:]
        other = swapped(jnp.where(first, high, low))
        return jnp.where(first, low, other), jnp.where(first, other, high)

    def gathered(piece):
        return lax.all_gather(piece, ("dp", "section"), axis=0, tiled=True)

    qkv_halves = halves(own_qkv)
    out_halves = halves(out_weight[0])
    up_halves = halves(own_up)
    down_halves = halves(own_down)
    qkv_weights = [gathered(qkv_halves[0])]
    mix_weights = []
    for layer in range(2):
        if layer:
            qkv_weights.append(gathered(qkv_halves[layer]))
        pieces = (out_halves[layer], up_halves[layer], down_halves[layer])
        if packed:
            mix_weights.append([lax.all_gather(jnp.stack(pieces), ("dp", "section"), axis=0, tiled=False)])
        else:
            mix_weights.append([gathered(piece) for piece in pieces])
    other_table = swapped(table)
    tables = (jnp.where(first, table, other_table), jnp.where(first, other_table, table))

    gains = jnp.pad(jnp.stack([attn_gain[0], ffn_gain[0]]), ((0, 14), (0, 0)))
    first_n1, *gain_rows = start(n, shards, x_in, gains)

    bucket_count = table.shape[0]
    onehot = (buckets[None, :] == jnp.arange(bucket_count, dtype=jnp.int32)[:, None]).astype(F32)
    offset_rows = [
        lax.dot_general(
            t.astype(F32), onehot, (((0,), (0,)), ((), ())), precision=HIGH, preferred_element_type=F32
        )
        for t in tables
    ]

    lanes = jnp.arange(LANES, dtype=jnp.int32) % 64
    same = seg[:, None] == lanes[None, :]
    ext_q = jnp.where((lanes < 8)[None, :] & ~same, NEG, 0.0).astype(BF16)
    ext_k = jnp.where((lanes < 8)[None, :] & same, 1.0, 0.0).astype(BF16)

    wide = max(hw, LANES)

    def pad(value):
        return value if hw == wide else jnp.pad(value, ((0, 0), (0, wide - hw)))

    saved = []
    x = x_in
    outs = []
    d_all = None
    for layer in range(2):
        n1 = norm_gather(n, x, gain_rows[2]) if layer else first_n1
        qkv = jnp.dot(n1, qkv_weights[layer], preferred_element_type=F32).astype(BF16)
        if hw < wide:
            qkv = jnp.concatenate([pad(qkv[:, i * hw : (i + 1) * hw]) for i in range(3)], axis=1)
        if layer:
            o, lse, back = attend(n, heads, dk, qkv, ext_q, ext_k, offset_rows[layer])
        else:
            o, lse, back, d_all = attend(n, heads, dk, qkv, ext_q, ext_k, offset_rows[layer], d_out)
        y, x1, n2, slope, hid = mix(
            n, hw, hidden, x, gain_rows[2 * layer + 1], back, mix_weights[layer]
        )
        saved.append((x, n1, qkv, o, lse, x1, n2, slope, hid, back))
        outs.append(y)
        x = y

    other = swapped(jnp.where(first, outs[1], outs[0]))
    section_outputs = jnp.stack(
        [jnp.where(first, outs[0], other), jnp.where(first, other, outs[1])]
    )[None, :, None]

    halves_g = [None, None]
    grads_w = [None, None]
    dxs = [None, None]
    smalls = [None, None]
    dy = d_out
    for layer in (1, 0):
        x, n1, qkv, o, lse, x1, n2, slope, hid, back = saved[layer]
        dx1, do, gr_ffn, *gr = mix_back(
            n, shards, hw, hidden, dy, x1, gain_rows[2 * layer + 1], slope, hid, n2, back,
            mix_weights[layer], **({"dy_all": d_all} if layer else {"g_w": grads_w[1]}),
        )
        if not layer:
            share_w = gr.pop()

        def scattered(value):
            return lax.psum_scatter(value, ("dp", "section"), scatter_dimension=0, tiled=True)

        if not packed:
            gr = [jnp.concatenate([part.reshape(2 * shards, -1, model) for part in gr], axis=1)]
        half = scattered(gr[0].reshape(-1, model))
        dqkv, d_rows, *gathered_g = attend_back(
            n, heads, dk, qkv, pad(do), o, lse, ext_q, ext_k, offset_rows[layer],
            None if layer else halves_g[1],
        )
        if hw < wide:
            dqkv = jnp.concatenate([dqkv[:, i * wide : i * wide + hw] for i in range(3)], axis=1)
        dx, dy, grads_w[layer], gr_attn = project_back(
            n, dqkv, x, dx1, gain_rows[2 * layer], n1, qkv_weights[layer]
        )
        dxs[layer] = dx
        gr_table = lax.dot_general(
            onehot, d_rows, (((1,), (1,)), ((), ())), precision=HIGH, preferred_element_type=F32
        )
        smalls[layer] = (gr_attn, gr_ffn, gr_table)
        halves_g[layer] = half

    other = swapped(jnp.where(first, dxs[1], dxs[0]))
    input_grads = jnp.stack(
        [jnp.where(first, dxs[0], other), jnp.where(first, other, dxs[1])]
    )[None, :, None]

    cut = model // shards
    small = []
    for gr_attn, gr_ffn, gr_table in smalls:
        flat = gr_table.reshape(shards, -1)
        flat = jnp.pad(flat, ((0, 0), (0, cut - flat.shape[1])))
        tile = jnp.stack([gr_attn.reshape(shards, cut), gr_ffn.reshape(shards, cut), flat], axis=1)
        small.append(jnp.pad(tile, ((0, 0), (0, 5), (0, 0))))
    all_g0, all_w0, all_w1, other_g, other_w, sums = finish(
        n, shards, jnp.stack(small), halves_g[0], grads_w[0], gathered_g[0], share_w
    )
    all_g1 = gathered_g[0]
    g_attn, g_ffn = sums[0:1], sums[1:2]
    g_table = sums[2, : bucket_count // shards * heads].reshape(1, bucket_count // shards, heads)

    if packed:
        g_down, g_up, g_out, g_query, g_key, g_value = (
            part[None] for part in assemble(n, shards, all_g0, all_g1, other_g, all_w0, all_w1, other_w)
        )
    else:
        low, high = jnp.where(first, all_g0, other_g), jnp.where(first, other_g, all_g1)
        sizes = [kept // 2, quarter * hidden // model, width // (2 * shards)]
        cuts = [sum(sizes[:i]) for i in range(4)]

        def joined(index):
            return jnp.stack([part[:, cuts[index] : cuts[index + 1]] for part in (low, high)], axis=1)

        g_down = joined(0).astype(F32).reshape(1, n * kept, model)
        whole = joined(1).reshape(n, depth, shards, kept)
        g_up = whole.transpose(1, 2, 0, 3).reshape(1, depth, ff).astype(F32)
        g_out = jnp.sum(joined(2).astype(F32), axis=0).reshape(1, depth, model)
        low, high = jnp.where(first, all_w0, other_w), jnp.where(first, other_w, all_w1)
        whole = jnp.stack([low, high], axis=1).reshape(n, depth, 3, hw)
        g_query, g_key, g_value = (
            whole[:, :, i].transpose(1, 0, 2).reshape(1, depth, width).astype(F32) for i in range(3)
        )

    return (
        section_outputs,
        input_grads,
        g_query,
        g_key,
        g_value,
        g_out,
        g_up,
        g_down,
        g_attn,
        g_ffn,
        g_table,
    )


def solution(mesh):
    return jax.shard_map(
        body,
        mesh=mesh,
        in_specs=(
            P(None, "dp", "seq", None),
            P(None, "dp", "seq", None),
            P(None, "dp", None),
            P(),
            P("section", "dp", None),
            P("section", "dp", None),
            P("section", "dp", None),
            P("section", "dp", None),
            P("section", "dp", None),
            P("section", "dp", None),
            P("section", "dp"),
            P("section", "dp"),
            P("section", None, "seq"),
        ),
        out_specs=(
            P("section", None, "dp", "seq", None),
            P("section", None, "dp", "seq", None),
            P("section", "dp", None),
            P("section", "dp", None),
            P("section", "dp", None),
            P("section", "dp", None),
            P("section", "dp", None),
            P("section", "dp", None),
            P("section", "dp"),
            P("section", "dp"),
            P("section", "dp", "seq"),
        ),
        check_vma=False,
    )
```

```python
import functools
import math

import jax
import jax.numpy as jnp
from jax import lax
from jax.experimental import pallas as pl
from jax.experimental.pallas import tpu as pltpu
from jax.sharding import PartitionSpec as P

EPSILON = 1e-06
NEG = -1e30
HIGH = lax.Precision.HIGHEST
MESH = pl.DeviceIdType.MESH
F32 = jnp.float32
BF16 = jnp.bfloat16
LANES = 128
QB = 256
VMEM_BYTES = 56 << 20

WHOLE = pl.BlockSpec(memory_space=pltpu.VMEM)
AWAY = pl.BlockSpec(memory_space=pl.ANY)


def mm(left, right):
    return jnp.dot(left, right, preferred_element_type=F32)


def mm_nt(left, right):
    return lax.dot_general(left, right, (((1,), (1,)), ((), ())), preferred_element_type=F32)


def mm_tn(left, right):
    return lax.dot_general(left, right, (((0,), (0,)), ((), ())), preferred_element_type=F32)


def inverse_rms(rows):
    return lax.rsqrt(jnp.mean(rows * rows, axis=-1, keepdims=True) + EPSILON)


def aligned(start, size):
    return pl.ds(pl.multiple_of(start, size), size)


def signal_and_wait(peers):
    barrier = pltpu.get_barrier_semaphore()
    for peer in peers:
        pl.semaphore_signal(barrier, inc=1, device_id=peer, device_id_type=MESH)
    pl.semaphore_wait(barrier, len(peers))


def others(axis, n):
    me = lax.axis_index(axis)
    return [{axis: lax.rem(me + k, n)} for k in range(1, n)]


def near(n):
    me = lax.axis_index("seq")
    return [{"seq": peer} for peer in (square(me) if n == 4 else ring(n, me))]


def square(me):
    return me + 1 - 2 * lax.rem(me, 2), lax.rem(me + 2, 4)


def ring(n, me):
    return [lax.rem(me + k, n) for k in range(1, n)]


def push(src, dst, send_sem, recv_sem, peer):
    return pltpu.make_async_remote_copy(
        src_ref=src,
        dst_ref=dst,
        send_sem=send_sem,
        recv_sem=recv_sem,
        device_id=peer if isinstance(peer, dict) else {"seq": peer},
        device_id_type=MESH,
    )


def sources(n):
    me = lax.axis_index("seq")
    if n == 4:
        along_x, along_y = square(me)
        return [me, along_x, along_y, square(along_y)[0]]
    return [lax.rem(me + n - k, n) for k in range(n)]


class Spread:
    def __init__(self, n, source, slot, rows, sems):
        self.n = n
        me = lax.axis_index("seq")
        self.order = sources(n)
        send, recv = sems
        if n != 4:
            self.copies = [
                push(source, slot(me, 0, rows), send.at[k], recv.at[k], peer)
                for k, peer in enumerate(ring(n, me), 1)
            ]
            return
        along_x, along_y = square(me)
        half = rows // 2

        def copy(number, owner, part, peer):
            here = source.at[pl.ds(part * half, half)] if owner is me else slot(owner, part * half, half)
            return push(here, slot(owner, part * half, half), send.at[number], recv.at[number], peer)

        self.copies = [
            copy(0, me, 0, along_x),
            copy(1, me, 1, along_y),
            copy(2, me, 1, along_x),
            copy(3, me, 0, along_y),
            copy(4, along_x, 0, along_y),
            copy(5, along_y, 1, along_x),
        ]

    def start(self):
        for copy in self.copies[:4] if self.n == 4 else self.copies:
            copy.start()

    def forward(self):
        if self.n == 4:
            for first, second in ((0, 4), (1, 5)):
                self.copies[first].wait_recv()
                self.copies[second].start()

    def arrive(self, k):
        if self.n == 4:
            for number in ((), (2,), (3,), (4, 5))[k]:
                self.copies[number].wait_recv()
        else:
            self.copies[k - 1].wait_recv()

    def sent(self):
        for copy in self.copies:
            copy.wait_send()

    def all(self):
        self.start()
        self.forward()
        for k in range(1, self.n):
            self.arrive(k)
        self.sent()


class Collect:
    def __init__(self, n, out, got, sems, mid=None):
        self.n = n
        self.out, self.got, self.mid = out, got, mid
        self.half = out.shape[1] // 2
        me = lax.axis_index("seq")
        self.order = sources(n)
        send, recv = sems
        if n != 4:
            self.copies = [
                push(out.at[k], got.at[k], send.at[k], recv.at[k], self.order[k]) for k in range(1, n)
            ]
            return
        along_x, along_y = square(me)

        def copy(number, chunk, part, peer):
            return push(self.piece(out, chunk, part), self.landing(number), send.at[number], recv.at[number], peer)

        self.copies = [
            copy(0, 1, 0, along_x),
            copy(1, 2, 1, along_y),
            copy(2, 3, 0, along_x),
            copy(3, 3, 1, along_y),
        ]
        for number, chunk, part, peer in ((4, 2, 0, along_y), (5, 1, 1, along_x)):
            source = self.piece(out, chunk, part) if mid is None else mid.at[number - 4]
            self.copies.append(
                push(source, self.landing(number), send.at[number], recv.at[number], peer)
            )

    def piece(self, ref, chunk, part):
        return ref.at[chunk, pl.ds(part * self.half, self.half)]

    def landing(self, number):
        return self.piece(self.got, number // 2, number % 2)

    def give(self, k, value):
        self.out[k] = value.astype(BF16)
        self.start(k)

    def start(self, k):
        if self.n == 4:
            for number in ((), (0,), (1,), (2, 3))[k]:
                self.copies[number].start()
        else:
            self.copies[k - 1].start()

    def relay(self):
        if self.n == 4:
            for number, chunk, part in ((2, 2, 0), (3, 1, 1)):
                self.copies[number].wait_recv()
                mine = self.piece(self.out, chunk, part)
                summed = (mine[...].astype(F32) + self.landing(number)[...].astype(F32)).astype(BF16)
                if self.mid is None:
                    mine[...] = summed
                else:
                    self.mid[number - 2] = summed
                self.copies[number + 2].start()

    def add_to(self, total):
        if self.n == 4:
            for number, part in ((0, 0), (1, 1), (4, 0), (5, 1)):
                self.copies[number].wait_recv()
                total[pl.ds(part * self.half, self.half)] += self.landing(number)[...].astype(F32)
        else:
            for k in range(1, self.n):
                self.copies[k - 1].wait_recv()
                total[...] += self.got[k].astype(F32)

    def sent(self):
        for copy in self.copies:
            copy.wait_send()


def way_sems(n):
    count = max(n, 6)
    return [pltpu.SemaphoreType.DMA((count,)), pltpu.SemaphoreType.DMA((count,))]


def row_slots(ref, tl):
    return lambda owner, first, rows: ref.at[pl.ds(pl.multiple_of(owner * tl + first, rows), rows)]


def chunk_slots(ref):
    return lambda owner, first, rows: ref.at[owner, pl.ds(first, rows)]


def cost(microseconds):
    return pl.CostEstimate(flops=int(microseconds * 1e9), bytes_accessed=0, transcendentals=0)


def params(collective_id=None):
    return pltpu.CompilerParams(
        collective_id=collective_id,
        has_side_effects=collective_id is not None,
        vmem_limit_bytes=VMEM_BYTES,
    )


def shape(dims, dtype):
    return jax.ShapeDtypeStruct(dims, dtype)


def start_kernel(n, shards, x_ref, own_ref, out_ref, a0_ref, f0_ref, a1_ref, f1_ref,
                 all_ref, send, recv, send_g, recv_g):
    tl = x_ref.shape[0]
    cut = own_ref.shape[1]
    me = lax.axis_index("seq")
    layer = lax.axis_index("section")
    row = lax.axis_index("dp")
    mine = aligned(me * tl, tl)
    peers = [
        {"section": lax.rem(layer + i, 2), "dp": lax.rem(row + j, shards)}
        for i in range(2)
        for j in range(shards)
        if i + j
    ]
    signal_and_wait(peers + near(n))
    copies = [
        push(own_ref, all_ref.at[layer, row], send_g.at[i], recv_g.at[i], peer)
        for i, peer in enumerate(peers)
    ]
    for copy in copies:
        copy.start()
    all_ref[layer, row] = own_ref[...]
    rows = x_ref[...].astype(F32)
    inv = inverse_rms(rows)
    for copy in copies:
        copy.wait()
    for z in range(shards):
        part = slice(z * cut, (z + 1) * cut)
        a0_ref[:, part] = all_ref[0, z, 0:1, :].astype(F32)
        f0_ref[:, part] = all_ref[0, z, 1:2, :].astype(F32)
        a1_ref[:, part] = all_ref[1, z, 0:1, :].astype(F32)
        f1_ref[:, part] = all_ref[1, z, 1:2, :].astype(F32)
    out_ref[mine] = (rows * inv * a0_ref[...]).astype(BF16)
    Spread(n, out_ref.at[mine], row_slots(out_ref, tl), tl, (send, recv)).all()


def start(n, shards, x, gains):
    tl, width = x.shape
    gain = shape((1, width), F32)
    return pl.pallas_call(
        functools.partial(start_kernel, n, shards),
        out_shape=(shape((n * tl, width), BF16), gain, gain, gain, gain),
        in_specs=[WHOLE] * 2,
        out_specs=(WHOLE,) * 5,
        scratch_shapes=[
            pltpu.VMEM((2, shards) + gains.shape, BF16),
            *way_sems(n),
            pltpu.SemaphoreType.DMA((2 * shards - 1,)),
            pltpu.SemaphoreType.DMA((2 * shards - 1,)),
        ],
        compiler_params=params(6),
        cost_estimate=cost(28),
        name="start",
    )(x, gains)


def gather_kernel(n, x_ref, gain_ref, w_any, out_ref, qkv_ref, w_ref, load, send, recv):
    tl = x_ref.shape[0]
    mine = aligned(lax.axis_index("seq") * tl, tl)
    weight = pltpu.make_async_copy(w_any, w_ref, load.at[0])
    weight.start()
    signal_and_wait(near(n))
    rows = x_ref[...].astype(F32)
    out_ref[mine] = (rows * inverse_rms(rows) * gain_ref[...]).astype(BF16)
    spread = Spread(n, out_ref.at[mine], row_slots(out_ref, tl), tl, (send, recv))
    spread.start()
    weight.wait()
    for k in range(n):
        where = aligned(spread.order[k] * tl, tl)
        if k:
            spread.arrive(k)
        qkv_ref[where] = mm(out_ref[where], w_ref[...]).astype(BF16)
        if not k:
            spread.forward()
    spread.sent()


def norm_gather(n, x, gain, w):
    tl, width = x.shape
    return pl.pallas_call(
        functools.partial(gather_kernel, n),
        out_shape=(shape((n * tl, width), BF16), shape((n * tl, w.shape[1]), BF16)),
        in_specs=[WHOLE] * 2 + [AWAY],
        out_specs=(WHOLE,) * 2,
        scratch_shapes=[pltpu.VMEM(w.shape, BF16), pltpu.SemaphoreType.DMA((1,)), *way_sems(n)],
        compiler_params=params(0),
        cost_estimate=cost(20),
        name="norm_gather",
    )(x, gain, w)


def toeplitz_rows(offset_row):
    spread = jnp.broadcast_to(offset_row, (LANES, offset_row.shape[1]))
    return pltpu.roll(spread, 0, 1, stride=1, stride_axis=0)


def attend_kernel(n, heads, dk, qkv_ref, eq_ref, ek_ref, rows_ref, chunk_ref,
                  o_ref, lse_ref, back_ref, chunks_ref,
                  bias_ref, kt_ref, qa_ref, send, recv, send_d, recv_d):
    length, wide = o_ref.shape
    tl = length // n
    group = QB // tl
    blocks = length // QB
    me = lax.axis_index("seq")
    mine = aligned(me * tl, tl)
    signal_and_wait(others("seq", n))
    spread = Spread(n, chunk_ref, chunk_slots(chunks_ref), chunk_ref.shape[0], (send_d, recv_d))
    spread.start()
    chunks_ref[me] = chunk_ref[...]
    lane = lax.broadcasted_iota(jnp.int32, (length, LANES), 1)
    lane_q = lax.broadcasted_iota(jnp.int32, (LANES, LANES), 1)
    pairs = (heads + 1) // 2
    for p in range(pairs):
        pair = pl.ds(p * LANES, LANES)
        k_pair = pl.ds(wide + p * LANES, LANES)
        v_pair = pl.ds(2 * wide + p * LANES, LANES)
        held = min(2, heads - 2 * p)
        for i in range(held):
            inside = (lane >= dk) if i else (lane < dk)
            qa_ref[i] = jnp.where(inside, qkv_ref[:, pair], eq_ref[...])
            kt_ref[i] = jnp.where(inside, qkv_ref[:, k_pair], ek_ref[...]).T
            bias_ref[i] = toeplitz_rows(rows_ref[2 * p + i : 2 * p + i + 1, :])

        def block(step, carry, p=p, pair=pair, v_pair=v_pair, held=held):
            b = lax.rem(lax.div(me, group) + 1 + step, blocks)
            rows = aligned(b * QB, QB)
            scores = [mm(qa_ref[i, rows, :], kt_ref[i]) for i in range(held)]
            for a in range(QB // LANES):
                tile = b * (QB // LANES) + a
                where = aligned(tile * LANES, LANES)
                off = pl.ds(pl.multiple_of(length - tile * LANES, LANES), length)
                lse = None if p == 0 else lse_ref[where, :]
                mixed = None
                for i in range(held):
                    part = scores[i][a * LANES : (a + 1) * LANES] + bias_ref[i, :, off]
                    peak = jnp.max(part, axis=-1, keepdims=True)
                    expo = jnp.exp(part - peak)
                    total = jnp.sum(expo, axis=-1, keepdims=True)
                    value = mm(expo.astype(BF16), qkv_ref[:, v_pair]) * (1.0 / total)
                    column = peak + jnp.log(total)
                    mixed = jnp.where(lane_q < dk, mixed, value) if i else value
                    if lse is None:
                        lse = jnp.broadcast_to(column, (LANES, LANES))
                    else:
                        lse = jnp.where(lane_q == 2 * p + i, column, lse)
                o_ref[where, pair] = mixed.astype(BF16)
                lse_ref[where, :] = lse
            for g in range(group):
                peer = b * group + g

                @pl.when(peer != me)
                def _(peer=peer):
                    push(
                        o_ref.at[aligned(peer * tl, tl), pair],
                        back_ref.at[me, :, pair],
                        send.at[p, peer],
                        recv.at[p, me],
                        peer,
                    ).start()

            return carry

        lax.fori_loop(0, blocks, block, 0)
        back_ref[me, :, pair] = o_ref[mine, pair]
        if p == 0:
            spread.forward()
    for k in range(1, n):
        spread.arrive(k)
    spread.sent()
    for p in range(pairs):
        pair = pl.ds(p * LANES, LANES)
        for k in range(1, n):
            peer = lax.rem(me + k, n)
            push(
                o_ref.at[aligned(peer * tl, tl), pair],
                back_ref.at[peer, :, pair],
                send.at[p, peer],
                recv.at[p, peer],
                peer,
            ).wait()


def attend(n, heads, dk, qkv, ext_q, ext_k, offset_rows, chunk):
    length, width = qkv.shape[0], qkv.shape[1] // 3
    span = offset_rows.shape[1]
    pair_sems = pltpu.SemaphoreType.DMA(((heads + 1) // 2, n))
    return pl.pallas_call(
        functools.partial(attend_kernel, n, heads, dk),
        out_shape=(
            shape((length, width), BF16),
            shape((length, LANES), F32),
            shape((n, length // n, width), BF16),
            shape((n,) + chunk.shape, BF16),
        ),
        in_specs=[WHOLE] * 5,
        out_specs=(WHOLE,) * 4,
        scratch_shapes=[
            pltpu.VMEM((2, LANES, span), F32),
            pltpu.VMEM((2, LANES, length), BF16),
            pltpu.VMEM((2, length, LANES), BF16),
            pair_sems,
            pair_sems,
            *way_sems(n),
        ],
        compiler_params=params(4 if chunk.shape[0] == length else 5),
        cost_estimate=cost(20),
        name="attend",
    )(qkv, ext_q, ext_k, offset_rows, chunk)


def three_parts(lane, value):
    first = value.astype(BF16).astype(F32)
    rest = value - first
    second = rest.astype(BF16).astype(F32)
    third = rest - second
    at = lax.rem(lane, 64)
    return jnp.where(at == 8, first, jnp.where(at == 9, second, jnp.where(at == 10, third, 0.0)))


def attend_back_kernel(n, heads, dk, summing, qkv_ref, do_any, o_ref, lse_ref, eq_ref, ek_ref, rows_ref,
                       *refs):
    length, wide = o_ref.shape
    span = rows_ref.shape[1]
    tl = length // n
    group = QB // tl
    blocks = length // QB
    me = lax.axis_index("seq")
    mine = aligned(me * tl, tl)
    signal_and_wait(others("seq", n))
    if summing:
        part_ref, own_ref, dqkv_ref, dr_ref, sum_ref = refs[:5]
        refs = refs[5:]
    else:
        g_ref, dqkv_ref, dr_ref, all_g = refs[:4]
        refs = refs[4:]
    (bias_ref, kt_ref, vt_ref, qa_ref, do_ref, qt_ref, dkt_ref, dvt_ref, dbias_ref, send, recv) = refs[:11]
    for k in range(1, n):
        peer = lax.rem(me + k, n)
        push(do_any.at[peer], do_ref.at[mine], send.at[peer], recv.at[me], peer).start()
    do_ref[mine] = do_any[me]
    if summing:
        mid_ref, got_ref, total_ref, send_y, recv_y = refs[11:]
        collect = Collect(n, part_ref, got_ref, (send_y, recv_y), mid_ref)
        for k in (3, 1, 2) if n == 4 else range(1, n):
            collect.start(k)
    else:
        spread = Spread(n, g_ref, chunk_slots(all_g), g_ref.shape[0], refs[11:])
        spread.start()
        all_g[me] = g_ref[...]
    lane = lax.broadcasted_iota(jnp.int32, (length, LANES), 1)
    lane_q = lax.broadcasted_iota(jnp.int32, (QB, LANES), 1)
    at = lax.rem(lane, 64)
    parts = (at >= 8) & (at <= 10)
    ones = jnp.where(parts, 1.0, 0.0)
    for p in range((heads + 1) // 2):
        pair = pl.ds(p * LANES, LANES)
        k_lanes = pl.ds(wide + p * LANES, LANES)
        v_lanes = pl.ds(2 * wide + p * LANES, LANES)
        held = min(2, heads - 2 * p)
        q_pair, k_pair, v_pair = qkv_ref[:, pair], qkv_ref[:, k_lanes], qkv_ref[:, v_lanes]
        qt_ref[...] = q_pair.T
        ek = (ek_ref[...].astype(F32) + ones).astype(BF16)
        for i in range(held):
            head = 2 * p + i
            inside = (lane >= dk) if i else (lane < dk)
            lse = lse_ref[:, head : head + 1]
            eq = (eq_ref[...].astype(F32) - three_parts(lane, lse)).astype(BF16)
            qa_ref[i] = jnp.where(inside, q_pair, eq)
            kt_ref[i] = jnp.where(inside, k_pair, ek).T
            vt_ref[i] = jnp.where(inside, v_pair, ones.astype(BF16)).T
            bias_ref[i] = toeplitz_rows(rows_ref[head : head + 1, :])
        dkt_ref[...] = jnp.zeros_like(dkt_ref)
        dvt_ref[...] = jnp.zeros_like(dvt_ref)
        dbias_ref[...] = jnp.zeros_like(dbias_ref)

        def block(step, carry, p=p, pair=pair, k_lanes=k_lanes, held=held):
            b = lax.rem(lax.div(me, group) + step, blocks)
            where = aligned(b * QB, QB)
            if p == 0:
                for g in range(group):
                    peer = b * group + g

                    @pl.when(peer != me)
                    def _(peer=peer):
                        rows = aligned(peer * tl, tl)
                        push(do_any.at[peer], do_ref.at[rows], send.at[peer], recv.at[peer], peer).wait()

            dq = None
            do_pair = do_ref[where, pair]
            do_t = do_pair.T
            weighed = do_pair.astype(F32) * o_ref[where, pair].astype(F32)
            for i in range(held):
                half = pl.ds(i * dk, dk)
                inside_q = (lane_q >= dk) if i else (lane_q < dk)
                delta = jnp.sum(jnp.where(inside_q, weighed, 0.0), axis=-1, keepdims=True)
                da = jnp.where(inside_q, do_pair, (-three_parts(lane_q, delta)).astype(BF16))
                scores = mm(qa_ref[i, where, :], kt_ref[i])
                lifted = mm(da, vt_ref[i])
                probs, grads = [], []
                for a in range(QB // LANES):
                    cut = slice(a * LANES, (a + 1) * LANES)
                    tile = b * (QB // LANES) + a
                    off = pl.ds(pl.multiple_of(length - tile * LANES, LANES), length)
                    prob = jnp.exp(scores[cut] + bias_ref[i, :, off])
                    grad = prob * lifted[cut]
                    dbias_ref[i, :, off] += grad
                    probs.append(prob.astype(BF16))
                    grads.append(grad.astype(BF16))
                prob = jnp.concatenate(probs, axis=0)
                grad = jnp.concatenate(grads, axis=0)
                value = mm(grad, qkv_ref[:, k_lanes])
                dq = jnp.where(lane_q < dk, dq, value) if i else value
                dkt_ref[half, :] += mm(qt_ref[half, where], grad)
                dvt_ref[half, :] += mm(do_t[i * dk : (i + 1) * dk], prob)
            dqkv_ref[where, pair] = dq.astype(BF16)
            return carry

        lax.fori_loop(0, length // QB, block, 0)
        dqkv_ref[:, k_lanes] = dkt_ref[...].T.astype(BF16)
        dqkv_ref[:, v_lanes] = dvt_ref[...].T.astype(BF16)
        place = lax.broadcasted_iota(jnp.int32, (8, span), 0)
        for i in range(held):
            folded = dbias_ref[i]
            rows = LANES
            while rows > 8:
                rows //= 2
                folded = folded[:rows] + pltpu.roll(folded[rows:], span - rows, 1)
            for bit in (4, 2, 1):
                folded = jnp.where(
                    lax.rem(lax.div(place, bit), 2) == 1, pltpu.roll(folded, span - bit, 1), folded
                )
            dr_ref[2 * p + i : 2 * p + i + 1, :] = jnp.sum(folded, axis=0, keepdims=True)
        if p == 0:
            if summing:
                collect.relay()
            else:
                spread.forward()
    if summing:
        total_ref[...] = own_ref[...]
        collect.add_to(total_ref)
        sum_ref[...] = total_ref[...].astype(BF16)
        collect.sent()
    else:
        for k in range(1, n):
            spread.arrive(k)
        spread.sent()


def attend_back(n, heads, dk, qkv, do, o, lse, ext_q, ext_k, offset_rows, chunk=None, parts=None, own=None):
    length, width = o.shape
    span = offset_rows.shape[1]
    operands = [qkv, do, o, lse, ext_q, ext_k, offset_rows]
    out_shape = [shape((length, 3 * width), BF16), shape((heads, span), F32)]
    sems = pltpu.SemaphoreType.DMA((n,))
    summing = parts is not None
    if summing:
        operands += [parts, own]
        out_shape.append(shape(own.shape, BF16))
        scratch = [
            pltpu.VMEM((2, own.shape[0] // 2, own.shape[1]), BF16),
            pltpu.VMEM(parts.shape, BF16),
            pltpu.VMEM(own.shape, F32),
        ]
    else:
        operands.append(chunk)
        out_shape.append(shape((n,) + chunk.shape, BF16))
        scratch = []
    return pl.pallas_call(
        functools.partial(attend_back_kernel, n, heads, dk, summing),
        out_shape=out_shape,
        in_specs=[WHOLE] * len(operands),
        out_specs=[WHOLE] * len(out_shape),
        scratch_shapes=[
            pltpu.VMEM((2, LANES, span), F32),
            pltpu.VMEM((2, LANES, length), BF16),
            pltpu.VMEM((2, LANES, length), BF16),
            pltpu.VMEM((2, length, LANES), BF16),
            pltpu.VMEM((length, width), BF16),
            pltpu.VMEM((LANES, length), BF16),
            pltpu.VMEM((LANES, length), F32),
            pltpu.VMEM((LANES, length), F32),
            pltpu.VMEM((2, LANES, span), F32),
            sems,
            sems,
            *scratch,
            *way_sems(n),
        ],
        compiler_params=params(9 if summing else 11),
        cost_estimate=cost(25),
        name="attend_back",
    )(*operands)


def weight_loads(sources, targets, sems):
    if len(sources) == 3:
        return [
            [pltpu.make_async_copy(src, dst, sems.at[j])]
            for j, (src, dst) in enumerate(zip(sources, targets))
        ]
    packed = sources[-1]
    pieces, count, rows = packed.shape[:3]
    groups = [
        [
            pltpu.make_async_copy(
                packed.at[i, j], targets[j - count].at[pl.ds(i * rows, rows)], sems.at[j * pieces + i]
            )
            for i in range(pieces)
        ]
        for j in range(count)
    ]
    if count == 2:
        blocks, _, cols = sources[0].shape
        groups.insert(
            0,
            [
                pltpu.make_async_copy(
                    sources[0].at[t], targets[0].at[:, pl.ds(t * cols, cols)], sems.at[2 * pieces + t]
                )
                for t in range(blocks)
            ],
        )
    return groups


def load_sems(weights):
    count = 3
    if len(weights) < 3:
        count = weights[-1].shape[0] * weights[-1].shape[1] + (weights[0].shape[0] if len(weights) == 2 else 0)
    return pltpu.SemaphoreType.DMA((count,))


def arrive(copies):
    for copy in copies:
        copy.wait()


def mix_kernel(n, hw, many, *refs):
    x_ref, gain_ref, back_ref = refs[:3]
    sources = refs[3 : 3 + many]
    (y_ref, x1_ref, n2_ref, slope_ref, hid_ref,
     wo_ref, up_ref, down_ref, out_ref, got_ref, total_ref,
     load, turn, send_n, recv_n, send_y, recv_y) = refs[3 + many :]
    core = lax.axis_index("section")
    other = {"section": 1 - core}
    tl = x_ref.shape[0]
    me = lax.axis_index("seq")
    mine = aligned(me * tl, tl)
    loads = weight_loads(sources, (wo_ref, up_ref, down_ref), load)
    for group in loads:
        for copy in group:
            copy.start()
    signal_and_wait(near(n) + [other])
    arrive(loads[0])
    total = x_ref[...].astype(F32)
    for s in range(n):
        total += mm(back_ref[s][:, :hw], wo_ref[s * hw : (s + 1) * hw, :])
    total_ref[...] = total
    x1 = total_ref[...]
    x1_ref[...] = x1
    n2_ref[mine] = (x1 * inverse_rms(x1) * gain_ref[...]).astype(BF16)
    spread = Spread(n, n2_ref.at[mine], row_slots(n2_ref, tl), tl, (send_n, recv_n))
    collect = Collect(n, out_ref, got_ref, (send_y, recv_y))

    @pl.when(core == 1)
    def _():
        pl.semaphore_wait(turn, 1)

    spread.start()
    arrive(loads[1])
    arrive(loads[2])
    for k in range(n):
        where = aligned(spread.order[k] * tl, tl)
        if k:
            spread.arrive(k)
        u = mm(n2_ref[where], up_ref[...])
        half = 0.5 + 0.5 * lax.erf(u * math.sqrt(0.5))
        hid = (u * half).astype(BF16)
        hid_ref[where] = hid
        slope_ref[where] = (
            half + u * (jnp.exp(-0.5 * u * u) * (1.0 / math.sqrt(2.0 * math.pi)))
        ).astype(BF16)
        part = mm(hid, down_ref[...])
        if k:
            collect.give(k, part)
        else:
            total_ref[...] += part
            spread.forward()

            @pl.when(core == 0)
            def _():
                pl.semaphore_signal(turn, inc=1, device_id=other, device_id_type=MESH)

    collect.relay()
    collect.add_to(total_ref)
    y_ref[...] = total_ref[...].astype(BF16)
    spread.sent()
    collect.sent()


def mix(n, hw, ff, x, gain, back, weights):
    tl, width = x.shape
    return pl.pallas_call(
        functools.partial(mix_kernel, n, hw, len(weights)),
        out_shape=(
            shape((tl, width), BF16),
            shape((tl, width), F32),
            shape((n * tl, width), BF16),
            shape((n * tl, ff), BF16),
            shape((n * tl, ff), BF16),
        ),
        in_specs=[WHOLE] * 3 + [AWAY] * len(weights),
        out_specs=(WHOLE,) * 5,
        scratch_shapes=[
            pltpu.VMEM((n * hw, width), BF16),
            pltpu.VMEM((width, ff), BF16),
            pltpu.VMEM((ff, width), BF16),
            pltpu.VMEM((n, tl, width), BF16),
            pltpu.VMEM((n, tl, width), BF16),
            pltpu.VMEM((tl, width), F32),
            load_sems(weights),
            pltpu.SemaphoreType.REGULAR,
            *way_sems(n),
            *way_sems(n),
        ],
        compiler_params=params(1),
        cost_estimate=cost(55),
        name="mix",
    )(x, gain, back, *weights)


def norm_back(x1, dn, dy, gain):
    inv = inverse_rms(x1)
    scaled = x1 * inv
    g_gain = jnp.sum(dn * scaled, axis=0, keepdims=True)
    lifted = dn * gain
    return dy + inv * (lifted - scaled * jnp.mean(lifted * scaled, axis=-1, keepdims=True)), g_gain


def turn_kernel(n, hw, many, *refs):
    x_ref, gain_ref, back_ref, dy_all = refs[:4]
    sources_w = refs[4 : 4 + many]
    refs = refs[4 + many :]
    part_ref, own_ref, dx1_ref, do_ref, g_gain_ref = refs[:5]
    g_refs = refs[5:6] if many < 3 else refs[5:8]
    (wo_ref, up_ref, down_ref, n2_ref, hid_ref, du_ref, out_ref, got_ref, total_ref,
     load, turn, send_n, recv_n, send_d, recv_d) = refs[5 + len(g_refs) :]
    tl = x_ref.shape[0]
    core = lax.axis_index("section")
    other = {"section": 1 - core}
    me = lax.axis_index("seq")
    mine = aligned(me * tl, tl)
    loads = weight_loads(sources_w, (wo_ref, up_ref, down_ref), load)
    for group in loads:
        for copy in group:
            copy.start()
    signal_and_wait(near(n) + [other])
    arrive(loads[0])
    total = x_ref[...].astype(F32)
    for s in range(n):
        total += mm(back_ref[s][:, :hw], wo_ref[s * hw : (s + 1) * hw, :])
    own_ref[...] = total
    x1 = own_ref[...]
    n2_ref[mine] = (x1 * inverse_rms(x1) * gain_ref[...]).astype(BF16)
    spread = Spread(n, n2_ref.at[mine], row_slots(n2_ref, tl), tl, (send_n, recv_n))
    collect = Collect(n, out_ref, got_ref, (send_d, recv_d))

    @pl.when(core == 1)
    def _():
        pl.semaphore_wait(turn, 1)

    spread.start()
    arrive(loads[1])
    arrive(loads[2])
    for k in range(n):
        where = aligned(spread.order[k] * tl, tl)
        if k:
            spread.arrive(k)
        u = mm(n2_ref[where], up_ref[...])
        half = 0.5 + 0.5 * lax.erf(u * math.sqrt(0.5))
        hid_ref[where] = (u * half).astype(BF16)
        slope = half + u * (jnp.exp(-0.5 * u * u) * (1.0 / math.sqrt(2.0 * math.pi)))
        du = (mm_nt(dy_all[where], down_ref[...]) * slope).astype(BF16)
        du_ref[where] = du
        part = mm_nt(du, up_ref[...])
        if k:
            collect.give(k, part)
        else:
            total_ref[...] = part
            spread.forward()

            @pl.when(core == 0)
            def _():
                pl.semaphore_signal(turn, inc=1, device_id=other, device_id_type=MESH)

    for k in range(1, n):
        part_ref[k] = mm(hid_ref[aligned(spread.order[k] * tl, tl)], down_ref[...]).astype(BF16)
    collect.relay()
    part_ref[0] = jnp.zeros_like(out_ref[0])
    own_ref[...] = x1 + mm(hid_ref[mine], down_ref[...])
    store_grad(g_refs, 0, hid_ref, dy_all)
    store_grad(g_refs, 1, n2_ref, du_ref)
    collect.add_to(total_ref)
    dx1, g_gain_ref[...] = norm_back(x1, total_ref[...], dy_all[mine].astype(F32), gain_ref[...])
    dx1_ref[...] = dx1
    d_attn = dx1.astype(BF16)
    for s in range(n):
        do_ref[s] = mm_nt(d_attn, wo_ref[s * hw : (s + 1) * hw, :]).astype(BF16)
        store_rows(g_refs, 2, s * hw, mm_tn(back_ref[s][:, :hw], d_attn).astype(BF16))
    spread.sent()
    collect.sent()


def grad_shapes(weights, hw, n, ff, width):
    if len(weights) < 3:
        pieces, _, rows = weights[-1].shape[:3]
        return [shape((pieces, 3, rows, width), BF16)]
    return [shape((ff, width), BF16), shape((width, ff), BF16), shape((n * hw, width), BF16)]


def turn_round(n, hw, ff, x, gain, back, weights, dy_all):
    tl, width = x.shape
    out_shape = [
        shape((n, tl, width), BF16),
        shape((tl, width), F32),
        shape((tl, width), F32),
        shape((n, tl, hw), BF16),
        shape((1, width), F32),
        *grad_shapes(weights, hw, n, ff, width),
    ]
    return pl.pallas_call(
        functools.partial(turn_kernel, n, hw, len(weights)),
        out_shape=out_shape,
        in_specs=[WHOLE] * 4 + [AWAY] * len(weights),
        out_specs=[WHOLE] * len(out_shape),
        scratch_shapes=[
            pltpu.VMEM((n * hw, width), BF16),
            pltpu.VMEM((width, ff), BF16),
            pltpu.VMEM((ff, width), BF16),
            pltpu.VMEM((n * tl, width), BF16),
            pltpu.VMEM((n * tl, ff), BF16),
            pltpu.VMEM((n * tl, ff), BF16),
            pltpu.VMEM((n, tl, width), BF16),
            pltpu.VMEM((n, tl, width), BF16),
            pltpu.VMEM((tl, width), F32),
            load_sems(weights),
            pltpu.SemaphoreType.REGULAR,
            *way_sems(n),
            *way_sems(n),
        ],
        compiler_params=params(2),
        cost_estimate=cost(60),
        name="turn_round",
    )(x, gain, back, dy_all, *weights)


def mix_back_kernel(n, shards, hw, many, *refs):
    dy_ref, x1_ref, gain_ref, slope_ref, hid_ref, n2_ref, back_ref = refs[:7]
    sources_w = refs[7 : 7 + many]
    w_grad_ref, dx1_ref, do_ref, g_gain_ref = refs[7 + many : 11 + many]
    refs = refs[11 + many :]
    g_refs = refs[:1] if many < 3 else refs[:3]
    (share_ref, wo_ref, up_ref, down_ref, du_ref, out_ref, got_ref, total_ref, dy_all, got_z,
     load, send_n, recv_n, send_d, recv_d, send_z, recv_z) = refs[len(g_refs) :]
    tl = dy_ref.shape[0]
    me = lax.axis_index("seq")
    row = lax.axis_index("dp")
    rows_g = share_ref.shape[0]
    mine = aligned(me * tl, tl)
    loads = weight_loads(sources_w, (wo_ref, up_ref, down_ref), load)
    for group in reversed(loads):
        for copy in group:
            copy.start()
    signal_and_wait(near(n) + others("dp", shards))
    spread = Spread(n, dy_ref, row_slots(dy_all, tl), tl, (send_d, recv_d))
    spread.start()
    along = []
    for k in range(1, shards):
        peer = lax.rem(row + k, shards)
        copy = push(
            w_grad_ref.at[aligned(peer * rows_g, rows_g)],
            got_z.at[k], send_z.at[k], recv_z.at[k], {"dp": peer},
        )
        copy.start()
        along.append(copy)
    dy_all[mine] = dy_ref[...]
    collect = Collect(n, out_ref, got_ref, (send_n, recv_n))
    arrive(loads[2])
    arrive(loads[1])
    for k in range(n):
        where = aligned(spread.order[k] * tl, tl)
        if k:
            spread.arrive(k)
        du = (mm_nt(dy_all[where], down_ref[...]) * slope_ref[where].astype(F32)).astype(BF16)
        du_ref[where] = du
        part = mm_nt(du, up_ref[...])
        if k:
            collect.give(k, part)
        else:
            spread.forward()
            total_ref[...] = part
    store_grad(g_refs, 0, hid_ref, dy_all)
    collect.relay()
    store_grad(g_refs, 1, n2_ref, du_ref)
    collect.add_to(total_ref)
    dx1, g_gain_ref[...] = norm_back(x1_ref[...], total_ref[...], dy_ref[...].astype(F32), gain_ref[...])
    dx1_ref[...] = dx1
    d_attn = dx1.astype(BF16)
    arrive(loads[0])
    for s in range(n):
        do_ref[s] = mm_nt(d_attn, wo_ref[s * hw : (s + 1) * hw, :]).astype(BF16)
        store_rows(g_refs, 2, s * hw, mm_tn(back_ref[s][:, :hw], d_attn).astype(BF16))
    share = w_grad_ref[aligned(row * rows_g, rows_g), :].astype(F32)
    for k in range(1, shards):
        along[k - 1].wait()
        share += got_z[k].astype(F32)
    share_ref[...] = share.astype(BF16)
    spread.sent()
    collect.sent()


def store_rows(refs, index, first, value):
    if len(refs) == 1 and len(refs[0].shape) == 4:
        rows = refs[0].shape[2]
        for i in range(value.shape[0] // rows):
            refs[0][first // rows + i, index] = value[i * rows : (i + 1) * rows]
    else:
        refs[index][pl.ds(first, value.shape[0]), :] = value


def store_grad(refs, index, left_ref, right_ref):
    rows = min(256, left_ref.shape[1])

    def block(b, carry):
        first = pl.multiple_of(b * rows, rows)
        store_rows(refs, index, first, mm_tn(left_ref[:, pl.ds(first, rows)], right_ref[...]).astype(BF16))
        return carry

    lax.fori_loop(0, left_ref.shape[1] // rows, block, 0)


def mix_back(n, shards, hw, ff, dy, x1, gain, slope, hid, n2, back, weights, w_grad):
    tl, width = dy.shape
    share = (w_grad.shape[0] // shards, w_grad.shape[1])
    row_sems = pltpu.SemaphoreType.DMA((shards,))
    out_shape = [
        shape((tl, width), F32),
        shape((n, tl, hw), BF16),
        shape((1, width), F32),
        *grad_shapes(weights, hw, n, ff, width),
        shape(share, BF16),
    ]
    return pl.pallas_call(
        functools.partial(mix_back_kernel, n, shards, hw, len(weights)),
        out_shape=out_shape,
        in_specs=[WHOLE] * 7 + [AWAY] * len(weights) + [WHOLE],
        out_specs=[WHOLE] * len(out_shape),
        scratch_shapes=[
            pltpu.VMEM((n * hw, width), BF16),
            pltpu.VMEM((width, ff), BF16),
            pltpu.VMEM((ff, width), BF16),
            pltpu.VMEM((n * tl, ff), BF16),
            pltpu.VMEM((n, tl, width), BF16),
            pltpu.VMEM((n, tl, width), BF16),
            pltpu.VMEM((tl, width), F32),
            pltpu.VMEM((n * tl, width), BF16),
            pltpu.VMEM((shards,) + share, BF16),
            load_sems(weights),
            *way_sems(n),
            *way_sems(n),
            row_sems,
            row_sems,
        ],
        compiler_params=params(7),
        cost_estimate=cost(50),
        name="mix_back",
    )(dy, x1, gain, slope, hid, n2, back, *weights, w_grad)


def project_back_kernel(n, dqkv_ref, x_ref, dx1_ref, gain_ref, n1_ref, w_any,
                        dx_ref, low_ref, g_w_ref, g_gain_ref,
                        w_ref, out_ref, got_ref, total_ref, load, send, recv):
    tl = x_ref.shape[0]
    weight = pltpu.make_async_copy(w_any, w_ref, load.at[0])
    weight.start()
    signal_and_wait(near(n))
    weight.wait()
    collect = Collect(n, out_ref, got_ref, (send, recv))

    def part(k):
        return mm_nt(dqkv_ref[aligned(collect.order[k] * tl, tl), :], w_ref[...])

    for k in (3, 1, 2) if n == 4 else range(1, n):
        collect.give(k, part(k))
    total_ref[...] = part(0)
    collect.relay()
    store_grad([g_w_ref], 0, n1_ref, dqkv_ref)
    collect.add_to(total_ref)
    dx, g_gain_ref[...] = norm_back(x_ref[...].astype(F32), total_ref[...], dx1_ref[...], gain_ref[...])
    dx_ref[...] = dx
    low_ref[...] = dx.astype(BF16)
    collect.sent()


def project_back(n, dqkv, x, dx1, gain, n1, w):
    tl, width = x.shape
    return pl.pallas_call(
        functools.partial(project_back_kernel, n),
        out_shape=(
            shape((tl, width), F32),
            shape((tl, width), BF16),
            shape(w.shape, BF16),
            shape((1, width), F32),
        ),
        in_specs=[WHOLE] * 5 + [AWAY],
        out_specs=(WHOLE,) * 4,
        scratch_shapes=[
            pltpu.VMEM(w.shape, BF16),
            pltpu.VMEM((n, tl, width), BF16),
            pltpu.VMEM((n, tl, width), BF16),
            pltpu.VMEM((tl, width), F32),
            pltpu.SemaphoreType.DMA((1,)),
            *way_sems(n),
        ],
        compiler_params=params(3),
        cost_estimate=cost(30),
        name="project_back",
    )(dqkv, x, dx1, gain, n1, w)


def finish_kernel(n, shards, small_ref, g0_ref, w0_ref, g1_ref, share1_ref,
                  all_g, all_w0, all_w1, other_g, other_w, sums_ref,
                  got_c, got_c1, sent_z, got_z, small_got, tile_got,
                  send_g, recv_g, send_w0, recv_w0, send_w1, recv_w1,
                  send_c, recv_c, send_z, recv_z, send_x, recv_x, send_s, recv_s, send_t, recv_t):
    me = lax.axis_index("seq")
    core = lax.axis_index("section")
    row = lax.axis_index("dp")
    rows = sent_z.shape[1]
    other = {"section": 1 - core}
    peers = [
        (lax.rem(core + i, 2), lax.rem(row + j, shards))
        for i in range(2)
        for j in range(shards)
        if i + j
    ]
    signal_and_wait([{"section": c, "dp": z} for c, z in peers] + others("seq", n))

    spread_g = Spread(n, g0_ref, chunk_slots(all_g), g0_ref.shape[0], (send_g, recv_g))
    spread_g.start()
    crossed = [
        push(w0_ref.at[aligned((2 * z + 1 - core) * rows, rows)], got_c.at[z], send_c.at[z], recv_c.at[z], other)
        for z in range(shards)
    ] + [
        push(share1_ref.at[aligned((1 - core) * rows, rows)], got_c1, send_c.at[shards], recv_c.at[shards], other)
    ]
    for copy in crossed:
        copy.start()
    smalls = [
        push(small_ref.at[c, z], small_got.at[i], send_s.at[i], recv_s.at[i], {"section": c, "dp": z})
        for i, (c, z) in enumerate(peers)
    ]
    for copy in smalls:
        copy.start()

    def cross(source, target, t, number):
        sem = number * n + t
        return push(source, target.at[t], send_x.at[sem], recv_x.at[sem], other)

    @pl.when(core == 0)
    def _():
        for t in range(n):
            cross(g1_ref.at[t], other_g, t, 0).start()

    @pl.when(core == 1)
    def _():
        cross(g0_ref, other_g, me, 0).start()

    all_g[me] = g0_ref[...]
    for copy in crossed:
        copy.wait_recv()
    along = []
    for k in range(1, shards):
        peer = lax.rem(row + k, shards)
        both = w0_ref[aligned((2 * peer + core) * rows, rows), :].astype(F32) + got_c[peer].astype(F32)
        sent_z[k] = both.astype(BF16)
        copy = push(sent_z.at[k], got_z.at[k], send_z.at[k], recv_z.at[k], {"dp": peer})
        copy.start()
        along.append(copy)
    half = share1_ref[aligned(core * rows, rows), :].astype(F32) + got_c1[...].astype(F32)
    all_w1[me] = half.astype(BF16)
    spread_w1 = Spread(n, all_w1.at[me], chunk_slots(all_w1), rows, (send_w1, recv_w1))
    spread_w1.start()

    tile = small_ref[core, row]
    for i, copy in enumerate(smalls):
        copy.wait()
        tile += small_got[i]
    tile_got[0] = tile
    tiles = []
    for k in range(1, n):
        copy = push(tile_got.at[0], tile_got.at[k], send_t.at[k], recv_t.at[k], lax.rem(me + k, n))
        copy.start()
        tiles.append(copy)

    spread_g.forward()
    half = w0_ref[aligned((2 * row + core) * rows, rows), :].astype(F32) + got_c[row].astype(F32)
    for k in range(1, shards):
        along[k - 1].wait()
        half += got_z[k].astype(F32)
    all_w0[me] = half.astype(BF16)
    spread_w0 = Spread(n, all_w0.at[me], chunk_slots(all_w0), rows, (send_w0, recv_w0))
    spread_w0.start()
    spread_w1.forward()
    spread_w0.forward()

    @pl.when(core == 0)
    def _():
        cross(all_w1.at[me], other_w, me, 1).start()

    @pl.when(core == 1)
    def _():
        cross(all_w0.at[me], other_w, me, 1).start()

    for k in range(1, n):
        source = spread_g.order[k]
        spread_g.arrive(k)

        @pl.when(core == 1)
        def _():
            cross(all_g.at[source], other_g, source, 0).start()

    total = tile
    for k in range(1, n):
        tiles[k - 1].wait()
        total += tile_got[k]
    line = lax.broadcasted_iota(jnp.int32, tile.shape, 0)
    sums_ref[...] = jnp.where(line < 2, total, tile)
    for k in range(1, n):
        source = spread_g.order[k]
        spread_w1.arrive(k)
        spread_w0.arrive(k)

        @pl.when(core == 0)
        def _():
            cross(all_w1.at[source], other_w, source, 1).start()

        @pl.when(core == 1)
        def _():
            cross(all_w0.at[source], other_w, source, 1).start()

    for t in range(n):
        cross(g0_ref, other_g, t, 0).wait()
        cross(got_c1, other_w, t, 1).wait()
    for copy in crossed:
        copy.wait_send()
    for spread in (spread_g, spread_w0, spread_w1):
        spread.sent()


def finish(n, shards, small, g0, w0, g1, share1):
    sems = pltpu.SemaphoreType.DMA((n,))
    cross_sems = pltpu.SemaphoreType.DMA((2 * n,))
    core_sems = pltpu.SemaphoreType.DMA((shards + 1,))
    row_sems = pltpu.SemaphoreType.DMA((shards,))
    small_sems = pltpu.SemaphoreType.DMA((2 * shards - 1,))
    tile = small.shape[2:]
    half = (share1.shape[0] // 2, share1.shape[1])
    gathered_w = shape((n,) + half, BF16)
    return pl.pallas_call(
        functools.partial(finish_kernel, n, shards),
        out_shape=(
            shape(g1.shape, BF16),
            gathered_w,
            gathered_w,
            shape(g1.shape, BF16),
            gathered_w,
            shape(tile, F32),
        ),
        in_specs=[WHOLE] * 5,
        out_specs=(WHOLE,) * 6,
        scratch_shapes=[
            pltpu.VMEM((shards,) + half, BF16),
            pltpu.VMEM(half, BF16),
            pltpu.VMEM((shards,) + half, BF16),
            pltpu.VMEM((shards,) + half, BF16),
            pltpu.VMEM((2 * shards - 1,) + tile, F32),
            pltpu.VMEM((n,) + tile, F32),
            *way_sems(n),
            *way_sems(n),
            *way_sems(n),
            core_sems, core_sems, row_sems, row_sems, cross_sems, cross_sems,
            small_sems, small_sems, sems, sems,
        ],
        compiler_params=params(8),
        cost_estimate=cost(45),
        name="finish",
    )(small, g0, w0, g1, share1)


def assemble_kernel(n, shards, g0_ref, g1_ref, other_g, w0_ref, w1_ref, other_w,
                    down_ref, up_ref, out_ref, q_ref, k_ref, v_ref):
    first = lax.axis_index("section") == 0
    quarter = other_w.shape[1]
    hw = other_w.shape[2] // 3
    kept = 2 * quarter
    total = [None, None]
    for t in range(n):
        for half in range(2):
            if half == 0:
                g = jnp.where(first, g0_ref[t], other_g[t]).astype(F32)
                w = jnp.where(first, w0_ref[t], other_w[t]).astype(F32)
            else:
                g = jnp.where(first, other_g[t], g1_ref[t]).astype(F32)
                w = jnp.where(first, other_w[t], w1_ref[t]).astype(F32)
            rows = slice(half * quarter, (half + 1) * quarter)
            down_ref[t * kept + half * quarter : t * kept + (half + 1) * quarter, :] = g[:quarter]
            for z in range(shards):
                at = (z * n + t) * kept
                up_ref[rows, at : at + kept] = g[quarter : 2 * quarter, z * kept : (z + 1) * kept]
            share = g[2 * quarter :]
            total[half] = share if t == 0 else total[half] + share
            if t == n - 1:
                out_ref[rows, :] = total[half]
            for i, ref in enumerate((q_ref, k_ref, v_ref)):
                ref[rows, t * hw : (t + 1) * hw] = w[:, i * hw : (i + 1) * hw]


def assemble(n, shards, g0, g1, other_g, w0, w1, other_w):
    quarter = other_w.shape[1]
    model = other_g.shape[2]
    hw = other_w.shape[2] // 3
    kept = 2 * quarter
    square = shape((2 * quarter, n * hw), F32)
    return pl.pallas_call(
        functools.partial(assemble_kernel, n, shards),
        out_shape=(
            shape((n * kept, model), F32),
            shape((2 * quarter, n * shards * kept), F32),
            shape((2 * quarter, model), F32),
            square, square, square,
        ),
        in_specs=[WHOLE] * 6,
        out_specs=(WHOLE,) * 6,
        compiler_params=params(),
        cost_estimate=cost(12),
        name="assemble",
    )(g0, g1, other_g, w0, w1, other_w)


def swapped(value):
    return lax.ppermute(value, "section", [(0, 1), (1, 0)])


def body(inputs, cotangent, segments, buckets, query_weight, key_weight, value_weight, out_weight,
         up_weight, down_weight, attn_gain, ffn_gain, bias_table):
    first = lax.axis_index("section") == 0
    turn = lax.axis_index("seq")
    n = lax.axis_size("seq")
    shards = lax.axis_size("dp")
    depth, width = query_weight.shape[1:]
    ff = up_weight.shape[2]
    heads = bias_table.shape[2]
    hw = width // n
    dk = hw // heads
    kept = down_weight.shape[1] // n
    hidden = ff // n
    model = inputs.shape[-1]
    quarter = model // (2 * shards)
    packed = hidden == model == width

    x_in = jnp.where(first, inputs[0, 0], inputs[1, 0])
    d_out = jnp.where(first, cotangent[0, 0], cotangent[1, 0])
    seg = jnp.where(first, segments[0, 0], segments[1, 0])

    def columns(weight):
        return lax.dynamic_slice_in_dim(weight[0], turn * hw, hw, axis=1)

    own_qkv = jnp.concatenate([columns(query_weight), columns(key_weight), columns(value_weight)], axis=1)
    own_up = jnp.concatenate(
        [
            lax.dynamic_slice_in_dim(up_weight[0], (z * n + turn) * kept, kept, axis=1)
            for z in range(shards)
        ],
        axis=1,
    )
    own_down = lax.dynamic_slice_in_dim(down_weight[0], turn * kept, kept, axis=0)
    table = bias_table[0]

    def halves(own):
        rows = own.shape[0] // 2
        low, high = own[:rows], own[rows:]
        other = swapped(jnp.where(first, high, low))
        return jnp.where(first, low, other), jnp.where(first, other, high)

    def gathered(piece):
        return lax.all_gather(piece, ("dp", "section"), axis=0, tiled=True)

    qkv_halves = halves(own_qkv)
    out_halves = halves(out_weight[0])
    up_halves = halves(own_up)
    down_halves = halves(own_down)
    cols = model // n
    out_cols = lax.dynamic_slice_in_dim(out_halves[0], turn * cols, cols, axis=1)
    first_weights = gathered(jnp.concatenate([qkv_halves[0], out_cols], axis=1))
    out_cols = first_weights[:, 3 * hw :]

    def packed_gather(pieces):
        return lax.all_gather(jnp.stack(pieces), ("dp", "section"), axis=0, tiled=False)

    if packed:
        mix_weights = [[packed_gather((up_halves[0], down_halves[0]))]]
    else:
        mix_weights = [[gathered(up_halves[0]), gathered(down_halves[0])]]
    qkv_weights = [first_weights[:, : 3 * hw], gathered(qkv_halves[1])]
    pieces = (out_halves[1], up_halves[1], down_halves[1])
    mix_weights.append([packed_gather(pieces)] if packed else [gathered(piece) for piece in pieces])
    other_table = swapped(table)
    tables = (jnp.where(first, table, other_table), jnp.where(first, other_table, table))

    gains = jnp.pad(jnp.stack([attn_gain[0], ffn_gain[0]]), ((0, 14), (0, 0)))
    first_n1, *gain_rows = start(n, shards, x_in, gains)

    bucket_count = table.shape[0]
    onehot = (buckets[None, :] == jnp.arange(bucket_count, dtype=jnp.int32)[:, None]).astype(F32)
    offset_rows = [
        lax.dot_general(
            t.astype(F32), onehot, (((0,), (0,)), ((), ())), precision=HIGH, preferred_element_type=F32
        )
        for t in tables
    ]

    lanes = jnp.arange(LANES, dtype=jnp.int32) % 64
    same = seg[:, None] == lanes[None, :]
    ext_q = jnp.where((lanes < 8)[None, :] & ~same, NEG, 0.0).astype(BF16)
    ext_k = jnp.where((lanes < 8)[None, :] & same, 1.0, 0.0).astype(BF16)

    wide = max(hw, LANES)

    def pad(value):
        return value if hw == wide else jnp.pad(value, [(0, 0)] * (value.ndim - 1) + [(0, wide - hw)])

    def scattered(gr):
        if not packed:
            gr = [jnp.concatenate([part.reshape(2 * shards, -1, model) for part in gr], axis=1)]
        return lax.psum_scatter(
            gr[0].reshape(-1, model), ("dp", "section"), scatter_dimension=0, tiled=True
        )

    def widened(qkv):
        if hw == wide:
            return qkv
        return jnp.concatenate([pad(qkv[:, i * hw : (i + 1) * hw]) for i in range(3)], axis=1)

    def narrowed(dqkv):
        if hw == wide:
            return dqkv
        return jnp.concatenate([dqkv[:, i * wide : i * wide + hw] for i in range(3)], axis=1)

    qkv0 = widened(jnp.dot(first_n1, qkv_weights[0], preferred_element_type=F32).astype(BF16))
    o0, lse0, back0, out_all = attend(n, heads, dk, qkv0, ext_q, ext_k, offset_rows[0], out_cols)
    mix_weights[0].insert(0, out_all if packed else out_all.transpose(1, 0, 2).reshape(width, model))
    y0, x1, n2, slope, hid = mix(n, hw, hidden, x_in, gain_rows[1], back0, mix_weights[0])
    n1, qkv1 = norm_gather(n, y0, gain_rows[2], qkv_weights[1])
    qkv1 = widened(qkv1)
    o1, lse1, back1, d_all = attend(n, heads, dk, qkv1, ext_q, ext_k, offset_rows[1], d_out)
    y_parts, y_own, dx1, do, gr_ffn1, *gr = turn_round(
        n, hw, hidden, y0, gain_rows[3], back1, mix_weights[1], d_all.reshape(-1, model)
    )
    half1 = scattered(gr)
    dqkv, d_rows1, y1 = attend_back(
        n, heads, dk, qkv1, pad(do), o1, lse1, ext_q, ext_k, offset_rows[1], parts=y_parts, own=y_own
    )
    d_in1, dy, w_grad1, gr_attn1 = project_back(
        n, narrowed(dqkv), y0, dx1, gain_rows[2], n1, qkv_weights[1]
    )
    dx1, do, gr_ffn0, *gr, share1 = mix_back(
        n, shards, hw, hidden, dy, x1, gain_rows[1], slope, hid, n2, back0, mix_weights[0], w_grad1
    )
    half0 = scattered(gr)
    dqkv, d_rows0, all_g1 = attend_back(
        n, heads, dk, qkv0, pad(do), o0, lse0, ext_q, ext_k, offset_rows[0], chunk=half1
    )
    d_in0, _, w_grad0, gr_attn0 = project_back(
        n, narrowed(dqkv), x_in, dx1, gain_rows[0], first_n1, qkv_weights[0]
    )

    other = swapped(jnp.where(first, y1, y0))
    section_outputs = jnp.stack([jnp.where(first, y0, other), jnp.where(first, other, y1)])[None, :, None]
    other = swapped(jnp.where(first, d_in1, d_in0))
    input_grads = jnp.stack([jnp.where(first, d_in0, other), jnp.where(first, other, d_in1)])[None, :, None]

    cut = model // shards
    small = []
    for gr_attn, gr_ffn, d_rows in ((gr_attn0, gr_ffn0, d_rows0), (gr_attn1, gr_ffn1, d_rows1)):
        gr_table = lax.dot_general(
            onehot, d_rows, (((1,), (1,)), ((), ())), precision=HIGH, preferred_element_type=F32
        )
        flat = gr_table.reshape(shards, -1)
        flat = jnp.pad(flat, ((0, 0), (0, cut - flat.shape[1])))
        tile = jnp.stack([gr_attn.reshape(shards, cut), gr_ffn.reshape(shards, cut), flat], axis=1)
        small.append(jnp.pad(tile, ((0, 0), (0, 5), (0, 0))))
    all_g0, all_w0, all_w1, other_g, other_w, sums = finish(
        n, shards, jnp.stack(small), half0, w_grad0, all_g1, share1
    )
    g_attn, g_ffn = sums[0:1], sums[1:2]
    g_table = sums[2, : bucket_count // shards * heads].reshape(1, bucket_count // shards, heads)

    if packed:
        g_down, g_up, g_out, g_query, g_key, g_value = (
            part[None] for part in assemble(n, shards, all_g0, all_g1, other_g, all_w0, all_w1, other_w)
        )
    else:
        low, high = jnp.where(first, all_g0, other_g), jnp.where(first, other_g, all_g1)
        sizes = [kept // 2, quarter * hidden // model, width // (2 * shards)]
        cuts = [sum(sizes[:i]) for i in range(4)]

        def joined(index):
            return jnp.stack([part[:, cuts[index] : cuts[index + 1]] for part in (low, high)], axis=1)

        g_down = joined(0).astype(F32).reshape(1, n * kept, model)
        whole = joined(1).reshape(n, depth, shards, kept)
        g_up = whole.transpose(1, 2, 0, 3).reshape(1, depth, ff).astype(F32)
        g_out = jnp.sum(joined(2).astype(F32), axis=0).reshape(1, depth, model)
        low, high = jnp.where(first, all_w0, other_w), jnp.where(first, other_w, all_w1)
        whole = jnp.stack([low, high], axis=1).reshape(n, depth, 3, hw)
        g_query, g_key, g_value = (
            whole[:, :, i].transpose(1, 0, 2).reshape(1, depth, width).astype(F32) for i in range(3)
        )

    return (
        section_outputs,
        input_grads,
        g_query,
        g_key,
        g_value,
        g_out,
        g_up,
        g_down,
        g_attn,
        g_ffn,
        g_table,
    )


def solution(mesh):
    return jax.shard_map(
        body,
        mesh=mesh,
        in_specs=(
            P(None, "dp", "seq", None),
            P(None, "dp", "seq", None),
            P(None, "dp", None),
            P(),
            P("section", "dp", None),
            P("section", "dp", None),
            P("section", "dp", None),
            P("section", "dp", None),
            P("section", "dp", None),
            P("section", "dp", None),
            P("section", "dp"),
            P("section", "dp"),
            P("section", None, "seq"),
        ),
        out_specs=(
            P("section", None, "dp", "seq", None),
            P("section", None, "dp", "seq", None),
            P("section", "dp", None),
            P("section", "dp", None),
            P("section", "dp", None),
            P("section", "dp", None),
            P("section", "dp", None),
            P("section", "dp", None),
            P("section", "dp"),
            P("section", "dp"),
            P("section", "dp", "seq"),
        ),
        check_vma=False,
    )
```

```python
import functools
import math

import jax
import jax.numpy as jnp
from jax import lax
from jax.experimental import pallas as pl
from jax.experimental.pallas import tpu as pltpu
from jax.sharding import PartitionSpec as P

EPSILON = 1e-06
NEG = -1e30
HIGH = lax.Precision.HIGHEST
MESH = pl.DeviceIdType.MESH
F32 = jnp.float32
BF16 = jnp.bfloat16
LANES = 128
QB = 256
VMEM_BYTES = 56 << 20

AWAY = pl.BlockSpec(memory_space=pl.ANY)


def mm(left, right):
    return jnp.dot(left, right, preferred_element_type=F32)


def mm_nt(left, right):
    return lax.dot_general(left, right, (((1,), (1,)), ((), ())), preferred_element_type=F32)


def mm_tn(left, right):
    return lax.dot_general(left, right, (((0,), (0,)), ((), ())), preferred_element_type=F32)


def inverse_rms(rows):
    return lax.rsqrt(jnp.mean(rows * rows, axis=-1, keepdims=True) + EPSILON)


def aligned(start, size):
    return pl.ds(pl.multiple_of(start, size), size)


def signal_and_wait(peers):
    barrier = pltpu.get_barrier_semaphore()
    for peer in peers:
        pl.semaphore_signal(barrier, inc=1, device_id=peer, device_id_type=MESH)
    pl.semaphore_wait(barrier, len(peers))


def others(axis, n):
    me = lax.axis_index(axis)
    return [{axis: lax.rem(me + k, n)} for k in range(1, n)]


def near(n):
    me = lax.axis_index("seq")
    return [{"seq": peer} for peer in (square(me) if n == 4 else ring(n, me))]


def square(me):
    return me + 1 - 2 * lax.rem(me, 2), lax.rem(me + 2, 4)


def ring(n, me):
    return [lax.rem(me + k, n) for k in range(1, n)]


def push(src, dst, send_sem, recv_sem, peer):
    return pltpu.make_async_remote_copy(
        src_ref=src,
        dst_ref=dst,
        send_sem=send_sem,
        recv_sem=recv_sem,
        device_id=peer if isinstance(peer, dict) else {"seq": peer},
        device_id_type=MESH,
    )


def sources(n):
    me = lax.axis_index("seq")
    if n == 4:
        along_x, along_y = square(me)
        return [me, along_x, along_y, square(along_y)[0]]
    return [lax.rem(me + n - k, n) for k in range(n)]


class Spread:
    def __init__(self, n, source, slot, rows, sems):
        self.n = n
        me = lax.axis_index("seq")
        self.order = sources(n)
        send, recv = sems
        if n != 4:
            self.copies = [
                push(source, slot(me, 0, rows), send.at[k], recv.at[k], peer)
                for k, peer in enumerate(ring(n, me), 1)
            ]
            return
        along_x, along_y = square(me)
        half = rows // 2

        def copy(number, owner, part, peer):
            here = source.at[pl.ds(part * half, half)] if owner is me else slot(owner, part * half, half)
            return push(here, slot(owner, part * half, half), send.at[number], recv.at[number], peer)

        self.copies = [
            copy(0, me, 0, along_x),
            copy(1, me, 1, along_y),
            copy(2, me, 1, along_x),
            copy(3, me, 0, along_y),
            copy(4, along_x, 0, along_y),
            copy(5, along_y, 1, along_x),
        ]

    def start(self):
        for copy in self.copies[:4] if self.n == 4 else self.copies:
            copy.start()

    def forward(self):
        if self.n == 4:
            for first, second in ((0, 4), (1, 5)):
                self.copies[first].wait_recv()
                self.copies[second].start()

    def arrive(self, k):
        if self.n == 4:
            for number in ((), (2,), (3,), (4, 5))[k]:
                self.copies[number].wait_recv()
        else:
            self.copies[k - 1].wait_recv()

    def sent(self):
        for copy in self.copies:
            copy.wait_send()

    def all(self):
        self.start()
        self.forward()
        for k in range(1, self.n):
            self.arrive(k)
        self.sent()


class Collect:
    def __init__(self, n, out, got, sems, mid=None):
        self.n = n
        self.out, self.got, self.mid = out, got, mid
        self.half = out.shape[1] // 2
        me = lax.axis_index("seq")
        self.order = sources(n)
        send, recv = sems
        if n != 4:
            self.copies = [
                push(out.at[k], got.at[k], send.at[k], recv.at[k], self.order[k]) for k in range(1, n)
            ]
            return
        along_x, along_y = square(me)

        def copy(number, chunk, part, peer):
            return push(self.piece(out, chunk, part), self.landing(number), send.at[number], recv.at[number], peer)

        self.copies = [
            copy(0, 1, 0, along_x),
            copy(1, 2, 1, along_y),
            copy(2, 3, 0, along_x),
            copy(3, 3, 1, along_y),
        ]
        for number, chunk, part, peer in ((4, 2, 0, along_y), (5, 1, 1, along_x)):
            source = self.piece(out, chunk, part) if mid is None else mid.at[number - 4]
            self.copies.append(
                push(source, self.landing(number), send.at[number], recv.at[number], peer)
            )

    def piece(self, ref, chunk, part):
        return ref.at[chunk, pl.ds(part * self.half, self.half)]

    def landing(self, number):
        return self.piece(self.got, number // 2, number % 2)

    def give(self, k, value):
        self.out[k] = value.astype(BF16)
        self.start(k)

    def start(self, k):
        if self.n == 4:
            for number in ((), (0,), (1,), (2, 3))[k]:
                self.copies[number].start()
        else:
            self.copies[k - 1].start()

    def relay(self):
        if self.n == 4:
            for number, chunk, part in ((2, 2, 0), (3, 1, 1)):
                self.copies[number].wait_recv()
                mine = self.piece(self.out, chunk, part)
                summed = (mine[...].astype(F32) + self.landing(number)[...].astype(F32)).astype(BF16)
                if self.mid is None:
                    mine[...] = summed
                else:
                    self.mid[number - 2] = summed
                self.copies[number + 2].start()

    def add_to(self, total):
        if self.n == 4:
            for number, part in ((0, 0), (1, 1), (4, 0), (5, 1)):
                self.copies[number].wait_recv()
                total[pl.ds(part * self.half, self.half)] += self.landing(number)[...].astype(F32)
        else:
            for k in range(1, self.n):
                self.copies[k - 1].wait_recv()
                total[...] += self.got[k].astype(F32)

    def sent(self):
        for copy in self.copies:
            copy.wait_send()


def way_sems(n):
    count = max(n, 6)
    return [pltpu.SemaphoreType.DMA((count,)), pltpu.SemaphoreType.DMA((count,))]


def row_slots(ref, tl):
    return lambda owner, first, rows: ref.at[pl.ds(pl.multiple_of(owner * tl + first, rows), rows)]


def chunk_slots(ref):
    return lambda owner, first, rows: ref.at[owner, pl.ds(first, rows)]


def cost(microseconds):
    return pl.CostEstimate(flops=int(microseconds * 1e9), bytes_accessed=0, transcendentals=0)


class Raw:
    def __init__(self, array):
        self.array = array


class Slots:
    def __init__(self, array):
        self.array = array


class Rows:
    def __init__(self, *arrays):
        self.array = arrays


class Late:
    def __init__(self, pairs, ref, sems):
        self.ref = ref
        self.copies = [pltpu.make_async_copy(src, dst, sems.at[i]) for i, (src, dst) in enumerate(pairs)]
        for copy in self.copies:
            copy.start()
        self.waiting = [True] * len(self.copies)

    def get(self, slot=None):
        for i, copy in enumerate(self.copies):
            if self.waiting[i] and (slot is None or slot == i):
                copy.wait()
                self.waiting[i] = False
        return self.ref


class Early:
    def __init__(self, target, ref, sems):
        self.target, self.ref, self.sems = target, ref, sems
        self.copies = []

    def flush(self, *part):
        src, dst = (self.ref.at[part], self.target.at[part]) if part else (self.ref, self.target)
        copy = pltpu.make_async_copy(src, dst, self.sems.at[len(self.copies)])
        copy.start()
        self.copies.append(copy)

    def done(self):
        if not self.copies:
            self.flush()
        for copy in self.copies:
            copy.wait()


def call(kernel, name, collective_id, microseconds, operands, outs, scratch):
    arrays, buffers, in_sems = [], [], []
    for operand in operands:
        array = operand.array if isinstance(operand, (Raw, Slots, Rows)) else operand
        arrays += array if isinstance(operand, Rows) else [array]
        if not isinstance(operand, Raw):
            copies = 1
            if isinstance(operand, Rows):
                dims = (sum(part.shape[0] for part in array),) + array[0].shape[1:]
                copies, dtype = len(array), array[0].dtype
            else:
                dims, dtype = array.shape, array.dtype
            if isinstance(operand, Slots):
                copies = dims[0]
            buffers.append(pltpu.VMEM(dims, dtype))
            in_sems.append(pltpu.SemaphoreType.DMA((copies,)))
    out_buffers = [pltpu.VMEM(dims, dtype) for dims, dtype, _ in outs]
    out_sems = [pltpu.SemaphoreType.DMA((flushes,)) for _, _, flushes in outs]

    def body(*refs):
        refs = list(refs)

        def take(count):
            taken = refs[:count]
            del refs[:count]
            return taken

        sources, targets = take(len(arrays)), take(len(outs))
        staged, results = take(len(buffers)), take(len(outs))
        staged_sems, result_sems = take(len(buffers)), take(len(outs))
        ins, at = [], 0
        for operand in operands:
            source = sources.pop(0)
            if isinstance(operand, Raw):
                ins.append(source)
                continue
            ref = staged[at]
            if isinstance(operand, Rows):
                pairs, first = [(source, ref.at[pl.ds(0, source.shape[0])])], source.shape[0]
                for _ in operand.array[1:]:
                    source = sources.pop(0)
                    pairs.append((source, ref.at[pl.ds(first, source.shape[0])]))
                    first += source.shape[0]
            elif isinstance(operand, Slots):
                pairs = [(source.at[i], ref.at[i]) for i in range(ref.shape[0])]
            else:
                pairs = [(source, ref)]
            ins.append(Late(pairs, ref, staged_sems[at]))
            at += 1
        early = [Early(*parts) for parts in zip(targets, results, result_sems)]
        kernel(ins, early, *refs)
        for late in ins:
            if isinstance(late, Late):
                late.get()
        for result in early:
            result.done()

    return pl.pallas_call(
        body,
        out_shape=[jax.ShapeDtypeStruct(dims, dtype) for dims, dtype, _ in outs],
        in_specs=[AWAY] * len(arrays),
        out_specs=[AWAY] * len(outs),
        scratch_shapes=[*buffers, *out_buffers, *in_sems, *out_sems, *scratch],
        compiler_params=pltpu.CompilerParams(
            collective_id=collective_id,
            has_side_effects=collective_id is not None,
            vmem_limit_bytes=VMEM_BYTES,
        ),
        cost_estimate=cost(microseconds),
        name=name,
    )(*arrays)


def start_kernel(n, shards, ins, outs, all_ref, send, recv, send_g, recv_g, send_z, recv_z, send_x, recv_x):
    x, own, piece = ins
    out, weight, *gains = outs
    tl = x.ref.shape[0]
    cut = own.ref.shape[1]
    me = lax.axis_index("seq")
    layer = lax.axis_index("section")
    row = lax.axis_index("dp")
    mine = aligned(me * tl, tl)
    peers = [
        {"section": lax.rem(layer + i, 2), "dp": lax.rem(row + j, shards)}
        for i in range(2)
        for j in range(shards)
        if i + j
    ]
    signal_and_wait(peers + near(n))
    own_ref = own.get()
    copies = [
        push(own_ref, all_ref.at[layer, row], send_g.at[i], recv_g.at[i], peer)
        for i, peer in enumerate(peers)
    ]
    for copy in copies:
        copy.start()
    all_ref[layer, row] = own_ref[...]
    weight.ref[row, layer] = piece.get()[...]

    def cross(z, core):
        ref = weight.ref.at[z, core]
        return push(ref, ref, send_x.at[z], recv_x.at[z], {"section": 1 - layer})

    along = []
    for k in range(1, shards):
        ref = weight.ref.at[row, layer]
        along.append(push(ref, ref, send_z.at[k], recv_z.at[k], {"dp": lax.rem(row + k, shards)}))
        along[-1].start()
    cross(row, layer).start()
    rows = x.get()[...].astype(F32)
    inv = inverse_rms(rows)
    for copy in copies:
        copy.wait()
    for z in range(shards):
        part = slice(z * cut, (z + 1) * cut)
        for i, gain in enumerate(gains):
            gain.ref[:, part] = all_ref[i // 2, z, i % 2 : i % 2 + 1, :].astype(F32)
    out.ref[mine] = (rows * inv * gains[0].ref[...]).astype(BF16)
    spread = Spread(n, out.ref.at[mine], row_slots(out.ref, tl), tl, (send, recv))
    spread.start()
    out.flush(mine)
    for gain in gains:
        gain.flush()
    spread.forward()
    for k in range(1, shards):
        along[k - 1].wait()
        cross(lax.rem(row + shards - k, shards), layer).start()
    for k in range(1, n):
        spread.arrive(k)
        out.flush(aligned(spread.order[k] * tl, tl))
    for z in range(shards):
        cross(z, 1 - layer).wait()
        weight.flush(z)
    spread.sent()


def start(n, shards, x, gains, piece):
    tl, width = x.shape
    small_sems = pltpu.SemaphoreType.DMA((2 * shards - 1,))
    row_sems = pltpu.SemaphoreType.DMA((shards,))
    return call(
        functools.partial(start_kernel, n, shards), "start", 6, 28,
        [x, gains, piece],
        [((n * tl, width), BF16, n), ((shards, 2) + piece.shape, BF16, shards)] + [((1, width), F32, 1)] * 4,
        [
            pltpu.VMEM((2, shards) + gains.shape, BF16),
            *way_sems(n),
            small_sems,
            small_sems,
            row_sems,
            row_sems,
            row_sems,
            row_sems,
        ],
    )


def gather_kernel(n, ins, outs, send, recv):
    x, gain, w = ins
    out, qkv = outs
    tl = x.ref.shape[0]
    mine = aligned(lax.axis_index("seq") * tl, tl)
    signal_and_wait(near(n))
    rows = x.get()[...].astype(F32)
    out.ref[mine] = (rows * inverse_rms(rows) * gain.get()[...]).astype(BF16)
    spread = Spread(n, out.ref.at[mine], row_slots(out.ref, tl), tl, (send, recv))
    spread.start()
    w.get()
    for k in range(n):
        where = aligned(spread.order[k] * tl, tl)
        if k:
            spread.arrive(k)
        out.flush(where)
        qkv.ref[where] = mm(out.ref[where], w.ref[...]).astype(BF16)
        qkv.flush(where)
        if not k:
            spread.forward()
    spread.sent()


def norm_gather(n, x, gain, w):
    tl, width = x.shape
    return call(
        functools.partial(gather_kernel, n), "norm_gather", 0, 20,
        [x, gain, w],
        [((n * tl, width), BF16, n), ((n * tl, w.shape[1]), BF16, n)],
        way_sems(n),
    )


def toeplitz_rows(offset_row):
    spread = jnp.broadcast_to(offset_row, (LANES, offset_row.shape[1]))
    return pltpu.roll(spread, 0, 1, stride=1, stride_axis=0)


def attend_kernel(n, heads, dk, ins, outs, bias_ref, kt_ref, qa_ref, send, recv, send_d, recv_d):
    chunk, qkv, eq, ek, rows = ins
    o, lse_out, back, chunks = outs
    o_ref, lse_ref, back_ref, chunks_ref = o.ref, lse_out.ref, back.ref, chunks.ref
    length, wide = o_ref.shape
    tl = length // n
    group = QB // tl
    blocks = length // QB
    me = lax.axis_index("seq")
    mine = aligned(me * tl, tl)
    signal_and_wait(others("seq", n))
    chunk_ref = chunk.get()
    spread = Spread(n, chunk_ref, chunk_slots(chunks_ref), chunk_ref.shape[0], (send_d, recv_d))
    spread.start()
    chunks_ref[me] = chunk_ref[...]
    chunks.flush(me)
    qkv_ref, eq_ref, ek_ref, rows_ref = qkv.get(), eq.get(), ek.get(), rows.get()
    lane = lax.broadcasted_iota(jnp.int32, (length, LANES), 1)
    lane_q = lax.broadcasted_iota(jnp.int32, (LANES, LANES), 1)
    pairs = (heads + 1) // 2
    for p in range(pairs):
        pair = pl.ds(p * LANES, LANES)
        k_pair = pl.ds(wide + p * LANES, LANES)
        v_pair = pl.ds(2 * wide + p * LANES, LANES)
        held = min(2, heads - 2 * p)
        for i in range(held):
            inside = (lane >= dk) if i else (lane < dk)
            qa_ref[i] = jnp.where(inside, qkv_ref[:, pair], eq_ref[...])
            kt_ref[i] = jnp.where(inside, qkv_ref[:, k_pair], ek_ref[...]).T
            bias_ref[i] = toeplitz_rows(rows_ref[2 * p + i : 2 * p + i + 1, :])

        def block(step, carry, p=p, pair=pair, v_pair=v_pair, held=held):
            b = lax.rem(lax.div(me, group) + 1 + step, blocks)
            rows = aligned(b * QB, QB)
            scores = [mm(qa_ref[i, rows, :], kt_ref[i]) for i in range(held)]
            for a in range(QB // LANES):
                tile = b * (QB // LANES) + a
                where = aligned(tile * LANES, LANES)
                off = pl.ds(pl.multiple_of(length - tile * LANES, LANES), length)
                lse = None if p == 0 else lse_ref[where, :]
                mixed = None
                for i in range(held):
                    part = scores[i][a * LANES : (a + 1) * LANES] + bias_ref[i, :, off]
                    peak = jnp.max(part, axis=-1, keepdims=True)
                    expo = jnp.exp(part - peak)
                    total = jnp.sum(expo, axis=-1, keepdims=True)
                    value = mm(expo.astype(BF16), qkv_ref[:, v_pair]) * (1.0 / total)
                    column = peak + jnp.log(total)
                    mixed = jnp.where(lane_q < dk, mixed, value) if i else value
                    if lse is None:
                        lse = jnp.broadcast_to(column, (LANES, LANES))
                    else:
                        lse = jnp.where(lane_q == 2 * p + i, column, lse)
                o_ref[where, pair] = mixed.astype(BF16)
                lse_ref[where, :] = lse
            for g in range(group):
                peer = b * group + g

                @pl.when(peer != me)
                def _(peer=peer):
                    push(
                        o_ref.at[aligned(peer * tl, tl), pair],
                        back_ref.at[me, :, pair],
                        send.at[p, peer],
                        recv.at[p, me],
                        peer,
                    ).start()

            return carry

        lax.fori_loop(0, blocks, block, 0)
        back_ref[me, :, pair] = o_ref[mine, pair]
        o.flush(slice(None), pair)
        if p == 0:
            spread.forward()
    lse_out.flush()
    for k in range(1, n):
        spread.arrive(k)
        chunks.flush(spread.order[k])
    spread.sent()
    for p in range(pairs):
        pair = pl.ds(p * LANES, LANES)
        for k in range(1, n):
            peer = lax.rem(me + k, n)
            push(
                o_ref.at[aligned(peer * tl, tl), pair],
                back_ref.at[peer, :, pair],
                send.at[p, peer],
                recv.at[p, peer],
                peer,
            ).wait()


def attend(n, heads, dk, qkv, ext_q, ext_k, offset_rows, chunk):
    length, width = qkv.shape[0], qkv.shape[1] // 3
    span = offset_rows.shape[1]
    pairs = (heads + 1) // 2
    pair_sems = pltpu.SemaphoreType.DMA((pairs, n))
    return call(
        functools.partial(attend_kernel, n, heads, dk), "attend", 4 if chunk.shape[0] == length else 5, 20,
        [chunk, qkv, ext_q, ext_k, offset_rows],
        [
            ((length, width), BF16, pairs),
            ((length, LANES), F32, 1),
            ((n, length // n, width), BF16, 1),
            ((n,) + chunk.shape, BF16, n),
        ],
        [
            pltpu.VMEM((2, LANES, span), F32),
            pltpu.VMEM((2, LANES, length), BF16),
            pltpu.VMEM((2, length, LANES), BF16),
            pair_sems,
            pair_sems,
            *way_sems(n),
        ],
    )


def three_parts(lane, value):
    first = value.astype(BF16).astype(F32)
    rest = value - first
    second = rest.astype(BF16).astype(F32)
    third = rest - second
    at = lax.rem(lane, 64)
    return jnp.where(at == 8, first, jnp.where(at == 9, second, jnp.where(at == 10, third, 0.0)))


def attend_back_kernel(n, heads, dk, summing, ins, outs, bias_ref, kt_ref, vt_ref, qa_ref, do_ref, qt_ref,
                       dkt_ref, dvt_ref, dbias_ref, send, recv, *refs):
    qkv, o, lse, eq, ek, rows, beside, *more = ins
    dqkv, dr, beside_out, *more_out = outs
    dqkv_ref, dr_ref = dqkv.ref, dr.ref
    length, wide = o.ref.shape
    span = rows.ref.shape[1]
    tl = length // n
    group = QB // tl
    blocks = length // QB
    me = lax.axis_index("seq")
    mine = aligned(me * tl, tl)
    signal_and_wait(others("seq", n))
    if summing:
        do, own = more
        mid_ref, got_ref, total_ref, send_y, recv_y = refs
        do_any = do.get()
        for k in range(1, n):
            peer = lax.rem(me + k, n)
            push(do_any.at[peer], do_ref.at[mine], send.at[peer], recv.at[me], peer).start()
        do_ref[mine] = do_any[me]
        collect = Collect(n, beside.get(), got_ref, (send_y, recv_y), mid_ref)
        for k in (3, 1, 2) if n == 4 else range(1, n):
            collect.start(k)
    else:
        dn2, x1, dy, gain, back, weights = more
        dx1_out, g_gain, g_out = more_out
        wo_ref, do_any, load, send_g, recv_g = refs
        loads = out_loads(weights, wo_ref, load)
        for copy in loads:
            copy.start()
        dx1, g_gain.ref[...] = norm_back(
            x1.get()[...], dn2.get()[...], dy.get()[...].astype(F32), gain.get()[...]
        )
        dx1_out.ref[...] = dx1
        dx1_out.flush()
        d_attn = dx1.astype(BF16)
        arrive(loads)
        back_ref = back.get()
        hw = wo_ref.shape[0] // n
        if hw < wide:
            do_any[...] = jnp.zeros_like(do_any)
        for k in range(1, n):
            peer = lax.rem(me + k, n)
            do_any[peer, :, :hw] = mm_nt(d_attn, wo_ref[aligned(peer * hw, hw), :]).astype(BF16)
            push(do_any.at[peer], do_ref.at[mine], send.at[peer], recv.at[me], peer).start()
        do_any[me, :, :hw] = mm_nt(d_attn, wo_ref[aligned(me * hw, hw), :]).astype(BF16)
        do_ref[mine] = do_any[me]
        g_ref = beside.get()
        spread = Spread(n, g_ref, chunk_slots(beside_out.ref), g_ref.shape[0], (send_g, recv_g))
        beside_out.ref[me] = g_ref[...]
        beside_out.flush(me)
        for t in range(n):
            g_out.ref[pl.ds(t * hw, hw), :] = mm_tn(back_ref[t][:, :hw], d_attn).astype(BF16)
        g_out.flush()
    qkv_ref, o_ref, lse_ref, eq_ref, ek_ref, rows_ref = (
        late.get() for late in (qkv, o, lse, eq, ek, rows)
    )
    lane = lax.broadcasted_iota(jnp.int32, (length, LANES), 1)
    lane_q = lax.broadcasted_iota(jnp.int32, (QB, LANES), 1)
    at = lax.rem(lane, 64)
    parts = (at >= 8) & (at <= 10)
    ones = jnp.where(parts, 1.0, 0.0)
    for p in range((heads + 1) // 2):
        pair = pl.ds(p * LANES, LANES)
        k_lanes = pl.ds(wide + p * LANES, LANES)
        v_lanes = pl.ds(2 * wide + p * LANES, LANES)
        held = min(2, heads - 2 * p)
        q_pair, k_pair, v_pair = qkv_ref[:, pair], qkv_ref[:, k_lanes], qkv_ref[:, v_lanes]
        qt_ref[...] = q_pair.T
        ek = (ek_ref[...].astype(F32) + ones).astype(BF16)
        for i in range(held):
            head = 2 * p + i
            inside = (lane >= dk) if i else (lane < dk)
            lse = lse_ref[:, head : head + 1]
            eq = (eq_ref[...].astype(F32) - three_parts(lane, lse)).astype(BF16)
            qa_ref[i] = jnp.where(inside, q_pair, eq)
            kt_ref[i] = jnp.where(inside, k_pair, ek).T
            vt_ref[i] = jnp.where(inside, v_pair, ones.astype(BF16)).T
            bias_ref[i] = toeplitz_rows(rows_ref[head : head + 1, :])
        dkt_ref[...] = jnp.zeros_like(dkt_ref)
        dvt_ref[...] = jnp.zeros_like(dvt_ref)
        dbias_ref[...] = jnp.zeros_like(dbias_ref)

        def given(peer):
            return push(
                do_any.at[peer], do_ref.at[aligned(peer * tl, tl)], send.at[peer], recv.at[peer], peer
            )

        if p == 0 and not summing:
            for k in range(1, n):
                given(lax.rem(me + k, n)).wait()
            spread.start()

        def block(step, carry, p=p, pair=pair, k_lanes=k_lanes, held=held):
            b = lax.rem(lax.div(me, group) + step, blocks)
            where = aligned(b * QB, QB)
            if p == 0 and summing:
                for g in range(group):
                    peer = b * group + g

                    @pl.when(peer != me)
                    def _(peer=peer):
                        given(peer).wait()

            dq = None
            do_pair = do_ref[where, pair]
            do_t = do_pair.T
            weighed = do_pair.astype(F32) * o_ref[where, pair].astype(F32)
            for i in range(held):
                half = pl.ds(i * dk, dk)
                inside_q = (lane_q >= dk) if i else (lane_q < dk)
                delta = jnp.sum(jnp.where(inside_q, weighed, 0.0), axis=-1, keepdims=True)
                da = jnp.where(inside_q, do_pair, (-three_parts(lane_q, delta)).astype(BF16))
                scores = mm(qa_ref[i, where, :], kt_ref[i])
                lifted = mm(da, vt_ref[i])
                probs, grads = [], []
                for a in range(QB // LANES):
                    cut = slice(a * LANES, (a + 1) * LANES)
                    tile = b * (QB // LANES) + a
                    off = pl.ds(pl.multiple_of(length - tile * LANES, LANES), length)
                    prob = jnp.exp(scores[cut] + bias_ref[i, :, off])
                    grad = prob * lifted[cut]
                    dbias_ref[i, :, off] += grad
                    probs.append(prob.astype(BF16))
                    grads.append(grad.astype(BF16))
                prob = jnp.concatenate(probs, axis=0)
                grad = jnp.concatenate(grads, axis=0)
                value = mm(grad, qkv_ref[:, k_lanes])
                dq = jnp.where(lane_q < dk, dq, value) if i else value
                dkt_ref[half, :] += mm(qt_ref[half, where], grad)
                dvt_ref[half, :] += mm(do_t[i * dk : (i + 1) * dk], prob)
            dqkv_ref[where, pair] = dq.astype(BF16)
            return carry

        lax.fori_loop(0, length // QB, block, 0)
        dqkv_ref[:, k_lanes] = dkt_ref[...].T.astype(BF16)
        dqkv_ref[:, v_lanes] = dvt_ref[...].T.astype(BF16)
        for lanes in (pair, k_lanes, v_lanes):
            dqkv.flush(slice(None), lanes)
        place = lax.broadcasted_iota(jnp.int32, (8, span), 0)
        for i in range(held):
            folded = dbias_ref[i]
            rows = LANES
            while rows > 8:
                rows //= 2
                folded = folded[:rows] + pltpu.roll(folded[rows:], span - rows, 1)
            for bit in (4, 2, 1):
                folded = jnp.where(
                    lax.rem(lax.div(place, bit), 2) == 1, pltpu.roll(folded, span - bit, 1), folded
                )
            dr_ref[2 * p + i : 2 * p + i + 1, :] = jnp.sum(folded, axis=0, keepdims=True)
        if p == 0:
            if summing:
                collect.relay()
            else:
                spread.forward()
    dr.flush()
    if summing:
        total_ref[...] = own.get()[...]
        collect.add_to(total_ref)
        beside_out.ref[...] = total_ref[...].astype(BF16)
        collect.sent()
    else:
        for k in range(1, n):
            spread.arrive(k)
            beside_out.flush(spread.order[k])
        spread.sent()


def out_loads(source, target, sems):
    if len(source.shape) == 2:
        return [pltpu.make_async_copy(source, target, sems.at[0])]
    blocks, _, cols = source.shape
    return [
        pltpu.make_async_copy(source.at[t], target.at[:, pl.ds(t * cols, cols)], sems.at[t])
        for t in range(blocks)
    ]


def attend_back(n, heads, dk, qkv, o, lse, ext_q, ext_k, offset_rows, beside, do=None, own=None, out_back=None):
    length, width = o.shape
    span = offset_rows.shape[1]
    sems = pltpu.SemaphoreType.DMA((n,))
    summing = out_back is None
    operands = [qkv, o, lse, ext_q, ext_k, offset_rows, beside]
    pairs = (heads + 1) // 2
    outs = [((length, 3 * width), BF16, 3 * pairs), ((heads, span), F32, 1)]
    if summing:
        operands += [do, own]
        outs.append((own.shape, BF16, 1))
        scratch = [
            pltpu.VMEM((2, own.shape[0] // 2, own.shape[1]), BF16),
            pltpu.VMEM(beside.shape, BF16),
            pltpu.VMEM(own.shape, F32),
        ]
    else:
        dn2, x1, dy, gain, back, wo = out_back
        tl, model = dn2.shape
        hd = wo.shape[-2]
        operands = [qkv, o, lse, ext_q, ext_k, offset_rows, beside, dn2, x1, dy, gain, back, Raw(wo)]
        outs += [
            ((n,) + beside.shape, BF16, n),
            ((tl, model), F32, 1),
            ((1, model), F32, 1),
            ((hd, model), BF16, 1),
        ]
        scratch = [
            pltpu.VMEM((hd, model), BF16),
            pltpu.VMEM((n, tl, width), BF16),
            sems,
        ]
    return call(
        functools.partial(attend_back_kernel, n, heads, dk, summing), "attend_back", 9 if summing else 11, 25,
        operands,
        outs,
        [
            pltpu.VMEM((2, LANES, span), F32),
            pltpu.VMEM((2, LANES, length), BF16),
            pltpu.VMEM((2, LANES, length), BF16),
            pltpu.VMEM((2, length, LANES), BF16),
            pltpu.VMEM((length, width), BF16),
            pltpu.VMEM((LANES, length), BF16),
            pltpu.VMEM((LANES, length), F32),
            pltpu.VMEM((LANES, length), F32),
            pltpu.VMEM((2, LANES, span), F32),
            sems,
            sems,
            *scratch,
            *way_sems(n),
        ],
    )


def weight_loads(sources, targets, sems):
    if len(sources) == 3:
        return [
            [pltpu.make_async_copy(src, dst, sems.at[j])] if dst is not None else None
            for j, (src, dst) in enumerate(zip(sources, targets))
        ]
    packed = sources[-1]
    pieces, count, rows = packed.shape[:3]
    groups = [
        [
            pltpu.make_async_copy(
                packed.at[i, j], targets[j - count].at[pl.ds(i * rows, rows)], sems.at[j * pieces + i]
            )
            for i in range(pieces)
        ]
        for j in range(count)
    ]
    if targets[0] is None:
        return [None] * (3 - count) + groups
    if count == 2:
        blocks, _, cols = sources[0].shape
        groups.insert(
            0,
            [
                pltpu.make_async_copy(
                    sources[0].at[t], targets[0].at[:, pl.ds(t * cols, cols)], sems.at[2 * pieces + t]
                )
                for t in range(blocks)
            ],
        )
    return groups


def load_sems(weights):
    count = 3
    if len(weights) < 3:
        count = weights[-1].shape[0] * weights[-1].shape[1] + (weights[0].shape[0] if len(weights) == 2 else 0)
    return pltpu.SemaphoreType.DMA((count,))


def arrive(copies):
    for copy in copies:
        copy.wait()


def mix_kernel(n, hw, ins, outs, wo_ref, up_ref, down_ref, out_ref, got_ref, total_ref,
               load, send_n, recv_n, send_y, recv_y):
    x, gain, back, *weights = ins
    y, x1_out, n2, slope, hid = outs
    n2_ref = n2.ref
    tl = x.ref.shape[0]
    me = lax.axis_index("seq")
    mine = aligned(me * tl, tl)
    loads = weight_loads(weights, (wo_ref, up_ref, down_ref), load)
    for group in loads:
        for copy in group:
            copy.start()
    signal_and_wait(near(n))
    back_ref = back.get()
    total = x.get()[...].astype(F32)
    arrive(loads[0])
    for s in range(n):
        total += mm(back_ref[s][:, :hw], wo_ref[s * hw : (s + 1) * hw, :])
    total_ref[...] = total
    x1 = total_ref[...]
    n2_ref[mine] = (x1 * inverse_rms(x1) * gain.get()[...]).astype(BF16)
    spread = Spread(n, n2_ref.at[mine], row_slots(n2_ref, tl), tl, (send_n, recv_n))
    collect = Collect(n, out_ref, got_ref, (send_y, recv_y))

    spread.start()
    x1_out.ref[...] = x1
    x1_out.flush()
    arrive(loads[1])
    arrive(loads[2])
    for k in range(n):
        where = aligned(spread.order[k] * tl, tl)
        if k:
            spread.arrive(k)
        n2.flush(where)
        u = mm(n2_ref[where], up_ref[...])
        half = 0.5 + 0.5 * lax.erf(u * math.sqrt(0.5))
        hidden = (u * half).astype(BF16)
        hid.ref[where] = hidden
        hid.flush(where)
        slope.ref[where] = (
            half + u * (jnp.exp(-0.5 * u * u) * (1.0 / math.sqrt(2.0 * math.pi)))
        ).astype(BF16)
        slope.flush(where)
        part = mm(hidden, down_ref[...])
        if k:
            collect.give(k, part)
        else:
            total_ref[...] += part
            spread.forward()

    collect.relay()
    collect.add_to(total_ref)
    y.ref[...] = total_ref[...].astype(BF16)
    y.flush()
    spread.sent()
    collect.sent()


def mix(n, hw, ff, x, gain, back, weights):
    tl, width = x.shape
    tokens = n * tl
    return call(
        functools.partial(mix_kernel, n, hw), "mix", 1, 45,
        [x, gain, back, *map(Raw, weights)],
        [
            ((tl, width), BF16, 1),
            ((tl, width), F32, 1),
            ((tokens, width), BF16, n),
            ((tokens, ff), BF16, n),
            ((tokens, ff), BF16, n),
        ],
        [
            pltpu.VMEM((n * hw, width), BF16),
            pltpu.VMEM((width, ff), BF16),
            pltpu.VMEM((ff, width), BF16),
            pltpu.VMEM((n, tl, width), BF16),
            pltpu.VMEM((n, tl, width), BF16),
            pltpu.VMEM((tl, width), F32),
            load_sems(weights),
            *way_sems(n),
            *way_sems(n),
        ],
    )


def norm_back(x1, dn, dy, gain):
    inv = inverse_rms(x1)
    scaled = x1 * inv
    g_gain = jnp.sum(dn * scaled, axis=0, keepdims=True)
    lifted = dn * gain
    return dy + inv * (lifted - scaled * jnp.mean(lifted * scaled, axis=-1, keepdims=True)), g_gain


def turn_kernel(n, hw, ins, outs, wo_ref, up_ref, down_ref, n2_ref, hid_ref, du_ref, out_ref, got_ref, total_ref,
                load, send_n, recv_n, send_d, recv_d):
    x, gain, back, dy, *weights = ins
    parts, own, dx1_out, do, g_gain, *grads = outs
    own_ref = own.ref
    tl = x.ref.shape[0]
    me = lax.axis_index("seq")
    mine = aligned(me * tl, tl)
    loads = weight_loads(weights, (wo_ref, up_ref, down_ref), load)
    for group in loads:
        for copy in group:
            copy.start()
    signal_and_wait(near(n))
    back_ref = back.get()
    total = x.get()[...].astype(F32)
    arrive(loads[0])
    for s in range(n):
        total += mm(back_ref[s][:, :hw], wo_ref[s * hw : (s + 1) * hw, :])
    own_ref[...] = total
    x1 = own_ref[...]
    gain_row = gain.get()[...]
    n2_ref[mine] = (x1 * inverse_rms(x1) * gain_row).astype(BF16)
    spread = Spread(n, n2_ref.at[mine], row_slots(n2_ref, tl), tl, (send_n, recv_n))
    collect = Collect(n, out_ref, got_ref, (send_d, recv_d))
    dy_all = dy.get()

    spread.start()
    arrive(loads[1])
    arrive(loads[2])
    for k in range(n):
        where = aligned(spread.order[k] * tl, tl)
        if k:
            spread.arrive(k)
        u = mm(n2_ref[where], up_ref[...])
        half = 0.5 + 0.5 * lax.erf(u * math.sqrt(0.5))
        hid_ref[where] = (u * half).astype(BF16)
        slope = half + u * (jnp.exp(-0.5 * u * u) * (1.0 / math.sqrt(2.0 * math.pi)))
        du = (mm_nt(dy_all[where], down_ref[...]) * slope).astype(BF16)
        du_ref[where] = du
        part = mm_nt(du, up_ref[...])
        if k:
            collect.give(k, part)
        else:
            total_ref[...] = part
            spread.forward()

    for k in range(1, n):
        parts.ref[k] = mm(hid_ref[aligned(spread.order[k] * tl, tl)], down_ref[...]).astype(BF16)
        parts.flush(k)
    collect.relay()
    parts.ref[0] = jnp.zeros_like(out_ref[0])
    parts.flush(0)
    own_ref[...] = x1 + mm(hid_ref[mine], down_ref[...])
    own.flush()
    store_grad(grads, 0, hid_ref, dy_all)
    store_grad(grads, 1, n2_ref, du_ref)
    collect.add_to(total_ref)
    dx1, g_gain.ref[...] = norm_back(x1, total_ref[...], dy_all[mine].astype(F32), gain_row)
    out_back(hw, dx1, dx1_out, do, grads, back_ref, wo_ref)
    spread.sent()
    collect.sent()


def out_back(hw, dx1, dx1_out, do, grads, back_ref, wo_ref):
    dx1_out.ref[...] = dx1
    dx1_out.flush()
    d_attn = dx1.astype(BF16)
    for s in range(back_ref.shape[0]):
        do.ref[s] = mm_nt(d_attn, wo_ref[s * hw : (s + 1) * hw, :]).astype(BF16)
        do.flush(s)
    for s in range(back_ref.shape[0]):
        store_rows(grads, 2, s * hw, mm_tn(back_ref[s][:, :hw], d_attn).astype(BF16))
    flush_grad(grads, 2)


def grad_shapes(weights, hw, n, ff, width):
    if len(weights) < 3:
        pieces, _, rows = weights[-1].shape[:3]
        return [((pieces, 3, rows, width), BF16, 3)]
    return [((ff, width), BF16, 1), ((width, ff), BF16, 1), ((n * hw, width), BF16, 1)]


def turn_round(n, hw, ff, x, gain, back, weights, dy_all):
    tl, width = x.shape
    return call(
        functools.partial(turn_kernel, n, hw), "turn_round", 2, 55,
        [x, gain, back, dy_all, *map(Raw, weights)],
        [
            ((n, tl, width), BF16, n),
            ((tl, width), F32, 1),
            ((tl, width), F32, 1),
            ((n, tl, hw), BF16, n),
            ((1, width), F32, 1),
            *grad_shapes(weights, hw, n, ff, width),
        ],
        [
            pltpu.VMEM((n * hw, width), BF16),
            pltpu.VMEM((width, ff), BF16),
            pltpu.VMEM((ff, width), BF16),
            pltpu.VMEM((n * tl, width), BF16),
            pltpu.VMEM((n * tl, ff), BF16),
            pltpu.VMEM((n * tl, ff), BF16),
            pltpu.VMEM((n, tl, width), BF16),
            pltpu.VMEM((n, tl, width), BF16),
            pltpu.VMEM((tl, width), F32),
            load_sems(weights),
            *way_sems(n),
            *way_sems(n),
        ],
    )


def mix_back_kernel(n, shards, ins, outs, up_ref, down_ref, du_ref, out_ref, got_ref, total_ref, dy_all,
                    got_c, sent_z, got_z, load, send_c, recv_c, send_n, recv_n, send_d, recv_d, send_z, recv_z):
    dy, w_grad, slope, hid, n2, *weights = ins
    dn2, half_out, *grads = outs
    tl = dy.ref.shape[0]
    me = lax.axis_index("seq")
    row = lax.axis_index("dp")
    core = lax.axis_index("section")
    other = {"section": 1 - core}
    rows = half_out.ref.shape[0]
    mine = aligned(me * tl, tl)
    loads = weight_loads(weights, (None, up_ref, down_ref), load)
    for group in reversed(loads[1:]):
        for copy in group:
            copy.start()
    signal_and_wait(near(n) + others("dp", shards) + [other])
    dy_ref = dy.get()
    spread = Spread(n, dy_ref, row_slots(dy_all, tl), tl, (send_d, recv_d))
    spread.start()
    w_grad_ref = w_grad.get()
    crossed = [
        push(w_grad_ref.at[aligned((2 * z + 1 - core) * rows, rows)], got_c.at[z], send_c.at[z], recv_c.at[z], other)
        for z in range(shards)
    ]
    for copy in crossed:
        copy.start()

    def both(z):
        return w_grad_ref[aligned((2 * z + core) * rows, rows), :].astype(F32) + got_c[z].astype(F32)

    dy_all[mine] = dy_ref[...]
    collect = Collect(n, out_ref, got_ref, (send_n, recv_n))
    arrive(loads[2])
    arrive(loads[1])
    slope_ref = slope.get()
    along = []
    for k in range(n):
        where = aligned(spread.order[k] * tl, tl)
        if k:
            spread.arrive(k)
        du = (mm_nt(dy_all[where], down_ref[...]) * slope_ref[where].astype(F32)).astype(BF16)
        du_ref[where] = du
        part = mm_nt(du, up_ref[...])
        if k:
            collect.give(k, part)
        else:
            spread.forward()
            dn2.ref[...] = part
            for copy in crossed:
                copy.wait()
            for i in range(1, shards):
                peer = lax.rem(row + i, shards)
                sent_z[i] = both(peer).astype(BF16)
                copy = push(sent_z.at[i], got_z.at[i], send_z.at[i], recv_z.at[i], {"dp": peer})
                copy.start()
                along.append(copy)
    store_grad(grads, 0, hid.get(), dy_all)
    collect.relay()
    store_grad(grads, 1, n2.get(), du_ref)
    half = both(row)
    for i in range(1, shards):
        along[i - 1].wait()
        half += got_z[i].astype(F32)
    half_out.ref[...] = half.astype(BF16)
    half_out.flush()
    collect.add_to(dn2.ref)
    spread.sent()
    collect.sent()


def flush_grad(grads, index):
    if len(grads) == 1:
        grads[0].flush(slice(None), index)
    else:
        grads[index].flush()


def store_rows(grads, index, first, value):
    if len(grads) == 1:
        ref = grads[0].ref
        rows = ref.shape[2]
        for i in range(value.shape[0] // rows):
            ref[first // rows + i, index] = value[i * rows : (i + 1) * rows]
    else:
        grads[index].ref[pl.ds(first, value.shape[0]), :] = value


def row_blocks(left_ref, right_ref, store):
    rows = min(256, left_ref.shape[1])

    def block(b, carry):
        first = pl.multiple_of(b * rows, rows)
        store(first, mm_tn(left_ref[:, pl.ds(first, rows)], right_ref[...]).astype(BF16))
        return carry

    lax.fori_loop(0, left_ref.shape[1] // rows, block, 0)


def store_grad(grads, index, left_ref, right_ref):
    row_blocks(left_ref, right_ref, functools.partial(store_rows, grads, index))
    flush_grad(grads, index)


def mix_back(n, shards, ff, dy, slope, hid, n2, weights, w_grad):
    tl, width = dy.shape
    half = (w_grad.shape[0] // (2 * shards), w_grad.shape[1])
    row_sems = pltpu.SemaphoreType.DMA((shards,))
    if len(weights) < 3:
        pieces, _, rows = weights[-1].shape[:3]
        grads = [((pieces, 2, rows, width), BF16, 2)]
    else:
        grads = [((ff, width), BF16, 1), ((width, ff), BF16, 1)]
    return call(
        functools.partial(mix_back_kernel, n, shards), "mix_back", 7, 40,
        [dy, w_grad, slope, hid, n2, *map(Raw, weights)],
        [((tl, width), F32, 1), (half, BF16, 1), *grads],
        [
            pltpu.VMEM((width, ff), BF16),
            pltpu.VMEM((ff, width), BF16),
            pltpu.VMEM((n * tl, ff), BF16),
            pltpu.VMEM((n, tl, width), BF16),
            pltpu.VMEM((n, tl, width), BF16),
            pltpu.VMEM((tl, width), F32),
            pltpu.VMEM((n * tl, width), BF16),
            pltpu.VMEM((shards,) + half, BF16),
            pltpu.VMEM((shards,) + half, BF16),
            pltpu.VMEM((shards,) + half, BF16),
            load_sems(weights),
            row_sems,
            row_sems,
            *way_sems(n),
            *way_sems(n),
            row_sems,
            row_sems,
        ],
    )


def project_back_kernel(n, shards, ins, outs, out_ref, got_ref, total_ref, send, recv, *refs):
    w, dqkv, n1, x, dx1, gain, *beside = ins
    dx_out, low, g_w, g_gain, *beside_out = outs
    me = lax.axis_index("seq")
    tl = x.ref.shape[0]
    if beside:
        got_c, sent_z, got_z, send_c, recv_c, send_z, recv_z, send_w, recv_w = refs
        row = lax.axis_index("dp")
        core = lax.axis_index("section")
        rows = got_c.shape[1]
        other = {"section": 1 - core}
        signal_and_wait(near(n) + others("dp", shards) + [other])
        g_out = beside[0].get()
        crossed = [
            push(g_out.at[aligned((2 * z + 1 - core) * rows, rows)], got_c.at[z], send_c.at[z], recv_c.at[z], other)
            for z in range(shards)
        ]
        for copy in crossed:
            copy.start()
    else:
        signal_and_wait(near(n))
    collect = Collect(n, out_ref, got_ref, (send, recv))
    w_ref, dqkv_ref = w.get(), dqkv.get()

    def part(k):
        return mm_nt(dqkv_ref[aligned(collect.order[k] * tl, tl), :], w_ref[...])

    for k in (3, 1, 2) if n == 4 else range(1, n):
        collect.give(k, part(k))
    if beside:

        def both(z):
            return g_out[aligned((2 * z + core) * rows, rows), :].astype(F32) + got_c[z].astype(F32)

        along = []
        for copy in crossed:
            copy.wait()
        for i in range(1, shards):
            peer = lax.rem(row + i, shards)
            sent_z[i] = both(peer).astype(BF16)
            along.append(push(sent_z.at[i], got_z.at[i], send_z.at[i], recv_z.at[i], {"dp": peer}))
            along[-1].start()
        half_w, all_w = beside[1].get(), beside_out[1].ref
        spread = Spread(n, half_w, chunk_slots(all_w), half_w.shape[0], (send_w, recv_w))
        spread.start()
        all_w[me] = half_w[...]
    total_ref[...] = part(0)
    collect.relay()

    def store(first, value):
        g_w.ref[pl.ds(first, value.shape[0]), :] = value

    row_blocks(n1.get(), dqkv_ref, store)
    g_w.flush()
    if beside:
        spread.forward()
    collect.add_to(total_ref)
    dx, g_gain.ref[...] = norm_back(x.get()[...].astype(F32), total_ref[...], dx1.get()[...], gain.get()[...])
    dx_out.ref[...] = dx
    dx_out.flush()
    low.ref[...] = dx.astype(BF16)
    low.flush()
    if beside:
        half = both(row)
        for i in range(1, shards):
            along[i - 1].wait()
            half += got_z[i].astype(F32)
        beside_out[0].ref[...] = half.astype(BF16)
        for k in range(1, n):
            spread.arrive(k)
        spread.sent()
    collect.sent()


def project_back(n, shards, dqkv, x, dx1, gain, n1, w, g_out=None, half_w=None):
    tl, width = x.shape
    operands = [w, dqkv, n1, x, dx1, gain]
    outs = [
        ((tl, width), F32, 1),
        ((tl, width), BF16, 1),
        ((width, dqkv.shape[1]), BF16, 1),
        ((1, width), F32, 1),
    ]
    scratch = []
    if g_out is not None:
        half = (g_out.shape[0] // (2 * shards), g_out.shape[1])
        operands += [g_out, half_w]
        outs += [(half, BF16, 1), ((n,) + half_w.shape, BF16, 1)]
        row_sems = pltpu.SemaphoreType.DMA((shards,))
        scratch = [pltpu.VMEM((shards,) + half, BF16)] * 3 + [row_sems] * 4 + way_sems(n)
    return call(
        functools.partial(project_back_kernel, n, shards), "project_back", 3 if g_out is None else 10, 22,
        operands,
        outs,
        [
            pltpu.VMEM((n, tl, width), BF16),
            pltpu.VMEM((n, tl, width), BF16),
            pltpu.VMEM((tl, width), F32),
            *way_sems(n),
            *scratch,
        ],
    )


def finish_kernel(n, shards, ins, outs, got_c, sent_z, got_z, small_got, tile_got,
                  send_g, recv_g, send_w0, recv_w0,
                  send_c, recv_c, send_z, recv_z, send_x, recv_x, send_s, recv_s, send_t, recv_t):
    g0, w0, w1, small, g1, y0, y1, d0, d1 = ins
    gathered_g, gathered_w0, other_g_out, other_w_out, sums, sections, d_inputs = outs
    all_g, all_w0 = gathered_g.ref, gathered_w0.ref
    other_g, other_w = other_g_out.ref, other_w_out.ref
    me = lax.axis_index("seq")
    core = lax.axis_index("section")
    row = lax.axis_index("dp")
    rows = sent_z.shape[1]
    other = {"section": 1 - core}
    peers = [
        (lax.rem(core + i, 2), lax.rem(row + j, shards))
        for i in range(2)
        for j in range(shards)
        if i + j
    ]
    signal_and_wait([{"section": c, "dp": z} for c, z in peers] + others("seq", n))

    g0_ref = g0.get()
    spread_g = Spread(n, g0_ref, chunk_slots(all_g), g0_ref.shape[0], (send_g, recv_g))
    spread_g.start()
    w0_ref = w0.get()
    crossed = [
        push(w0_ref.at[aligned((2 * z + 1 - core) * rows, rows)], got_c.at[z], send_c.at[z], recv_c.at[z], other)
        for z in range(shards)
    ]
    for copy in crossed:
        copy.start()
    small_ref = small.get()
    smalls = [
        push(small_ref.at[c, z], small_got.at[i], send_s.at[i], recv_s.at[i], {"section": c, "dp": z})
        for i, (c, z) in enumerate(peers)
    ]
    for copy in smalls:
        copy.start()

    def cross(source, target, t, number):
        sem = number * n + t
        return push(source, target.at[t], send_x.at[sem], recv_x.at[sem], other)

    def cross_rows(source, target, number):
        sem = 2 * n + number
        return push(source, target, send_x.at[sem], recv_x.at[sem], other)

    w1_ref, g1_ref, y0_ref, y1_ref, d0_ref, d1_ref = (late.get() for late in (w1, g1, y0, y1, d0, d1))

    @pl.when(core == 0)
    def _():
        cross_rows(y1_ref, sections.ref.at[0], 0).start()
        cross_rows(d1_ref, d_inputs.ref.at[0], 1).start()
        for t in range(n):
            cross(w1_ref.at[t], other_w, t, 1).start()
            cross(g1_ref.at[t], other_g, t, 0).start()
        sections.ref[0] = y0_ref[...]
        d_inputs.ref[0] = d0_ref[...]

    @pl.when(core == 1)
    def _():
        cross_rows(y0_ref, sections.ref.at[1], 0).start()
        cross_rows(d0_ref, d_inputs.ref.at[1], 1).start()
        cross(g0_ref, other_g, me, 0).start()
        sections.ref[1] = y1_ref[...]
        d_inputs.ref[1] = d1_ref[...]

    all_g[me] = g0_ref[...]
    gathered_g.flush(me)
    for copy in crossed:
        copy.wait_recv()
    along = []
    for k in range(1, shards):
        peer = lax.rem(row + k, shards)
        both = w0_ref[aligned((2 * peer + core) * rows, rows), :].astype(F32) + got_c[peer].astype(F32)
        sent_z[k] = both.astype(BF16)
        copy = push(sent_z.at[k], got_z.at[k], send_z.at[k], recv_z.at[k], {"dp": peer})
        copy.start()
        along.append(copy)

    tile = small_ref[core, row]
    for i, copy in enumerate(smalls):
        copy.wait()
        tile += small_got[i]
    tile_got[0] = tile
    tiles = []
    for k in range(1, n):
        copy = push(tile_got.at[0], tile_got.at[k], send_t.at[k], recv_t.at[k], lax.rem(me + k, n))
        copy.start()
        tiles.append(copy)

    spread_g.forward()
    half = w0_ref[aligned((2 * row + core) * rows, rows), :].astype(F32) + got_c[row].astype(F32)
    for k in range(1, shards):
        along[k - 1].wait()
        half += got_z[k].astype(F32)
    all_w0[me] = half.astype(BF16)
    gathered_w0.flush(me)
    spread_w0 = Spread(n, all_w0.at[me], chunk_slots(all_w0), rows, (send_w0, recv_w0))
    spread_w0.start()
    spread_w0.forward()

    @pl.when(core == 1)
    def _():
        cross(all_w0.at[me], other_w, me, 1).start()

    for k in range(1, n):
        source = spread_g.order[k]
        spread_g.arrive(k)
        gathered_g.flush(source)

        @pl.when(core == 1)
        def _():
            cross(all_g.at[source], other_g, source, 0).start()

    total = tile
    for k in range(1, n):
        tiles[k - 1].wait()
        total += tile_got[k]
    line = lax.broadcasted_iota(jnp.int32, tile.shape, 0)
    sums.ref[...] = jnp.where(line < 2, total, tile)
    for number, (source, target) in enumerate(((y0_ref, sections), (d0_ref, d_inputs))):
        cross_rows(source, target.ref.at[0], number).wait()
        target.flush()
    for k in range(1, n):
        source = spread_g.order[k]
        spread_w0.arrive(k)
        gathered_w0.flush(source)

        @pl.when(core == 1)
        def _():
            cross(all_w0.at[source], other_w, source, 1).start()

    for t in [me] + spread_g.order[1:]:
        cross(g0_ref, other_g, t, 0).wait()
        other_g_out.flush(t)
    for t in [me] + spread_g.order[1:]:
        cross(got_c.at[0], other_w, t, 1).wait()
        other_w_out.flush(t)
    for copy in crossed:
        copy.wait_send()
    for spread in (spread_g, spread_w0):
        spread.sent()


def finish(n, shards, small, g0, w0, g1, w1, y0, y1, d0, d1):
    sems = pltpu.SemaphoreType.DMA((n,))
    cross_sems = pltpu.SemaphoreType.DMA((2 * n + 2,))
    row_sems = pltpu.SemaphoreType.DMA((shards,))
    small_sems = pltpu.SemaphoreType.DMA((2 * shards - 1,))
    tile = small.shape[2:]
    half = w1.shape[1:]
    gathered_w = ((n,) + half, BF16, n)
    return call(
        functools.partial(finish_kernel, n, shards), "finish", 8, 48,
        [Rows(*g0), w0, w1, small, g1, y0, y1, d0, d1],
        [
            (g1.shape, BF16, n),
            gathered_w,
            (g1.shape, BF16, n),
            gathered_w,
            (tile, F32, 1),
            ((2,) + y0.shape, BF16, 1),
            ((2,) + d0.shape, F32, 1),
        ],
        [
            pltpu.VMEM((shards,) + half, BF16),
            pltpu.VMEM((shards,) + half, BF16),
            pltpu.VMEM((shards,) + half, BF16),
            pltpu.VMEM((2 * shards - 1,) + tile, F32),
            pltpu.VMEM((n,) + tile, F32),
            *way_sems(n),
            *way_sems(n),
            row_sems, row_sems, row_sems, row_sems, cross_sems, cross_sems,
            small_sems, small_sems, sems, sems,
        ],
    )


def assemble_kernel(n, shards, ins, outs):
    g0, other_g, g1, w0, other_w, w1 = ins
    down, up, out, *qkv = outs
    first = lax.axis_index("section") == 0
    quarter = other_w.ref.shape[1]
    hw = other_w.ref.shape[2] // 3
    kept = 2 * quarter
    total = [None, None]
    for t in range(n):
        for late in ins:
            late.get(t)
        for half in range(2):
            if half == 0:
                g = jnp.where(first, g0.ref[t], other_g.ref[t]).astype(F32)
                w = jnp.where(first, w0.ref[t], other_w.ref[t]).astype(F32)
            else:
                g = jnp.where(first, other_g.ref[t], g1.ref[t]).astype(F32)
                w = jnp.where(first, other_w.ref[t], w1.ref[t]).astype(F32)
            rows = slice(half * quarter, (half + 1) * quarter)
            down.ref[t * kept + half * quarter : t * kept + (half + 1) * quarter, :] = g[:quarter]
            for z in range(shards):
                at = (z * n + t) * kept
                up.ref[rows, at : at + kept] = g[quarter : 2 * quarter, z * kept : (z + 1) * kept]
            share = g[2 * quarter :]
            total[half] = share if t == 0 else total[half] + share
            if t == n - 1:
                out.ref[rows, :] = total[half]
            for i, grad in enumerate(qkv):
                grad.ref[rows, t * hw : (t + 1) * hw] = w[:, i * hw : (i + 1) * hw]
        down.flush(pl.ds(t * kept, kept))
        for z in range(shards):
            up.flush(slice(None), pl.ds((z * n + t) * kept, kept))
        for grad in qkv:
            grad.flush(slice(None), pl.ds(t * hw, hw))


def assemble(n, shards, g0, g1, other_g, w0, w1, other_w):
    quarter = other_w.shape[1]
    model = other_g.shape[2]
    hw = other_w.shape[2] // 3
    kept = 2 * quarter
    return call(
        functools.partial(assemble_kernel, n, shards), "assemble", None, 8,
        [Slots(array) for array in (g0, other_g, g1, w0, other_w, w1)],
        [
            ((n * kept, model), F32, n),
            ((2 * quarter, n * shards * kept), F32, n * shards),
            ((2 * quarter, model), F32, 1),
        ]
        + [((2 * quarter, n * hw), F32, n)] * 3,
        [],
    )


def swapped(value):
    return lax.ppermute(value, "section", [(0, 1), (1, 0)])


def body(inputs, cotangent, segments, buckets, query_weight, key_weight, value_weight, out_weight,
         up_weight, down_weight, attn_gain, ffn_gain, bias_table):
    first = lax.axis_index("section") == 0
    turn = lax.axis_index("seq")
    n = lax.axis_size("seq")
    shards = lax.axis_size("dp")
    depth, width = query_weight.shape[1:]
    ff = up_weight.shape[2]
    heads = bias_table.shape[2]
    hw = width // n
    dk = hw // heads
    kept = down_weight.shape[1] // n
    hidden = ff // n
    model = inputs.shape[-1]
    quarter = model // (2 * shards)
    packed = hidden == model == width

    x_in = jnp.where(first, inputs[0, 0], inputs[1, 0])
    d_out = jnp.where(first, cotangent[0, 0], cotangent[1, 0])
    seg = jnp.where(first, segments[0, 0], segments[1, 0])

    def columns(weight):
        return lax.dynamic_slice_in_dim(weight[0], turn * hw, hw, axis=1)

    own_qkv = jnp.concatenate([columns(query_weight), columns(key_weight), columns(value_weight)], axis=1)
    own_up = jnp.concatenate(
        [
            lax.dynamic_slice_in_dim(up_weight[0], (z * n + turn) * kept, kept, axis=1)
            for z in range(shards)
        ],
        axis=1,
    )
    own_down = lax.dynamic_slice_in_dim(down_weight[0], turn * kept, kept, axis=0)
    table = bias_table[0]

    def halves(own):
        rows = own.shape[0] // 2
        low, high = own[:rows], own[rows:]
        other = swapped(jnp.where(first, high, low))
        return jnp.where(first, low, other), jnp.where(first, other, high)

    def gathered(piece):
        return lax.all_gather(piece, ("dp", "section"), axis=0, tiled=True)

    qkv_halves = halves(own_qkv)
    out_halves = halves(out_weight[0])
    up_halves = halves(own_up)
    down_halves = halves(own_down)
    cols = model // n
    out_cols = lax.dynamic_slice_in_dim(out_halves[0], turn * cols, cols, axis=1)
    first_qkv = gathered(qkv_halves[0])

    def packed_gather(pieces):
        return lax.all_gather(jnp.stack(pieces), ("dp", "section"), axis=0, tiled=False)

    if packed:
        mix_weights = [[packed_gather((up_halves[0], down_halves[0]))]]
    else:
        mix_weights = [[gathered(up_halves[0]), gathered(down_halves[0])]]
    second_qkv = gathered(qkv_halves[1])
    pieces = (out_halves[1], up_halves[1], down_halves[1])
    mix_weights.append([packed_gather(pieces)] if packed else [gathered(piece) for piece in pieces])
    other_table = swapped(table)
    tables = (jnp.where(first, table, other_table), jnp.where(first, other_table, table))

    gains = jnp.pad(jnp.stack([attn_gain[0], ffn_gain[0]]), ((0, 14), (0, 0)))
    first_n1, out_cols, *gain_rows = start(n, shards, x_in, gains, out_cols)
    out_cols = out_cols.reshape(width, cols)

    bucket_count = table.shape[0]
    onehot = (buckets[None, :] == jnp.arange(bucket_count, dtype=jnp.int32)[:, None]).astype(F32)
    offset_rows = [
        lax.dot_general(
            t.astype(F32), onehot, (((0,), (0,)), ((), ())), precision=HIGH, preferred_element_type=F32
        )
        for t in tables
    ]

    lanes = jnp.arange(LANES, dtype=jnp.int32) % 64
    same = seg[:, None] == lanes[None, :]
    ext_q = jnp.where((lanes < 8)[None, :] & ~same, NEG, 0.0).astype(BF16)
    ext_k = jnp.where((lanes < 8)[None, :] & same, 1.0, 0.0).astype(BF16)

    wide = max(hw, LANES)

    def pad(value):
        return value if hw == wide else jnp.pad(value, [(0, 0)] * (value.ndim - 1) + [(0, wide - hw)])

    def scattered(gr):
        if not packed:
            gr = [jnp.concatenate([part.reshape(2 * shards, -1, model) for part in gr], axis=1)]
        return lax.psum_scatter(
            gr[0].reshape(-1, model), ("dp", "section"), scatter_dimension=0, tiled=True
        )

    def widened(qkv):
        if hw == wide:
            return qkv
        return jnp.concatenate([pad(qkv[:, i * hw : (i + 1) * hw]) for i in range(3)], axis=1)

    def narrowed(dqkv):
        if hw == wide:
            return dqkv
        return jnp.concatenate([dqkv[:, i * wide : i * wide + hw] for i in range(3)], axis=1)

    qkv0 = widened(jnp.dot(first_n1, first_qkv, preferred_element_type=F32).astype(BF16))
    o0, lse0, back0, out_all = attend(n, heads, dk, qkv0, ext_q, ext_k, offset_rows[0], out_cols)
    mix_weights[0].insert(0, out_all if packed else out_all.transpose(1, 0, 2).reshape(width, model))
    y0, x1, n2, slope, hid = mix(n, hw, hidden, x_in, gain_rows[1], back0, mix_weights[0])
    n1, qkv1 = norm_gather(n, y0, gain_rows[2], second_qkv)
    qkv1 = widened(qkv1)
    o1, lse1, back1, d_all = attend(n, heads, dk, qkv1, ext_q, ext_k, offset_rows[1], d_out)
    y_parts, y_own, dx1, do, gr_ffn1, *gr = turn_round(
        n, hw, hidden, y0, gain_rows[3], back1, mix_weights[1], d_all.reshape(-1, model)
    )
    half1 = scattered(gr)
    dqkv, d_rows1, y1 = attend_back(
        n, heads, dk, qkv1, o1, lse1, ext_q, ext_k, offset_rows[1], y_parts, do=pad(do), own=y_own
    )
    d_in1, dy, w_grad1, gr_attn1 = project_back(
        n, shards, narrowed(dqkv), y0, dx1, gain_rows[2], n1, second_qkv
    )
    dn2, half_w1, *gr = mix_back(n, shards, hidden, dy, slope, hid, n2, mix_weights[0], w_grad1)
    half0 = scattered(gr)
    dqkv, d_rows0, all_g1, dx1, gr_ffn0, gr_out = attend_back(
        n, heads, dk, qkv0, o0, lse0, ext_q, ext_k, offset_rows[0], half1,
        out_back=(dn2, x1, dy, gain_rows[1], back0, mix_weights[0][0]),
    )
    d_in0, _, w_grad0, gr_attn0, half_out, all_w1 = project_back(
        n, shards, narrowed(dqkv), x_in, dx1, gain_rows[0], first_n1, first_qkv, gr_out, half_w1
    )

    cut = model // shards
    small = []
    for gr_attn, gr_ffn, d_rows in ((gr_attn0, gr_ffn0, d_rows0), (gr_attn1, gr_ffn1, d_rows1)):
        gr_table = lax.dot_general(
            onehot, d_rows, (((1,), (1,)), ((), ())), precision=HIGH, preferred_element_type=F32
        )
        flat = gr_table.reshape(shards, -1)
        flat = jnp.pad(flat, ((0, 0), (0, cut - flat.shape[1])))
        tile = jnp.stack([gr_attn.reshape(shards, cut), gr_ffn.reshape(shards, cut), flat], axis=1)
        small.append(jnp.pad(tile, ((0, 0), (0, 5), (0, 0))))
    all_g0, all_w0, other_g, other_w, sums, section_outputs, input_grads = finish(
        n, shards, jnp.stack(small), (half0, half_out), w_grad0, all_g1, all_w1, y0, y1, d_in0, d_in1
    )
    section_outputs, input_grads = section_outputs[None, :, None], input_grads[None, :, None]
    g_attn, g_ffn = sums[0:1], sums[1:2]
    g_table = sums[2, : bucket_count // shards * heads].reshape(1, bucket_count // shards, heads)

    if packed:
        g_down, g_up, g_out, g_query, g_key, g_value = (
            part[None] for part in assemble(n, shards, all_g0, all_g1, other_g, all_w0, all_w1, other_w)
        )
    else:
        low, high = jnp.where(first, all_g0, other_g), jnp.where(first, other_g, all_g1)
        sizes = [kept // 2, quarter * hidden // model, width // (2 * shards)]
        cuts = [sum(sizes[:i]) for i in range(4)]

        def joined(index):
            return jnp.stack([part[:, cuts[index] : cuts[index + 1]] for part in (low, high)], axis=1)

        g_down = joined(0).astype(F32).reshape(1, n * kept, model)
        whole = joined(1).reshape(n, depth, shards, kept)
        g_up = whole.transpose(1, 2, 0, 3).reshape(1, depth, ff).astype(F32)
        g_out = jnp.sum(joined(2).astype(F32), axis=0).reshape(1, depth, model)
        low, high = jnp.where(first, all_w0, other_w), jnp.where(first, other_w, all_w1)
        whole = jnp.stack([low, high], axis=1).reshape(n, depth, 3, hw)
        g_query, g_key, g_value = (
            whole[:, :, i].transpose(1, 0, 2).reshape(1, depth, width).astype(F32) for i in range(3)
        )

    return (
        section_outputs,
        input_grads,
        g_query,
        g_key,
        g_value,
        g_out,
        g_up,
        g_down,
        g_attn,
        g_ffn,
        g_table,
    )


def solution(mesh):
    return jax.shard_map(
        body,
        mesh=mesh,
        in_specs=(
            P(None, "dp", "seq", None),
            P(None, "dp", "seq", None),
            P(None, "dp", None),
            P(),
            P("section", "dp", None),
            P("section", "dp", None),
            P("section", "dp", None),
            P("section", "dp", None),
            P("section", "dp", None),
            P("section", "dp", None),
            P("section", "dp"),
            P("section", "dp"),
            P("section", None, "seq"),
        ),
        out_specs=(
            P("section", None, "dp", "seq", None),
            P("section", None, "dp", "seq", None),
            P("section", "dp", None),
            P("section", "dp", None),
            P("section", "dp", None),
            P("section", "dp", None),
            P("section", "dp", None),
            P("section", "dp", None),
            P("section", "dp"),
            P("section", "dp"),
            P("section", "dp", "seq"),
        ),
        check_vma=False,
    )
```

```python
import functools
import math

import jax
import jax.numpy as jnp
from jax import lax
from jax.experimental import pallas as pl
from jax.experimental.pallas import tpu as pltpu
from jax.sharding import PartitionSpec as P

EPSILON = 1e-06
NEG = -1e30
HIGH = lax.Precision.HIGHEST
MESH = pl.DeviceIdType.MESH
F32 = jnp.float32
BF16 = jnp.bfloat16
LANES = 128
QB = 256
VMEM_BYTES = 60 << 20

AWAY = pl.BlockSpec(memory_space=pl.ANY)


def mm(left, right):
    return jnp.dot(left, right, preferred_element_type=F32)


def mm_nt(left, right):
    return lax.dot_general(left, right, (((1,), (1,)), ((), ())), preferred_element_type=F32)


def mm_tn(left, right):
    return lax.dot_general(left, right, (((0,), (0,)), ((), ())), preferred_element_type=F32)


def inverse_rms(rows):
    return lax.rsqrt(jnp.mean(rows * rows, axis=-1, keepdims=True) + EPSILON)


def aligned(start, size):
    return pl.ds(pl.multiple_of(start, size), size)


def signal_and_wait(peers):
    barrier = pltpu.get_barrier_semaphore()
    for peer in peers:
        pl.semaphore_signal(barrier, inc=1, device_id=peer, device_id_type=MESH)
    pl.semaphore_wait(barrier, len(peers))


def others(axis, n):
    me = lax.axis_index(axis)
    return [{axis: lax.rem(me + k, n)} for k in range(1, n)]


def other_core():
    return {"section": 1 - lax.axis_index("section")}


def cores_and_rows(shards):
    core, row = lax.axis_index("section"), lax.axis_index("dp")
    return [
        {"section": lax.rem(core + i, 2), "dp": lax.rem(row + j, shards)}
        for i in range(2)
        for j in range(shards)
        if i + j
    ]


def near(n):
    me = lax.axis_index("seq")
    return [{"seq": peer} for peer in (square(me) if n == 4 else ring(n, me))]


def square(me):
    return me + 1 - 2 * lax.rem(me, 2), lax.rem(me + 2, 4)


def ring(n, me):
    return [lax.rem(me + k, n) for k in range(1, n)]


def push(src, dst, send_sem, recv_sem, peer):
    return pltpu.make_async_remote_copy(
        src_ref=src,
        dst_ref=dst,
        send_sem=send_sem,
        recv_sem=recv_sem,
        device_id=peer if isinstance(peer, dict) else {"seq": peer},
        device_id_type=MESH,
    )


def sources(n):
    me = lax.axis_index("seq")
    if n == 4:
        along_x, along_y = square(me)
        return [me, along_x, along_y, square(along_y)[0]]
    return [lax.rem(me + n - k, n) for k in range(n)]


class Spread:
    def __init__(self, n, source, slot, rows, sems):
        self.n = n
        me = lax.axis_index("seq")
        self.order = sources(n)
        send, recv = sems
        if n != 4:
            self.copies = [
                push(source, slot(me, 0, rows), send.at[k], recv.at[k], peer)
                for k, peer in enumerate(ring(n, me), 1)
            ]
            return
        along_x, along_y = square(me)
        half = rows // 2

        def copy(number, owner, part, peer):
            here = source.at[pl.ds(part * half, half)] if owner is me else slot(owner, part * half, half)
            return push(here, slot(owner, part * half, half), send.at[number], recv.at[number], peer)

        self.copies = [
            copy(0, me, 0, along_x),
            copy(1, me, 1, along_y),
            copy(2, me, 1, along_x),
            copy(3, me, 0, along_y),
            copy(4, along_x, 0, along_y),
            copy(5, along_y, 1, along_x),
        ]

    def start(self):
        self.start_some(True)
        self.start_some(False)

    def start_some(self, first):
        if self.n == 4:
            for copy in self.copies[:2] if first else self.copies[2:4]:
                copy.start()
        elif first:
            for copy in self.copies:
                copy.start()

    def forward(self):
        if self.n == 4:
            for first, second in ((0, 4), (1, 5)):
                self.copies[first].wait_recv()
                self.copies[second].start()

    def arrive(self, k):
        if self.n == 4:
            for number in ((), (2,), (3,), (4, 5))[k]:
                self.copies[number].wait_recv()
        else:
            self.copies[k - 1].wait_recv()

    def sent(self):
        for copy in self.copies:
            copy.wait_send()

    def all(self):
        self.start()
        self.forward()
        for k in range(1, self.n):
            self.arrive(k)
        self.sent()


class Collect:
    def __init__(self, n, out, got, sems, mid=None):
        self.n = n
        self.out, self.got, self.mid = out, got, mid
        self.half = out.shape[1] // 2
        me = lax.axis_index("seq")
        self.order = sources(n)
        send, recv = sems
        if n != 4:
            self.copies = [
                push(out.at[k], got.at[k], send.at[k], recv.at[k], self.order[k]) for k in range(1, n)
            ]
            return
        along_x, along_y = square(me)

        def copy(number, chunk, part, peer):
            return push(self.piece(out, chunk, part), self.landing(number), send.at[number], recv.at[number], peer)

        self.copies = [
            copy(0, 1, 0, along_x),
            copy(1, 2, 1, along_y),
            copy(2, 3, 0, along_x),
            copy(3, 3, 1, along_y),
        ]
        for number, chunk, part, peer in ((4, 2, 0, along_y), (5, 1, 1, along_x)):
            source = self.piece(out, chunk, part) if mid is None else mid.at[number - 4]
            self.copies.append(
                push(source, self.landing(number), send.at[number], recv.at[number], peer)
            )

    def piece(self, ref, chunk, part):
        return ref.at[chunk, pl.ds(part * self.half, self.half)]

    def landing(self, number):
        return self.piece(self.got, number // 2, number % 2)

    def give(self, k, value):
        self.out[k] = value.astype(BF16)
        self.start(k)

    def start(self, k):
        if self.n == 4:
            for number in ((), (0,), (1,), (2, 3))[k]:
                self.copies[number].start()
        else:
            self.copies[k - 1].start()

    def relay(self):
        if self.n == 4:
            for number, chunk, part in ((2, 2, 0), (3, 1, 1)):
                self.copies[number].wait_recv()
                mine = self.piece(self.out, chunk, part)
                summed = (mine[...].astype(F32) + self.landing(number)[...].astype(F32)).astype(BF16)
                if self.mid is None:
                    mine[...] = summed
                else:
                    self.mid[number - 2] = summed
                self.copies[number + 2].start()

    def add_to(self, total):
        if self.n == 4:
            for number, part in ((0, 0), (1, 1), (4, 0), (5, 1)):
                self.copies[number].wait_recv()
                total[pl.ds(part * self.half, self.half)] += self.landing(number)[...].astype(F32)
        else:
            for k in range(1, self.n):
                self.copies[k - 1].wait_recv()
                total[...] += self.got[k].astype(F32)

    def sent(self):
        for copy in self.copies:
            copy.wait_send()


def way_sems(n):
    count = max(n, 6)
    return [pltpu.SemaphoreType.DMA((count,)), pltpu.SemaphoreType.DMA((count,))]


def row_slots(ref, tl):
    return lambda owner, first, rows: ref.at[pl.ds(pl.multiple_of(owner * tl + first, rows), rows)]


def chunk_slots(ref):
    return lambda owner, first, rows: ref.at[owner, pl.ds(first, rows)]


def cost(microseconds):
    return pl.CostEstimate(flops=int(microseconds * 1e9), bytes_accessed=0, transcendentals=0)


class Raw:
    def __init__(self, array):
        self.array = array


class Slots:
    def __init__(self, array):
        self.array = array


class Rows:
    def __init__(self, *arrays):
        self.array = arrays


class Late:
    def __init__(self, pairs, ref, sems):
        self.ref = ref
        self.copies = [pltpu.make_async_copy(src, dst, sems.at[i]) for i, (src, dst) in enumerate(pairs)]
        for copy in self.copies:
            copy.start()
        self.waiting = [True] * len(self.copies)

    def get(self, slot=None):
        for i, copy in enumerate(self.copies):
            if self.waiting[i] and (slot is None or slot == i):
                copy.wait()
                self.waiting[i] = False
        return self.ref


class Early:
    def __init__(self, target, ref, sems):
        self.target, self.ref, self.sems = target, ref, sems
        self.copies = []

    def flush(self, *part):
        src, dst = (self.ref.at[part], self.target.at[part]) if part else (self.ref, self.target)
        copy = pltpu.make_async_copy(src, dst, self.sems.at[len(self.copies)])
        copy.start()
        self.copies.append(copy)

    def get(self):
        return self.ref

    def done(self):
        if not self.copies:
            self.flush()
        for copy in self.copies:
            copy.wait()


class Held:
    def __init__(self, ref):
        self.ref = ref

    def get(self, slot=None):
        return self.ref

    def flush(self, *part):
        pass


class Reduce:
    def __init__(self, shards, value, got_c, sent_z, got_z, send_c, recv_c, send_z, recv_z):
        self.value, self.got_c, self.got_z, self.sent_z = value, got_c, got_z, sent_z
        self.row, self.core = lax.axis_index("dp"), lax.axis_index("section")
        self.rows = got_c.shape[1]
        self.shards = shards
        self.crossed = [
            push(
                value.at[self.part(z, 1 - self.core)],
                got_c.at[z], send_c.at[z], recv_c.at[z], {"section": 1 - self.core},
            )
            for z in range(shards)
        ]
        self.along = [
            push(
                sent_z.at[k], got_z.at[k], send_z.at[k], recv_z.at[k], {"dp": lax.rem(self.row + k, shards)}
            )
            for k in range(1, shards)
        ]

    def part(self, z, core):
        return aligned((2 * z + core) * self.rows, self.rows)

    def both(self, z):
        return self.value[self.part(z, self.core), :].astype(F32) + self.got_c[z].astype(F32)

    def start(self):
        for copy in self.crossed:
            copy.start()

    def forward(self):
        for copy in self.crossed:
            copy.wait()
        for k in range(1, self.shards):
            self.sent_z[k] = self.both(lax.rem(self.row + k, self.shards)).astype(BF16)
            self.along[k - 1].start()

    def result(self):
        half = self.both(self.row)
        for k in range(1, self.shards):
            self.along[k - 1].wait()
            half += self.got_z[k].astype(F32)
        return half.astype(BF16)


class AllSum:
    def __init__(self, n, value, out, c_out, c_got, total, send_c, recv_c, send_s, recv_s):
        self.n, self.value, self.out, self.c_got, self.total = n, value, out, c_got, total
        self.me = lax.axis_index("seq")
        self.rows = total.shape[0]
        self.order = sources(n)
        if n == 4:
            self.collect = Collect(n, c_out, c_got, (send_c, recv_c))
            mine = out.ref.at[self.part(self.me)]
            self.spread = Spread(n, mine, row_slots(out.ref, self.rows), self.rows, (send_s, recv_s))
        else:
            self.spread = Spread(n, value, chunk_slots(c_got), self.rows, (send_s, recv_s))

    def part(self, owner):
        return aligned(owner * self.rows, self.rows)

    def start(self):
        if self.n == 4:
            for k in (3, 1, 2):
                self.collect.give(k, self.value[self.part(self.order[k]), :])
            self.total[...] = self.value[self.part(self.me), :].astype(F32)
        else:
            self.spread.start()

    def relay(self):
        if self.n == 4:
            self.collect.relay()

    def share(self):
        if self.n == 4:
            self.collect.add_to(self.total)
            self.out.ref[self.part(self.me), :] = self.total[...].astype(BF16)
            self.spread.start()

    def forward(self):
        self.spread.forward()

    def done(self):
        for k in range(1, self.n):
            self.spread.arrive(k)
        if self.n == 4:
            self.collect.sent()
        else:
            self.total[...] = self.value[...].astype(F32)
            for k in range(1, self.n):
                self.total[...] += self.c_got[self.order[k]].astype(F32)
            self.out.ref[...] = self.total[...].astype(BF16)
        self.spread.sent()
        self.out.flush()


def sum_scratch(n, rows, width):
    if n == 4:
        rows //= n
    landing = pltpu.VMEM((n, rows, width), BF16)
    return [landing, landing, pltpu.VMEM((rows, width), F32), *way_sems(n), *way_sems(n)]


def reduce_scratch(shards, half):
    return [pltpu.VMEM((shards,) + half, BF16)] * 3 + [pltpu.SemaphoreType.DMA((shards,))] * 4


def call(kernel, name, collective_id, microseconds, operands, outs, scratch, peers=None):
    arrays, buffers, in_sems = [], [], []
    for operand in operands:
        array = operand.array if isinstance(operand, (Raw, Slots, Rows)) else operand
        arrays += array if isinstance(operand, Rows) else [array]
        if not isinstance(operand, Raw):
            copies = 1
            if isinstance(operand, Rows):
                dims = (sum(part.shape[0] for part in array),) + array[0].shape[1:]
                copies, dtype = len(array), array[0].dtype
            else:
                dims, dtype = array.shape, array.dtype
            if isinstance(operand, Slots):
                copies = dims[0]
            buffers.append(pltpu.VMEM(dims, dtype))
            in_sems.append(pltpu.SemaphoreType.DMA((copies,)))
    out_buffers = [pltpu.VMEM(dims, dtype) for dims, dtype, _ in outs]
    out_sems = [pltpu.SemaphoreType.DMA((flushes,)) for _, _, flushes in outs]

    def body(*refs):
        refs = list(refs)

        def take(count):
            taken = refs[:count]
            del refs[:count]
            return taken

        sources, targets = take(len(arrays)), take(len(outs))
        staged, results = take(len(buffers)), take(len(outs))
        staged_sems, result_sems = take(len(buffers)), take(len(outs))
        ins, at = [], 0
        for operand in operands:
            source = sources.pop(0)
            if isinstance(operand, Raw):
                ins.append(source)
                continue
            ref = staged[at]
            if isinstance(operand, Rows):
                pairs, first = [(source, ref.at[pl.ds(0, source.shape[0])])], source.shape[0]
                for _ in operand.array[1:]:
                    source = sources.pop(0)
                    pairs.append((source, ref.at[pl.ds(first, source.shape[0])]))
                    first += source.shape[0]
            elif isinstance(operand, Slots):
                pairs = [(source.at[i], ref.at[i]) for i in range(ref.shape[0])]
            else:
                pairs = [(source, ref)]
            ins.append(Late(pairs, ref, staged_sems[at]))
            at += 1
        early = [Early(*parts) for parts in zip(targets, results, result_sems)]
        if peers is not None:
            signal_and_wait(peers())
        kernel(ins, early, *refs)
        for late in ins:
            if isinstance(late, Late):
                late.get()
        for result in early:
            result.done()

    return pl.pallas_call(
        body,
        out_shape=[jax.ShapeDtypeStruct(dims, dtype) for dims, dtype, _ in outs],
        in_specs=[AWAY] * len(arrays),
        out_specs=[AWAY] * len(outs),
        scratch_shapes=[*buffers, *out_buffers, *in_sems, *out_sems, *scratch],
        compiler_params=pltpu.CompilerParams(
            collective_id=collective_id,
            has_side_effects=collective_id is not None,
            vmem_limit_bytes=VMEM_BYTES,
        ),
        cost_estimate=cost(microseconds),
        name=name,
    )(*arrays)


def start_kernel(n, shards, ins, outs, all_ref, send, recv, send_g, recv_g, send_z, recv_z, send_x, recv_x):
    x, own, piece = ins
    out, weight, *gains = outs
    tl = x.ref.shape[0]
    cut = own.ref.shape[1]
    me = lax.axis_index("seq")
    layer = lax.axis_index("section")
    row = lax.axis_index("dp")
    mine = aligned(me * tl, tl)
    peers = cores_and_rows(shards)
    own_ref = own.get()
    copies = [
        push(own_ref, all_ref.at[layer, row], send_g.at[i], recv_g.at[i], peer)
        for i, peer in enumerate(peers)
    ]
    for copy in copies:
        copy.start()
    all_ref[layer, row] = own_ref[...]
    weight.ref[row, layer] = piece.get()[...]

    def cross(z, core):
        ref = weight.ref.at[z, core]
        return push(ref, ref, send_x.at[z], recv_x.at[z], {"section": 1 - layer})

    along = []
    for k in range(1, shards):
        ref = weight.ref.at[row, layer]
        along.append(push(ref, ref, send_z.at[k], recv_z.at[k], {"dp": lax.rem(row + k, shards)}))
        along[-1].start()
    cross(row, layer).start()
    rows = x.get()[...].astype(F32)
    inv = inverse_rms(rows)
    for copy in copies:
        copy.wait()
    for z in range(shards):
        part = slice(z * cut, (z + 1) * cut)
        for i, gain in enumerate(gains):
            gain.ref[:, part] = all_ref[i // 2, z, i % 2 : i % 2 + 1, :].astype(F32)
    out.ref[mine] = (rows * inv * gains[0].ref[...]).astype(BF16)
    spread = Spread(n, out.ref.at[mine], row_slots(out.ref, tl), tl, (send, recv))
    spread.start()
    out.flush(mine)
    for gain in gains:
        gain.flush()
    spread.forward()
    for k in range(1, shards):
        along[k - 1].wait()
        cross(lax.rem(row + shards - k, shards), layer).start()
    for k in range(1, n):
        spread.arrive(k)
        out.flush(aligned(spread.order[k] * tl, tl))
    for z in range(shards):
        cross(z, 1 - layer).wait()
        weight.flush(z)
    spread.sent()


def start(n, shards, x, gains, piece):
    tl, width = x.shape
    small_sems = pltpu.SemaphoreType.DMA((2 * shards - 1,))
    row_sems = pltpu.SemaphoreType.DMA((shards,))
    return call(
        functools.partial(start_kernel, n, shards), "start", 6, 28,
        [x, gains, piece],
        [((n * tl, width), BF16, n), ((shards, 2) + piece.shape, BF16, shards)] + [((1, width), F32, 1)] * 4,
        [
            pltpu.VMEM((2, shards) + gains.shape, BF16),
            *way_sems(n),
            small_sems,
            small_sems,
            row_sems,
            row_sems,
            row_sems,
            row_sems,
        ],
        lambda: cores_and_rows(shards) + near(n),
    )


def gather_kernel(n, ins, outs, send, recv):
    x, gain, w = ins
    out, qkv = outs
    tl = x.ref.shape[0]
    mine = aligned(lax.axis_index("seq") * tl, tl)
    rows = x.get()[...].astype(F32)
    out.ref[mine] = (rows * inverse_rms(rows) * gain.get()[...]).astype(BF16)
    spread = Spread(n, out.ref.at[mine], row_slots(out.ref, tl), tl, (send, recv))
    spread.start()
    w.get()
    for k in range(n):
        where = aligned(spread.order[k] * tl, tl)
        if k:
            spread.arrive(k)
        out.flush(where)
        qkv.ref[where] = mm(out.ref[where], w.ref[...]).astype(BF16)
        qkv.flush(where)
        if not k:
            spread.forward()
    spread.sent()


def norm_gather(n, x, gain, w):
    tl, width = x.shape
    return call(
        functools.partial(gather_kernel, n), "norm_gather", 0, 20,
        [x, gain, w],
        [((n * tl, width), BF16, n), ((n * tl, w.shape[1]), BF16, n)],
        way_sems(n),
        lambda: near(n),
    )


def toeplitz_rows(offset_row):
    spread = jnp.broadcast_to(offset_row, (LANES, offset_row.shape[1]))
    return pltpu.roll(spread, 0, 1, stride=1, stride_axis=0)


def attend_kernel(n, heads, dk, ins, outs, bias_ref, kt_ref, qa_ref, send, recv, send_d, recv_d):
    chunk, qkv, eq, ek, rows = ins
    o, lse_out, back, chunks = outs
    o_ref, lse_ref, back_ref, chunks_ref = o.ref, lse_out.ref, back.ref, chunks.ref
    length, wide = o_ref.shape
    tl = length // n
    group = QB // tl
    blocks = length // QB
    me = lax.axis_index("seq")
    mine = aligned(me * tl, tl)
    chunk_ref = chunk.get()
    spread = Spread(n, chunk_ref, chunk_slots(chunks_ref), chunk_ref.shape[0], (send_d, recv_d))
    spread.start()
    chunks_ref[me] = chunk_ref[...]
    chunks.flush(me)
    qkv_ref, eq_ref, ek_ref, rows_ref = qkv.get(), eq.get(), ek.get(), rows.get()
    lane = lax.broadcasted_iota(jnp.int32, (length, LANES), 1)
    lane_q = lax.broadcasted_iota(jnp.int32, (LANES, LANES), 1)
    pairs = (heads + 1) // 2
    for p in range(pairs):
        pair = pl.ds(p * LANES, LANES)
        k_pair = pl.ds(wide + p * LANES, LANES)
        v_pair = pl.ds(2 * wide + p * LANES, LANES)
        held = min(2, heads - 2 * p)
        for i in range(held):
            inside = (lane >= dk) if i else (lane < dk)
            qa_ref[i] = jnp.where(inside, qkv_ref[:, pair], eq_ref[...])
            kt_ref[i] = jnp.where(inside, qkv_ref[:, k_pair], ek_ref[...]).T
            bias_ref[i] = toeplitz_rows(rows_ref[2 * p + i : 2 * p + i + 1, :])

        def block(step, carry, p=p, pair=pair, v_pair=v_pair, held=held):
            b = lax.rem(lax.div(me, group) + 1 + step, blocks)
            rows = aligned(b * QB, QB)
            scores = [mm(qa_ref[i, rows, :], kt_ref[i]) for i in range(held)]
            for a in range(QB // LANES):
                tile = b * (QB // LANES) + a
                where = aligned(tile * LANES, LANES)
                off = pl.ds(pl.multiple_of(length - tile * LANES, LANES), length)
                lse = None if p == 0 else lse_ref[where, :]
                mixed = None
                for i in range(held):
                    part = scores[i][a * LANES : (a + 1) * LANES] + bias_ref[i, :, off]
                    peak = jnp.max(part, axis=-1, keepdims=True)
                    expo = jnp.exp(part - peak)
                    total = jnp.sum(expo, axis=-1, keepdims=True)
                    value = mm(expo.astype(BF16), qkv_ref[:, v_pair]) * (1.0 / total)
                    column = peak + jnp.log(total)
                    mixed = jnp.where(lane_q < dk, mixed, value) if i else value
                    if lse is None:
                        lse = jnp.broadcast_to(column, (LANES, LANES))
                    else:
                        lse = jnp.where(lane_q == 2 * p + i, column, lse)
                o_ref[where, pair] = mixed.astype(BF16)
                lse_ref[where, :] = lse
            for g in range(group):
                peer = b * group + g

                @pl.when(peer != me)
                def _(peer=peer):
                    push(
                        o_ref.at[aligned(peer * tl, tl), pair],
                        back_ref.at[me, :, pair],
                        send.at[p, peer],
                        recv.at[p, me],
                        peer,
                    ).start()

            return carry

        lax.fori_loop(0, blocks, block, 0)
        back_ref[me, :, pair] = o_ref[mine, pair]
        o.flush(slice(None), pair)
        if p == 0:
            spread.forward()
    lse_out.flush()
    for k in range(1, n):
        spread.arrive(k)
        chunks.flush(spread.order[k])
    spread.sent()
    for p in range(pairs):
        pair = pl.ds(p * LANES, LANES)
        for k in range(1, n):
            peer = lax.rem(me + k, n)
            push(
                o_ref.at[aligned(peer * tl, tl), pair],
                back_ref.at[peer, :, pair],
                send.at[p, peer],
                recv.at[p, peer],
                peer,
            ).wait()


def attend(n, heads, dk, qkv, ext_q, ext_k, offset_rows, chunk):
    length, width = qkv.shape[0], qkv.shape[1] // 3
    span = offset_rows.shape[1]
    pairs = (heads + 1) // 2
    pair_sems = pltpu.SemaphoreType.DMA((pairs, n))
    return call(
        functools.partial(attend_kernel, n, heads, dk), "attend", 4 if chunk.shape[0] == length else 5, 20,
        [chunk, qkv, ext_q, ext_k, offset_rows],
        [
            ((length, width), BF16, pairs),
            ((length, LANES), F32, 1),
            ((n, length // n, width), BF16, 1),
            ((n,) + chunk.shape, BF16, n),
        ],
        [
            pltpu.VMEM((2, LANES, span), F32),
            pltpu.VMEM((2, LANES, length), BF16),
            pltpu.VMEM((2, length, LANES), BF16),
            pair_sems,
            pair_sems,
            *way_sems(n),
        ],
        lambda: others("seq", n),
    )


def three_parts(lane, value):
    first = value.astype(BF16).astype(F32)
    rest = value - first
    second = rest.astype(BF16).astype(F32)
    third = rest - second
    at = lax.rem(lane, 64)
    return jnp.where(at == 8, first, jnp.where(at == 9, second, jnp.where(at == 10, third, 0.0)))


def attend_back_kernel(n, heads, dk, summing, ins, outs, bias_ref, kt_ref, vt_ref, qa_ref, do_ref, qt_ref,
                       dkt_ref, dvt_ref, dbias_ref, send, recv, *refs):
    qkv, o, lse, eq, ek, rows, beside, *more = ins
    dqkv, dr, beside_out, *more_out = outs
    dqkv_ref, dr_ref = dqkv.ref, dr.ref
    length, wide = o.ref.shape
    span = rows.ref.shape[1]
    tl = length // n
    group = QB // tl
    blocks = length // QB
    me = lax.axis_index("seq")
    mine = aligned(me * tl, tl)
    if summing:
        do, own = more
        mid_ref, got_ref, send_y, recv_y = refs
        do_any = do.get()
        for k in range(1, n):
            peer = lax.rem(me + k, n)
            push(do_any.at[peer], do_ref.at[mine], send.at[peer], recv.at[me], peer).start()
        do_ref[mine] = do_any[me]
        collect = Collect(n, beside.get(), got_ref, (send_y, recv_y), mid_ref)

        def start_beside():
            for k in (3, 1, 2) if n == 4 else range(1, n):
                collect.start(k)

    else:
        dn2, x1, dy, gain, back, weights = more
        dx1_out, g_gain, g_out, reduce, beside_next, summed = more_out
        wo_ref, do_any, load, send_g, recv_g = refs
        loads = out_loads(weights, wo_ref, load)
        for copy in loads:
            copy.start()
        rows_g = beside_out.ref.shape[1]
        g_ref = beside.get().at[pl.ds(0, rows_g)]
        spread = Spread(n, g_ref, chunk_slots(beside_out.ref), rows_g, (send_g, recv_g))
        spread.start_some(True)

        def start_beside():
            spread.start_some(False)
            summed.start()

        dx1, g_gain.ref[...] = norm_back(
            x1.get()[...], dn2.get()[...], dy.get()[...].astype(F32), gain.get()[...]
        )
        dx1_out.ref[...] = dx1
        dx1_out.flush()
        d_attn = dx1.astype(BF16)
        arrive(loads)
        back_ref = back.get()
        hw = wo_ref.shape[0] // n
        if hw < wide:
            do_any[...] = jnp.zeros_like(do_any)
        for k in range(1, n):
            peer = lax.rem(me + k, n)
            do_any[peer, :, :hw] = mm_nt(d_attn, wo_ref[aligned(peer * hw, hw), :]).astype(BF16)
            push(do_any.at[peer], do_ref.at[mine], send.at[peer], recv.at[me], peer).start()
        do_any[me, :, :hw] = mm_nt(d_attn, wo_ref[aligned(me * hw, hw), :]).astype(BF16)
        do_ref[mine] = do_any[me]
        beside_out.ref[me] = g_ref[...]
        beside_out.flush(me)
        for t in range(n):
            g_out.ref[pl.ds(t * hw, hw), :] = mm_tn(back_ref[t][:, :hw], d_attn).astype(BF16)
        reduce.start()
    qkv_ref, o_ref, lse_ref, eq_ref, ek_ref, rows_ref = (
        late.get() for late in (qkv, o, lse, eq, ek, rows)
    )
    lane = lax.broadcasted_iota(jnp.int32, (length, LANES), 1)
    lane_q = lax.broadcasted_iota(jnp.int32, (QB, LANES), 1)
    at = lax.rem(lane, 64)
    parts = (at >= 8) & (at <= 10)
    ones = jnp.where(parts, 1.0, 0.0)
    for p in range((heads + 1) // 2):
        pair = pl.ds(p * LANES, LANES)
        k_lanes = pl.ds(wide + p * LANES, LANES)
        v_lanes = pl.ds(2 * wide + p * LANES, LANES)
        held = min(2, heads - 2 * p)
        q_pair, k_pair, v_pair = qkv_ref[:, pair], qkv_ref[:, k_lanes], qkv_ref[:, v_lanes]
        qt_ref[...] = q_pair.T
        ek = (ek_ref[...].astype(F32) + ones).astype(BF16)
        for i in range(held):
            head = 2 * p + i
            inside = (lane >= dk) if i else (lane < dk)
            lse = lse_ref[:, head : head + 1]
            eq = (eq_ref[...].astype(F32) - three_parts(lane, lse)).astype(BF16)
            qa_ref[i] = jnp.where(inside, q_pair, eq)
            kt_ref[i] = jnp.where(inside, k_pair, ek).T
            vt_ref[i] = jnp.where(inside, v_pair, ones.astype(BF16)).T
            bias_ref[i] = toeplitz_rows(rows_ref[head : head + 1, :])
        dkt_ref[...] = jnp.zeros_like(dkt_ref)
        dvt_ref[...] = jnp.zeros_like(dvt_ref)
        dbias_ref[...] = jnp.zeros_like(dbias_ref)

        def given(peer):
            return push(
                do_any.at[peer], do_ref.at[aligned(peer * tl, tl)], send.at[peer], recv.at[peer], peer
            )

        def block(step, carry, p=p, pair=pair, k_lanes=k_lanes, held=held):
            b = lax.rem(lax.div(me, group) + step, blocks)
            where = aligned(b * QB, QB)
            if p == 0:
                for g in range(group):
                    peer = b * group + g

                    @pl.when(peer != me)
                    def _(peer=peer):
                        given(peer).wait()

                pl.when(step == 1)(start_beside)


            dq = None
            do_pair = do_ref[where, pair]
            do_t = do_pair.T
            weighed = do_pair.astype(F32) * o_ref[where, pair].astype(F32)
            for i in range(held):
                half = pl.ds(i * dk, dk)
                inside_q = (lane_q >= dk) if i else (lane_q < dk)
                delta = jnp.sum(jnp.where(inside_q, weighed, 0.0), axis=-1, keepdims=True)
                da = jnp.where(inside_q, do_pair, (-three_parts(lane_q, delta)).astype(BF16))
                scores = mm(qa_ref[i, where, :], kt_ref[i])
                lifted = mm(da, vt_ref[i])
                probs, grads = [], []
                for a in range(QB // LANES):
                    cut = slice(a * LANES, (a + 1) * LANES)
                    tile = b * (QB // LANES) + a
                    off = pl.ds(pl.multiple_of(length - tile * LANES, LANES), length)
                    prob = jnp.exp(scores[cut] + bias_ref[i, :, off])
                    grad = prob * lifted[cut]
                    dbias_ref[i, :, off] += grad
                    probs.append(prob.astype(BF16))
                    grads.append(grad.astype(BF16))
                prob = jnp.concatenate(probs, axis=0)
                grad = jnp.concatenate(grads, axis=0)
                value = mm(grad, qkv_ref[:, k_lanes])
                dq = jnp.where(lane_q < dk, dq, value) if i else value
                dkt_ref[half, :] += mm(qt_ref[half, where], grad)
                dvt_ref[half, :] += mm(do_t[i * dk : (i + 1) * dk], prob)
            dqkv_ref[where, pair] = dq.astype(BF16)
            return carry

        lax.fori_loop(0, length // QB, block, 0)
        dqkv_ref[:, k_lanes] = dkt_ref[...].T.astype(BF16)
        dqkv_ref[:, v_lanes] = dvt_ref[...].T.astype(BF16)
        for lanes in (pair, k_lanes, v_lanes):
            dqkv.flush(slice(None), lanes)
        place = lax.broadcasted_iota(jnp.int32, (8, span), 0)
        for i in range(held):
            folded = dbias_ref[i]
            rows = LANES
            while rows > 8:
                rows //= 2
                folded = folded[:rows] + pltpu.roll(folded[rows:], span - rows, 1)
            for bit in (4, 2, 1):
                folded = jnp.where(
                    lax.rem(lax.div(place, bit), 2) == 1, pltpu.roll(folded, span - bit, 1), folded
                )
            dr_ref[2 * p + i : 2 * p + i + 1, :] = jnp.sum(folded, axis=0, keepdims=True)
        if p == 0:
            if summing:
                collect.relay()
            else:
                reduce.forward()
                spread.forward()
                summed.relay()
                beside_next.start()
    dr.flush()
    if summing:
        collect.add_to(own.get())
        beside_out.ref[...] = own.ref[...].astype(BF16)
        beside_out.flush()
        collect.sent()
    else:
        for k in range(1, n):
            spread.arrive(k)
            beside_out.flush(spread.order[k])
        spread.sent()
        summed.share()
        beside_next.forward()


def out_loads(source, target, sems):
    if len(source.shape) == 2:
        return [pltpu.make_async_copy(source, target, sems.at[0])]
    blocks, _, cols = source.shape
    return [
        pltpu.make_async_copy(source.at[t], target.at[:, pl.ds(t * cols, cols)], sems.at[t])
        for t in range(blocks)
    ]


def attend_back_scratch(heads, length, width, span, n):
    sems = pltpu.SemaphoreType.DMA((n,))
    return [
        pltpu.VMEM((2, LANES, span), F32),
        pltpu.VMEM((2, LANES, length), BF16),
        pltpu.VMEM((2, LANES, length), BF16),
        pltpu.VMEM((2, length, LANES), BF16),
        pltpu.VMEM((length, width), BF16),
        pltpu.VMEM((LANES, length), BF16),
        pltpu.VMEM((LANES, length), F32),
        pltpu.VMEM((LANES, length), F32),
        pltpu.VMEM((2, LANES, span), F32),
        sems,
        sems,
    ]


def weight_loads(sources, targets, sems):
    if len(sources) == 3:
        return [
            [pltpu.make_async_copy(src, dst, sems.at[j])] if dst is not None else None
            for j, (src, dst) in enumerate(zip(sources, targets))
        ]
    packed = sources[-1]
    pieces, count, rows = packed.shape[:3]
    groups = [
        [
            pltpu.make_async_copy(
                packed.at[i, j], targets[j - count].at[pl.ds(i * rows, rows)], sems.at[j * pieces + i]
            )
            for i in range(pieces)
        ]
        for j in range(count)
    ]
    if targets[0] is None:
        return [None] * (3 - count) + groups
    if count == 2:
        blocks, _, cols = sources[0].shape
        groups.insert(
            0,
            [
                pltpu.make_async_copy(
                    sources[0].at[t], targets[0].at[:, pl.ds(t * cols, cols)], sems.at[2 * pieces + t]
                )
                for t in range(blocks)
            ],
        )
    return groups


def load_sems(weights):
    count = 3
    if len(weights) < 3:
        count = weights[-1].shape[0] * weights[-1].shape[1] + (weights[0].shape[0] if len(weights) == 2 else 0)
    return pltpu.SemaphoreType.DMA((count,))


def arrive(copies):
    for copy in copies:
        copy.wait()


def mix_kernel(n, hw, ins, outs, wo_ref, up_ref, down_ref, out_ref, got_ref, total_ref,
               load, send_n, recv_n, send_y, recv_y):
    x, gain, back, *weights = ins
    y, x1_out, n2, slope, hid = outs
    n2_ref = n2.ref
    tl = x.ref.shape[0]
    me = lax.axis_index("seq")
    mine = aligned(me * tl, tl)
    loads = weight_loads(weights, (wo_ref, up_ref, down_ref), load)
    for group in loads:
        for copy in group:
            copy.start()
    back_ref = back.get()
    total = x.get()[...].astype(F32)
    arrive(loads[0])
    for s in range(n):
        total += mm(back_ref[s][:, :hw], wo_ref[s * hw : (s + 1) * hw, :])
    total_ref[...] = total
    x1 = total_ref[...]
    n2_ref[mine] = (x1 * inverse_rms(x1) * gain.get()[...]).astype(BF16)
    spread = Spread(n, n2_ref.at[mine], row_slots(n2_ref, tl), tl, (send_n, recv_n))
    collect = Collect(n, out_ref, got_ref, (send_y, recv_y))

    spread.start()
    x1_out.ref[...] = x1
    x1_out.flush()
    arrive(loads[1])
    arrive(loads[2])
    for k in range(n):
        where = aligned(spread.order[k] * tl, tl)
        if k:
            spread.arrive(k)
        n2.flush(where)
        u = mm(n2_ref[where], up_ref[...])
        half = 0.5 + 0.5 * lax.erf(u * math.sqrt(0.5))
        hidden = (u * half).astype(BF16)
        hid.ref[where] = hidden
        hid.flush(where)
        slope.ref[where] = (
            half + u * (jnp.exp(-0.5 * u * u) * (1.0 / math.sqrt(2.0 * math.pi)))
        ).astype(BF16)
        slope.flush(where)
        part = mm(hidden, down_ref[...])
        if k:
            collect.give(k, part)
        else:
            total_ref[...] += part
            spread.forward()

    collect.relay()
    collect.add_to(total_ref)
    y.ref[...] = total_ref[...].astype(BF16)
    y.flush()
    spread.sent()
    collect.sent()


def mix(n, hw, ff, x, gain, back, weights):
    tl, width = x.shape
    tokens = n * tl
    return call(
        functools.partial(mix_kernel, n, hw), "mix", 1, 45,
        [x, gain, back, *map(Raw, weights)],
        [
            ((tl, width), BF16, 1),
            ((tl, width), F32, 1),
            ((tokens, width), BF16, n),
            ((tokens, ff), BF16, n),
            ((tokens, ff), BF16, n),
        ],
        [
            pltpu.VMEM((n * hw, width), BF16),
            pltpu.VMEM((width, ff), BF16),
            pltpu.VMEM((ff, width), BF16),
            pltpu.VMEM((n, tl, width), BF16),
            pltpu.VMEM((n, tl, width), BF16),
            pltpu.VMEM((tl, width), F32),
            load_sems(weights),
            *way_sems(n),
            *way_sems(n),
        ],
        lambda: near(n),
    )


def norm_back(x1, dn, dy, gain):
    inv = inverse_rms(x1)
    scaled = x1 * inv
    g_gain = jnp.sum(dn * scaled, axis=0, keepdims=True)
    lifted = dn * gain
    return dy + inv * (lifted - scaled * jnp.mean(lifted * scaled, axis=-1, keepdims=True)), g_gain


def turn_kernel(n, hw, ins, outs, wo_ref, up_ref, down_ref, n2_ref, hid_ref, du_ref, out_ref, got_ref, total_ref,
                load, send_n, recv_n, send_d, recv_d):
    x, gain, back, dy, *weights = ins
    parts, own, dx1_out, do, g_gain, *grads = outs
    own_ref = own.ref
    tl = x.ref.shape[0]
    me = lax.axis_index("seq")
    mine = aligned(me * tl, tl)
    loads = weight_loads(weights, (wo_ref, up_ref, down_ref), load)
    for group in loads:
        for copy in group:
            copy.start()
    back_ref = back.get()
    total = x.get()[...].astype(F32)
    arrive(loads[0])
    for s in range(n):
        total += mm(back_ref[s][:, :hw], wo_ref[s * hw : (s + 1) * hw, :])
    own_ref[...] = total
    x1 = own_ref[...]
    gain_row = gain.get()[...]
    n2_ref[mine] = (x1 * inverse_rms(x1) * gain_row).astype(BF16)
    spread = Spread(n, n2_ref.at[mine], row_slots(n2_ref, tl), tl, (send_n, recv_n))
    collect = Collect(n, out_ref, got_ref, (send_d, recv_d))
    dy_all = dy.get()

    spread.start()
    arrive(loads[1])
    arrive(loads[2])
    for k in range(n):
        where = aligned(spread.order[k] * tl, tl)
        if k:
            spread.arrive(k)
        u = mm(n2_ref[where], up_ref[...])
        half = 0.5 + 0.5 * lax.erf(u * math.sqrt(0.5))
        hid_ref[where] = (u * half).astype(BF16)
        slope = half + u * (jnp.exp(-0.5 * u * u) * (1.0 / math.sqrt(2.0 * math.pi)))
        du = (mm_nt(dy_all[where], down_ref[...]) * slope).astype(BF16)
        du_ref[where] = du
        part = mm_nt(du, up_ref[...])
        if k:
            collect.give(k, part)
        else:
            total_ref[...] = part
            spread.forward()

    for k in range(1, n):
        parts.ref[k] = mm(hid_ref[aligned(spread.order[k] * tl, tl)], down_ref[...]).astype(BF16)
        parts.flush(k)
    collect.relay()
    parts.ref[0] = jnp.zeros_like(out_ref[0])
    parts.flush(0)
    own_ref[...] = x1 + mm(hid_ref[mine], down_ref[...])
    own.flush()
    store_grad(grads, 0, hid_ref, dy_all)
    store_grad(grads, 1, n2_ref, du_ref)
    collect.add_to(total_ref)
    dx1, g_gain.ref[...] = norm_back(x1, total_ref[...], dy_all[mine].astype(F32), gain_row)
    out_back(hw, dx1, dx1_out, do, grads, back_ref, wo_ref)
    spread.sent()
    collect.sent()


def out_back(hw, dx1, dx1_out, do, grads, back_ref, wo_ref):
    dx1_out.ref[...] = dx1
    dx1_out.flush()
    d_attn = dx1.astype(BF16)
    for s in range(back_ref.shape[0]):
        do.ref[s] = mm_nt(d_attn, wo_ref[s * hw : (s + 1) * hw, :]).astype(BF16)
        do.flush(s)
    for s in range(back_ref.shape[0]):
        store_rows(grads, 2, s * hw, mm_tn(back_ref[s][:, :hw], d_attn).astype(BF16))
    flush_grad(grads, 2)


def grad_shapes(weights, hw, n, ff, width):
    if len(weights) < 3:
        pieces, _, rows = weights[-1].shape[:3]
        return [((pieces, 3, rows, width), BF16, 3)]
    return [((ff, width), BF16, 1), ((width, ff), BF16, 1), ((n * hw, width), BF16, 1)]


def turn_round(n, hw, ff, x, gain, back, weights, dy_all):
    tl, width = x.shape
    return call(
        functools.partial(turn_kernel, n, hw), "turn_round", 2, 55,
        [x, gain, back, dy_all, *map(Raw, weights)],
        [
            ((n, tl, width), BF16, n),
            ((tl, width), F32, 1),
            ((tl, width), F32, 1),
            ((n, tl, hw), BF16, n),
            ((1, width), F32, 1),
            *grad_shapes(weights, hw, n, ff, width),
        ],
        [
            pltpu.VMEM((n * hw, width), BF16),
            pltpu.VMEM((width, ff), BF16),
            pltpu.VMEM((ff, width), BF16),
            pltpu.VMEM((n * tl, width), BF16),
            pltpu.VMEM((n * tl, ff), BF16),
            pltpu.VMEM((n * tl, ff), BF16),
            pltpu.VMEM((n, tl, width), BF16),
            pltpu.VMEM((n, tl, width), BF16),
            pltpu.VMEM((tl, width), F32),
            load_sems(weights),
            *way_sems(n),
            *way_sems(n),
        ],
        lambda: near(n),
    )


def mix_back_kernel(n, shards, loads, ins, outs, up_ref, down_ref, out_ref, got_ref, dy_all,
                    send_n, recv_n, send_d, recv_d, *reduce_refs):
    dy, w_grad, slope, hid, n2 = ins
    dn2, half_out, *grads = outs
    tl = dy.ref.shape[0]
    mine = aligned(lax.axis_index("seq") * tl, tl)
    dy_ref = dy.get()
    spread = Spread(n, dy_ref, row_slots(dy_all, tl), tl, (send_d, recv_d))
    spread.start()
    reduce = Reduce(shards, w_grad.get(), *reduce_refs)
    reduce.start()
    dy_all[mine] = dy_ref[...]
    collect = Collect(n, out_ref, got_ref, (send_n, recv_n))
    arrive(loads[2])
    arrive(loads[1])
    du_ref = slope.get()
    for k in range(n):
        where = aligned(spread.order[k] * tl, tl)
        if k:
            spread.arrive(k)
        du = (mm_nt(dy_all[where], down_ref[...]) * du_ref[where].astype(F32)).astype(BF16)
        du_ref[where] = du
        part = mm_nt(du, up_ref[...])
        if k:
            collect.give(k, part)
        else:
            spread.forward()
            dn2.ref[...] = part
            reduce.forward()
    store_grad(grads, 0, hid.get(), dy_all)
    collect.relay()
    store_grad(grads, 1, n2.get(), du_ref)
    half_out.ref[...] = reduce.result()
    half_out.flush()
    collect.add_to(dn2.ref)
    spread.sent()
    collect.sent()


def flush_grad(grads, index):
    if len(grads) == 1:
        grads[0].flush(slice(None), index)
    else:
        grads[index].flush()


def store_rows(grads, index, first, value):
    if len(grads) == 1:
        ref = grads[0].ref
        rows = ref.shape[2]
        for i in range(value.shape[0] // rows):
            ref[first // rows + i, index] = value[i * rows : (i + 1) * rows]
    else:
        grads[index].ref[pl.ds(first, value.shape[0]), :] = value


def row_blocks(left_ref, right_ref, store):
    rows = min(256, left_ref.shape[1])

    def block(b, carry):
        first = pl.multiple_of(b * rows, rows)
        store(first, mm_tn(left_ref[:, pl.ds(first, rows)], right_ref[...]).astype(BF16))
        return carry

    lax.fori_loop(0, left_ref.shape[1] // rows, block, 0)


def store_grad(grads, index, left_ref, right_ref):
    row_blocks(left_ref, right_ref, functools.partial(store_rows, grads, index))
    flush_grad(grads, index)


def project_back_kernel(n, ins, outs, out_ref, got_ref, total_ref, send, recv):
    w, dqkv, n1, x, dx1, gain = ins
    dx_out, low, g_w, g_gain = outs
    tl = x.ref.shape[0]
    collect = Collect(n, out_ref, got_ref, (send, recv))
    w_ref, dqkv_ref = w.get(), dqkv.get()

    def part(k):
        return mm_nt(dqkv_ref[aligned(collect.order[k] * tl, tl), :], w_ref[...])

    for k in (3, 1, 2) if n == 4 else range(1, n):
        collect.give(k, part(k))
    total_ref[...] = part(0)
    collect.relay()

    def store(first, value):
        g_w.ref[pl.ds(first, value.shape[0]), :] = value

    row_blocks(n1.get(), dqkv_ref, store)
    g_w.flush()
    collect.add_to(total_ref)
    dx, g_gain.ref[...] = norm_back(x.get()[...].astype(F32), total_ref[...], dx1.get()[...], gain.get()[...])
    dx_out.ref[...] = dx
    dx_out.flush()
    low.ref[...] = dx.astype(BF16)
    low.flush()
    collect.sent()


def back_across_kernel(n, shards, heads, dk, ins, outs, dqkv, g_w, out_ref, got_p, total_ref, send_p, recv_p,
                       up_ref, down_ref, got_m, dy_all, load, *refs):
    attend_ins, (w, n1, x, dx1, gain), (slope, hid, n2), weights = ins[:9], ins[9:14], ins[14:17], ins[17:]
    dr, y, dx, low, g_gain, dn2, half_w, *grads = outs
    loads = weight_loads(weights, (None, up_ref, down_ref), load)
    for group in reversed(loads[1:]):
        for copy in group:
            copy.start()
    attend_back_kernel(n, heads, dk, True, attend_ins, [Held(dqkv), dr, y], *refs[:15])
    project_back_kernel(
        n, [w, Held(dqkv), n1, x, dx1, gain], [dx, low, Held(g_w), g_gain],
        out_ref, got_p, total_ref, send_p, recv_p,
    )
    mix_back_kernel(
        n, shards, loads, [low, Held(g_w), slope, hid, n2], [dn2, half_w, *grads],
        up_ref, down_ref, out_ref, got_m, dy_all, *refs[15:],
    )


def back_across(n, shards, heads, dk, ff, qkv, o, lse, ext_q, ext_k, offset_rows, parts, do, own,
                w, n1, x, dx1, gain, slope, hid, n2, weights):
    length, wide = o.shape
    span = offset_rows.shape[1]
    tl, width = x.shape
    half = (width // (2 * shards), w.shape[1])
    if len(weights) < 3:
        pieces, _, rows = weights[-1].shape[:3]
        grads = [((pieces, 2, rows, width), BF16, 2)]
    else:
        grads = [((ff, width), BF16, 1), ((width, ff), BF16, 1)]
    return call(
        functools.partial(back_across_kernel, n, shards, heads, dk), "back_across", 9, 85,
        [qkv, o, lse, ext_q, ext_k, offset_rows, parts, do, own, w, n1, x, dx1, gain, slope, hid, n2,
         *map(Raw, weights)],
        [
            ((heads, span), F32, 1),
            ((tl, width), BF16, 1),
            ((tl, width), F32, 1),
            ((tl, width), BF16, 1),
            ((1, width), F32, 1),
            ((tl, width), F32, 1),
            (half, BF16, 1),
            *grads,
        ],
        [
            pltpu.VMEM((length, 3 * wide), BF16),
            pltpu.VMEM(w.shape, BF16),
            pltpu.VMEM((n, tl, width), BF16),
            pltpu.VMEM((n, tl, width), BF16),
            pltpu.VMEM((tl, width), F32),
            *way_sems(n),
            pltpu.VMEM((width, ff), BF16),
            pltpu.VMEM((ff, width), BF16),
            pltpu.VMEM((n, tl, width), BF16),
            pltpu.VMEM((n * tl, width), BF16),
            load_sems(weights),
            *attend_back_scratch(heads, length, wide, span, n),
            pltpu.VMEM((2, tl // 2, width), BF16),
            pltpu.VMEM((n, tl, width), BF16),
            *way_sems(n),
            *way_sems(n),
            *way_sems(n),
            *reduce_scratch(shards, half),
        ],
        lambda: others("seq", n) + others("dp", shards) + [other_core()],
    )


def back_first_kernel(n, shards, heads, dk, ins, outs, dqkv, dx1, low, g_out, out_ref, got_ref, total_ref,
                      send_p, recv_p, send_w, recv_w, *refs):
    attend_ins, (w, n1, x, gain, half_w) = ins[:13], ins[13:]
    dr, all_g, g_ffn, dx, g_w, g_gain, half_out, all_w, out_last = outs
    reduce = Reduce(shards, g_out, *refs[:7])
    half_g = attend_ins[6].get()
    rows = out_last.ref.shape[0]
    last = half_g.at[pl.ds(half_g.shape[0] - rows, rows)]
    summed = AllSum(n, last, out_last, *refs[7:14])
    half = half_w.get()
    spread = Spread(n, half, chunk_slots(all_w.ref), half.shape[0], (send_w, recv_w))
    all_w.ref[lax.axis_index("seq")] = half[...]
    attend_back_kernel(
        n, heads, dk, False, attend_ins,
        [Held(dqkv), dr, all_g, Held(dx1), g_ffn, Held(g_out), reduce, spread, summed], *refs[14:]
    )
    summed.forward()
    project_back_kernel(
        n, [w, Held(dqkv), n1, x, Held(dx1), gain], [dx, Held(low), g_w, g_gain],
        out_ref, got_ref, total_ref, send_p, recv_p,
    )
    half_out.ref[...] = reduce.result()
    for k in range(1, n):
        spread.arrive(k)
    spread.sent()
    summed.done()


def back_first(n, shards, heads, dk, qkv, o, lse, ext_q, ext_k, offset_rows, half_g, dn2, x1, dy, g_ffn, back, wo,
               w, n1, x, gain, half_w):
    length, wide = o.shape
    span = offset_rows.shape[1]
    tl, width = x.shape
    hd = wo.shape[-2]
    half_out = (hd // (2 * shards), width)
    return call(
        functools.partial(back_first_kernel, n, shards, heads, dk), "back_first", 11, 65,
        [qkv, o, lse, ext_q, ext_k, offset_rows, half_g, dn2, x1, dy, g_ffn, back, Raw(wo), w, n1, x, gain, half_w],
        [
            ((heads, span), F32, 1),
            ((n, half_g.shape[0] - half_out[0], width), BF16, n),
            ((1, width), F32, 1),
            ((tl, width), F32, 1),
            (w.shape, BF16, 1),
            ((1, width), F32, 1),
            (half_out, BF16, 1),
            ((n,) + half_w.shape, BF16, 1),
            (half_out, BF16, 1),
        ],
        [
            pltpu.VMEM((length, 3 * wide), BF16),
            pltpu.VMEM((tl, width), F32),
            pltpu.VMEM((tl, width), BF16),
            pltpu.VMEM((hd, width), BF16),
            pltpu.VMEM((n, tl, width), BF16),
            pltpu.VMEM((n, tl, width), BF16),
            pltpu.VMEM((tl, width), F32),
            *way_sems(n),
            *way_sems(n),
            *reduce_scratch(shards, half_out),
            *sum_scratch(n, *half_out),
            *attend_back_scratch(heads, length, wide, span, n),
            pltpu.VMEM((hd, width), BF16),
            pltpu.VMEM((n, tl, wide), BF16),
            pltpu.SemaphoreType.DMA((n,)),
            *way_sems(n),
        ],
        lambda: others("seq", n) + others("dp", shards) + [other_core()],
    )


def finish_kernel(n, shards, ins, outs, small_got, tile_got, send_g, recv_g, send_w0, recv_w0,
                  send_x, recv_x, send_s, recv_s, send_t, recv_t, *refs):
    g0, w0, out0, w1, small, g1, out1, y0, y1, d0, d1 = ins
    gathered_g, gathered_w0, out0_out, other_g_out, other_w_out, other_out, sums, sections, d_inputs = outs
    all_g, all_w0 = gathered_g.ref, gathered_w0.ref
    other_g, other_w = other_g_out.ref, other_w_out.ref
    me = lax.axis_index("seq")
    core = lax.axis_index("section")
    row = lax.axis_index("dp")
    other = other_core()
    peers = cores_and_rows(shards)

    g0_ref = g0.get()
    spread_g = Spread(n, g0_ref, chunk_slots(all_g), g0_ref.shape[0], (send_g, recv_g))
    spread_g.start()
    reduce = Reduce(shards, w0.get(), *refs[:7])
    reduce.start()
    summed = AllSum(n, out0.get(), out0_out, *refs[7:])
    summed.start()
    small_ref = small.get()
    smalls = [
        push(small_ref.at[peer["section"], peer["dp"]], small_got.at[i], send_s.at[i], recv_s.at[i], peer)
        for i, peer in enumerate(peers)
    ]
    for copy in smalls:
        copy.start()

    def cross(source, target, t, number):
        sem = number * n + t
        return push(source, target.at[t], send_x.at[sem], recv_x.at[sem], other)

    def cross_rows(source, target, number):
        sem = 2 * n + number
        return push(source, target, send_x.at[sem], recv_x.at[sem], other)

    w1_ref, g1_ref, out1_ref, y0_ref, y1_ref, d0_ref, d1_ref = (
        late.get() for late in (w1, g1, out1, y0, y1, d0, d1)
    )

    @pl.when(core == 0)
    def _():
        cross_rows(y1_ref, sections.ref.at[0], 0).start()
        cross_rows(d1_ref, d_inputs.ref.at[0], 1).start()
        cross_rows(out1_ref, other_out.ref, 2).start()
        for t in range(n):
            cross(w1_ref.at[t], other_w, t, 1).start()
            cross(g1_ref.at[t], other_g, t, 0).start()
        sections.ref[0] = y0_ref[...]
        d_inputs.ref[0] = d0_ref[...]

    @pl.when(core == 1)
    def _():
        cross_rows(y0_ref, sections.ref.at[1], 0).start()
        cross_rows(d0_ref, d_inputs.ref.at[1], 1).start()
        cross(g0_ref, other_g, me, 0).start()
        sections.ref[1] = y1_ref[...]
        d_inputs.ref[1] = d1_ref[...]

    all_g[me] = g0_ref[...]
    gathered_g.flush(me)
    reduce.forward()
    summed.relay()

    tile = small_ref[core, row]
    for i, copy in enumerate(smalls):
        copy.wait()
        tile += small_got[i]
    tile_got[0] = tile
    tiles = []
    for k in range(1, n):
        copy = push(tile_got.at[0], tile_got.at[k], send_t.at[k], recv_t.at[k], lax.rem(me + k, n))
        copy.start()
        tiles.append(copy)

    spread_g.forward()
    summed.share()
    all_w0[me] = reduce.result()
    gathered_w0.flush(me)
    spread_w0 = Spread(n, all_w0.at[me], chunk_slots(all_w0), all_w0.shape[1], (send_w0, recv_w0))
    spread_w0.start()
    summed.forward()
    spread_w0.forward()

    @pl.when(core == 1)
    def _():
        cross(all_w0.at[me], other_w, me, 1).start()

    for k in range(1, n):
        source = spread_g.order[k]
        spread_g.arrive(k)
        gathered_g.flush(source)

        @pl.when(core == 1)
        def _():
            cross(all_g.at[source], other_g, source, 0).start()

    summed.done()

    @pl.when(core == 1)
    def _():
        cross_rows(out0_out.ref, other_out.ref, 2).start()

    total = tile
    for k in range(1, n):
        tiles[k - 1].wait()
        total += tile_got[k]
    line = lax.broadcasted_iota(jnp.int32, tile.shape, 0)
    sums.ref[...] = jnp.where(line < 2, total, tile)
    for number, (source, target) in enumerate(((y0_ref, sections), (d0_ref, d_inputs))):
        cross_rows(source, target.ref.at[0], number).wait()
        target.flush()
    for k in range(1, n):
        source = spread_g.order[k]
        spread_w0.arrive(k)
        gathered_w0.flush(source)

        @pl.when(core == 1)
        def _():
            cross(all_w0.at[source], other_w, source, 1).start()

    cross_rows(out0_out.ref, other_out.ref, 2).wait()
    other_out.flush()
    for t in [me] + spread_g.order[1:]:
        cross(g0_ref, other_g, t, 0).wait()
        other_g_out.flush(t)
    for t in [me] + spread_g.order[1:]:
        cross(all_w0.at[0], other_w, t, 1).wait()
        other_w_out.flush(t)
    for spread in (spread_g, spread_w0):
        spread.sent()


def finish(n, shards, small, g0, out0, w0, g1, out1, w1, y0, y1, d0, d1):
    sems = pltpu.SemaphoreType.DMA((n,))
    cross_sems = pltpu.SemaphoreType.DMA((2 * n + 3,))
    small_sems = pltpu.SemaphoreType.DMA((2 * shards - 1,))
    tile = small.shape[2:]
    half = w1.shape[1:]
    gathered_w = ((n,) + half, BF16, n)
    return call(
        functools.partial(finish_kernel, n, shards), "finish", 8, 48,
        [g0, w0, out0, w1, small, g1, out1, y0, y1, d0, d1],
        [
            (g1.shape, BF16, n),
            gathered_w,
            (out0.shape, BF16, 1),
            (g1.shape, BF16, n),
            gathered_w,
            (out0.shape, BF16, 1),
            (tile, F32, 1),
            ((2,) + y0.shape, BF16, 1),
            ((2,) + d0.shape, F32, 1),
        ],
        [
            pltpu.VMEM((2 * shards - 1,) + tile, F32),
            pltpu.VMEM((n,) + tile, F32),
            *way_sems(n),
            *way_sems(n),
            cross_sems, cross_sems, small_sems, small_sems, sems, sems,
            *reduce_scratch(shards, half),
            *sum_scratch(n, *out0.shape),
        ],
        lambda: cores_and_rows(shards) + others("seq", n),
    )


def assemble_kernel(n, shards, ins, outs):
    g0, other_g, g1, w0, other_w, w1, out0, other_out, out1 = ins
    down, up, out, *qkv = outs
    first = lax.axis_index("section") == 0
    quarter = other_w.ref.shape[1]
    hw = other_w.ref.shape[2] // 3
    kept = 2 * quarter
    for t in range(n):
        for late in ins[:6]:
            late.get(t)
        for half in range(2):
            if half == 0:
                g = jnp.where(first, g0.ref[t], other_g.ref[t]).astype(F32)
                w = jnp.where(first, w0.ref[t], other_w.ref[t]).astype(F32)
            else:
                g = jnp.where(first, other_g.ref[t], g1.ref[t]).astype(F32)
                w = jnp.where(first, other_w.ref[t], w1.ref[t]).astype(F32)
            rows = slice(half * quarter, (half + 1) * quarter)
            down.ref[t * kept + half * quarter : t * kept + (half + 1) * quarter, :] = g[:quarter]
            for z in range(shards):
                at = (z * n + t) * kept
                up.ref[rows, at : at + kept] = g[quarter : 2 * quarter, z * kept : (z + 1) * kept]
            for i, grad in enumerate(qkv):
                grad.ref[rows, t * hw : (t + 1) * hw] = w[:, i * hw : (i + 1) * hw]
        down.flush(pl.ds(t * kept, kept))
        for z in range(shards):
            up.flush(slice(None), pl.ds((z * n + t) * kept, kept))
        for grad in qkv:
            grad.flush(slice(None), pl.ds(t * hw, hw))
    out.ref[:quarter, :] = jnp.where(first, out0.get()[...], other_out.get()[...]).astype(F32)
    out.ref[quarter:, :] = jnp.where(first, other_out.ref[...], out1.get()[...]).astype(F32)


def assemble(n, shards, g0, g1, other_g, w0, w1, other_w, out0, out1, other_out):
    quarter = other_w.shape[1]
    model = other_g.shape[2]
    hw = other_w.shape[2] // 3
    kept = 2 * quarter
    return call(
        functools.partial(assemble_kernel, n, shards), "assemble", None, 8,
        [Slots(array) for array in (g0, other_g, g1, w0, other_w, w1)] + [out0, other_out, out1],
        [
            ((n * kept, model), F32, n),
            ((2 * quarter, n * shards * kept), F32, n * shards),
            ((2 * quarter, model), F32, 1),
        ]
        + [((2 * quarter, n * hw), F32, n)] * 3,
        [],
    )


def swapped(value):
    return lax.ppermute(value, "section", [(0, 1), (1, 0)])


def body(inputs, cotangent, segments, buckets, query_weight, key_weight, value_weight, out_weight,
         up_weight, down_weight, attn_gain, ffn_gain, bias_table):
    first = lax.axis_index("section") == 0
    turn = lax.axis_index("seq")
    n = lax.axis_size("seq")
    shards = lax.axis_size("dp")
    depth, width = query_weight.shape[1:]
    ff = up_weight.shape[2]
    heads = bias_table.shape[2]
    hw = width // n
    dk = hw // heads
    kept = down_weight.shape[1] // n
    hidden = ff // n
    model = inputs.shape[-1]
    quarter = model // (2 * shards)
    packed = hidden == model == width

    x_in = jnp.where(first, inputs[0, 0], inputs[1, 0])
    d_out = jnp.where(first, cotangent[0, 0], cotangent[1, 0])
    seg = jnp.where(first, segments[0, 0], segments[1, 0])

    wide = max(hw, LANES)

    def pad(value):
        return value if hw == wide else jnp.pad(value, [(0, 0)] * (value.ndim - 1) + [(0, wide - hw)])

    def columns(weight):
        return pad(lax.dynamic_slice_in_dim(weight[0], turn * hw, hw, axis=1))

    own_qkv = jnp.concatenate([columns(query_weight), columns(key_weight), columns(value_weight)], axis=1)
    own_up = jnp.concatenate(
        [
            lax.dynamic_slice_in_dim(up_weight[0], (z * n + turn) * kept, kept, axis=1)
            for z in range(shards)
        ],
        axis=1,
    )
    own_down = lax.dynamic_slice_in_dim(down_weight[0], turn * kept, kept, axis=0)
    table = bias_table[0]

    def halves(own):
        rows = own.shape[0] // 2
        low, high = own[:rows], own[rows:]
        other = swapped(jnp.where(first, high, low))
        return jnp.where(first, low, other), jnp.where(first, other, high)

    def gathered(piece):
        return lax.all_gather(piece, ("dp", "section"), axis=0, tiled=True)

    qkv_halves = halves(own_qkv)
    out_halves = halves(out_weight[0])
    up_halves = halves(own_up)
    down_halves = halves(own_down)
    cols = model // n
    out_cols = lax.dynamic_slice_in_dim(out_halves[0], turn * cols, cols, axis=1)
    first_qkv = gathered(qkv_halves[0])

    def packed_gather(pieces):
        return lax.all_gather(jnp.stack(pieces), ("dp", "section"), axis=0, tiled=False)

    if packed:
        mix_weights = [[packed_gather((up_halves[0], down_halves[0]))]]
    else:
        mix_weights = [[gathered(up_halves[0]), gathered(down_halves[0])]]
    second_qkv = gathered(qkv_halves[1])
    pieces = (out_halves[1], up_halves[1], down_halves[1])
    mix_weights.append([packed_gather(pieces)] if packed else [gathered(piece) for piece in pieces])
    other_table = swapped(table)
    tables = (jnp.where(first, table, other_table), jnp.where(first, other_table, table))

    gains = jnp.pad(jnp.stack([attn_gain[0], ffn_gain[0]]), ((0, 14), (0, 0)))
    first_n1, out_cols, *gain_rows = start(n, shards, x_in, gains, out_cols)
    out_cols = out_cols.reshape(width, cols)

    bucket_count = table.shape[0]
    onehot = (buckets[None, :] == jnp.arange(bucket_count, dtype=jnp.int32)[:, None]).astype(F32)
    offset_rows = [
        lax.dot_general(
            t.astype(F32), onehot, (((0,), (0,)), ((), ())), precision=HIGH, preferred_element_type=F32
        )
        for t in tables
    ]

    lanes = jnp.arange(LANES, dtype=jnp.int32) % 64
    same = seg[:, None] == lanes[None, :]
    ext_q = jnp.where((lanes < 8)[None, :] & ~same, NEG, 0.0).astype(BF16)
    ext_k = jnp.where((lanes < 8)[None, :] & same, 1.0, 0.0).astype(BF16)

    def scattered(gr):
        if not packed:
            gr = [jnp.concatenate([part.reshape(2 * shards, -1, model) for part in gr], axis=1)]
        return lax.psum_scatter(
            gr[0].reshape(-1, model), ("dp", "section"), scatter_dimension=0, tiled=True
        )

    qkv0 = jnp.dot(first_n1, first_qkv, preferred_element_type=F32).astype(BF16)
    o0, lse0, back0, out_all = attend(n, heads, dk, qkv0, ext_q, ext_k, offset_rows[0], out_cols)
    mix_weights[0].insert(0, out_all if packed else out_all.transpose(1, 0, 2).reshape(width, model))
    y0, x1, n2, slope, hid = mix(n, hw, hidden, x_in, gain_rows[1], back0, mix_weights[0])
    n1, qkv1 = norm_gather(n, y0, gain_rows[2], second_qkv)
    o1, lse1, back1, d_all = attend(n, heads, dk, qkv1, ext_q, ext_k, offset_rows[1], d_out)
    y_parts, y_own, dx1, do, gr_ffn1, *gr = turn_round(
        n, hw, hidden, y0, gain_rows[3], back1, mix_weights[1], d_all.reshape(-1, model)
    )
    half1 = scattered(gr)
    d_rows1, y1, d_in1, dy, gr_attn1, dn2, half_w1, *gr = back_across(
        n, shards, heads, dk, hidden, qkv1, o1, lse1, ext_q, ext_k, offset_rows[1], y_parts, pad(do), y_own,
        second_qkv, n1, y0, dx1, gain_rows[2], slope, hid, n2, mix_weights[0],
    )
    half0 = scattered(gr)
    d_rows0, all_g1, gr_ffn0, d_in0, w_grad0, gr_attn0, half_out, all_w1, out1 = back_first(
        n, shards, heads, dk, qkv0, o0, lse0, ext_q, ext_k, offset_rows[0], half1,
        dn2, x1, dy, gain_rows[1], back0, mix_weights[0][0],
        first_qkv, first_n1, x_in, gain_rows[0], half_w1,
    )

    cut = model // shards
    small = []
    for gr_attn, gr_ffn, d_rows in ((gr_attn0, gr_ffn0, d_rows0), (gr_attn1, gr_ffn1, d_rows1)):
        gr_table = lax.dot_general(
            onehot, d_rows, (((1,), (1,)), ((), ())), precision=HIGH, preferred_element_type=F32
        )
        flat = gr_table.reshape(shards, -1)
        flat = jnp.pad(flat, ((0, 0), (0, cut - flat.shape[1])))
        tile = jnp.stack([gr_attn.reshape(shards, cut), gr_ffn.reshape(shards, cut), flat], axis=1)
        small.append(jnp.pad(tile, ((0, 0), (0, 5), (0, 0))))
    all_g0, all_w0, out0, other_g, other_w, other_out, sums, section_outputs, input_grads = finish(
        n, shards, jnp.stack(small), half0, half_out, w_grad0, all_g1, out1, all_w1, y0, y1, d_in0, d_in1
    )
    section_outputs, input_grads = section_outputs[None, :, None], input_grads[None, :, None]
    g_attn, g_ffn = sums[0:1], sums[1:2]
    g_table = sums[2, : bucket_count // shards * heads].reshape(1, bucket_count // shards, heads)

    if packed:
        g_down, g_up, g_out, g_query, g_key, g_value = (
            part[None] for part in assemble(
                n, shards, all_g0, all_g1, other_g, all_w0, all_w1, other_w, out0, out1, other_out
            )
        )
    else:
        low, high = jnp.where(first, all_g0, other_g), jnp.where(first, other_g, all_g1)
        sizes = [kept // 2, quarter * hidden // model]
        cuts = [sum(sizes[:i]) for i in range(3)]

        def joined(index):
            return jnp.stack([part[:, cuts[index] : cuts[index + 1]] for part in (low, high)], axis=1)

        g_down = joined(0).astype(F32).reshape(1, n * kept, model)
        whole = joined(1).reshape(n, depth, shards, kept)
        g_up = whole.transpose(1, 2, 0, 3).reshape(1, depth, ff).astype(F32)
        low, high = jnp.where(first, out0, other_out), jnp.where(first, other_out, out1)
        g_out = jnp.concatenate([low, high], axis=0).astype(F32)[None]
        low, high = jnp.where(first, all_w0, other_w), jnp.where(first, other_w, all_w1)
        whole = jnp.stack([low, high], axis=1).reshape(n, depth, 3, wide)[..., :hw]
        g_query, g_key, g_value = (
            whole[:, :, i].transpose(1, 0, 2).reshape(1, depth, width).astype(F32) for i in range(3)
        )

    return (
        section_outputs,
        input_grads,
        g_query,
        g_key,
        g_value,
        g_out,
        g_up,
        g_down,
        g_attn,
        g_ffn,
        g_table,
    )


def solution(mesh):
    return jax.shard_map(
        body,
        mesh=mesh,
        in_specs=(
            P(None, "dp", "seq", None),
            P(None, "dp", "seq", None),
            P(None, "dp", None),
            P(),
            P("section", "dp", None),
            P("section", "dp", None),
            P("section", "dp", None),
            P("section", "dp", None),
            P("section", "dp", None),
            P("section", "dp", None),
            P("section", "dp"),
            P("section", "dp"),
            P("section", None, "seq"),
        ),
        out_specs=(
            P("section", None, "dp", "seq", None),
            P("section", None, "dp", "seq", None),
            P("section", "dp", None),
            P("section", "dp", None),
            P("section", "dp", None),
            P("section", "dp", None),
            P("section", "dp", None),
            P("section", "dp", None),
            P("section", "dp"),
            P("section", "dp"),
            P("section", "dp", "seq"),
        ),
        check_vma=False,
    )
```

```python
import functools
import math

import jax
import jax.numpy as jnp
from jax import lax
from jax.experimental import pallas as pl
from jax.experimental.pallas import tpu as pltpu
from jax.sharding import PartitionSpec as P

EPSILON = 1e-06
NEG = -1e30
HIGH = lax.Precision.HIGHEST
MESH = pl.DeviceIdType.MESH
F32 = jnp.float32
BF16 = jnp.bfloat16
LANES = 128
QB = 256
VMEM_BYTES = 60 << 20

AWAY = pl.BlockSpec(memory_space=pl.ANY)


def mm(left, right):
    return jnp.dot(left, right, preferred_element_type=F32)


def mm_nt(left, right):
    return lax.dot_general(left, right, (((1,), (1,)), ((), ())), preferred_element_type=F32)


def mm_tn(left, right):
    return lax.dot_general(left, right, (((0,), (0,)), ((), ())), preferred_element_type=F32)


def inverse_rms(rows):
    return lax.rsqrt(jnp.mean(rows * rows, axis=-1, keepdims=True) + EPSILON)


def aligned(start, size):
    return pl.ds(pl.multiple_of(start, size), size)


def signal_and_wait(peers):
    barrier = pltpu.get_barrier_semaphore()
    for peer in peers:
        pl.semaphore_signal(barrier, inc=1, device_id=peer, device_id_type=MESH)
    pl.semaphore_wait(barrier, len(peers))


def others(axis, n):
    me = lax.axis_index(axis)
    return [{axis: lax.rem(me + k, n)} for k in range(1, n)]


def other_core():
    return {"section": 1 - lax.axis_index("section")}


def cores_and_rows(shards):
    core, row = lax.axis_index("section"), lax.axis_index("dp")
    return [
        {"section": lax.rem(core + i, 2), "dp": lax.rem(row + j, shards)}
        for i in range(2)
        for j in range(shards)
        if i + j
    ]


def near(n):
    me = lax.axis_index("seq")
    return [{"seq": peer} for peer in (square(me) if n == 4 else ring(n, me))]


def square(me):
    return me + 1 - 2 * lax.rem(me, 2), lax.rem(me + 2, 4)


def ring(n, me):
    return [lax.rem(me + k, n) for k in range(1, n)]


def push(src, dst, send_sem, recv_sem, peer):
    return pltpu.make_async_remote_copy(
        src_ref=src,
        dst_ref=dst,
        send_sem=send_sem,
        recv_sem=recv_sem,
        device_id=peer if isinstance(peer, dict) else {"seq": peer},
        device_id_type=MESH,
    )


def sources(n):
    me = lax.axis_index("seq")
    if n == 4:
        along_x, along_y = square(me)
        return [me, along_x, along_y, square(along_y)[0]]
    return [lax.rem(me + n - k, n) for k in range(n)]


class Spread:
    def __init__(self, n, source, slot, rows, sems):
        self.n = n
        me = lax.axis_index("seq")
        self.order = sources(n)
        send, recv = sems
        if n != 4:
            self.copies = [
                push(source, slot(me, 0, rows), send.at[k], recv.at[k], peer)
                for k, peer in enumerate(ring(n, me), 1)
            ]
            return
        along_x, along_y = square(me)
        half = rows // 2

        def copy(number, owner, part, peer):
            here = source.at[pl.ds(part * half, half)] if owner is me else slot(owner, part * half, half)
            return push(here, slot(owner, part * half, half), send.at[number], recv.at[number], peer)

        self.copies = [
            copy(0, me, 0, along_x),
            copy(1, me, 1, along_y),
            copy(2, me, 1, along_x),
            copy(3, me, 0, along_y),
            copy(4, along_x, 0, along_y),
            copy(5, along_y, 1, along_x),
        ]

    def start(self):
        self.start_some(True)
        self.start_some(False)

    def start_some(self, first):
        if self.n == 4:
            for copy in self.copies[:2] if first else self.copies[2:4]:
                copy.start()
        elif first:
            for copy in self.copies:
                copy.start()

    def forward(self):
        if self.n == 4:
            for first, second in ((0, 4), (1, 5)):
                self.copies[first].wait_recv()
                self.copies[second].start()

    def arrive(self, k):
        if self.n == 4:
            for number in ((), (2,), (3,), (4, 5))[k]:
                self.copies[number].wait_recv()
        else:
            self.copies[k - 1].wait_recv()

    def sent(self):
        for copy in self.copies:
            copy.wait_send()

    def all(self):
        self.start()
        self.forward()
        for k in range(1, self.n):
            self.arrive(k)
        self.sent()


class Collect:
    def __init__(self, n, out, got, sems, mid=None):
        self.n = n
        self.out, self.got, self.mid = out, got, mid
        self.half = out.shape[1] // 2
        me = lax.axis_index("seq")
        self.order = sources(n)
        send, recv = sems
        if n != 4:
            self.copies = [
                push(out.at[k], got.at[k], send.at[k], recv.at[k], self.order[k]) for k in range(1, n)
            ]
            return
        along_x, along_y = square(me)

        def copy(number, chunk, part, peer):
            return push(self.piece(out, chunk, part), self.landing(number), send.at[number], recv.at[number], peer)

        self.copies = [
            copy(0, 1, 0, along_x),
            copy(1, 2, 1, along_y),
            copy(2, 3, 0, along_x),
            copy(3, 3, 1, along_y),
        ]
        for number, chunk, part, peer in ((4, 2, 0, along_y), (5, 1, 1, along_x)):
            source = self.piece(out, chunk, part) if mid is None else mid.at[number - 4]
            self.copies.append(
                push(source, self.landing(number), send.at[number], recv.at[number], peer)
            )

    def piece(self, ref, chunk, part):
        return ref.at[chunk, pl.ds(part * self.half, self.half)]

    def landing(self, number):
        return self.piece(self.got, number // 2, number % 2)

    def give(self, k, value):
        self.out[k] = value.astype(BF16)
        self.start(k)

    def start(self, k):
        if self.n == 4:
            for number in ((), (0,), (1,), (2, 3))[k]:
                self.copies[number].start()
        else:
            self.copies[k - 1].start()

    def relay(self):
        if self.n == 4:
            for number, chunk, part in ((2, 2, 0), (3, 1, 1)):
                self.copies[number].wait_recv()
                mine = self.piece(self.out, chunk, part)
                summed = (mine[...].astype(F32) + self.landing(number)[...].astype(F32)).astype(BF16)
                if self.mid is None:
                    mine[...] = summed
                else:
                    self.mid[number - 2] = summed
                self.copies[number + 2].start()

    def add_to(self, total):
        if self.n == 4:
            for number, part in ((0, 0), (1, 1), (4, 0), (5, 1)):
                self.copies[number].wait_recv()
                total[pl.ds(part * self.half, self.half)] += self.landing(number)[...].astype(F32)
        else:
            for k in range(1, self.n):
                self.copies[k - 1].wait_recv()
                total[...] += self.got[k].astype(F32)

    def sent(self):
        for copy in self.copies:
            copy.wait_send()


def way_sems(n):
    count = max(n, 6)
    return [pltpu.SemaphoreType.DMA((count,)), pltpu.SemaphoreType.DMA((count,))]


def row_slots(ref, tl):
    return lambda owner, first, rows: ref.at[pl.ds(pl.multiple_of(owner * tl + first, rows), rows)]


def chunk_slots(ref):
    return lambda owner, first, rows: ref.at[owner, pl.ds(first, rows)]


def cost(microseconds):
    return pl.CostEstimate(flops=int(microseconds * 1e9), bytes_accessed=0, transcendentals=0)


class Raw:
    def __init__(self, array):
        self.array = array


class Slots:
    def __init__(self, array):
        self.array = array


class Rows:
    def __init__(self, *arrays):
        self.array = arrays


class Late:
    def __init__(self, pairs, ref, sems):
        self.ref = ref
        self.copies = [pltpu.make_async_copy(src, dst, sems.at[i]) for i, (src, dst) in enumerate(pairs)]
        for copy in self.copies:
            copy.start()
        self.waiting = [True] * len(self.copies)

    def get(self, slot=None):
        for i, copy in enumerate(self.copies):
            if self.waiting[i] and (slot is None or slot == i):
                copy.wait()
                self.waiting[i] = False
        return self.ref


class Early:
    def __init__(self, target, ref, sems):
        self.target, self.ref, self.sems = target, ref, sems
        self.copies = []

    def flush(self, *part):
        src, dst = (self.ref.at[part], self.target.at[part]) if part else (self.ref, self.target)
        copy = pltpu.make_async_copy(src, dst, self.sems.at[len(self.copies)])
        copy.start()
        self.copies.append(copy)

    def get(self):
        return self.ref

    def done(self):
        if not self.copies:
            self.flush()
        for copy in self.copies:
            copy.wait()


class Held:
    def __init__(self, ref):
        self.ref = ref

    def get(self, slot=None):
        return self.ref

    def flush(self, *part):
        pass


class Reduce:
    def __init__(self, shards, value, got_c, sent_z, got_z, send_c, recv_c, send_z, recv_z):
        self.value, self.got_c, self.got_z, self.sent_z = value, got_c, got_z, sent_z
        self.row, self.core = lax.axis_index("dp"), lax.axis_index("section")
        self.rows = got_c.shape[1]
        self.shards = shards
        self.crossed = [
            push(
                value.at[self.part(z, 1 - self.core)],
                got_c.at[z], send_c.at[z], recv_c.at[z], {"section": 1 - self.core},
            )
            for z in range(shards)
        ]
        self.along = [
            push(
                sent_z.at[k], got_z.at[k], send_z.at[k], recv_z.at[k], {"dp": lax.rem(self.row + k, shards)}
            )
            for k in range(1, shards)
        ]

    def part(self, z, core):
        return aligned((2 * z + core) * self.rows, self.rows)

    def both(self, z):
        return self.value[self.part(z, self.core), :].astype(F32) + self.got_c[z].astype(F32)

    def start(self):
        for copy in self.crossed:
            copy.start()

    def forward(self):
        for copy in self.crossed:
            copy.wait()
        for k in range(1, self.shards):
            self.sent_z[k] = self.both(lax.rem(self.row + k, self.shards)).astype(BF16)
            self.along[k - 1].start()

    def result(self):
        half = self.both(self.row)
        for k in range(1, self.shards):
            self.along[k - 1].wait()
            half += self.got_z[k].astype(F32)
        return half.astype(BF16)


class Across:
    def __init__(self, shards, block, got, send, recv):
        self.shards, self.block, self.got = shards, block, got
        self.core = lax.axis_index("section")
        self.copies = [
            push(block(z, 1 - self.core), got.at[z], send.at[z], recv.at[z], {"section": 1 - self.core})
            for z in range(shards)
        ]

    def start(self):
        for copy in self.copies:
            copy.start()

    def sum(self, z):
        self.copies[z].wait()
        return (self.block(z, self.core)[...].astype(F32) + self.got[z].astype(F32)).astype(BF16)


class Along:
    def __init__(self, shards, value, got, send, recv):
        self.shards, self.value, self.got = shards, value, got
        self.row = lax.axis_index("dp")
        self.copies = []
        for k in range(1, shards):
            peer = lax.rem(self.row + k, shards)
            self.copies.append(push(value.at[peer], got.at[k], send.at[k], recv.at[k], {"dp": peer}))

    def start(self):
        for copy in self.copies:
            copy.start()

    def result(self):
        total = self.value[self.row].astype(F32)
        for k, copy in enumerate(self.copies, 1):
            copy.wait()
            total += self.got[k].astype(F32)
        return total.astype(BF16)


class AllSum:
    def __init__(self, n, value, out, c_out, c_got, total, send_c, recv_c, send_s, recv_s):
        self.n, self.value, self.out, self.c_got, self.total = n, value, out, c_got, total
        self.me = lax.axis_index("seq")
        self.rows = total.shape[0]
        self.order = sources(n)
        if n == 4:
            self.collect = Collect(n, c_out, c_got, (send_c, recv_c))
            mine = out.ref.at[self.part(self.me)]
            self.spread = Spread(n, mine, row_slots(out.ref, self.rows), self.rows, (send_s, recv_s))
        else:
            self.spread = Spread(n, value, chunk_slots(c_got), self.rows, (send_s, recv_s))

    def part(self, owner):
        return aligned(owner * self.rows, self.rows)

    def start(self):
        if self.n == 4:
            for k in (3, 1, 2):
                self.collect.give(k, self.value[self.part(self.order[k]), :])
            self.total[...] = self.value[self.part(self.me), :].astype(F32)
        else:
            self.spread.start()

    def relay(self):
        if self.n == 4:
            self.collect.relay()

    def share(self):
        if self.n == 4:
            self.collect.add_to(self.total)
            self.out.ref[self.part(self.me), :] = self.total[...].astype(BF16)
            self.spread.start()

    def forward(self):
        self.spread.forward()

    def done(self):
        for k in range(1, self.n):
            self.spread.arrive(k)
        if self.n == 4:
            self.collect.sent()
        else:
            self.total[...] = self.value[...].astype(F32)
            for k in range(1, self.n):
                self.total[...] += self.c_got[self.order[k]].astype(F32)
            self.out.ref[...] = self.total[...].astype(BF16)
        self.spread.sent()
        self.out.flush()


def sum_scratch(n, rows, width):
    if n == 4:
        rows //= n
    landing = pltpu.VMEM((n, rows, width), BF16)
    return [landing, landing, pltpu.VMEM((rows, width), F32), *way_sems(n), *way_sems(n)]


def reduce_scratch(shards, half):
    return [pltpu.VMEM((shards,) + half, BF16)] * 3 + [pltpu.SemaphoreType.DMA((shards,))] * 4


def call(kernel, name, collective_id, microseconds, operands, outs, scratch, peers=None):
    arrays, buffers, in_sems = [], [], []
    for operand in operands:
        array = operand.array if isinstance(operand, (Raw, Slots, Rows)) else operand
        arrays += array if isinstance(operand, Rows) else [array]
        if not isinstance(operand, Raw):
            copies = 1
            if isinstance(operand, Rows):
                dims = (sum(part.shape[0] for part in array),) + array[0].shape[1:]
                copies, dtype = len(array), array[0].dtype
            else:
                dims, dtype = array.shape, array.dtype
            if isinstance(operand, Slots):
                copies = dims[0]
            buffers.append(pltpu.VMEM(dims, dtype))
            in_sems.append(pltpu.SemaphoreType.DMA((copies,)))
    out_buffers = [pltpu.VMEM(dims, dtype) for dims, dtype, flushes in outs if flushes]
    out_sems = [pltpu.SemaphoreType.DMA((flushes,)) for _, _, flushes in outs if flushes]

    def body(*refs):
        refs = list(refs)

        def take(count):
            taken = refs[:count]
            del refs[:count]
            return taken

        sources, targets = take(len(arrays)), take(len(outs))
        staged, results = take(len(buffers)), take(len(out_buffers))
        staged_sems, result_sems = take(len(buffers)), take(len(out_buffers))
        ins, at = [], 0
        for operand in operands:
            source = sources.pop(0)
            if isinstance(operand, Raw):
                ins.append(source)
                continue
            ref = staged[at]
            if isinstance(operand, Rows):
                pairs, first = [(source, ref.at[pl.ds(0, source.shape[0])])], source.shape[0]
                for _ in operand.array[1:]:
                    source = sources.pop(0)
                    pairs.append((source, ref.at[pl.ds(first, source.shape[0])]))
                    first += source.shape[0]
            elif isinstance(operand, Slots):
                pairs = [(source.at[i], ref.at[i]) for i in range(ref.shape[0])]
            else:
                pairs = [(source, ref)]
            ins.append(Late(pairs, ref, staged_sems[at]))
            at += 1
        early = [
            Early(target, results.pop(0), result_sems.pop(0)) if flushes else target
            for target, (_, _, flushes) in zip(targets, outs)
        ]
        if peers is not None:
            signal_and_wait(peers())
        kernel(ins, early, *refs)
        for late in ins:
            if isinstance(late, Late):
                late.get()
        for result in early:
            if isinstance(result, Early):
                result.done()

    return pl.pallas_call(
        body,
        out_shape=[jax.ShapeDtypeStruct(dims, dtype) for dims, dtype, _ in outs],
        in_specs=[AWAY] * len(arrays),
        out_specs=[AWAY] * len(outs),
        scratch_shapes=[*buffers, *out_buffers, *in_sems, *out_sems, *scratch],
        compiler_params=pltpu.CompilerParams(
            collective_id=collective_id,
            has_side_effects=collective_id is not None,
            vmem_limit_bytes=VMEM_BYTES,
        ),
        cost_estimate=cost(microseconds),
        name=name,
    )(*arrays)


def start_kernel(n, shards, ins, outs, all_ref, send, recv, send_g, recv_g, send_z, recv_z, send_x, recv_x):
    x, own, piece = ins
    out, weight, *gains = outs
    tl = x.ref.shape[0]
    cut = own.ref.shape[1]
    me = lax.axis_index("seq")
    layer = lax.axis_index("section")
    row = lax.axis_index("dp")
    mine = aligned(me * tl, tl)
    peers = cores_and_rows(shards)
    own_ref = own.get()
    copies = [
        push(own_ref, all_ref.at[layer, row], send_g.at[i], recv_g.at[i], peer)
        for i, peer in enumerate(peers)
    ]
    for copy in copies:
        copy.start()
    all_ref[layer, row] = own_ref[...]
    weight.ref[row, layer] = piece.get()[...]

    def cross(z, core):
        ref = weight.ref.at[z, core]
        return push(ref, ref, send_x.at[z], recv_x.at[z], {"section": 1 - layer})

    along = []
    for k in range(1, shards):
        ref = weight.ref.at[row, layer]
        along.append(push(ref, ref, send_z.at[k], recv_z.at[k], {"dp": lax.rem(row + k, shards)}))
        along[-1].start()
    cross(row, layer).start()
    rows = x.get()[...].astype(F32)
    inv = inverse_rms(rows)
    for copy in copies:
        copy.wait()
    for z in range(shards):
        part = slice(z * cut, (z + 1) * cut)
        for i, gain in enumerate(gains):
            gain.ref[:, part] = all_ref[i // 2, z, i % 2 : i % 2 + 1, :].astype(F32)
    out.ref[mine] = (rows * inv * gains[0].ref[...]).astype(BF16)
    spread = Spread(n, out.ref.at[mine], row_slots(out.ref, tl), tl, (send, recv))
    spread.start()
    out.flush(mine)
    for gain in gains:
        gain.flush()
    spread.forward()
    for k in range(1, shards):
        along[k - 1].wait()
        cross(lax.rem(row + shards - k, shards), layer).start()
    for k in range(1, n):
        spread.arrive(k)
        out.flush(aligned(spread.order[k] * tl, tl))
    for z in range(shards):
        cross(z, 1 - layer).wait()
        weight.flush(z)
    spread.sent()


def start(n, shards, x, gains, piece):
    tl, width = x.shape
    small_sems = pltpu.SemaphoreType.DMA((2 * shards - 1,))
    row_sems = pltpu.SemaphoreType.DMA((shards,))
    return call(
        functools.partial(start_kernel, n, shards), "start", 6, 28,
        [x, gains, piece],
        [((n * tl, width), BF16, n), ((shards, 2) + piece.shape, BF16, shards)] + [((1, width), F32, 1)] * 4,
        [
            pltpu.VMEM((2, shards) + gains.shape, BF16),
            *way_sems(n),
            small_sems,
            small_sems,
            row_sems,
            row_sems,
            row_sems,
            row_sems,
        ],
        lambda: cores_and_rows(shards) + near(n),
    )


def gather_kernel(n, ins, outs, send, recv):
    x, gain, w = ins
    out, qkv = outs
    tl = x.ref.shape[0]
    mine = aligned(lax.axis_index("seq") * tl, tl)
    rows = x.get()[...].astype(F32)
    out.ref[mine] = (rows * inverse_rms(rows) * gain.get()[...]).astype(BF16)
    spread = Spread(n, out.ref.at[mine], row_slots(out.ref, tl), tl, (send, recv))
    spread.start()
    w.get()
    for k in range(n):
        where = aligned(spread.order[k] * tl, tl)
        if k:
            spread.arrive(k)
        out.flush(where)
        qkv.ref[where] = mm(out.ref[where], w.ref[...]).astype(BF16)
        qkv.flush(where)
        if not k:
            spread.forward()
    spread.sent()


def norm_gather(n, x, gain, w):
    tl, width = x.shape
    return call(
        functools.partial(gather_kernel, n), "norm_gather", 0, 20,
        [x, gain, w],
        [((n * tl, width), BF16, n), ((n * tl, w.shape[1]), BF16, n)],
        way_sems(n),
        lambda: near(n),
    )


def toeplitz_rows(offset_row):
    spread = jnp.broadcast_to(offset_row, (LANES, offset_row.shape[1]))
    return pltpu.roll(spread, 0, 1, stride=1, stride_axis=0)


def attend_kernel(n, heads, dk, ins, outs, bias_ref, kt_ref, qa_ref, send, recv, send_d, recv_d):
    chunk, qkv, eq, ek, rows = ins
    o, lse_out, back, chunks = outs
    o_ref, lse_ref, back_ref, chunks_ref = o.ref, lse_out.ref, back.ref, chunks.ref
    length, wide = o_ref.shape
    tl = length // n
    group = QB // tl
    blocks = length // QB
    me = lax.axis_index("seq")
    mine = aligned(me * tl, tl)
    chunk_ref = chunk.get()
    spread = Spread(n, chunk_ref, chunk_slots(chunks_ref), chunk_ref.shape[0], (send_d, recv_d))
    spread.start()
    chunks_ref[me] = chunk_ref[...]
    chunks.flush(me)
    qkv_ref, eq_ref, ek_ref, rows_ref = qkv.get(), eq.get(), ek.get(), rows.get()
    lane = lax.broadcasted_iota(jnp.int32, (length, LANES), 1)
    lane_q = lax.broadcasted_iota(jnp.int32, (LANES, LANES), 1)
    pairs = (heads + 1) // 2
    for p in range(pairs):
        pair = pl.ds(p * LANES, LANES)
        k_pair = pl.ds(wide + p * LANES, LANES)
        v_pair = pl.ds(2 * wide + p * LANES, LANES)
        held = min(2, heads - 2 * p)
        for i in range(held):
            inside = (lane >= dk) if i else (lane < dk)
            qa_ref[i] = jnp.where(inside, qkv_ref[:, pair], eq_ref[...])
            kt_ref[i] = jnp.where(inside, qkv_ref[:, k_pair], ek_ref[...]).T
            bias_ref[i] = toeplitz_rows(rows_ref[2 * p + i : 2 * p + i + 1, :])

        def block(step, carry, p=p, pair=pair, v_pair=v_pair, held=held):
            b = lax.rem(lax.div(me, group) + 1 + step, blocks)
            rows = aligned(b * QB, QB)
            scores = [mm(qa_ref[i, rows, :], kt_ref[i]) for i in range(held)]
            for a in range(QB // LANES):
                tile = b * (QB // LANES) + a
                where = aligned(tile * LANES, LANES)
                off = pl.ds(pl.multiple_of(length - tile * LANES, LANES), length)
                lse = None if p == 0 else lse_ref[where, :]
                mixed = None
                for i in range(held):
                    part = scores[i][a * LANES : (a + 1) * LANES] + bias_ref[i, :, off]
                    peak = jnp.max(part, axis=-1, keepdims=True)
                    expo = jnp.exp(part - peak)
                    total = jnp.sum(expo, axis=-1, keepdims=True)
                    value = mm(expo.astype(BF16), qkv_ref[:, v_pair]) * (1.0 / total)
                    column = peak + jnp.log(total)
                    mixed = jnp.where(lane_q < dk, mixed, value) if i else value
                    if lse is None:
                        lse = jnp.broadcast_to(column, (LANES, LANES))
                    else:
                        lse = jnp.where(lane_q == 2 * p + i, column, lse)
                o_ref[where, pair] = mixed.astype(BF16)
                lse_ref[where, :] = lse
            for g in range(group):
                peer = b * group + g

                @pl.when(peer != me)
                def _(peer=peer):
                    push(
                        o_ref.at[aligned(peer * tl, tl), pair],
                        back_ref.at[me, :, pair],
                        send.at[p, peer],
                        recv.at[p, me],
                        peer,
                    ).start()

            return carry

        lax.fori_loop(0, blocks, block, 0)
        back_ref[me, :, pair] = o_ref[mine, pair]
        o.flush(slice(None), pair)
        if p == 0:
            spread.forward()
    lse_out.flush()
    for k in range(1, n):
        spread.arrive(k)
        chunks.flush(spread.order[k])
    spread.sent()
    for p in range(pairs):
        pair = pl.ds(p * LANES, LANES)
        for k in range(1, n):
            peer = lax.rem(me + k, n)
            push(
                o_ref.at[aligned(peer * tl, tl), pair],
                back_ref.at[peer, :, pair],
                send.at[p, peer],
                recv.at[p, peer],
                peer,
            ).wait()


def attend(n, heads, dk, qkv, ext_q, ext_k, offset_rows, chunk):
    length, width = qkv.shape[0], qkv.shape[1] // 3
    span = offset_rows.shape[1]
    pairs = (heads + 1) // 2
    pair_sems = pltpu.SemaphoreType.DMA((pairs, n))
    return call(
        functools.partial(attend_kernel, n, heads, dk), "attend", 4 if chunk.shape[0] == length else 5, 20,
        [chunk, qkv, ext_q, ext_k, offset_rows],
        [
            ((length, width), BF16, pairs),
            ((length, LANES), F32, 1),
            ((n, length // n, width), BF16, 1),
            ((n,) + chunk.shape, BF16, n),
        ],
        [
            pltpu.VMEM((2, LANES, span), F32),
            pltpu.VMEM((2, LANES, length), BF16),
            pltpu.VMEM((2, length, LANES), BF16),
            pair_sems,
            pair_sems,
            *way_sems(n),
        ],
        lambda: others("seq", n),
    )


def three_parts(lane, value):
    first = value.astype(BF16).astype(F32)
    rest = value - first
    second = rest.astype(BF16).astype(F32)
    third = rest - second
    at = lax.rem(lane, 64)
    return jnp.where(at == 8, first, jnp.where(at == 9, second, jnp.where(at == 10, third, 0.0)))


def attend_back_kernel(n, heads, dk, summing, ins, outs, bias_ref, kt_ref, vt_ref, qa_ref, do_ref, qt_ref,
                       dkt_ref, dvt_ref, dbias_ref, send, recv, *refs):
    qkv, o, lse, eq, ek, rows, beside, *more = ins
    dqkv, dr, beside_out, *more_out = outs
    dqkv_ref, dr_ref = dqkv.ref, dr.ref
    length, wide = o.ref.shape
    span = rows.ref.shape[1]
    tl = length // n
    group = QB // tl
    blocks = length // QB
    me = lax.axis_index("seq")
    mine = aligned(me * tl, tl)
    if summing:
        do, own = more
        mid_ref, got_ref, send_y, recv_y = refs
        do_any = do.get()
        for k in range(1, n):
            peer = lax.rem(me + k, n)
            push(do_any.at[peer], do_ref.at[mine], send.at[peer], recv.at[me], peer).start()
        do_ref[mine] = do_any[me]
        collect = Collect(n, beside.get(), got_ref, (send_y, recv_y), mid_ref)

        def start_beside():
            for k in (3, 1, 2) if n == 4 else range(1, n):
                collect.start(k)

    else:
        dn2, x1, dy, gain, back, weights = more
        dx1_out, g_gain, g_out, reduce, beside_next, summed = more_out
        wo_ref, do_any, load, send_g, recv_g = refs
        loads = out_loads(weights, wo_ref, load)
        for copy in loads:
            copy.start()
        rows_g = beside_out.ref.shape[1]
        g_ref = beside.get().at[pl.ds(0, rows_g)]
        spread = Spread(n, g_ref, chunk_slots(beside_out.ref), rows_g, (send_g, recv_g))
        spread.start_some(True)

        def start_beside():
            spread.start_some(False)
            summed.start()

        dx1, g_gain.ref[...] = norm_back(
            x1.get()[...], dn2.get()[...], dy.get()[...].astype(F32), gain.get()[...]
        )
        dx1_out.ref[...] = dx1
        dx1_out.flush()
        d_attn = dx1.astype(BF16)
        arrive(loads)
        back_ref = back.get()
        hw = wo_ref.shape[0] // n
        if hw < wide:
            do_any[...] = jnp.zeros_like(do_any)
        for k in range(1, n):
            peer = lax.rem(me + k, n)
            do_any[peer, :, :hw] = mm_nt(d_attn, wo_ref[aligned(peer * hw, hw), :]).astype(BF16)
            push(do_any.at[peer], do_ref.at[mine], send.at[peer], recv.at[me], peer).start()
        do_any[me, :, :hw] = mm_nt(d_attn, wo_ref[aligned(me * hw, hw), :]).astype(BF16)
        do_ref[mine] = do_any[me]
        beside_out.ref[me] = g_ref[...]
        beside_out.flush(me)
        for t in range(n):
            g_out.ref[pl.ds(t * hw, hw), :] = mm_tn(back_ref[t][:, :hw], d_attn).astype(BF16)
        reduce.start()
    qkv_ref, o_ref, lse_ref, eq_ref, ek_ref, rows_ref = (
        late.get() for late in (qkv, o, lse, eq, ek, rows)
    )
    lane = lax.broadcasted_iota(jnp.int32, (length, LANES), 1)
    lane_q = lax.broadcasted_iota(jnp.int32, (QB, LANES), 1)
    at = lax.rem(lane, 64)
    parts = (at >= 8) & (at <= 10)
    ones = jnp.where(parts, 1.0, 0.0)
    for p in range((heads + 1) // 2):
        pair = pl.ds(p * LANES, LANES)
        k_lanes = pl.ds(wide + p * LANES, LANES)
        v_lanes = pl.ds(2 * wide + p * LANES, LANES)
        held = min(2, heads - 2 * p)
        q_pair, k_pair, v_pair = qkv_ref[:, pair], qkv_ref[:, k_lanes], qkv_ref[:, v_lanes]
        qt_ref[...] = q_pair.T
        ek = (ek_ref[...].astype(F32) + ones).astype(BF16)
        for i in range(held):
            head = 2 * p + i
            inside = (lane >= dk) if i else (lane < dk)
            lse = lse_ref[:, head : head + 1]
            eq = (eq_ref[...].astype(F32) - three_parts(lane, lse)).astype(BF16)
            qa_ref[i] = jnp.where(inside, q_pair, eq)
            kt_ref[i] = jnp.where(inside, k_pair, ek).T
            vt_ref[i] = jnp.where(inside, v_pair, ones.astype(BF16)).T
            bias_ref[i] = toeplitz_rows(rows_ref[head : head + 1, :])
        dkt_ref[...] = jnp.zeros_like(dkt_ref)
        dvt_ref[...] = jnp.zeros_like(dvt_ref)
        dbias_ref[...] = jnp.zeros_like(dbias_ref)

        def given(peer):
            return push(
                do_any.at[peer], do_ref.at[aligned(peer * tl, tl)], send.at[peer], recv.at[peer], peer
            )

        def block(step, carry, p=p, pair=pair, k_lanes=k_lanes, held=held):
            b = lax.rem(lax.div(me, group) + step, blocks)
            where = aligned(b * QB, QB)
            if p == 0:
                for g in range(group):
                    peer = b * group + g

                    @pl.when(peer != me)
                    def _(peer=peer):
                        given(peer).wait()

                pl.when(step == 1)(start_beside)


            dq = None
            do_pair = do_ref[where, pair]
            do_t = do_pair.T
            weighed = do_pair.astype(F32) * o_ref[where, pair].astype(F32)
            for i in range(held):
                half = pl.ds(i * dk, dk)
                inside_q = (lane_q >= dk) if i else (lane_q < dk)
                delta = jnp.sum(jnp.where(inside_q, weighed, 0.0), axis=-1, keepdims=True)
                da = jnp.where(inside_q, do_pair, (-three_parts(lane_q, delta)).astype(BF16))
                scores = mm(qa_ref[i, where, :], kt_ref[i])
                lifted = mm(da, vt_ref[i])
                probs, grads = [], []
                for a in range(QB // LANES):
                    cut = slice(a * LANES, (a + 1) * LANES)
                    tile = b * (QB // LANES) + a
                    off = pl.ds(pl.multiple_of(length - tile * LANES, LANES), length)
                    prob = jnp.exp(scores[cut] + bias_ref[i, :, off])
                    grad = prob * lifted[cut]
                    dbias_ref[i, :, off] += grad
                    probs.append(prob.astype(BF16))
                    grads.append(grad.astype(BF16))
                prob = jnp.concatenate(probs, axis=0)
                grad = jnp.concatenate(grads, axis=0)
                value = mm(grad, qkv_ref[:, k_lanes])
                dq = jnp.where(lane_q < dk, dq, value) if i else value
                dkt_ref[half, :] += mm(qt_ref[half, where], grad)
                dvt_ref[half, :] += mm(do_t[i * dk : (i + 1) * dk], prob)
            dqkv_ref[where, pair] = dq.astype(BF16)
            return carry

        lax.fori_loop(0, length // QB, block, 0)
        dqkv_ref[:, k_lanes] = dkt_ref[...].T.astype(BF16)
        dqkv_ref[:, v_lanes] = dvt_ref[...].T.astype(BF16)
        for lanes in (pair, k_lanes, v_lanes):
            dqkv.flush(slice(None), lanes)
        place = lax.broadcasted_iota(jnp.int32, (8, span), 0)
        for i in range(held):
            folded = dbias_ref[i]
            rows = LANES
            while rows > 8:
                rows //= 2
                folded = folded[:rows] + pltpu.roll(folded[rows:], span - rows, 1)
            for bit in (4, 2, 1):
                folded = jnp.where(
                    lax.rem(lax.div(place, bit), 2) == 1, pltpu.roll(folded, span - bit, 1), folded
                )
            dr_ref[2 * p + i : 2 * p + i + 1, :] = jnp.sum(folded, axis=0, keepdims=True)
        if p == 0:
            if summing:
                collect.relay()
            else:
                reduce.forward()
                spread.forward()
                summed.relay()
                beside_next.start()
    dr.flush()
    if summing:
        collect.add_to(own.get())
        beside_out.ref[...] = own.ref[...].astype(BF16)
        beside_out.flush()
        collect.sent()
    else:
        for k in range(1, n):
            spread.arrive(k)
            beside_out.flush(spread.order[k])
        spread.sent()
        summed.share()
        beside_next.forward()


def out_loads(source, target, sems):
    if len(source.shape) == 2:
        return [pltpu.make_async_copy(source, target, sems.at[0])]
    blocks, _, cols = source.shape
    return [
        pltpu.make_async_copy(source.at[t], target.at[:, pl.ds(t * cols, cols)], sems.at[t])
        for t in range(blocks)
    ]


def attend_back_scratch(heads, length, width, span, n):
    sems = pltpu.SemaphoreType.DMA((n,))
    return [
        pltpu.VMEM((2, LANES, span), F32),
        pltpu.VMEM((2, LANES, length), BF16),
        pltpu.VMEM((2, LANES, length), BF16),
        pltpu.VMEM((2, length, LANES), BF16),
        pltpu.VMEM((length, width), BF16),
        pltpu.VMEM((LANES, length), BF16),
        pltpu.VMEM((LANES, length), F32),
        pltpu.VMEM((LANES, length), F32),
        pltpu.VMEM((2, LANES, span), F32),
        sems,
        sems,
    ]


def weight_loads(sources, targets, sems):
    if len(sources) == 3:
        return [
            [pltpu.make_async_copy(src, dst, sems.at[j])] if dst is not None else None
            for j, (src, dst) in enumerate(zip(sources, targets))
        ]
    packed = sources[-1]
    pieces, count, rows = packed.shape[:3]
    groups = [
        [
            pltpu.make_async_copy(
                packed.at[i, j], targets[j - count].at[pl.ds(i * rows, rows)], sems.at[j * pieces + i]
            )
            for i in range(pieces)
        ]
        for j in range(count)
    ]
    if targets[0] is None:
        return [None] * (3 - count) + groups
    if count == 2:
        blocks, _, cols = sources[0].shape
        groups.insert(
            0,
            [
                pltpu.make_async_copy(
                    sources[0].at[t], targets[0].at[:, pl.ds(t * cols, cols)], sems.at[2 * pieces + t]
                )
                for t in range(blocks)
            ],
        )
    return groups


def load_sems(weights):
    count = 3
    if len(weights) < 3:
        count = weights[-1].shape[0] * weights[-1].shape[1] + (weights[0].shape[0] if len(weights) == 2 else 0)
    return pltpu.SemaphoreType.DMA((count,))


def arrive(copies):
    for copy in copies:
        copy.wait()


def mix_kernel(n, hw, ins, outs, wo_ref, up_ref, down_ref, out_ref, got_ref, total_ref,
               load, send_n, recv_n, send_y, recv_y):
    x, gain, back, *weights = ins
    y, x1_out, n2, slope, hid = outs
    n2_ref = n2.ref
    tl = x.ref.shape[0]
    me = lax.axis_index("seq")
    mine = aligned(me * tl, tl)
    loads = weight_loads(weights, (wo_ref, up_ref, down_ref), load)
    for group in loads:
        for copy in group:
            copy.start()
    back_ref = back.get()
    total = x.get()[...].astype(F32)
    arrive(loads[0])
    for s in range(n):
        total += mm(back_ref[s][:, :hw], wo_ref[s * hw : (s + 1) * hw, :])
    total_ref[...] = total
    x1 = total_ref[...]
    n2_ref[mine] = (x1 * inverse_rms(x1) * gain.get()[...]).astype(BF16)
    spread = Spread(n, n2_ref.at[mine], row_slots(n2_ref, tl), tl, (send_n, recv_n))
    collect = Collect(n, out_ref, got_ref, (send_y, recv_y))

    spread.start()
    x1_out.ref[...] = x1
    x1_out.flush()
    arrive(loads[1])
    arrive(loads[2])
    for k in range(n):
        where = aligned(spread.order[k] * tl, tl)
        if k:
            spread.arrive(k)
        n2.flush(where)
        u = mm(n2_ref[where], up_ref[...])
        half = 0.5 + 0.5 * lax.erf(u * math.sqrt(0.5))
        hidden = (u * half).astype(BF16)
        hid.ref[where] = hidden
        hid.flush(where)
        slope.ref[where] = (
            half + u * (jnp.exp(-0.5 * u * u) * (1.0 / math.sqrt(2.0 * math.pi)))
        ).astype(BF16)
        slope.flush(where)
        part = mm(hidden, down_ref[...])
        if k:
            collect.give(k, part)
        else:
            total_ref[...] += part
            spread.forward()

    collect.relay()
    collect.add_to(total_ref)
    y.ref[...] = total_ref[...].astype(BF16)
    y.flush()
    spread.sent()
    collect.sent()


def mix(n, hw, ff, x, gain, back, weights):
    tl, width = x.shape
    tokens = n * tl
    return call(
        functools.partial(mix_kernel, n, hw), "mix", 1, 45,
        [x, gain, back, *map(Raw, weights)],
        [
            ((tl, width), BF16, 1),
            ((tl, width), F32, 1),
            ((tokens, width), BF16, n),
            ((tokens, ff), BF16, n),
            ((tokens, ff), BF16, n),
        ],
        [
            pltpu.VMEM((n * hw, width), BF16),
            pltpu.VMEM((width, ff), BF16),
            pltpu.VMEM((ff, width), BF16),
            pltpu.VMEM((n, tl, width), BF16),
            pltpu.VMEM((n, tl, width), BF16),
            pltpu.VMEM((tl, width), F32),
            load_sems(weights),
            *way_sems(n),
            *way_sems(n),
        ],
        lambda: near(n),
    )


def norm_back(x1, dn, dy, gain):
    inv = inverse_rms(x1)
    scaled = x1 * inv
    g_gain = jnp.sum(dn * scaled, axis=0, keepdims=True)
    lifted = dn * gain
    return dy + inv * (lifted - scaled * jnp.mean(lifted * scaled, axis=-1, keepdims=True)), g_gain


def turn_kernel(n, hw, ins, outs, wo_ref, up_ref, down_ref, n2_ref, hid_ref, du_ref, out_ref, got_ref, total_ref,
                load, send_n, recv_n, send_d, recv_d):
    x, gain, back, dy, *weights = ins
    parts, own, dx1_out, do, g_gain, *grads = outs
    own_ref = own.ref
    tl = x.ref.shape[0]
    me = lax.axis_index("seq")
    mine = aligned(me * tl, tl)
    loads = weight_loads(weights, (wo_ref, up_ref, down_ref), load)
    for group in loads:
        for copy in group:
            copy.start()
    back_ref = back.get()
    total = x.get()[...].astype(F32)
    arrive(loads[0])
    for s in range(n):
        total += mm(back_ref[s][:, :hw], wo_ref[s * hw : (s + 1) * hw, :])
    own_ref[...] = total
    x1 = own_ref[...]
    gain_row = gain.get()[...]
    n2_ref[mine] = (x1 * inverse_rms(x1) * gain_row).astype(BF16)
    spread = Spread(n, n2_ref.at[mine], row_slots(n2_ref, tl), tl, (send_n, recv_n))
    collect = Collect(n, out_ref, got_ref, (send_d, recv_d))
    dy_all = dy.get()

    spread.start()
    arrive(loads[1])
    arrive(loads[2])
    for k in range(n):
        where = aligned(spread.order[k] * tl, tl)
        if k:
            spread.arrive(k)
        u = mm(n2_ref[where], up_ref[...])
        half = 0.5 + 0.5 * lax.erf(u * math.sqrt(0.5))
        hid_ref[where] = (u * half).astype(BF16)
        slope = half + u * (jnp.exp(-0.5 * u * u) * (1.0 / math.sqrt(2.0 * math.pi)))
        du = (mm_nt(dy_all[where], down_ref[...]) * slope).astype(BF16)
        du_ref[where] = du
        part = mm_nt(du, up_ref[...])
        if k:
            collect.give(k, part)
        else:
            total_ref[...] = part
            spread.forward()

    for k in range(1, n):
        parts.ref[k] = mm(hid_ref[aligned(spread.order[k] * tl, tl)], down_ref[...]).astype(BF16)
        parts.flush(k)
    collect.relay()
    parts.ref[0] = jnp.zeros_like(out_ref[0])
    parts.flush(0)
    own_ref[...] = x1 + mm(hid_ref[mine], down_ref[...])
    own.flush()
    store_grad(grads, 0, hid_ref, dy_all)
    store_grad(grads, 1, n2_ref, du_ref)
    collect.add_to(total_ref)
    dx1, g_gain.ref[...] = norm_back(x1, total_ref[...], dy_all[mine].astype(F32), gain_row)
    out_back(hw, dx1, dx1_out, do, grads, back_ref, wo_ref)
    spread.sent()
    collect.sent()


def out_back(hw, dx1, dx1_out, do, grads, back_ref, wo_ref):
    dx1_out.ref[...] = dx1
    dx1_out.flush()
    d_attn = dx1.astype(BF16)
    for s in range(back_ref.shape[0]):
        do.ref[s] = mm_nt(d_attn, wo_ref[s * hw : (s + 1) * hw, :]).astype(BF16)
        do.flush(s)
    for s in range(back_ref.shape[0]):
        store_rows(grads, 2, s * hw, mm_tn(back_ref[s][:, :hw], d_attn).astype(BF16))
    flush_grad(grads, 2)


def grad_shapes(weights, hw, n, ff, width):
    if len(weights) < 3:
        pieces, _, rows = weights[-1].shape[:3]
        return [((pieces, 3, rows, width), BF16, 3)]
    return [((ff, width), BF16, 1), ((width, ff), BF16, 1), ((n * hw, width), BF16, 1)]


def turn_round(n, hw, ff, x, gain, back, weights, dy_all):
    tl, width = x.shape
    return call(
        functools.partial(turn_kernel, n, hw), "turn_round", 2, 55,
        [x, gain, back, dy_all, *map(Raw, weights)],
        [
            ((n, tl, width), BF16, n),
            ((tl, width), F32, 1),
            ((tl, width), F32, 1),
            ((n, tl, hw), BF16, n),
            ((1, width), F32, 1),
            *grad_shapes(weights, hw, n, ff, width),
        ],
        [
            pltpu.VMEM((n * hw, width), BF16),
            pltpu.VMEM((width, ff), BF16),
            pltpu.VMEM((ff, width), BF16),
            pltpu.VMEM((n * tl, width), BF16),
            pltpu.VMEM((n * tl, ff), BF16),
            pltpu.VMEM((n * tl, ff), BF16),
            pltpu.VMEM((n, tl, width), BF16),
            pltpu.VMEM((n, tl, width), BF16),
            pltpu.VMEM((tl, width), F32),
            load_sems(weights),
            *way_sems(n),
            *way_sems(n),
        ],
        lambda: near(n),
    )


def mix_back_kernel(n, shards, loads, ins, outs, up_ref, down_ref, out_ref, got_ref, dy_all,
                    send_n, recv_n, send_d, recv_d, *reduce_refs):
    dy, w_grad, slope, hid, n2 = ins
    dn2, half_out, *grads = outs
    blocks = len(grads) == 1
    if blocks:
        sums_out, sum_sems, packed, got_0, got_1, send_0, recv_0, send_1, recv_1 = reduce_refs[7:]
        reduce_refs = reduce_refs[:7]
        grads = [Held(packed)]
        across = [
            Across(shards, lambda z, core, j=j: packed.at[2 * z + core, j], got, send, recv)
            for j, (got, send, recv) in enumerate(((got_0, send_0, recv_0), (got_1, send_1, recv_1)))
        ]
    tl = dy.ref.shape[0]
    mine = aligned(lax.axis_index("seq") * tl, tl)
    dy_ref = dy.get()
    spread = Spread(n, dy_ref, row_slots(dy_all, tl), tl, (send_d, recv_d))
    spread.start()
    reduce = Reduce(shards, w_grad.get(), *reduce_refs)
    reduce.start()
    dy_all[mine] = dy_ref[...]
    collect = Collect(n, out_ref, got_ref, (send_n, recv_n))
    arrive(loads[2])
    arrive(loads[1])
    du_ref = slope.get()
    for k in range(n):
        where = aligned(spread.order[k] * tl, tl)
        if k:
            spread.arrive(k)
        du = (mm_nt(dy_all[where], down_ref[...]) * du_ref[where].astype(F32)).astype(BF16)
        du_ref[where] = du
        part = mm_nt(du, up_ref[...])
        if k:
            collect.give(k, part)
        else:
            spread.forward()
            dn2.ref[...] = part
            reduce.forward()
    store_grad(grads, 0, hid.get(), dy_all)
    if blocks:
        across[0].start()
    collect.relay()
    store_grad(grads, 1, n2.get(), du_ref)
    copies = []
    if blocks:
        across[1].start()
        rows = packed.shape[2]
        for j in range(2):
            for z in range(shards):
                part = pl.ds((2 * z + j) * rows, rows)
                hid.ref[part, :] = across[j].sum(z)
                copies.append(
                    pltpu.make_async_copy(hid.ref.at[part], sums_out.at[part], sum_sems.at[2 * z + j])
                )
                copies[-1].start()
    half_out.ref[...] = reduce.result()
    half_out.flush()
    collect.add_to(dn2.ref)
    dn2.flush()
    arrive(copies)
    spread.sent()
    collect.sent()


def flush_grad(grads, index):
    if len(grads) == 1:
        grads[0].flush(slice(None), index)
    else:
        grads[index].flush()


def store_rows(grads, index, first, value):
    if len(grads) == 1:
        ref = grads[0].ref
        rows = ref.shape[2]
        for i in range(value.shape[0] // rows):
            ref[first // rows + i, index] = value[i * rows : (i + 1) * rows]
    else:
        grads[index].ref[pl.ds(first, value.shape[0]), :] = value


def row_blocks(left_ref, right_ref, store):
    rows = min(256, left_ref.shape[1])

    def block(b, carry):
        first = pl.multiple_of(b * rows, rows)
        store(first, mm_tn(left_ref[:, pl.ds(first, rows)], right_ref[...]).astype(BF16))
        return carry

    lax.fori_loop(0, left_ref.shape[1] // rows, block, 0)


def store_grad(grads, index, left_ref, right_ref):
    row_blocks(left_ref, right_ref, functools.partial(store_rows, grads, index))
    flush_grad(grads, index)


def project_back_kernel(n, ins, outs, out_ref, got_ref, total_ref, send, recv):
    w, dqkv, n1, x, dx1, gain = ins
    dx_out, low, g_w, g_gain = outs
    tl = x.ref.shape[0]
    collect = Collect(n, out_ref, got_ref, (send, recv))
    w_ref, dqkv_ref = w.get(), dqkv.get()

    def part(k):
        return mm_nt(dqkv_ref[aligned(collect.order[k] * tl, tl), :], w_ref[...])

    for k in (3, 1, 2) if n == 4 else range(1, n):
        collect.give(k, part(k))
    total_ref[...] = part(0)
    collect.relay()

    def store(first, value):
        g_w.ref[pl.ds(first, value.shape[0]), :] = value

    row_blocks(n1.get(), dqkv_ref, store)
    g_w.flush()
    collect.add_to(total_ref)
    dx, g_gain.ref[...] = norm_back(x.get()[...].astype(F32), total_ref[...], dx1.get()[...], gain.get()[...])
    dx_out.ref[...] = dx
    dx_out.flush()
    low.ref[...] = dx.astype(BF16)
    low.flush()
    collect.sent()


def back_across_kernel(n, shards, heads, dk, ins, outs, dqkv, g_w, out_ref, got_p, send_p, recv_p,
                       up_ref, down_ref, got_m, dy_all, load, *refs):
    attend_ins, (w, n1, x, dx1, gain), (slope, hid, n2), weights = ins[:9], ins[9:14], ins[14:17], ins[17:]
    dr, y, dx, low, g_gain, dn2, half_w, *grads = outs
    loads = weight_loads(weights, (None, up_ref, down_ref), load)
    for group in reversed(loads[1:]):
        for copy in group:
            copy.start()
    attend_back_kernel(n, heads, dk, True, attend_ins, [Held(dqkv), dr, y], *refs[:15])
    project_back_kernel(
        n, [w, Held(dqkv), n1, x, dx1, gain], [dx, low, Held(g_w), g_gain],
        out_ref, got_p, dn2.ref, send_p, recv_p,
    )
    mix_back_kernel(
        n, shards, loads, [low, Held(g_w), slope, hid, n2], [dn2, half_w, *grads],
        up_ref, down_ref, out_ref, got_m, dy_all, *refs[15:26], *(grads if len(grads) == 1 else []), *refs[26:],
    )


def back_across(n, shards, heads, dk, ff, qkv, o, lse, ext_q, ext_k, offset_rows, parts, do, own,
                w, n1, x, dx1, gain, slope, hid, n2, weights):
    length, wide = o.shape
    span = offset_rows.shape[1]
    tl, width = x.shape
    half = (width // (2 * shards), w.shape[1])
    sum_refs = []
    if len(weights) < 3:
        pieces, _, rows = weights[-1].shape[:3]
        grads = [((shards * 2 * rows, width), BF16, None)]
        row_sems = pltpu.SemaphoreType.DMA((shards,))
        sum_refs = [
            pltpu.SemaphoreType.DMA((2 * shards,)),
            pltpu.VMEM((pieces, 2, rows, width), BF16),
            pltpu.VMEM((shards, rows, width), BF16),
            pltpu.VMEM((shards, rows, width), BF16),
            row_sems, row_sems, row_sems, row_sems,
        ]
    else:
        grads = [((ff, width), BF16, 1), ((width, ff), BF16, 1)]
    return call(
        functools.partial(back_across_kernel, n, shards, heads, dk), "back_across", 9, 85,
        [qkv, o, lse, ext_q, ext_k, offset_rows, parts, do, own, w, n1, x, dx1, gain, slope, hid, n2,
         *map(Raw, weights)],
        [
            ((heads, span), F32, 1),
            ((tl, width), BF16, 1),
            ((tl, width), F32, 1),
            ((tl, width), BF16, 1),
            ((1, width), F32, 1),
            ((tl, width), F32, 1),
            (half, BF16, 1),
            *grads,
        ],
        [
            pltpu.VMEM((length, 3 * wide), BF16),
            pltpu.VMEM(w.shape, BF16),
            pltpu.VMEM((n, tl, width), BF16),
            pltpu.VMEM((n, tl, width), BF16),
            *way_sems(n),
            pltpu.VMEM((width, ff), BF16),
            pltpu.VMEM((ff, width), BF16),
            pltpu.VMEM((n, tl, width), BF16),
            pltpu.VMEM((n * tl, width), BF16),
            load_sems(weights),
            *attend_back_scratch(heads, length, wide, span, n),
            pltpu.VMEM((2, tl // 2, width), BF16),
            pltpu.VMEM((n, tl, width), BF16),
            *way_sems(n),
            *way_sems(n),
            *way_sems(n),
            *reduce_scratch(shards, half),
            *sum_refs,
        ],
        lambda: others("seq", n) + others("dp", shards) + [other_core()],
    )


def back_first_kernel(n, shards, heads, dk, ins, outs, dqkv, dx1, low, g_out, out_ref, got_ref, total_ref,
                      send_p, recv_p, send_w, recv_w, *refs):
    attend_ins, (w, n1, x, gain, half_w) = ins[:13], ins[13:]
    dr, all_g, g_ffn, dx, g_w, g_gain, half_out, all_w, out_last = outs
    reduce = Reduce(shards, g_out, *refs[:7])
    half_g = attend_ins[6].get()
    rows = out_last.ref.shape[0]
    last = half_g.at[pl.ds(half_g.shape[0] - rows, rows)]
    summed = AllSum(n, last, out_last, *refs[7:14])
    half = half_w.get()
    spread = Spread(n, half, chunk_slots(all_w.ref), half.shape[0], (send_w, recv_w))
    all_w.ref[lax.axis_index("seq")] = half[...]
    attend_back_kernel(
        n, heads, dk, False, attend_ins,
        [Held(dqkv), dr, all_g, Held(dx1), g_ffn, Held(g_out), reduce, spread, summed], *refs[14:]
    )
    summed.forward()
    project_back_kernel(
        n, [w, Held(dqkv), n1, x, Held(dx1), gain], [dx, Held(low), g_w, g_gain],
        out_ref, got_ref, total_ref, send_p, recv_p,
    )
    half_out.ref[...] = reduce.result()
    for k in range(1, n):
        spread.arrive(k)
    spread.sent()
    summed.done()


def back_first(n, shards, heads, dk, qkv, o, lse, ext_q, ext_k, offset_rows, half_g, dn2, x1, dy, g_ffn, back, wo,
               w, n1, x, gain, half_w):
    length, wide = o.shape
    span = offset_rows.shape[1]
    tl, width = x.shape
    hd = wo.shape[-2]
    half_out = (hd // (2 * shards), width)
    return call(
        functools.partial(back_first_kernel, n, shards, heads, dk), "back_first", 11, 65,
        [qkv, o, lse, ext_q, ext_k, offset_rows, half_g, dn2, x1, dy, g_ffn, back, Raw(wo), w, n1, x, gain, half_w],
        [
            ((heads, span), F32, 1),
            ((n, half_g.shape[0] - half_out[0], width), BF16, n),
            ((1, width), F32, 1),
            ((tl, width), F32, 1),
            (w.shape, BF16, 1),
            ((1, width), F32, 1),
            (half_out, BF16, 1),
            ((n,) + half_w.shape, BF16, 1),
            (half_out, BF16, 1),
        ],
        [
            pltpu.VMEM((length, 3 * wide), BF16),
            pltpu.VMEM((tl, width), F32),
            pltpu.VMEM((tl, width), BF16),
            pltpu.VMEM((hd, width), BF16),
            pltpu.VMEM((n, tl, width), BF16),
            pltpu.VMEM((n, tl, width), BF16),
            pltpu.VMEM((tl, width), F32),
            *way_sems(n),
            *way_sems(n),
            *reduce_scratch(shards, half_out),
            *sum_scratch(n, *half_out),
            *attend_back_scratch(heads, length, wide, span, n),
            pltpu.VMEM((hd, width), BF16),
            pltpu.VMEM((n, tl, wide), BF16),
            pltpu.SemaphoreType.DMA((n,)),
            *way_sems(n),
        ],
        lambda: others("seq", n) + others("dp", shards) + [other_core()],
    )


def finish_kernel(n, shards, ins, outs, small_got, tile_got, send_g, recv_g, send_w0, recv_w0,
                  send_x, recv_x, send_s, recv_s, send_t, recv_t, *refs):
    g0, w0, out0, w1, small, g1, out1, y0, y1, d0, d1 = ins
    gathered_g, gathered_w0, out0_out, other_g_out, other_w_out, other_out, sums, sections, d_inputs = outs
    all_g, all_w0 = gathered_g.ref, gathered_w0.ref
    other_g, other_w = other_g_out.ref, other_w_out.ref
    me = lax.axis_index("seq")
    core = lax.axis_index("section")
    row = lax.axis_index("dp")
    other = other_core()
    peers = cores_and_rows(shards)

    reduce = Reduce(shards, w0.get(), *refs[:7])
    reduce.start()
    summed = AllSum(n, out0.get(), out0_out, *refs[7:])
    summed.start()
    g0_ref = g0.get()
    spread_g = Spread(n, g0_ref, chunk_slots(all_g), g0_ref.shape[0], (send_g, recv_g))
    spread_g.start()
    small_ref = small.get()
    smalls = [
        push(small_ref.at[peer["section"], peer["dp"]], small_got.at[i], send_s.at[i], recv_s.at[i], peer)
        for i, peer in enumerate(peers)
    ]
    for copy in smalls:
        copy.start()

    def cross(source, target, t, number):
        sem = number * n + t
        return push(source, target.at[t], send_x.at[sem], recv_x.at[sem], other)

    def cross_rows(source, target, number):
        sem = 2 * n + number
        return push(source, target, send_x.at[sem], recv_x.at[sem], other)

    w1_ref, g1_ref, out1_ref, y0_ref, y1_ref, d0_ref, d1_ref = (
        late.get() for late in (w1, g1, out1, y0, y1, d0, d1)
    )

    @pl.when(core == 0)
    def _():
        cross_rows(y1_ref, sections.ref.at[0], 0).start()
        cross_rows(d1_ref, d_inputs.ref.at[0], 1).start()
        cross_rows(out1_ref, other_out.ref, 2).start()
        for t in range(n):
            cross(w1_ref.at[t], other_w, t, 1).start()
            cross(g1_ref.at[t], other_g, t, 0).start()
        sections.ref[0] = y0_ref[...]
        d_inputs.ref[0] = d0_ref[...]

    @pl.when(core == 1)
    def _():
        cross_rows(y0_ref, sections.ref.at[1], 0).start()
        cross_rows(d0_ref, d_inputs.ref.at[1], 1).start()
        cross(g0_ref, other_g, me, 0).start()
        sections.ref[1] = y1_ref[...]
        d_inputs.ref[1] = d1_ref[...]

    all_g[me] = g0_ref[...]
    gathered_g.flush(me)
    reduce.forward()
    summed.relay()

    tile = small_ref[core, row]
    for i, copy in enumerate(smalls):
        copy.wait()
        tile += small_got[i]
    tile_got[0] = tile
    tiles = []
    for k in range(1, n):
        copy = push(tile_got.at[0], tile_got.at[k], send_t.at[k], recv_t.at[k], lax.rem(me + k, n))
        copy.start()
        tiles.append(copy)

    spread_g.forward()
    summed.share()
    all_w0[me] = reduce.result()
    gathered_w0.flush(me)
    spread_w0 = Spread(n, all_w0.at[me], chunk_slots(all_w0), all_w0.shape[1], (send_w0, recv_w0))
    spread_w0.start()
    summed.forward()
    spread_w0.forward()

    @pl.when(core == 1)
    def _():
        cross(all_w0.at[me], other_w, me, 1).start()

    for k in range(1, n):
        source = spread_g.order[k]
        spread_g.arrive(k)
        gathered_g.flush(source)

        @pl.when(core == 1)
        def _():
            cross(all_g.at[source], other_g, source, 0).start()

    summed.done()

    @pl.when(core == 1)
    def _():
        cross_rows(out0_out.ref, other_out.ref, 2).start()

    total = tile
    for k in range(1, n):
        tiles[k - 1].wait()
        total += tile_got[k]
    line = lax.broadcasted_iota(jnp.int32, tile.shape, 0)
    sums.ref[...] = jnp.where(line < 2, total, tile)
    for number, (source, target) in enumerate(((y0_ref, sections), (d0_ref, d_inputs))):
        cross_rows(source, target.ref.at[0], number).wait()
        target.flush()
    for k in range(1, n):
        source = spread_g.order[k]
        spread_w0.arrive(k)
        gathered_w0.flush(source)

        @pl.when(core == 1)
        def _():
            cross(all_w0.at[source], other_w, source, 1).start()

    cross_rows(out0_out.ref, other_out.ref, 2).wait()
    other_out.flush()
    for t in [me] + spread_g.order[1:]:
        cross(g0_ref, other_g, t, 0).wait()
        other_g_out.flush(t)
    for t in [me] + spread_g.order[1:]:
        cross(all_w0.at[0], other_w, t, 1).wait()
        other_w_out.flush(t)
    for spread in (spread_g, spread_w0):
        spread.sent()


def finish(n, shards, small, g0, out0, w0, g1, out1, w1, y0, y1, d0, d1):
    sems = pltpu.SemaphoreType.DMA((n,))
    cross_sems = pltpu.SemaphoreType.DMA((2 * n + 3,))
    small_sems = pltpu.SemaphoreType.DMA((2 * shards - 1,))
    tile = small.shape[2:]
    half = w1.shape[1:]
    gathered_w = ((n,) + half, BF16, n)
    return call(
        functools.partial(finish_kernel, n, shards), "finish", 8, 48,
        [g0, w0, out0, w1, small, g1, out1, y0, y1, d0, d1],
        [
            (g1.shape, BF16, n),
            gathered_w,
            (out0.shape, BF16, 1),
            (g1.shape, BF16, n),
            gathered_w,
            (out0.shape, BF16, 1),
            (tile, F32, 1),
            ((2,) + y0.shape, BF16, 1),
            ((2,) + d0.shape, F32, 1),
        ],
        [
            pltpu.VMEM((2 * shards - 1,) + tile, F32),
            pltpu.VMEM((n,) + tile, F32),
            *way_sems(n),
            *way_sems(n),
            cross_sems, cross_sems, small_sems, small_sems, sems, sems,
            *reduce_scratch(shards, half),
            *sum_scratch(n, *out0.shape),
        ],
        lambda: cores_and_rows(shards) + others("seq", n),
    )


def assemble_kernel(n, shards, ins, outs):
    g0, other_g, g1, w0, other_w, w1, out0, other_out, out1 = ins
    down, up, out, *qkv = outs
    first = lax.axis_index("section") == 0
    quarter = other_w.ref.shape[1]
    hw = other_w.ref.shape[2] // 3
    kept = 2 * quarter
    for t in range(n):
        for late in ins[:6]:
            late.get(t)
        for half in range(2):
            if half == 0:
                g = jnp.where(first, g0.ref[t], other_g.ref[t]).astype(F32)
                w = jnp.where(first, w0.ref[t], other_w.ref[t]).astype(F32)
            else:
                g = jnp.where(first, other_g.ref[t], g1.ref[t]).astype(F32)
                w = jnp.where(first, other_w.ref[t], w1.ref[t]).astype(F32)
            rows = slice(half * quarter, (half + 1) * quarter)
            down.ref[t * kept + half * quarter : t * kept + (half + 1) * quarter, :] = g[:quarter]
            for z in range(shards):
                at = (z * n + t) * kept
                up.ref[rows, at : at + kept] = g[quarter : 2 * quarter, z * kept : (z + 1) * kept]
            for i, grad in enumerate(qkv):
                grad.ref[rows, t * hw : (t + 1) * hw] = w[:, i * hw : (i + 1) * hw]
        down.flush(pl.ds(t * kept, kept))
        for z in range(shards):
            up.flush(slice(None), pl.ds((z * n + t) * kept, kept))
        for grad in qkv:
            grad.flush(slice(None), pl.ds(t * hw, hw))
    out.ref[:quarter, :] = jnp.where(first, out0.get()[...], other_out.get()[...]).astype(F32)
    out.ref[quarter:, :] = jnp.where(first, other_out.ref[...], out1.get()[...]).astype(F32)


def assemble(n, shards, g0, g1, other_g, w0, w1, other_w, out0, out1, other_out):
    quarter = other_w.shape[1]
    model = other_g.shape[2]
    hw = other_w.shape[2] // 3
    kept = 2 * quarter
    return call(
        functools.partial(assemble_kernel, n, shards), "assemble", None, 8,
        [Slots(array) for array in (g0, other_g, g1, w0, other_w, w1)] + [out0, other_out, out1],
        [
            ((n * kept, model), F32, n),
            ((2 * quarter, n * shards * kept), F32, n * shards),
            ((2 * quarter, model), F32, 1),
        ]
        + [((2 * quarter, n * hw), F32, n)] * 3,
        [],
    )


def swapped(value):
    return lax.ppermute(value, "section", [(0, 1), (1, 0)])


def body(inputs, cotangent, segments, buckets, query_weight, key_weight, value_weight, out_weight,
         up_weight, down_weight, attn_gain, ffn_gain, bias_table):
    first = lax.axis_index("section") == 0
    turn = lax.axis_index("seq")
    n = lax.axis_size("seq")
    shards = lax.axis_size("dp")
    depth, width = query_weight.shape[1:]
    ff = up_weight.shape[2]
    heads = bias_table.shape[2]
    hw = width // n
    dk = hw // heads
    kept = down_weight.shape[1] // n
    hidden = ff // n
    model = inputs.shape[-1]
    quarter = model // (2 * shards)
    packed = hidden == model == width

    x_in = jnp.where(first, inputs[0, 0], inputs[1, 0])
    d_out = jnp.where(first, cotangent[0, 0], cotangent[1, 0])
    seg = jnp.where(first, segments[0, 0], segments[1, 0])

    wide = max(hw, LANES)

    def pad(value):
        return value if hw == wide else jnp.pad(value, [(0, 0)] * (value.ndim - 1) + [(0, wide - hw)])

    def columns(weight):
        return pad(lax.dynamic_slice_in_dim(weight[0], turn * hw, hw, axis=1))

    own_qkv = jnp.concatenate([columns(query_weight), columns(key_weight), columns(value_weight)], axis=1)
    own_up = jnp.concatenate(
        [
            lax.dynamic_slice_in_dim(up_weight[0], (z * n + turn) * kept, kept, axis=1)
            for z in range(shards)
        ],
        axis=1,
    )
    own_down = lax.dynamic_slice_in_dim(down_weight[0], turn * kept, kept, axis=0)
    table = bias_table[0]

    def halves(own):
        rows = own.shape[0] // 2
        low, high = own[:rows], own[rows:]
        other = swapped(jnp.where(first, high, low))
        return jnp.where(first, low, other), jnp.where(first, other, high)

    def gathered(piece):
        return lax.all_gather(piece, ("dp", "section"), axis=0, tiled=True)

    qkv_halves = halves(own_qkv)
    out_halves = halves(out_weight[0])
    up_halves = halves(own_up)
    down_halves = halves(own_down)
    cols = model // n
    out_cols = lax.dynamic_slice_in_dim(out_halves[0], turn * cols, cols, axis=1)
    first_qkv = gathered(qkv_halves[0])

    def packed_gather(pieces):
        return lax.all_gather(jnp.stack(pieces), ("dp", "section"), axis=0, tiled=False)

    if packed:
        mix_weights = [[packed_gather((up_halves[0], down_halves[0]))]]
    else:
        mix_weights = [[gathered(up_halves[0]), gathered(down_halves[0])]]
    second_qkv = gathered(qkv_halves[1])
    pieces = (out_halves[1], up_halves[1], down_halves[1])
    mix_weights.append([packed_gather(pieces)] if packed else [gathered(piece) for piece in pieces])
    other_table = swapped(table)
    tables = (jnp.where(first, table, other_table), jnp.where(first, other_table, table))

    gains = jnp.pad(jnp.stack([attn_gain[0], ffn_gain[0]]), ((0, 14), (0, 0)))
    first_n1, out_cols, *gain_rows = start(n, shards, x_in, gains, out_cols)
    out_cols = out_cols.reshape(width, cols)

    bucket_count = table.shape[0]
    onehot = (buckets[None, :] == jnp.arange(bucket_count, dtype=jnp.int32)[:, None]).astype(F32)
    offset_rows = [
        lax.dot_general(
            t.astype(F32), onehot, (((0,), (0,)), ((), ())), precision=HIGH, preferred_element_type=F32
        )
        for t in tables
    ]

    lanes = jnp.arange(LANES, dtype=jnp.int32) % 64
    same = seg[:, None] == lanes[None, :]
    ext_q = jnp.where((lanes < 8)[None, :] & ~same, NEG, 0.0).astype(BF16)
    ext_k = jnp.where((lanes < 8)[None, :] & same, 1.0, 0.0).astype(BF16)

    def scattered(gr):
        if not packed:
            gr = [jnp.concatenate([part.reshape(2 * shards, -1, model) for part in gr], axis=1)]
        return lax.psum_scatter(
            gr[0].reshape(-1, model), ("dp", "section"), scatter_dimension=0, tiled=True
        )

    qkv0 = jnp.dot(first_n1, first_qkv, preferred_element_type=F32).astype(BF16)
    o0, lse0, back0, out_all = attend(n, heads, dk, qkv0, ext_q, ext_k, offset_rows[0], out_cols)
    mix_weights[0].insert(0, out_all if packed else out_all.transpose(1, 0, 2).reshape(width, model))
    y0, x1, n2, slope, hid = mix(n, hw, hidden, x_in, gain_rows[1], back0, mix_weights[0])
    n1, qkv1 = norm_gather(n, y0, gain_rows[2], second_qkv)
    o1, lse1, back1, d_all = attend(n, heads, dk, qkv1, ext_q, ext_k, offset_rows[1], d_out)
    y_parts, y_own, dx1, do, gr_ffn1, *gr = turn_round(
        n, hw, hidden, y0, gain_rows[3], back1, mix_weights[1], d_all.reshape(-1, model)
    )
    half1 = scattered(gr)
    d_rows1, y1, d_in1, dy, gr_attn1, dn2, half_w1, *gr = back_across(
        n, shards, heads, dk, hidden, qkv1, o1, lse1, ext_q, ext_k, offset_rows[1], y_parts, pad(do), y_own,
        second_qkv, n1, y0, dx1, gain_rows[2], slope, hid, n2, mix_weights[0],
    )
    if packed:
        half0 = lax.psum_scatter(gr[0], "dp", scatter_dimension=0, tiled=True)
    else:
        half0 = scattered(gr)
    d_rows0, all_g1, gr_ffn0, d_in0, w_grad0, gr_attn0, half_out, all_w1, out1 = back_first(
        n, shards, heads, dk, qkv0, o0, lse0, ext_q, ext_k, offset_rows[0], half1,
        dn2, x1, dy, gain_rows[1], back0, mix_weights[0][0],
        first_qkv, first_n1, x_in, gain_rows[0], half_w1,
    )

    cut = model // shards
    small = []
    for gr_attn, gr_ffn, d_rows in ((gr_attn0, gr_ffn0, d_rows0), (gr_attn1, gr_ffn1, d_rows1)):
        gr_table = lax.dot_general(
            onehot, d_rows, (((1,), (1,)), ((), ())), precision=HIGH, preferred_element_type=F32
        )
        flat = gr_table.reshape(shards, -1)
        flat = jnp.pad(flat, ((0, 0), (0, cut - flat.shape[1])))
        tile = jnp.stack([gr_attn.reshape(shards, cut), gr_ffn.reshape(shards, cut), flat], axis=1)
        small.append(jnp.pad(tile, ((0, 0), (0, 5), (0, 0))))
    all_g0, all_w0, out0, other_g, other_w, other_out, sums, section_outputs, input_grads = finish(
        n, shards, jnp.stack(small), half0, half_out, w_grad0, all_g1, out1, all_w1, y0, y1, d_in0, d_in1
    )
    section_outputs, input_grads = section_outputs[None, :, None], input_grads[None, :, None]
    g_attn, g_ffn = sums[0:1], sums[1:2]
    g_table = sums[2, : bucket_count // shards * heads].reshape(1, bucket_count // shards, heads)

    if packed:
        g_down, g_up, g_out, g_query, g_key, g_value = (
            part[None] for part in assemble(
                n, shards, all_g0, all_g1, other_g, all_w0, all_w1, other_w, out0, out1, other_out
            )
        )
    else:
        low, high = jnp.where(first, all_g0, other_g), jnp.where(first, other_g, all_g1)
        sizes = [kept // 2, quarter * hidden // model]
        cuts = [sum(sizes[:i]) for i in range(3)]

        def joined(index):
            return jnp.stack([part[:, cuts[index] : cuts[index + 1]] for part in (low, high)], axis=1)

        g_down = joined(0).astype(F32).reshape(1, n * kept, model)
        whole = joined(1).reshape(n, depth, shards, kept)
        g_up = whole.transpose(1, 2, 0, 3).reshape(1, depth, ff).astype(F32)
        low, high = jnp.where(first, out0, other_out), jnp.where(first, other_out, out1)
        g_out = jnp.concatenate([low, high], axis=0).astype(F32)[None]
        low, high = jnp.where(first, all_w0, other_w), jnp.where(first, other_w, all_w1)
        whole = jnp.stack([low, high], axis=1).reshape(n, depth, 3, wide)[..., :hw]
        g_query, g_key, g_value = (
            whole[:, :, i].transpose(1, 0, 2).reshape(1, depth, width).astype(F32) for i in range(3)
        )

    return (
        section_outputs,
        input_grads,
        g_query,
        g_key,
        g_value,
        g_out,
        g_up,
        g_down,
        g_attn,
        g_ffn,
        g_table,
    )


def solution(mesh):
    return jax.shard_map(
        body,
        mesh=mesh,
        in_specs=(
            P(None, "dp", "seq", None),
            P(None, "dp", "seq", None),
            P(None, "dp", None),
            P(),
            P("section", "dp", None),
            P("section", "dp", None),
            P("section", "dp", None),
            P("section", "dp", None),
            P("section", "dp", None),
            P("section", "dp", None),
            P("section", "dp"),
            P("section", "dp"),
            P("section", None, "seq"),
        ),
        out_specs=(
            P("section", None, "dp", "seq", None),
            P("section", None, "dp", "seq", None),
            P("section", "dp", None),
            P("section", "dp", None),
            P("section", "dp", None),
            P("section", "dp", None),
            P("section", "dp", None),
            P("section", "dp", None),
            P("section", "dp"),
            P("section", "dp"),
            P("section", "dp", "seq"),
        ),
        check_vma=False,
    )
```

```python
import functools
import math

import jax
import jax.numpy as jnp
from jax import lax
from jax.experimental import pallas as pl
from jax.experimental.pallas import tpu as pltpu
from jax.sharding import PartitionSpec as P

EPSILON = 1e-06
NEG = -1e30
HIGH = lax.Precision.HIGHEST
MESH = pl.DeviceIdType.MESH
F32 = jnp.float32
BF16 = jnp.bfloat16
LANES = 128
QB = 256
VMEM_BYTES = 60 << 20

AWAY = pl.BlockSpec(memory_space=pl.ANY)


def mm(left, right):
    return jnp.dot(left, right, preferred_element_type=F32)


def mm_nt(left, right):
    return lax.dot_general(left, right, (((1,), (1,)), ((), ())), preferred_element_type=F32)


def mm_tn(left, right):
    return lax.dot_general(left, right, (((0,), (0,)), ((), ())), preferred_element_type=F32)


def inverse_rms(rows):
    return lax.rsqrt(jnp.mean(rows * rows, axis=-1, keepdims=True) + EPSILON)


def aligned(start, size):
    return pl.ds(pl.multiple_of(start, size), size)


def signal_and_wait(peers):
    barrier = pltpu.get_barrier_semaphore()
    for peer in peers:
        pl.semaphore_signal(barrier, inc=1, device_id=peer, device_id_type=MESH)
    pl.semaphore_wait(barrier, len(peers))


def others(axis, n):
    me = lax.axis_index(axis)
    return [{axis: lax.rem(me + k, n)} for k in range(1, n)]


def other_core():
    return {"section": 1 - lax.axis_index("section")}


def cores_and_rows(shards):
    core, row = lax.axis_index("section"), lax.axis_index("dp")
    return [
        {"section": lax.rem(core + i, 2), "dp": lax.rem(row + j, shards)}
        for i in range(2)
        for j in range(shards)
        if i + j
    ]


def near(n):
    me = lax.axis_index("seq")
    return [{"seq": peer} for peer in (square(me) if n == 4 else ring(n, me))]


def square(me):
    return me + 1 - 2 * lax.rem(me, 2), lax.rem(me + 2, 4)


def ring(n, me):
    return [lax.rem(me + k, n) for k in range(1, n)]


def push(src, dst, send_sem, recv_sem, peer):
    return pltpu.make_async_remote_copy(
        src_ref=src,
        dst_ref=dst,
        send_sem=send_sem,
        recv_sem=recv_sem,
        device_id=peer if isinstance(peer, dict) else {"seq": peer},
        device_id_type=MESH,
    )


def sources(n):
    me = lax.axis_index("seq")
    if n == 4:
        along_x, along_y = square(me)
        return [me, along_x, along_y, square(along_y)[0]]
    return [lax.rem(me + n - k, n) for k in range(n)]


class Spread:
    def __init__(self, n, source, slot, rows, sems):
        self.n = n
        me = lax.axis_index("seq")
        self.order = sources(n)
        send, recv = sems
        if n != 4:
            self.copies = [
                push(source, slot(me, 0, rows), send.at[k], recv.at[k], peer)
                for k, peer in enumerate(ring(n, me), 1)
            ]
            return
        along_x, along_y = square(me)
        half = rows // 2

        def copy(number, owner, part, peer):
            here = source.at[pl.ds(part * half, half)] if owner is me else slot(owner, part * half, half)
            return push(here, slot(owner, part * half, half), send.at[number], recv.at[number], peer)

        self.copies = [
            copy(0, me, 0, along_x),
            copy(1, me, 1, along_y),
            copy(2, me, 1, along_x),
            copy(3, me, 0, along_y),
            copy(4, along_x, 0, along_y),
            copy(5, along_y, 1, along_x),
        ]

    def start(self):
        self.start_some(True)
        self.start_some(False)

    def start_some(self, first):
        if self.n == 4:
            for copy in self.copies[:2] if first else self.copies[2:4]:
                copy.start()
        elif first:
            for copy in self.copies:
                copy.start()

    def forward(self):
        if self.n == 4:
            for first, second in ((0, 4), (1, 5)):
                self.copies[first].wait_recv()
                self.copies[second].start()

    def arrive(self, k):
        if self.n == 4:
            for number in ((), (2,), (3,), (4, 5))[k]:
                self.copies[number].wait_recv()
        else:
            self.copies[k - 1].wait_recv()

    def sent(self):
        for copy in self.copies:
            copy.wait_send()

    def all(self):
        self.start()
        self.forward()
        for k in range(1, self.n):
            self.arrive(k)
        self.sent()


class Collect:
    def __init__(self, n, out, got, sems, mid=None):
        self.n = n
        self.out, self.got, self.mid = out, got, mid
        self.half = out.shape[1] // 2
        me = lax.axis_index("seq")
        self.order = sources(n)
        send, recv = sems
        if n != 4:
            self.copies = [
                push(out.at[k], got.at[k], send.at[k], recv.at[k], self.order[k]) for k in range(1, n)
            ]
            return
        along_x, along_y = square(me)

        def copy(number, chunk, part, peer):
            return push(self.piece(out, chunk, part), self.landing(number), send.at[number], recv.at[number], peer)

        self.copies = [
            copy(0, 1, 0, along_x),
            copy(1, 2, 1, along_y),
            copy(2, 3, 0, along_x),
            copy(3, 3, 1, along_y),
        ]
        for number, chunk, part, peer in ((4, 2, 0, along_y), (5, 1, 1, along_x)):
            source = self.piece(out, chunk, part) if mid is None else mid.at[number - 4]
            self.copies.append(
                push(source, self.landing(number), send.at[number], recv.at[number], peer)
            )

    def piece(self, ref, chunk, part):
        return ref.at[chunk, pl.ds(part * self.half, self.half)]

    def landing(self, number):
        return self.piece(self.got, number // 2, number % 2)

    def give(self, k, value):
        self.out[k] = value.astype(BF16)
        self.start(k)

    def start(self, k):
        if self.n == 4:
            for number in ((), (0,), (1,), (2, 3))[k]:
                self.copies[number].start()
        else:
            self.copies[k - 1].start()

    def relay(self):
        if self.n == 4:
            for number, chunk, part in ((2, 2, 0), (3, 1, 1)):
                self.copies[number].wait_recv()
                mine = self.piece(self.out, chunk, part)
                summed = (mine[...].astype(F32) + self.landing(number)[...].astype(F32)).astype(BF16)
                if self.mid is None:
                    mine[...] = summed
                else:
                    self.mid[number - 2] = summed
                self.copies[number + 2].start()

    def add_to(self, total):
        if self.n == 4:
            for number, part in ((0, 0), (1, 1), (4, 0), (5, 1)):
                self.copies[number].wait_recv()
                total[pl.ds(part * self.half, self.half)] += self.landing(number)[...].astype(F32)
        else:
            for k in range(1, self.n):
                self.copies[k - 1].wait_recv()
                total[...] += self.got[k].astype(F32)

    def sent(self):
        for copy in self.copies:
            copy.wait_send()


def way_sems(n):
    count = max(n, 6)
    return [pltpu.SemaphoreType.DMA((count,)), pltpu.SemaphoreType.DMA((count,))]


def row_slots(ref, tl):
    return lambda owner, first, rows: ref.at[pl.ds(pl.multiple_of(owner * tl + first, rows), rows)]


def chunk_slots(ref):
    return lambda owner, first, rows: ref.at[owner, pl.ds(first, rows)]


def cost(microseconds):
    return pl.CostEstimate(flops=int(microseconds * 1e9), bytes_accessed=0, transcendentals=0)


class Raw:
    def __init__(self, array):
        self.array = array


class Slots:
    def __init__(self, array):
        self.array = array


class Rows:
    def __init__(self, *arrays):
        self.array = arrays


class Late:
    def __init__(self, pairs, ref, sems):
        self.ref = ref
        self.copies = [pltpu.make_async_copy(src, dst, sems.at[i]) for i, (src, dst) in enumerate(pairs)]
        for copy in self.copies:
            copy.start()
        self.waiting = [True] * len(self.copies)

    def get(self, slot=None):
        for i, copy in enumerate(self.copies):
            if self.waiting[i] and (slot is None or slot == i):
                copy.wait()
                self.waiting[i] = False
        return self.ref


class Early:
    def __init__(self, target, ref, sems):
        self.target, self.ref, self.sems = target, ref, sems
        self.copies = []

    def flush(self, *part):
        src, dst = (self.ref.at[part], self.target.at[part]) if part else (self.ref, self.target)
        copy = pltpu.make_async_copy(src, dst, self.sems.at[len(self.copies)])
        copy.start()
        self.copies.append(copy)

    def get(self):
        return self.ref

    def done(self):
        if not self.copies:
            self.flush()
        for copy in self.copies:
            copy.wait()


class Held:
    def __init__(self, ref):
        self.ref = ref

    def get(self, slot=None):
        return self.ref

    def flush(self, *part):
        pass


class Reduce:
    def __init__(self, shards, value, got_c, sent_z, got_z, send_c, recv_c, send_z, recv_z):
        self.value, self.got_c, self.got_z, self.sent_z = value, got_c, got_z, sent_z
        self.row, self.core = lax.axis_index("dp"), lax.axis_index("section")
        self.rows = got_c.shape[1]
        self.shards = shards
        self.crossed = [
            push(
                value.at[self.part(z, 1 - self.core)],
                got_c.at[z], send_c.at[z], recv_c.at[z], {"section": 1 - self.core},
            )
            for z in range(shards)
        ]
        self.along = [
            push(
                sent_z.at[k], got_z.at[k], send_z.at[k], recv_z.at[k], {"dp": lax.rem(self.row + k, shards)}
            )
            for k in range(1, shards)
        ]

    def part(self, z, core):
        return aligned((2 * z + core) * self.rows, self.rows)

    def both(self, z):
        return self.value[self.part(z, self.core), :].astype(F32) + self.got_c[z].astype(F32)

    def start(self):
        for copy in self.crossed:
            copy.start()

    def forward(self):
        for copy in self.crossed:
            copy.wait()
        for k in range(1, self.shards):
            self.sent_z[k] = self.both(lax.rem(self.row + k, self.shards)).astype(BF16)
            self.along[k - 1].start()

    def result(self):
        half = self.both(self.row)
        for k in range(1, self.shards):
            self.along[k - 1].wait()
            half += self.got_z[k].astype(F32)
        return half.astype(BF16)


class Across:
    def __init__(self, shards, block, got, send, recv):
        self.shards, self.block, self.got = shards, block, got
        self.core = lax.axis_index("section")
        self.copies = [
            push(block(z, 1 - self.core), got.at[z], send.at[z], recv.at[z], {"section": 1 - self.core})
            for z in range(shards)
        ]

    def start(self):
        for copy in self.copies:
            copy.start()

    def sum(self, z):
        self.copies[z].wait()
        return (self.block(z, self.core)[...].astype(F32) + self.got[z].astype(F32)).astype(BF16)


class Along:
    def __init__(self, shards, value, got, send, recv):
        self.shards, self.value, self.got = shards, value, got
        self.row = lax.axis_index("dp")
        self.copies = []
        for k in range(1, shards):
            peer = lax.rem(self.row + k, shards)
            self.copies.append(push(value.at[peer], got.at[k], send.at[k], recv.at[k], {"dp": peer}))

    def start(self):
        for copy in self.copies:
            copy.start()

    def result(self):
        total = self.value[self.row].astype(F32)
        for k, copy in enumerate(self.copies, 1):
            copy.wait()
            total += self.got[k].astype(F32)
        return total.astype(BF16)


class AllSum:
    def __init__(self, n, value, out, c_out, c_got, total, send_c, recv_c, send_s, recv_s):
        self.n, self.value, self.out, self.c_got, self.total = n, value, out, c_got, total
        self.me = lax.axis_index("seq")
        self.rows = total.shape[0]
        self.order = sources(n)
        if n == 4:
            self.collect = Collect(n, c_out, c_got, (send_c, recv_c))
            mine = out.ref.at[self.part(self.me)]
            self.spread = Spread(n, mine, row_slots(out.ref, self.rows), self.rows, (send_s, recv_s))
        else:
            self.spread = Spread(n, value, chunk_slots(c_got), self.rows, (send_s, recv_s))

    def part(self, owner):
        return aligned(owner * self.rows, self.rows)

    def start(self):
        if self.n == 4:
            for k in (3, 1, 2):
                self.collect.give(k, self.value[self.part(self.order[k]), :])
            self.total[...] = self.value[self.part(self.me), :].astype(F32)
        else:
            self.spread.start()

    def relay(self):
        if self.n == 4:
            self.collect.relay()

    def share(self):
        if self.n == 4:
            self.collect.add_to(self.total)
            self.out.ref[self.part(self.me), :] = self.total[...].astype(BF16)
            self.spread.start()

    def forward(self):
        self.spread.forward()

    def done(self):
        for k in range(1, self.n):
            self.spread.arrive(k)
        if self.n == 4:
            self.collect.sent()
        else:
            self.total[...] = self.value[...].astype(F32)
            for k in range(1, self.n):
                self.total[...] += self.c_got[self.order[k]].astype(F32)
            self.out.ref[...] = self.total[...].astype(BF16)
        self.spread.sent()
        self.out.flush()


def sum_scratch(n, rows, width):
    if n == 4:
        rows //= n
    landing = pltpu.VMEM((n, rows, width), BF16)
    return [landing, landing, pltpu.VMEM((rows, width), F32), *way_sems(n), *way_sems(n)]


def reduce_scratch(shards, half):
    return [pltpu.VMEM((shards,) + half, BF16)] * 3 + [pltpu.SemaphoreType.DMA((shards,))] * 4


def call(kernel, name, collective_id, microseconds, operands, outs, scratch, peers=None):
    arrays, buffers, in_sems = [], [], []
    for operand in operands:
        array = operand.array if isinstance(operand, (Raw, Slots, Rows)) else operand
        arrays += array if isinstance(operand, Rows) else [array]
        if not isinstance(operand, Raw):
            copies = 1
            if isinstance(operand, Rows):
                dims = (sum(part.shape[0] for part in array),) + array[0].shape[1:]
                copies, dtype = len(array), array[0].dtype
            else:
                dims, dtype = array.shape, array.dtype
            if isinstance(operand, Slots):
                copies = dims[0]
            buffers.append(pltpu.VMEM(dims, dtype))
            in_sems.append(pltpu.SemaphoreType.DMA((copies,)))
    out_buffers = [pltpu.VMEM(dims, dtype) for dims, dtype, flushes in outs if flushes]
    out_sems = [pltpu.SemaphoreType.DMA((flushes,)) for _, _, flushes in outs if flushes]

    def body(*refs):
        refs = list(refs)

        def take(count):
            taken = refs[:count]
            del refs[:count]
            return taken

        sources, targets = take(len(arrays)), take(len(outs))
        staged, results = take(len(buffers)), take(len(out_buffers))
        staged_sems, result_sems = take(len(buffers)), take(len(out_buffers))
        ins, at = [], 0
        for operand in operands:
            source = sources.pop(0)
            if isinstance(operand, Raw):
                ins.append(source)
                continue
            ref = staged[at]
            if isinstance(operand, Rows):
                pairs, first = [(source, ref.at[pl.ds(0, source.shape[0])])], source.shape[0]
                for _ in operand.array[1:]:
                    source = sources.pop(0)
                    pairs.append((source, ref.at[pl.ds(first, source.shape[0])]))
                    first += source.shape[0]
            elif isinstance(operand, Slots):
                pairs = [(source.at[i], ref.at[i]) for i in range(ref.shape[0])]
            else:
                pairs = [(source, ref)]
            ins.append(Late(pairs, ref, staged_sems[at]))
            at += 1
        early = [
            Early(target, results.pop(0), result_sems.pop(0)) if flushes else target
            for target, (_, _, flushes) in zip(targets, outs)
        ]
        if peers is not None:
            signal_and_wait(peers())
        kernel(ins, early, *refs)
        for late in ins:
            if isinstance(late, Late):
                late.get()
        for result in early:
            if isinstance(result, Early):
                result.done()

    return pl.pallas_call(
        body,
        out_shape=[jax.ShapeDtypeStruct(dims, dtype) for dims, dtype, _ in outs],
        in_specs=[AWAY] * len(arrays),
        out_specs=[AWAY] * len(outs),
        scratch_shapes=[*buffers, *out_buffers, *in_sems, *out_sems, *scratch],
        compiler_params=pltpu.CompilerParams(
            collective_id=collective_id,
            has_side_effects=collective_id is not None,
            vmem_limit_bytes=VMEM_BYTES,
        ),
        cost_estimate=cost(microseconds),
        name=name,
    )(*arrays)


def start_kernel(n, shards, ins, outs, all_ref, send, recv, send_g, recv_g, send_z, recv_z, send_x, recv_x):
    x, own, piece = ins
    out, weight, *gains = outs
    tl = x.ref.shape[0]
    cut = own.ref.shape[1]
    me = lax.axis_index("seq")
    layer = lax.axis_index("section")
    row = lax.axis_index("dp")
    mine = aligned(me * tl, tl)
    peers = cores_and_rows(shards)
    own_ref = own.get()
    copies = [
        push(own_ref, all_ref.at[layer, row], send_g.at[i], recv_g.at[i], peer)
        for i, peer in enumerate(peers)
    ]
    for copy in copies:
        copy.start()
    all_ref[layer, row] = own_ref[...]
    weight.ref[row, layer] = piece.get()[...]

    def cross(z, core):
        ref = weight.ref.at[z, core]
        return push(ref, ref, send_x.at[z], recv_x.at[z], {"section": 1 - layer})

    rows = x.get()[...].astype(F32)
    inv = inverse_rms(rows)
    for copy in copies:
        copy.wait()
    for z in range(shards):
        part = slice(z * cut, (z + 1) * cut)
        for i, gain in enumerate(gains):
            gain.ref[:, part] = all_ref[i // 2, z, i % 2 : i % 2 + 1, :].astype(F32)
    out.ref[mine] = (rows * inv * gains[0].ref[...]).astype(BF16)
    spread = Spread(n, out.ref.at[mine], row_slots(out.ref, tl), tl, (send, recv))
    spread.start()
    out.flush(mine)
    for gain in gains:
        gain.flush()
    spread.forward()
    along = []
    for k in range(1, shards):
        ref = weight.ref.at[row, layer]
        along.append(push(ref, ref, send_z.at[k], recv_z.at[k], {"dp": lax.rem(row + k, shards)}))
        along[-1].start()
    cross(row, layer).start()
    for k in range(1, n):
        spread.arrive(k)
        out.flush(aligned(spread.order[k] * tl, tl))
    for k in range(1, shards):
        along[k - 1].wait()
        cross(lax.rem(row + shards - k, shards), layer).start()
    for z in range(shards):
        cross(z, 1 - layer).wait()
        weight.flush(z)
    spread.sent()


def start(n, shards, x, gains, piece):
    tl, width = x.shape
    small_sems = pltpu.SemaphoreType.DMA((2 * shards - 1,))
    row_sems = pltpu.SemaphoreType.DMA((shards,))
    return call(
        functools.partial(start_kernel, n, shards), "start", 6, 28,
        [x, gains, piece],
        [((n * tl, width), BF16, n), ((shards, 2) + piece.shape, BF16, shards)] + [((1, width), F32, 1)] * 4,
        [
            pltpu.VMEM((2, shards) + gains.shape, BF16),
            *way_sems(n),
            small_sems,
            small_sems,
            row_sems,
            row_sems,
            row_sems,
            row_sems,
        ],
        lambda: cores_and_rows(shards) + near(n),
    )


def gather_kernel(n, ins, outs, send, recv):
    x, gain, w = ins
    out, qkv = outs
    tl = x.ref.shape[0]
    mine = aligned(lax.axis_index("seq") * tl, tl)
    rows = x.get()[...].astype(F32)
    out.ref[mine] = (rows * inverse_rms(rows) * gain.get()[...]).astype(BF16)
    spread = Spread(n, out.ref.at[mine], row_slots(out.ref, tl), tl, (send, recv))
    spread.start()
    w.get()
    for k in range(n):
        where = aligned(spread.order[k] * tl, tl)
        if k:
            spread.arrive(k)
        out.flush(where)
        qkv.ref[where] = mm(out.ref[where], w.ref[...]).astype(BF16)
        qkv.flush(where)
        if not k:
            spread.forward()
    spread.sent()


def norm_gather(n, x, gain, w):
    tl, width = x.shape
    return call(
        functools.partial(gather_kernel, n), "norm_gather", 0, 20,
        [x, gain, w],
        [((n * tl, width), BF16, n), ((n * tl, w.shape[1]), BF16, n)],
        way_sems(n),
        lambda: near(n),
    )


def toeplitz_rows(offset_row):
    spread = jnp.broadcast_to(offset_row, (LANES, offset_row.shape[1]))
    return pltpu.roll(spread, 0, 1, stride=1, stride_axis=0)


def attend_kernel(n, heads, dk, ins, outs, bias_ref, kt_ref, qa_ref, send, recv, send_d, recv_d):
    chunk, qkv, eq, ek, rows = ins
    o, lse_out, back, chunks = outs
    o_ref, lse_ref, back_ref, chunks_ref = o.ref, lse_out.ref, back.ref, chunks.ref
    length, wide = o_ref.shape
    tl = length // n
    group = QB // tl
    blocks = length // QB
    me = lax.axis_index("seq")
    mine = aligned(me * tl, tl)
    chunk_ref = chunk.get()
    spread = Spread(n, chunk_ref, chunk_slots(chunks_ref), chunk_ref.shape[0], (send_d, recv_d))
    spread.start()
    chunks_ref[me] = chunk_ref[...]
    chunks.flush(me)
    qkv_ref, eq_ref, ek_ref, rows_ref = qkv.get(), eq.get(), ek.get(), rows.get()
    lane = lax.broadcasted_iota(jnp.int32, (length, LANES), 1)
    lane_q = lax.broadcasted_iota(jnp.int32, (LANES, LANES), 1)
    pairs = (heads + 1) // 2
    for p in range(pairs):
        pair = pl.ds(p * LANES, LANES)
        k_pair = pl.ds(wide + p * LANES, LANES)
        v_pair = pl.ds(2 * wide + p * LANES, LANES)
        held = min(2, heads - 2 * p)
        for i in range(held):
            inside = (lane >= dk) if i else (lane < dk)
            qa_ref[i] = jnp.where(inside, qkv_ref[:, pair], eq_ref[...])
            kt_ref[i] = jnp.where(inside, qkv_ref[:, k_pair], ek_ref[...]).T
            bias_ref[i] = toeplitz_rows(rows_ref[2 * p + i : 2 * p + i + 1, :])

        def block(step, carry, p=p, pair=pair, v_pair=v_pair, held=held):
            b = lax.rem(lax.div(me, group) + 1 + step, blocks)
            rows = aligned(b * QB, QB)
            scores = [mm(qa_ref[i, rows, :], kt_ref[i]) for i in range(held)]
            for a in range(QB // LANES):
                tile = b * (QB // LANES) + a
                where = aligned(tile * LANES, LANES)
                off = pl.ds(pl.multiple_of(length - tile * LANES, LANES), length)
                lse = None if p == 0 else lse_ref[where, :]
                mixed = None
                for i in range(held):
                    part = scores[i][a * LANES : (a + 1) * LANES] + bias_ref[i, :, off]
                    peak = jnp.max(part, axis=-1, keepdims=True)
                    expo = jnp.exp(part - peak)
                    total = jnp.sum(expo, axis=-1, keepdims=True)
                    value = mm(expo.astype(BF16), qkv_ref[:, v_pair]) * (1.0 / total)
                    column = peak + jnp.log(total)
                    mixed = jnp.where(lane_q < dk, mixed, value) if i else value
                    if lse is None:
                        lse = jnp.broadcast_to(column, (LANES, LANES))
                    else:
                        lse = jnp.where(lane_q == 2 * p + i, column, lse)
                o_ref[where, pair] = mixed.astype(BF16)
                lse_ref[where, :] = lse
            for g in range(group):
                peer = b * group + g

                @pl.when(peer != me)
                def _(peer=peer):
                    push(
                        o_ref.at[aligned(peer * tl, tl), pair],
                        back_ref.at[me, :, pair],
                        send.at[p, peer],
                        recv.at[p, me],
                        peer,
                    ).start()

            return carry

        lax.fori_loop(0, blocks, block, 0)
        back_ref[me, :, pair] = o_ref[mine, pair]
        o.flush(slice(None), pair)
        if p == 0:
            spread.forward()
    lse_out.flush()
    for k in range(1, n):
        spread.arrive(k)
        chunks.flush(spread.order[k])
    spread.sent()
    for p in range(pairs):
        pair = pl.ds(p * LANES, LANES)
        for k in range(1, n):
            peer = lax.rem(me + k, n)
            push(
                o_ref.at[aligned(peer * tl, tl), pair],
                back_ref.at[peer, :, pair],
                send.at[p, peer],
                recv.at[p, peer],
                peer,
            ).wait()


def attend(n, heads, dk, qkv, ext_q, ext_k, offset_rows, chunk):
    length, width = qkv.shape[0], qkv.shape[1] // 3
    span = offset_rows.shape[1]
    pairs = (heads + 1) // 2
    pair_sems = pltpu.SemaphoreType.DMA((pairs, n))
    return call(
        functools.partial(attend_kernel, n, heads, dk), "attend", 4 if chunk.shape[0] == length else 5, 20,
        [chunk, qkv, ext_q, ext_k, offset_rows],
        [
            ((length, width), BF16, pairs),
            ((length, LANES), F32, 1),
            ((n, length // n, width), BF16, 1),
            ((n,) + chunk.shape, BF16, n),
        ],
        [
            pltpu.VMEM((2, LANES, span), F32),
            pltpu.VMEM((2, LANES, length), BF16),
            pltpu.VMEM((2, length, LANES), BF16),
            pair_sems,
            pair_sems,
            *way_sems(n),
        ],
        lambda: others("seq", n),
    )


def three_parts(lane, value):
    first = value.astype(BF16).astype(F32)
    rest = value - first
    second = rest.astype(BF16).astype(F32)
    third = rest - second
    at = lax.rem(lane, 64)
    return jnp.where(at == 8, first, jnp.where(at == 9, second, jnp.where(at == 10, third, 0.0)))


def attend_back_kernel(n, heads, dk, summing, ins, outs, bias_ref, kt_ref, vt_ref, qa_ref, do_ref, qt_ref,
                       dkt_ref, dvt_ref, dbias_ref, send, recv, *refs):
    qkv, o, lse, eq, ek, rows, beside, *more = ins
    dqkv, dr, beside_out, *more_out = outs
    dqkv_ref, dr_ref = dqkv.ref, dr.ref
    length, wide = o.ref.shape
    span = rows.ref.shape[1]
    tl = length // n
    group = QB // tl
    blocks = length // QB
    me = lax.axis_index("seq")
    mine = aligned(me * tl, tl)
    if summing:
        do, own = more
        mid_ref, got_ref, send_y, recv_y = refs
        do_any = do.get()
        for k in range(1, n):
            peer = lax.rem(me + k, n)
            push(do_any.at[peer], do_ref.at[mine], send.at[peer], recv.at[me], peer).start()
        do_ref[mine] = do_any[me]
        collect = Collect(n, beside.get(), got_ref, (send_y, recv_y), mid_ref)

        def start_beside():
            for k in (3, 1, 2) if n == 4 else range(1, n):
                collect.start(k)

    else:
        dn2, x1, dy, gain, back, weights = more
        dx1_out, g_gain, g_out, reduce, beside_next, summed = more_out
        wo_ref, do_any, load, send_g, recv_g = refs
        loads = out_loads(weights, wo_ref, load)
        for copy in loads:
            copy.start()
        rows_g = beside_out.ref.shape[1]
        g_ref = beside.get().at[pl.ds(0, rows_g)]
        spread = Spread(n, g_ref, chunk_slots(beside_out.ref), rows_g, (send_g, recv_g))
        spread.start_some(True)

        def start_beside():
            spread.start_some(False)
            summed.start()

        dx1, g_gain.ref[...] = norm_back(
            x1.get()[...], dn2.get()[...], dy.get()[...].astype(F32), gain.get()[...]
        )
        dx1_out.ref[...] = dx1
        dx1_out.flush()
        d_attn = dx1.astype(BF16)
        arrive(loads)
        back_ref = back.get()
        hw = wo_ref.shape[0] // n
        if hw < wide:
            do_any[...] = jnp.zeros_like(do_any)
        for k in range(1, n):
            peer = lax.rem(me + k, n)
            do_any[peer, :, :hw] = mm_nt(d_attn, wo_ref[aligned(peer * hw, hw), :]).astype(BF16)
            push(do_any.at[peer], do_ref.at[mine], send.at[peer], recv.at[me], peer).start()
        do_any[me, :, :hw] = mm_nt(d_attn, wo_ref[aligned(me * hw, hw), :]).astype(BF16)
        do_ref[mine] = do_any[me]
        beside_out.ref[me] = g_ref[...]
        beside_out.flush(me)
        for t in range(n):
            g_out.ref[pl.ds(t * hw, hw), :] = mm_tn(back_ref[t][:, :hw], d_attn).astype(BF16)
        reduce.start()
    qkv_ref, o_ref, lse_ref, eq_ref, ek_ref, rows_ref = (
        late.get() for late in (qkv, o, lse, eq, ek, rows)
    )
    lane = lax.broadcasted_iota(jnp.int32, (length, LANES), 1)
    lane_q = lax.broadcasted_iota(jnp.int32, (QB, LANES), 1)
    at = lax.rem(lane, 64)
    parts = (at >= 8) & (at <= 10)
    ones = jnp.where(parts, 1.0, 0.0)
    for p in range((heads + 1) // 2):
        pair = pl.ds(p * LANES, LANES)
        k_lanes = pl.ds(wide + p * LANES, LANES)
        v_lanes = pl.ds(2 * wide + p * LANES, LANES)
        held = min(2, heads - 2 * p)
        q_pair, k_pair, v_pair = qkv_ref[:, pair], qkv_ref[:, k_lanes], qkv_ref[:, v_lanes]
        qt_ref[...] = q_pair.T
        ek = (ek_ref[...].astype(F32) + ones).astype(BF16)
        for i in range(held):
            head = 2 * p + i
            inside = (lane >= dk) if i else (lane < dk)
            lse = lse_ref[:, head : head + 1]
            eq = (eq_ref[...].astype(F32) - three_parts(lane, lse)).astype(BF16)
            qa_ref[i] = jnp.where(inside, q_pair, eq)
            kt_ref[i] = jnp.where(inside, k_pair, ek).T
            vt_ref[i] = jnp.where(inside, v_pair, ones.astype(BF16)).T
            bias_ref[i] = toeplitz_rows(rows_ref[head : head + 1, :])
        dkt_ref[...] = jnp.zeros_like(dkt_ref)
        dvt_ref[...] = jnp.zeros_like(dvt_ref)
        dbias_ref[...] = jnp.zeros_like(dbias_ref)

        def given(peer):
            return push(
                do_any.at[peer], do_ref.at[aligned(peer * tl, tl)], send.at[peer], recv.at[peer], peer
            )

        def block(step, carry, p=p, pair=pair, k_lanes=k_lanes, held=held):
            b = lax.rem(lax.div(me, group) + step, blocks)
            where = aligned(b * QB, QB)
            if p == 0:
                for g in range(group):
                    peer = b * group + g

                    @pl.when(peer != me)
                    def _(peer=peer):
                        given(peer).wait()

                pl.when(step == 1)(start_beside)


            dq = None
            do_pair = do_ref[where, pair]
            do_t = do_pair.T
            weighed = do_pair.astype(F32) * o_ref[where, pair].astype(F32)
            for i in range(held):
                half = pl.ds(i * dk, dk)
                inside_q = (lane_q >= dk) if i else (lane_q < dk)
                delta = jnp.sum(jnp.where(inside_q, weighed, 0.0), axis=-1, keepdims=True)
                da = jnp.where(inside_q, do_pair, (-three_parts(lane_q, delta)).astype(BF16))
                scores = mm(qa_ref[i, where, :], kt_ref[i])
                lifted = mm(da, vt_ref[i])
                probs, grads = [], []
                for a in range(QB // LANES):
                    cut = slice(a * LANES, (a + 1) * LANES)
                    tile = b * (QB // LANES) + a
                    off = pl.ds(pl.multiple_of(length - tile * LANES, LANES), length)
                    prob = jnp.exp(scores[cut] + bias_ref[i, :, off])
                    grad = prob * lifted[cut]
                    dbias_ref[i, :, off] += grad
                    probs.append(prob.astype(BF16))
                    grads.append(grad.astype(BF16))
                prob = jnp.concatenate(probs, axis=0)
                grad = jnp.concatenate(grads, axis=0)
                value = mm(grad, qkv_ref[:, k_lanes])
                dq = jnp.where(lane_q < dk, dq, value) if i else value
                dkt_ref[half, :] += mm(qt_ref[half, where], grad)
                dvt_ref[half, :] += mm(do_t[i * dk : (i + 1) * dk], prob)
            dqkv_ref[where, pair] = dq.astype(BF16)
            return carry

        lax.fori_loop(0, length // QB, block, 0)
        dqkv_ref[:, k_lanes] = dkt_ref[...].T.astype(BF16)
        dqkv_ref[:, v_lanes] = dvt_ref[...].T.astype(BF16)
        for lanes in (pair, k_lanes, v_lanes):
            dqkv.flush(slice(None), lanes)
        place = lax.broadcasted_iota(jnp.int32, (8, span), 0)
        for i in range(held):
            folded = dbias_ref[i]
            rows = LANES
            while rows > 8:
                rows //= 2
                folded = folded[:rows] + pltpu.roll(folded[rows:], span - rows, 1)
            for bit in (4, 2, 1):
                folded = jnp.where(
                    lax.rem(lax.div(place, bit), 2) == 1, pltpu.roll(folded, span - bit, 1), folded
                )
            dr_ref[2 * p + i : 2 * p + i + 1, :] = jnp.sum(folded, axis=0, keepdims=True)
        if p == 0:
            if summing:
                collect.relay()
            else:
                reduce.forward()
                spread.forward()
                summed.relay()
                beside_next.start()
    dr.flush()
    if summing:
        collect.add_to(own.get())
        beside_out.ref[...] = own.ref[...].astype(BF16)
        beside_out.flush()
        collect.sent()
    else:
        for k in range(1, n):
            spread.arrive(k)
            beside_out.flush(spread.order[k])
        spread.sent()
        summed.share()
        beside_next.forward()


def out_loads(source, target, sems):
    if len(source.shape) == 2:
        return [pltpu.make_async_copy(source, target, sems.at[0])]
    blocks, _, cols = source.shape
    return [
        pltpu.make_async_copy(source.at[t], target.at[:, pl.ds(t * cols, cols)], sems.at[t])
        for t in range(blocks)
    ]


def attend_back_scratch(heads, length, width, span, n):
    sems = pltpu.SemaphoreType.DMA((n,))
    return [
        pltpu.VMEM((2, LANES, span), F32),
        pltpu.VMEM((2, LANES, length), BF16),
        pltpu.VMEM((2, LANES, length), BF16),
        pltpu.VMEM((2, length, LANES), BF16),
        pltpu.VMEM((length, width), BF16),
        pltpu.VMEM((LANES, length), BF16),
        pltpu.VMEM((LANES, length), F32),
        pltpu.VMEM((LANES, length), F32),
        pltpu.VMEM((2, LANES, span), F32),
        sems,
        sems,
    ]


def weight_loads(sources, targets, sems):
    if len(sources) == 3:
        return [
            [pltpu.make_async_copy(src, dst, sems.at[j])] if dst is not None else None
            for j, (src, dst) in enumerate(zip(sources, targets))
        ]
    packed = sources[-1]
    pieces, count, rows = packed.shape[:3]
    groups = [
        [
            pltpu.make_async_copy(
                packed.at[i, j], targets[j - count].at[pl.ds(i * rows, rows)], sems.at[j * pieces + i]
            )
            for i in range(pieces)
        ]
        for j in range(count)
    ]
    if targets[0] is None:
        return [None] * (3 - count) + groups
    if count == 2:
        blocks, _, cols = sources[0].shape
        groups.insert(
            0,
            [
                pltpu.make_async_copy(
                    sources[0].at[t], targets[0].at[:, pl.ds(t * cols, cols)], sems.at[2 * pieces + t]
                )
                for t in range(blocks)
            ],
        )
    return groups


def load_sems(weights):
    count = 3
    if len(weights) < 3:
        count = weights[-1].shape[0] * weights[-1].shape[1] + (weights[0].shape[0] if len(weights) == 2 else 0)
    return pltpu.SemaphoreType.DMA((count,))


def arrive(copies):
    for copy in copies:
        copy.wait()


def mix_kernel(n, hw, ins, outs, wo_ref, up_ref, down_ref, out_ref, got_ref, total_ref,
               load, send_n, recv_n, send_y, recv_y):
    x, gain, back, *weights = ins
    y, x1_out, n2, slope, hid = outs
    n2_ref = n2.ref
    tl = x.ref.shape[0]
    me = lax.axis_index("seq")
    mine = aligned(me * tl, tl)
    loads = weight_loads(weights, (wo_ref, up_ref, down_ref), load)
    for group in loads:
        for copy in group:
            copy.start()
    back_ref = back.get()
    total = x.get()[...].astype(F32)
    arrive(loads[0])
    for s in range(n):
        total += mm(back_ref[s][:, :hw], wo_ref[s * hw : (s + 1) * hw, :])
    total_ref[...] = total
    x1 = total_ref[...]
    n2_ref[mine] = (x1 * inverse_rms(x1) * gain.get()[...]).astype(BF16)
    spread = Spread(n, n2_ref.at[mine], row_slots(n2_ref, tl), tl, (send_n, recv_n))
    collect = Collect(n, out_ref, got_ref, (send_y, recv_y))

    spread.start()
    x1_out.ref[...] = x1
    x1_out.flush()
    arrive(loads[1])
    arrive(loads[2])
    for k in range(n):
        where = aligned(spread.order[k] * tl, tl)
        if k:
            spread.arrive(k)
        n2.flush(where)
        u = mm(n2_ref[where], up_ref[...])
        half = 0.5 + 0.5 * lax.erf(u * math.sqrt(0.5))
        hidden = (u * half).astype(BF16)
        hid.ref[where] = hidden
        hid.flush(where)
        slope.ref[where] = (
            half + u * (jnp.exp(-0.5 * u * u) * (1.0 / math.sqrt(2.0 * math.pi)))
        ).astype(BF16)
        slope.flush(where)
        part = mm(hidden, down_ref[...])
        if k:
            collect.give(k, part)
        else:
            total_ref[...] += part
            spread.forward()

    collect.relay()
    collect.add_to(total_ref)
    y.ref[...] = total_ref[...].astype(BF16)
    y.flush()
    spread.sent()
    collect.sent()


def mix(n, hw, ff, x, gain, back, weights):
    tl, width = x.shape
    tokens = n * tl
    return call(
        functools.partial(mix_kernel, n, hw), "mix", 1, 45,
        [x, gain, back, *map(Raw, weights)],
        [
            ((tl, width), BF16, 1),
            ((tl, width), F32, 1),
            ((tokens, width), BF16, n),
            ((tokens, ff), BF16, n),
            ((tokens, ff), BF16, n),
        ],
        [
            pltpu.VMEM((n * hw, width), BF16),
            pltpu.VMEM((width, ff), BF16),
            pltpu.VMEM((ff, width), BF16),
            pltpu.VMEM((n, tl, width), BF16),
            pltpu.VMEM((n, tl, width), BF16),
            pltpu.VMEM((tl, width), F32),
            load_sems(weights),
            *way_sems(n),
            *way_sems(n),
        ],
        lambda: near(n),
    )


def norm_back(x1, dn, dy, gain):
    inv = inverse_rms(x1)
    scaled = x1 * inv
    g_gain = jnp.sum(dn * scaled, axis=0, keepdims=True)
    lifted = dn * gain
    return dy + inv * (lifted - scaled * jnp.mean(lifted * scaled, axis=-1, keepdims=True)), g_gain


def turn_kernel(n, hw, ins, outs, wo_ref, up_ref, down_ref, n2_ref, hid_ref, du_ref, out_ref, got_ref, total_ref,
                load, send_n, recv_n, send_d, recv_d):
    x, gain, back, dy, *weights = ins
    parts, own, dx1_out, do, g_gain, *grads = outs
    own_ref = own.ref
    tl = x.ref.shape[0]
    me = lax.axis_index("seq")
    mine = aligned(me * tl, tl)
    loads = weight_loads(weights, (wo_ref, up_ref, down_ref), load)
    for group in loads:
        for copy in group:
            copy.start()
    back_ref = back.get()
    total = x.get()[...].astype(F32)
    arrive(loads[0])
    for s in range(n):
        total += mm(back_ref[s][:, :hw], wo_ref[s * hw : (s + 1) * hw, :])
    own_ref[...] = total
    x1 = own_ref[...]
    gain_row = gain.get()[...]
    n2_ref[mine] = (x1 * inverse_rms(x1) * gain_row).astype(BF16)
    spread = Spread(n, n2_ref.at[mine], row_slots(n2_ref, tl), tl, (send_n, recv_n))
    collect = Collect(n, out_ref, got_ref, (send_d, recv_d))
    dy_all = dy.get()

    spread.start()
    arrive(loads[1])
    arrive(loads[2])
    for k in range(n):
        where = aligned(spread.order[k] * tl, tl)
        if k:
            spread.arrive(k)
        u = mm(n2_ref[where], up_ref[...])
        half = 0.5 + 0.5 * lax.erf(u * math.sqrt(0.5))
        hid_ref[where] = (u * half).astype(BF16)
        slope = half + u * (jnp.exp(-0.5 * u * u) * (1.0 / math.sqrt(2.0 * math.pi)))
        du = (mm_nt(dy_all[where], down_ref[...]) * slope).astype(BF16)
        du_ref[where] = du
        part = mm_nt(du, up_ref[...])
        if k:
            collect.give(k, part)
        else:
            total_ref[...] = part
            spread.forward()

    for k in range(1, n):
        parts.ref[k] = mm(hid_ref[aligned(spread.order[k] * tl, tl)], down_ref[...]).astype(BF16)
        parts.flush(k)
    collect.relay()
    parts.ref[0] = jnp.zeros_like(out_ref[0])
    parts.flush(0)
    own_ref[...] = x1 + mm(hid_ref[mine], down_ref[...])
    own.flush()
    store_grad(grads, 0, hid_ref, dy_all)
    store_grad(grads, 1, n2_ref, du_ref)
    collect.add_to(total_ref)
    dx1, g_gain.ref[...] = norm_back(x1, total_ref[...], dy_all[mine].astype(F32), gain_row)
    out_back(hw, dx1, dx1_out, do, grads, back_ref, wo_ref)
    spread.sent()
    collect.sent()


def out_back(hw, dx1, dx1_out, do, grads, back_ref, wo_ref):
    dx1_out.ref[...] = dx1
    dx1_out.flush()
    d_attn = dx1.astype(BF16)
    for s in range(back_ref.shape[0]):
        do.ref[s] = mm_nt(d_attn, wo_ref[s * hw : (s + 1) * hw, :]).astype(BF16)
        do.flush(s)
    for s in range(back_ref.shape[0]):
        store_rows(grads, 2, s * hw, mm_tn(back_ref[s][:, :hw], d_attn).astype(BF16))
    flush_grad(grads, 2)


def grad_shapes(weights, hw, n, ff, width):
    if len(weights) < 3:
        pieces, _, rows = weights[-1].shape[:3]
        return [((pieces, 3, rows, width), BF16, 3)]
    return [((ff, width), BF16, 1), ((width, ff), BF16, 1), ((n * hw, width), BF16, 1)]


def turn_round(n, hw, ff, x, gain, back, weights, dy_all):
    tl, width = x.shape
    return call(
        functools.partial(turn_kernel, n, hw), "turn_round", 2, 55,
        [x, gain, back, dy_all, *map(Raw, weights)],
        [
            ((n, tl, width), BF16, n),
            ((tl, width), F32, 1),
            ((tl, width), F32, 1),
            ((n, tl, hw), BF16, n),
            ((1, width), F32, 1),
            *grad_shapes(weights, hw, n, ff, width),
        ],
        [
            pltpu.VMEM((n * hw, width), BF16),
            pltpu.VMEM((width, ff), BF16),
            pltpu.VMEM((ff, width), BF16),
            pltpu.VMEM((n * tl, width), BF16),
            pltpu.VMEM((n * tl, ff), BF16),
            pltpu.VMEM((n * tl, ff), BF16),
            pltpu.VMEM((n, tl, width), BF16),
            pltpu.VMEM((n, tl, width), BF16),
            pltpu.VMEM((tl, width), F32),
            load_sems(weights),
            *way_sems(n),
            *way_sems(n),
        ],
        lambda: near(n),
    )


def mix_back_kernel(n, shards, loads, ins, outs, up_ref, down_ref, out_ref, got_ref, dy_all,
                    send_n, recv_n, send_d, recv_d, *reduce_refs):
    dy, w_grad, slope, hid, n2 = ins
    dn2, half_out, *grads = outs
    blocks = len(grads) == 1
    if blocks:
        sums_out, sum_sems, packed, got_0, got_1, send_0, recv_0, send_1, recv_1 = reduce_refs[7:]
        reduce_refs = reduce_refs[:7]
        grads = [Held(packed)]
        across = [
            Across(shards, lambda z, core, j=j: packed.at[2 * z + core, j], got, send, recv)
            for j, (got, send, recv) in enumerate(((got_0, send_0, recv_0), (got_1, send_1, recv_1)))
        ]
    tl = dy.ref.shape[0]
    mine = aligned(lax.axis_index("seq") * tl, tl)
    dy_ref = dy.get()
    spread = Spread(n, dy_ref, row_slots(dy_all, tl), tl, (send_d, recv_d))
    spread.start()
    reduce = Reduce(shards, w_grad.get(), *reduce_refs)
    reduce.start()
    dy_all[mine] = dy_ref[...]
    collect = Collect(n, out_ref, got_ref, (send_n, recv_n))
    arrive(loads[2])
    arrive(loads[1])
    du_ref = slope.get()
    for k in range(n):
        where = aligned(spread.order[k] * tl, tl)
        if k:
            spread.arrive(k)
        du = (mm_nt(dy_all[where], down_ref[...]) * du_ref[where].astype(F32)).astype(BF16)
        du_ref[where] = du
        part = mm_nt(du, up_ref[...])
        if k:
            collect.give(k, part)
        else:
            spread.forward()
            dn2.ref[...] = part
            reduce.forward()
    store_grad(grads, 0, hid.get(), dy_all)
    if blocks:
        across[0].start()
    collect.relay()
    store_grad(grads, 1, n2.get(), du_ref)
    copies = []
    if blocks:
        across[1].start()
        rows = packed.shape[2]
        for j in range(2):
            for z in range(shards):
                part = pl.ds((2 * z + j) * rows, rows)
                hid.ref[part, :] = across[j].sum(z)
                copies.append(
                    pltpu.make_async_copy(hid.ref.at[part], sums_out.at[part], sum_sems.at[2 * z + j])
                )
                copies[-1].start()
    half_out.ref[...] = reduce.result()
    half_out.flush()
    collect.add_to(dn2.ref)
    dn2.flush()
    arrive(copies)
    spread.sent()
    collect.sent()


def flush_grad(grads, index):
    if len(grads) == 1:
        grads[0].flush(slice(None), index)
    else:
        grads[index].flush()


def store_rows(grads, index, first, value):
    if len(grads) == 1:
        ref = grads[0].ref
        rows = ref.shape[2]
        for i in range(value.shape[0] // rows):
            ref[first // rows + i, index] = value[i * rows : (i + 1) * rows]
    else:
        grads[index].ref[pl.ds(first, value.shape[0]), :] = value


def row_blocks(left_ref, right_ref, store):
    rows = min(256, left_ref.shape[1])

    def block(b, carry):
        first = pl.multiple_of(b * rows, rows)
        store(first, mm_tn(left_ref[:, pl.ds(first, rows)], right_ref[...]).astype(BF16))
        return carry

    lax.fori_loop(0, left_ref.shape[1] // rows, block, 0)


def store_grad(grads, index, left_ref, right_ref):
    row_blocks(left_ref, right_ref, functools.partial(store_rows, grads, index))
    flush_grad(grads, index)


def project_back_kernel(n, ins, outs, out_ref, got_ref, total_ref, send, recv):
    w, dqkv, n1, x, dx1, gain = ins
    dx_out, low, g_w, g_gain = outs
    tl = x.ref.shape[0]
    collect = Collect(n, out_ref, got_ref, (send, recv))
    w_ref, dqkv_ref = w.get(), dqkv.get()

    def part(k):
        return mm_nt(dqkv_ref[aligned(collect.order[k] * tl, tl), :], w_ref[...])

    for k in (3, 1, 2) if n == 4 else range(1, n):
        collect.give(k, part(k))
    total_ref[...] = part(0)
    collect.relay()

    def store(first, value):
        g_w.ref[pl.ds(first, value.shape[0]), :] = value

    row_blocks(n1.get(), dqkv_ref, store)
    g_w.flush()
    collect.add_to(total_ref)
    dx, g_gain.ref[...] = norm_back(x.get()[...].astype(F32), total_ref[...], dx1.get()[...], gain.get()[...])
    dx_out.ref[...] = dx
    dx_out.flush()
    low.ref[...] = dx.astype(BF16)
    low.flush()
    collect.sent()


def back_across_kernel(n, shards, heads, dk, ins, outs, dqkv, g_w, out_ref, got_p, send_p, recv_p,
                       up_ref, down_ref, got_m, dy_all, load, *refs):
    attend_ins, (w, n1, x, dx1, gain), (slope, hid, n2), weights = ins[:9], ins[9:14], ins[14:17], ins[17:]
    dr, y, dx, low, g_gain, dn2, half_w, *grads = outs
    loads = weight_loads(weights, (None, up_ref, down_ref), load)
    for group in reversed(loads[1:]):
        for copy in group:
            copy.start()
    attend_back_kernel(n, heads, dk, True, attend_ins, [Held(dqkv), dr, y], *refs[:15])
    project_back_kernel(
        n, [w, Held(dqkv), n1, x, dx1, gain], [dx, low, Held(g_w), g_gain],
        out_ref, got_p, dn2.ref, send_p, recv_p,
    )
    mix_back_kernel(
        n, shards, loads, [low, Held(g_w), slope, hid, n2], [dn2, half_w, *grads],
        up_ref, down_ref, out_ref, got_m, dy_all, *refs[15:26], *(grads if len(grads) == 1 else []), *refs[26:],
    )


def back_across(n, shards, heads, dk, ff, qkv, o, lse, ext_q, ext_k, offset_rows, parts, do, own,
                w, n1, x, dx1, gain, slope, hid, n2, weights):
    length, wide = o.shape
    span = offset_rows.shape[1]
    tl, width = x.shape
    half = (width // (2 * shards), w.shape[1])
    sum_refs = []
    if len(weights) < 3:
        pieces, _, rows = weights[-1].shape[:3]
        grads = [((shards * 2 * rows, width), BF16, None)]
        row_sems = pltpu.SemaphoreType.DMA((shards,))
        sum_refs = [
            pltpu.SemaphoreType.DMA((2 * shards,)),
            pltpu.VMEM((pieces, 2, rows, width), BF16),
            pltpu.VMEM((shards, rows, width), BF16),
            pltpu.VMEM((shards, rows, width), BF16),
            row_sems, row_sems, row_sems, row_sems,
        ]
    else:
        grads = [((ff, width), BF16, 1), ((width, ff), BF16, 1)]
    return call(
        functools.partial(back_across_kernel, n, shards, heads, dk), "back_across", 9, 85,
        [qkv, o, lse, ext_q, ext_k, offset_rows, parts, do, own, w, n1, x, dx1, gain, slope, hid, n2,
         *map(Raw, weights)],
        [
            ((heads, span), F32, 1),
            ((tl, width), BF16, 1),
            ((tl, width), F32, 1),
            ((tl, width), BF16, 1),
            ((1, width), F32, 1),
            ((tl, width), F32, 1),
            (half, BF16, 1),
            *grads,
        ],
        [
            pltpu.VMEM((length, 3 * wide), BF16),
            pltpu.VMEM(w.shape, BF16),
            pltpu.VMEM((n, tl, width), BF16),
            pltpu.VMEM((n, tl, width), BF16),
            *way_sems(n),
            pltpu.VMEM((width, ff), BF16),
            pltpu.VMEM((ff, width), BF16),
            pltpu.VMEM((n, tl, width), BF16),
            pltpu.VMEM((n * tl, width), BF16),
            load_sems(weights),
            *attend_back_scratch(heads, length, wide, span, n),
            pltpu.VMEM((2, tl // 2, width), BF16),
            pltpu.VMEM((n, tl, width), BF16),
            *way_sems(n),
            *way_sems(n),
            *way_sems(n),
            *reduce_scratch(shards, half),
            *sum_refs,
        ],
        lambda: others("seq", n) + others("dp", shards) + [other_core()],
    )


def back_first_kernel(n, shards, heads, dk, ins, outs, dqkv, dx1, low, g_out, out_ref, got_ref, total_ref,
                      send_p, recv_p, send_w, recv_w, *refs):
    attend_ins, (w, n1, x, gain, half_w) = ins[:13], ins[13:]
    dr, all_g, g_ffn, dx, g_w, g_gain, half_out, all_w, out_last = outs
    reduce = Reduce(shards, g_out, *refs[:7])
    half_g = attend_ins[6].get()
    rows = out_last.ref.shape[0]
    last = half_g.at[pl.ds(half_g.shape[0] - rows, rows)]
    summed = AllSum(n, last, out_last, *refs[7:14])
    half = half_w.get()
    spread = Spread(n, half, chunk_slots(all_w.ref), half.shape[0], (send_w, recv_w))
    all_w.ref[lax.axis_index("seq")] = half[...]
    attend_back_kernel(
        n, heads, dk, False, attend_ins,
        [Held(dqkv), dr, all_g, Held(dx1), g_ffn, Held(g_out), reduce, spread, summed], *refs[14:]
    )
    summed.forward()
    project_back_kernel(
        n, [w, Held(dqkv), n1, x, Held(dx1), gain], [dx, Held(low), g_w, g_gain],
        out_ref, got_ref, total_ref, send_p, recv_p,
    )
    half_out.ref[...] = reduce.result()
    for k in range(1, n):
        spread.arrive(k)
    spread.sent()
    summed.done()


def back_first(n, shards, heads, dk, qkv, o, lse, ext_q, ext_k, offset_rows, half_g, dn2, x1, dy, g_ffn, back, wo,
               w, n1, x, gain, half_w):
    length, wide = o.shape
    span = offset_rows.shape[1]
    tl, width = x.shape
    hd = wo.shape[-2]
    half_out = (hd // (2 * shards), width)
    return call(
        functools.partial(back_first_kernel, n, shards, heads, dk), "back_first", 11, 65,
        [qkv, o, lse, ext_q, ext_k, offset_rows, half_g, dn2, x1, dy, g_ffn, back, Raw(wo), w, n1, x, gain, half_w],
        [
            ((heads, span), F32, 1),
            ((n, half_g.shape[0] - half_out[0], width), BF16, n),
            ((1, width), F32, 1),
            ((tl, width), F32, 1),
            (w.shape, BF16, 1),
            ((1, width), F32, 1),
            (half_out, BF16, 1),
            ((n,) + half_w.shape, BF16, 1),
            (half_out, BF16, 1),
        ],
        [
            pltpu.VMEM((length, 3 * wide), BF16),
            pltpu.VMEM((tl, width), F32),
            pltpu.VMEM((tl, width), BF16),
            pltpu.VMEM((hd, width), BF16),
            pltpu.VMEM((n, tl, width), BF16),
            pltpu.VMEM((n, tl, width), BF16),
            pltpu.VMEM((tl, width), F32),
            *way_sems(n),
            *way_sems(n),
            *reduce_scratch(shards, half_out),
            *sum_scratch(n, *half_out),
            *attend_back_scratch(heads, length, wide, span, n),
            pltpu.VMEM((hd, width), BF16),
            pltpu.VMEM((n, tl, wide), BF16),
            pltpu.SemaphoreType.DMA((n,)),
            *way_sems(n),
        ],
        lambda: others("seq", n) + others("dp", shards) + [other_core()],
    )


def finish_kernel(n, shards, ins, outs, small_got, tile_got, send_g, recv_g, send_w0, recv_w0,
                  send_x, recv_x, send_s, recv_s, send_t, recv_t, *refs):
    g0, w0, out0, w1, small, g1, out1, y0, y1, d0, d1 = ins
    gathered_g, gathered_w0, out0_out, other_g_out, other_w_out, other_out, sums, sections, d_inputs = outs
    all_g, all_w0 = gathered_g.ref, gathered_w0.ref
    other_g, other_w = other_g_out.ref, other_w_out.ref
    me = lax.axis_index("seq")
    core = lax.axis_index("section")
    row = lax.axis_index("dp")
    other = other_core()
    peers = cores_and_rows(shards)

    reduce = Reduce(shards, w0.get(), *refs[:7])
    reduce.start()
    summed = AllSum(n, out0.get(), out0_out, *refs[7:])
    summed.start()
    g0_ref = g0.get()
    spread_g = Spread(n, g0_ref, chunk_slots(all_g), g0_ref.shape[0], (send_g, recv_g))
    spread_g.start()
    small_ref = small.get()
    smalls = [
        push(small_ref.at[peer["section"], peer["dp"]], small_got.at[i], send_s.at[i], recv_s.at[i], peer)
        for i, peer in enumerate(peers)
    ]
    for copy in smalls:
        copy.start()

    def cross(source, target, t, number):
        sem = number * n + t
        return push(source, target.at[t], send_x.at[sem], recv_x.at[sem], other)

    def cross_rows(source, target, number):
        sem = 2 * n + number
        return push(source, target, send_x.at[sem], recv_x.at[sem], other)

    w1_ref, g1_ref, out1_ref, y0_ref, y1_ref, d0_ref, d1_ref = (
        late.get() for late in (w1, g1, out1, y0, y1, d0, d1)
    )

    @pl.when(core == 0)
    def _():
        cross_rows(y1_ref, sections.ref.at[0], 0).start()
        cross_rows(d1_ref, d_inputs.ref.at[0], 1).start()
        cross_rows(out1_ref, other_out.ref, 2).start()
        for t in range(n):
            cross(w1_ref.at[t], other_w, t, 1).start()
            cross(g1_ref.at[t], other_g, t, 0).start()
        sections.ref[0] = y0_ref[...]
        d_inputs.ref[0] = d0_ref[...]

    @pl.when(core == 1)
    def _():
        cross_rows(y0_ref, sections.ref.at[1], 0).start()
        cross_rows(d0_ref, d_inputs.ref.at[1], 1).start()
        cross(g0_ref, other_g, me, 0).start()
        sections.ref[1] = y1_ref[...]
        d_inputs.ref[1] = d1_ref[...]

    all_g[me] = g0_ref[...]
    gathered_g.flush(me)
    reduce.forward()
    summed.relay()

    tile = small_ref[core, row]
    for i, copy in enumerate(smalls):
        copy.wait()
        tile += small_got[i]
    tile_got[0] = tile
    tiles = []
    for k in range(1, n):
        copy = push(tile_got.at[0], tile_got.at[k], send_t.at[k], recv_t.at[k], lax.rem(me + k, n))
        copy.start()
        tiles.append(copy)

    spread_g.forward()
    summed.share()
    all_w0[me] = reduce.result()
    gathered_w0.flush(me)
    spread_w0 = Spread(n, all_w0.at[me], chunk_slots(all_w0), all_w0.shape[1], (send_w0, recv_w0))
    spread_w0.start()
    summed.forward()
    spread_w0.forward()

    @pl.when(core == 1)
    def _():
        cross(all_w0.at[me], other_w, me, 1).start()

    for k in range(1, n):
        source = spread_g.order[k]
        spread_g.arrive(k)
        gathered_g.flush(source)

        @pl.when(core == 1)
        def _():
            cross(all_g.at[source], other_g, source, 0).start()

    summed.done()

    @pl.when(core == 1)
    def _():
        cross_rows(out0_out.ref, other_out.ref, 2).start()

    total = tile
    for k in range(1, n):
        tiles[k - 1].wait()
        total += tile_got[k]
    line = lax.broadcasted_iota(jnp.int32, tile.shape, 0)
    sums.ref[...] = jnp.where(line < 2, total, tile)
    for number, (source, target) in enumerate(((y0_ref, sections), (d0_ref, d_inputs))):
        cross_rows(source, target.ref.at[0], number).wait()
        target.flush()
    for k in range(1, n):
        source = spread_g.order[k]
        spread_w0.arrive(k)
        gathered_w0.flush(source)

        @pl.when(core == 1)
        def _():
            cross(all_w0.at[source], other_w, source, 1).start()

    cross_rows(out0_out.ref, other_out.ref, 2).wait()
    other_out.flush()
    for t in [me] + spread_g.order[1:]:
        cross(g0_ref, other_g, t, 0).wait()
        other_g_out.flush(t)
    for t in [me] + spread_g.order[1:]:
        cross(all_w0.at[0], other_w, t, 1).wait()
        other_w_out.flush(t)
    for spread in (spread_g, spread_w0):
        spread.sent()


def finish(n, shards, small, g0, out0, w0, g1, out1, w1, y0, y1, d0, d1):
    sems = pltpu.SemaphoreType.DMA((n,))
    cross_sems = pltpu.SemaphoreType.DMA((2 * n + 3,))
    small_sems = pltpu.SemaphoreType.DMA((2 * shards - 1,))
    tile = small.shape[2:]
    half = w1.shape[1:]
    gathered_w = ((n,) + half, BF16, n)
    return call(
        functools.partial(finish_kernel, n, shards), "finish", 8, 48,
        [g0, w0, out0, w1, small, g1, out1, y0, y1, d0, d1],
        [
            (g1.shape, BF16, n),
            gathered_w,
            (out0.shape, BF16, 1),
            (g1.shape, BF16, n),
            gathered_w,
            (out0.shape, BF16, 1),
            (tile, F32, 1),
            ((2,) + y0.shape, BF16, 1),
            ((2,) + d0.shape, F32, 1),
        ],
        [
            pltpu.VMEM((2 * shards - 1,) + tile, F32),
            pltpu.VMEM((n,) + tile, F32),
            *way_sems(n),
            *way_sems(n),
            cross_sems, cross_sems, small_sems, small_sems, sems, sems,
            *reduce_scratch(shards, half),
            *sum_scratch(n, *out0.shape),
        ],
        lambda: cores_and_rows(shards) + others("seq", n),
    )


def assemble_kernel(n, shards, ins, outs):
    g0, other_g, g1, w0, other_w, w1, out0, other_out, out1 = ins
    down, up, out, *qkv = outs
    first = lax.axis_index("section") == 0
    quarter = other_w.ref.shape[1]
    hw = other_w.ref.shape[2] // 3
    kept = 2 * quarter
    for t in range(n):
        for late in ins[:6]:
            late.get(t)
        for half in range(2):
            if half == 0:
                g = jnp.where(first, g0.ref[t], other_g.ref[t]).astype(F32)
                w = jnp.where(first, w0.ref[t], other_w.ref[t]).astype(F32)
            else:
                g = jnp.where(first, other_g.ref[t], g1.ref[t]).astype(F32)
                w = jnp.where(first, other_w.ref[t], w1.ref[t]).astype(F32)
            rows = slice(half * quarter, (half + 1) * quarter)
            down.ref[t * kept + half * quarter : t * kept + (half + 1) * quarter, :] = g[:quarter]
            for z in range(shards):
                at = (z * n + t) * kept
                up.ref[rows, at : at + kept] = g[quarter : 2 * quarter, z * kept : (z + 1) * kept]
            for i, grad in enumerate(qkv):
                grad.ref[rows, t * hw : (t + 1) * hw] = w[:, i * hw : (i + 1) * hw]
        down.flush(pl.ds(t * kept, kept))
        for z in range(shards):
            up.flush(slice(None), pl.ds((z * n + t) * kept, kept))
        for grad in qkv:
            grad.flush(slice(None), pl.ds(t * hw, hw))
    out.ref[:quarter, :] = jnp.where(first, out0.get()[...], other_out.get()[...]).astype(F32)
    out.ref[quarter:, :] = jnp.where(first, other_out.ref[...], out1.get()[...]).astype(F32)


def assemble(n, shards, g0, g1, other_g, w0, w1, other_w, out0, out1, other_out):
    quarter = other_w.shape[1]
    model = other_g.shape[2]
    hw = other_w.shape[2] // 3
    kept = 2 * quarter
    return call(
        functools.partial(assemble_kernel, n, shards), "assemble", None, 8,
        [Slots(array) for array in (g0, other_g, g1, w0, other_w, w1)] + [out0, other_out, out1],
        [
            ((n * kept, model), F32, n),
            ((2 * quarter, n * shards * kept), F32, n * shards),
            ((2 * quarter, model), F32, 1),
        ]
        + [((2 * quarter, n * hw), F32, n)] * 3,
        [],
    )


def swapped(value):
    return lax.ppermute(value, "section", [(0, 1), (1, 0)])


def body(inputs, cotangent, segments, buckets, query_weight, key_weight, value_weight, out_weight,
         up_weight, down_weight, attn_gain, ffn_gain, bias_table):
    first = lax.axis_index("section") == 0
    turn = lax.axis_index("seq")
    n = lax.axis_size("seq")
    shards = lax.axis_size("dp")
    depth, width = query_weight.shape[1:]
    ff = up_weight.shape[2]
    heads = bias_table.shape[2]
    hw = width // n
    dk = hw // heads
    kept = down_weight.shape[1] // n
    hidden = ff // n
    model = inputs.shape[-1]
    quarter = model // (2 * shards)
    packed = hidden == model == width

    x_in = jnp.where(first, inputs[0, 0], inputs[1, 0])
    d_out = jnp.where(first, cotangent[0, 0], cotangent[1, 0])
    seg = jnp.where(first, segments[0, 0], segments[1, 0])

    wide = max(hw, LANES)

    def pad(value):
        return value if hw == wide else jnp.pad(value, [(0, 0)] * (value.ndim - 1) + [(0, wide - hw)])

    def columns(weight):
        return pad(lax.dynamic_slice_in_dim(weight[0], turn * hw, hw, axis=1))

    own_qkv = jnp.concatenate([columns(query_weight), columns(key_weight), columns(value_weight)], axis=1)
    own_up = jnp.concatenate(
        [
            lax.dynamic_slice_in_dim(up_weight[0], (z * n + turn) * kept, kept, axis=1)
            for z in range(shards)
        ],
        axis=1,
    )
    own_down = lax.dynamic_slice_in_dim(down_weight[0], turn * kept, kept, axis=0)
    table = bias_table[0]

    def halves(own):
        rows = own.shape[0] // 2
        low, high = own[:rows], own[rows:]
        other = swapped(jnp.where(first, high, low))
        return jnp.where(first, low, other), jnp.where(first, other, high)

    def gathered(piece):
        return lax.all_gather(piece, ("dp", "section"), axis=0, tiled=True)

    qkv_halves = halves(own_qkv)
    out_halves = halves(out_weight[0])
    up_halves = halves(own_up)
    down_halves = halves(own_down)
    cols = model // n
    out_cols = lax.dynamic_slice_in_dim(out_halves[0], turn * cols, cols, axis=1)
    first_qkv = gathered(qkv_halves[0])

    def packed_gather(pieces):
        return lax.all_gather(jnp.stack(pieces), ("dp", "section"), axis=0, tiled=False)

    if packed:
        mix_weights = [[packed_gather((up_halves[0], down_halves[0]))]]
    else:
        mix_weights = [[gathered(up_halves[0]), gathered(down_halves[0])]]
    second_qkv = gathered(qkv_halves[1])
    pieces = (out_halves[1], up_halves[1], down_halves[1])
    mix_weights.append([packed_gather(pieces)] if packed else [gathered(piece) for piece in pieces])
    other_table = swapped(table)
    tables = (jnp.where(first, table, other_table), jnp.where(first, other_table, table))

    gains = jnp.pad(jnp.stack([attn_gain[0], ffn_gain[0]]), ((0, 14), (0, 0)))
    first_n1, out_cols, *gain_rows = start(n, shards, x_in, gains, out_cols)
    out_cols = out_cols.reshape(width, cols)

    bucket_count = table.shape[0]
    onehot = (buckets[None, :] == jnp.arange(bucket_count, dtype=jnp.int32)[:, None]).astype(F32)
    offset_rows = [
        lax.dot_general(
            t.astype(F32), onehot, (((0,), (0,)), ((), ())), precision=HIGH, preferred_element_type=F32
        )
        for t in tables
    ]

    lanes = jnp.arange(LANES, dtype=jnp.int32) % 64
    same = seg[:, None] == lanes[None, :]
    ext_q = jnp.where((lanes < 8)[None, :] & ~same, NEG, 0.0).astype(BF16)
    ext_k = jnp.where((lanes < 8)[None, :] & same, 1.0, 0.0).astype(BF16)

    def scattered(gr):
        if not packed:
            gr = [jnp.concatenate([part.reshape(2 * shards, -1, model) for part in gr], axis=1)]
        return lax.psum_scatter(
            gr[0].reshape(-1, model), ("dp", "section"), scatter_dimension=0, tiled=True
        )

    qkv0 = jnp.dot(first_n1, first_qkv, preferred_element_type=F32).astype(BF16)
    o0, lse0, back0, out_all = attend(n, heads, dk, qkv0, ext_q, ext_k, offset_rows[0], out_cols)
    mix_weights[0].insert(0, out_all if packed else out_all.transpose(1, 0, 2).reshape(width, model))
    y0, x1, n2, slope, hid = mix(n, hw, hidden, x_in, gain_rows[1], back0, mix_weights[0])
    n1, qkv1 = norm_gather(n, y0, gain_rows[2], second_qkv)
    o1, lse1, back1, d_all = attend(n, heads, dk, qkv1, ext_q, ext_k, offset_rows[1], d_out)
    y_parts, y_own, dx1, do, gr_ffn1, *gr = turn_round(
        n, hw, hidden, y0, gain_rows[3], back1, mix_weights[1], d_all.reshape(-1, model)
    )
    half1 = scattered(gr)
    d_rows1, y1, d_in1, dy, gr_attn1, dn2, half_w1, *gr = back_across(
        n, shards, heads, dk, hidden, qkv1, o1, lse1, ext_q, ext_k, offset_rows[1], y_parts, pad(do), y_own,
        second_qkv, n1, y0, dx1, gain_rows[2], slope, hid, n2, mix_weights[0],
    )
    if packed:
        half0 = lax.psum_scatter(gr[0], "dp", scatter_dimension=0, tiled=True)
    else:
        half0 = scattered(gr)
    d_rows0, all_g1, gr_ffn0, d_in0, w_grad0, gr_attn0, half_out, all_w1, out1 = back_first(
        n, shards, heads, dk, qkv0, o0, lse0, ext_q, ext_k, offset_rows[0], half1,
        dn2, x1, dy, gain_rows[1], back0, mix_weights[0][0],
        first_qkv, first_n1, x_in, gain_rows[0], half_w1,
    )

    cut = model // shards
    small = []
    for gr_attn, gr_ffn, d_rows in ((gr_attn0, gr_ffn0, d_rows0), (gr_attn1, gr_ffn1, d_rows1)):
        gr_table = lax.dot_general(
            onehot, d_rows, (((1,), (1,)), ((), ())), precision=HIGH, preferred_element_type=F32
        )
        flat = gr_table.reshape(shards, -1)
        flat = jnp.pad(flat, ((0, 0), (0, cut - flat.shape[1])))
        tile = jnp.stack([gr_attn.reshape(shards, cut), gr_ffn.reshape(shards, cut), flat], axis=1)
        small.append(jnp.pad(tile, ((0, 0), (0, 5), (0, 0))))
    all_g0, all_w0, out0, other_g, other_w, other_out, sums, section_outputs, input_grads = finish(
        n, shards, jnp.stack(small), half0, half_out, w_grad0, all_g1, out1, all_w1, y0, y1, d_in0, d_in1
    )
    section_outputs, input_grads = section_outputs[None, :, None], input_grads[None, :, None]
    g_attn, g_ffn = sums[0:1], sums[1:2]
    g_table = sums[2, : bucket_count // shards * heads].reshape(1, bucket_count // shards, heads)

    if packed:
        g_down, g_up, g_out, g_query, g_key, g_value = (
            part[None] for part in assemble(
                n, shards, all_g0, all_g1, other_g, all_w0, all_w1, other_w, out0, out1, other_out
            )
        )
    else:
        low, high = jnp.where(first, all_g0, other_g), jnp.where(first, other_g, all_g1)
        sizes = [kept // 2, quarter * hidden // model]
        cuts = [sum(sizes[:i]) for i in range(3)]

        def joined(index):
            return jnp.stack([part[:, cuts[index] : cuts[index + 1]] for part in (low, high)], axis=1)

        g_down = joined(0).astype(F32).reshape(1, n * kept, model)
        whole = joined(1).reshape(n, depth, shards, kept)
        g_up = whole.transpose(1, 2, 0, 3).reshape(1, depth, ff).astype(F32)
        low, high = jnp.where(first, out0, other_out), jnp.where(first, other_out, out1)
        g_out = jnp.concatenate([low, high], axis=0).astype(F32)[None]
        low, high = jnp.where(first, all_w0, other_w), jnp.where(first, other_w, all_w1)
        whole = jnp.stack([low, high], axis=1).reshape(n, depth, 3, wide)[..., :hw]
        g_query, g_key, g_value = (
            whole[:, :, i].transpose(1, 0, 2).reshape(1, depth, width).astype(F32) for i in range(3)
        )

    return (
        section_outputs,
        input_grads,
        g_query,
        g_key,
        g_value,
        g_out,
        g_up,
        g_down,
        g_attn,
        g_ffn,
        g_table,
    )


def solution(mesh):
    return jax.shard_map(
        body,
        mesh=mesh,
        in_specs=(
            P(None, "dp", "seq", None),
            P(None, "dp", "seq", None),
            P(None, "dp", None),
            P(),
            P("section", "dp", None),
            P("section", "dp", None),
            P("section", "dp", None),
            P("section", "dp", None),
            P("section", "dp", None),
            P("section", "dp", None),
            P("section", "dp"),
            P("section", "dp"),
            P("section", None, "seq"),
        ),
        out_specs=(
            P("section", None, "dp", "seq", None),
            P("section", None, "dp", "seq", None),
            P("section", "dp", None),
            P("section", "dp", None),
            P("section", "dp", None),
            P("section", "dp", None),
            P("section", "dp", None),
            P("section", "dp", None),
            P("section", "dp"),
            P("section", "dp"),
            P("section", "dp", "seq"),
        ),
        check_vma=False,
    )
```
